128 devices in a mesh: seq: 32 (over z, y, core), mp: 4 (over x).
Axes of the slice: x: 4, y: 4, z: 4, core: 2. Of those that a mesh axis runs over, the one named last changes fastest.
Arguments:
- tokens: bfloat16 [2, 8192, 1792], P(None, 'seq'), may hold values from -6 to 6
- cotangent: bfloat16 [2, 8192, 1792], P(None, 'seq'), may hold values from -6 to 6
- lengths: int32 [2], replicated, may hold values from 2048 to 8192, as said below
- rate_codes: int32 [16], P('mp'), may hold values from 8 to 47
- inproj: float32 [1792, 2320], P('seq', 'mp'), may hold values from -0.125 to 0.125
- inproj_first: float32 [1792, 2320], P('seq', 'mp'), may hold values from -384 to 384
- inproj_second: float32 [1792, 2320], P('seq', 'mp'), may hold values from 4096 to 16384
- outproj: float32 [1792, 1792], P('mp', 'seq'), may hold values from -0.5 to 0.5
- outproj_first: float32 [1792, 1792], P('mp', 'seq'), may hold values from -384 to 384
- outproj_second: float32 [1792, 1792], P('mp', 'seq'), may hold values from 4096 to 16384
- gateproj: float32 [1792, 4864], P('seq', 'mp'), may hold values from -0.125 to 0.125
- gateproj_first: float32 [1792, 4864], P('seq', 'mp'), may hold values from -384 to 384
- gateproj_second: float32 [1792, 4864], P('seq', 'mp'), may hold values from 4096 to 16384
- upproj: float32 [1792, 4864], P('seq', 'mp'), may hold values from -0.125 to 0.125
- upproj_first: float32 [1792, 4864], P('seq', 'mp'), may hold values from -384 to 384
- upproj_second: float32 [1792, 4864], P('seq', 'mp'), may hold values from 4096 to 16384
- downproj: float32 [4864, 1792], P('mp', 'seq'), may hold values from -0.078125 to 0.078125
- downproj_first: float32 [4864, 1792], P('mp', 'seq'), may hold values from -384 to 384
- downproj_second: float32 [4864, 1792], P('mp', 'seq'), may hold values from 4096 to 16384
- convtaps: float32 [3, 1792], P(None, ('mp', 'seq')), may hold values from -3 to 3
- convtaps_first: float32 [3, 1792], P(None, ('mp', 'seq')), may hold values from -384 to 384
- convtaps_second: float32 [3, 1792], P(None, ('mp', 'seq')), may hold values from 4096 to 16384
- normgains: float32 [2, 1792], P(None, 'seq'), may hold values from 0.5 to 1.5
- normgains_first: float32 [2, 1792], P(None, 'seq'), may hold values from -384 to 384
- normgains_second: float32 [2, 1792], P(None, 'seq'), may hold values from 4096 to 16384
Outputs:
- block_out: bfloat16 [2, 8192, 1792], P(None, 'seq')
- token_grad: bfloat16 [2, 8192, 1792], P(None, 'seq')
- updated_inproj: float32 [1792, 2320], P('seq', 'mp')
- newmoment_inproj: float32 [1792, 2320], P('seq', 'mp')
- newsquare_inproj: float32 [1792, 2320], P('seq', 'mp')
- updated_outproj: float32 [1792, 1792], P('mp', 'seq')
- newmoment_outproj: float32 [1792, 1792], P('mp', 'seq')
- newsquare_outproj: float32 [1792, 1792], P('mp', 'seq')
- updated_gateproj: float32 [1792, 4864], P('seq', 'mp')
- newmoment_gateproj: float32 [1792, 4864], P('seq', 'mp')
- newsquare_gateproj: float32 [1792, 4864], P('seq', 'mp')
- updated_upproj: float32 [1792, 4864], P('seq', 'mp')
- newmoment_upproj: float32 [1792, 4864], P('seq', 'mp')
- newsquare_upproj: float32 [1792, 4864], P('seq', 'mp')
- updated_downproj: float32 [4864, 1792], P('mp', 'seq')
- newmoment_downproj: float32 [4864, 1792], P('mp', 'seq')
- newsquare_downproj: float32 [4864, 1792], P('mp', 'seq')
- updated_convtaps: float32 [3, 1792], P(None, ('mp', 'seq'))
- newmoment_convtaps: float32 [3, 1792], P(None, ('mp', 'seq'))
- newsquare_convtaps: float32 [3, 1792], P(None, ('mp', 'seq'))
- updated_normgains: float32 [2, 1792], P(None, 'seq')
- newmoment_normgains: float32 [2, 1792], P(None, 'seq')
- newsquare_normgains: float32 [2, 1792], P(None, 'seq')
- lamb_norms: float32 [7, 2], replicated
The draws below stay inside these ranges and needn't reach their ends.
Inputs may be any that keep to these rules, and one draw needn't show every extreme that they name: Each of the 2 lengths lies between 2048 and 8192; at least one sequence fills all 8192 slots.
All inputs are finite; a program needn't handle non-finite values.
Results may differ from the reference program's by a relative error of at most 0.0095.
The reference program's roundings to bfloat16 on the way count: a program that leaves them out, or rounds other values in their place, can miss the bound.
Values may be sent and summed in bfloat16 or wider, within the bound.
No kernel may reach another device: no remote copies, remote signals or barrier semaphores. Data moves between devices by JAX's collectives and lax.ppermute only.
A program may use at most 256 MiB of HBM per device.

```python
import math
import jax
import jax.numpy as jnp
from jax import lax

D = 1792
H = 16
DH = 112
FEAT = 16
FF = 4864
TAPS = 3
STEP = 7
NSEQ = 2
SEQ_CAP = 8192
GROUP = 256
NFEAT = 273
IN_COLS = 2320


def draw_lengths(key, part):
    key = jax.random.fold_in(key, 11)
    length_key, pick_key = jax.random.split(key)
    drawn_lengths = jax.random.randint(length_key, (NSEQ,), SEQ_CAP // 4, SEQ_CAP + 1)
    chosen_index = jax.random.randint(pick_key, (), 0, NSEQ)
    return jnp.where(jnp.arange(NSEQ) == chosen_index, SEQ_CAP, drawn_lengths).astype(jnp.int32)


def with_ends(values, stream_key, smallest, top_value):
    dims = values.shape
    index_at = [jax.random.randint(jax.random.fold_in(stream_key, axis), (), 0, dims[axis]) for axis in range(len(dims))]
    values = values.at[tuple(index_at)].set(smallest)
    longest = dims.index(max(dims))
    index_at[longest] = (index_at[longest] + 1) % dims[longest]
    return values.at[tuple(index_at)].set(top_value)


def shard_levels(stream_key, shape, cuts, low, largest):
    def one(dim, shards_of):
        draws = jax.random.uniform(jax.random.fold_in(jax.random.fold_in(stream_key, 6), dim), (shards_of,), jnp.float32, low / len(cuts), largest / len(cuts))
        return jnp.repeat(jnp.exp(draws), shape[dim] // shards_of).reshape((-1,) + (1,) * (len(shape) - dim - 1))

    gain = one(*cuts[0])
    for cut in cuts[1:]:
        gain = gain * one(*cut)
    return gain


def scatter_about(own_key, dims, spread, bound, cuts=(), kind=jnp.bfloat16):
    factor_of = shard_levels(own_key, dims, cuts, -0.22, 0.18) if cuts else 1.0
    drawn = jax.random.normal(own_key, dims, jnp.float32) * spread * factor_of
    return jnp.minimum(jnp.maximum(drawn, -bound), bound).astype(kind)


def setup_inputs(seed: int = 0) -> dict:
    arg_keys = jax.random.split(jax.random.key(seed), 26)
    return {
        "tokens": scatter_about(arg_keys[0], (NSEQ, SEQ_CAP, D), 1.0, 6.0, ((1, 32),)),
        "cotangent": scatter_about(arg_keys[1], (NSEQ, SEQ_CAP, D), 1.0, 6.0, ((1, 32),)),
        "lengths": draw_lengths(jax.random.fold_in(arg_keys[25], 71), 0),
        "rate_codes": with_ends(jax.random.randint(arg_keys[3], (H,), 8, 48), jax.random.fold_in(arg_keys[3], 1), 8, 47).astype(jnp.int32),
        "inproj": scatter_about(arg_keys[4], (D, IN_COLS), D ** -0.5, 0.125, ((0, 32), (1, 4)), jnp.float32),
        "inproj_first": scatter_about(arg_keys[5], (D, IN_COLS), (0.5 * (NSEQ * SEQ_CAP) ** 0.5), 384.0, ((0, 32), (1, 4)), jnp.float32),
        "inproj_second": jnp.clip(jnp.exp(math.log(16384.0) - 1.3862944 * jax.random.uniform(arg_keys[6], (D, IN_COLS), jnp.float32) ** shard_levels(arg_keys[6], (D, IN_COLS), ((0, 32), (1, 4)), -0.2, 0.2)), 4096.0, 16384.0),
        "outproj": scatter_about(arg_keys[7], (H * DH, D), DH ** -0.5, 0.5, ((0, 4), (1, 32)), jnp.float32),
        "outproj_first": scatter_about(arg_keys[8], (H * DH, D), (0.5 * (NSEQ * SEQ_CAP) ** 0.5), 384.0, ((0, 4), (1, 32)), jnp.float32),
        "outproj_second": jnp.clip(jnp.exp(math.log(16384.0) - 1.3862944 * jax.random.uniform(arg_keys[9], (H * DH, D), jnp.float32) ** shard_levels(arg_keys[9], (H * DH, D), ((0, 4), (1, 32)), -0.2, 0.2)), 4096.0, 16384.0),
        "gateproj": scatter_about(arg_keys[10], (D, FF), D ** -0.5, 0.125, ((0, 32), (1, 4)), jnp.float32),
        "gateproj_first": scatter_about(arg_keys[11], (D, FF), (0.5 * (NSEQ * SEQ_CAP) ** 0.5), 384.0, ((0, 32), (1, 4)), jnp.float32),
        "gateproj_second": jnp.clip(jnp.exp(math.log(16384.0) - 1.3862944 * jax.random.uniform(arg_keys[12], (D, FF), jnp.float32) ** shard_levels(arg_keys[12], (D, FF), ((0, 32), (1, 4)), -0.2, 0.2)), 4096.0, 16384.0),
        "upproj": scatter_about(arg_keys[13], (D, FF), D ** -0.5, 0.125, ((0, 32), (1, 4)), jnp.float32),
        "upproj_first": scatter_about(arg_keys[14], (D, FF), (0.5 * (NSEQ * SEQ_CAP) ** 0.5), 384.0, ((0, 32), (1, 4)), jnp.float32),
        "upproj_second": jnp.clip(jnp.exp(math.log(16384.0) - 1.3862944 * jax.random.uniform(arg_keys[15], (D, FF), jnp.float32) ** shard_levels(arg_keys[15], (D, FF), ((0, 32), (1, 4)), -0.2, 0.2)), 4096.0, 16384.0),
        "downproj": scatter_about(arg_keys[16], (FF, D), FF ** -0.5, 0.078125, ((0, 4), (1, 32)), jnp.float32),
        "downproj_first": scatter_about(arg_keys[17], (FF, D), (0.5 * (NSEQ * SEQ_CAP) ** 0.5), 384.0, ((0, 4), (1, 32)), jnp.float32),
        "downproj_second": jnp.clip(jnp.exp(math.log(16384.0) - 1.3862944 * jax.random.uniform(arg_keys[18], (FF, D), jnp.float32) ** shard_levels(arg_keys[18], (FF, D), ((0, 4), (1, 32)), -0.2, 0.2)), 4096.0, 16384.0),
        "convtaps": scatter_about(arg_keys[19], (TAPS, H * DH), 0.6, 3.0, ((1, 128),), jnp.float32),
        "convtaps_first": scatter_about(arg_keys[20], (TAPS, H * DH), (0.5 * (NSEQ * SEQ_CAP) ** 0.5), 384.0, ((1, 128),), jnp.float32),
        "convtaps_second": jnp.clip(jnp.exp(math.log(16384.0) - 1.3862944 * jax.random.uniform(arg_keys[21], (TAPS, H * DH), jnp.float32) ** shard_levels(arg_keys[21], (TAPS, H * DH), ((1, 128),), -0.2, 0.2)), 4096.0, 16384.0),
        "normgains": jnp.clip(1.0 + 0.1 * jax.random.normal(arg_keys[22], (2, D), jnp.float32), 0.5, 1.5),
        "normgains_first": scatter_about(arg_keys[23], (2, D), (0.5 * (NSEQ * SEQ_CAP) ** 0.5), 384.0, ((1, 32),), jnp.float32),
        "normgains_second": jnp.clip(jnp.exp(math.log(16384.0) - 1.3862944 * jax.random.uniform(arg_keys[24], (2, D), jnp.float32) ** shard_levels(arg_keys[24], (2, D), ((1, 32),), -0.2, 0.2)), 4096.0, 16384.0),
    }


@jax.custom_vjp
def low(v):
    return lax.optimization_barrier(v.astype(jnp.bfloat16)).astype(jnp.float32)

@jax.custom_vjp
def low_back(v):
    return v

def low_keep(v):
    return (low(v), None)

def low_pass(kept, grad):
    return (grad,)

def back_keep(v):
    return (v, None)

def back_low(kept, grad):
    return (low(grad),)
low.defvjp(low_keep, low_pass)
low_back.defvjp(back_keep, back_low)
highest = lax.Precision.HIGHEST
root_half = 0.5 ** 0.5
eps_norm = 1e-05
eps_adam = 1e-06
decay_rate = 0.01
learn_rate = 0.3
beta_value = 0.5

def features(scaled):
    count = scaled.shape[-1]
    outer = (scaled[..., :, None] * scaled[..., None, :]).reshape(scaled.shape[:-1] + (count * count,))
    ones = jnp.ones(scaled.shape[:-1] + (1,), scaled.dtype)
    return jnp.concatenate([ones, scaled, outer * root_half], -1)

def block_step(state, pieces):
    query, keys, values, logdec = pieces
    cumul = jnp.cumsum(logdec, axis=1)
    feat_q = features(query * 0.5)
    feat_k = features(keys * 0.5)
    inter = jnp.einsum('bthf,bhfe->bthe', feat_q * jnp.exp(cumul)[..., None], state, precision=highest)
    dots = jnp.einsum('bthd,buhd->bhtu', query, keys, precision=highest) * 0.25
    kernel = 1.0 + dots + 0.5 * dots * dots
    cumh = jnp.moveaxis(cumul, 1, 2)
    diff = cumh[..., :, None] - cumh[..., None, :]
    causal = jnp.tril(jnp.ones((GROUP, GROUP), bool))
    weights = jnp.where(causal, kernel * jnp.exp(jnp.where(causal, diff, 0.0)), 0.0)
    intra = jnp.einsum('bhtu,buhe->bthe', weights, values, precision=highest)
    ending = cumul[:, -1]
    tail = jnp.exp(ending[:, None] - cumul)
    fresh = jnp.einsum('buhf,buhe->bhfe', feat_k * tail[..., None], values, precision=highest)
    state = jnp.exp(ending)[..., None, None] * state + fresh
    return (state, inter + intra)

def split_blocks(array):
    shaped = array.reshape((NSEQ, SEQ_CAP // GROUP, GROUP) + array.shape[2:])
    return jnp.moveaxis(shaped, 1, 0)

def mixer(query, keys, values, logdec):
    start = jnp.zeros((NSEQ, H, NFEAT, DH + 1), jnp.float32)
    pieces = (split_blocks(query), split_blocks(keys), split_blocks(values), split_blocks(logdec))
    final_state, outputs = lax.scan(jax.checkpoint(block_step), start, pieces)
    return jnp.moveaxis(outputs, 0, 1).reshape(NSEQ, SEQ_CAP, H, DH + 1)

def rms_scale(rows):
    return lax.rsqrt(lax.optimization_barrier(jnp.mean(rows * rows, -1, keepdims=True)) + eps_norm)

def forward(tokens, inproj, outproj, gateproj, upproj, downproj, convtaps, normgains, rates, keep):
    flat = tokens.reshape(-1, D)
    gains = low(normgains)
    normed_one = low(flat * rms_scale(flat) * gains[0])
    proj = low_back(jnp.dot(normed_one, low(inproj), precision=highest))
    proj = proj.reshape(NSEQ, SEQ_CAP, H, 2 * FEAT + DH + 1)
    query = proj[..., :FEAT]
    keys = proj[..., FEAT:2 * FEAT]
    raw = proj[..., 2 * FEAT:2 * FEAT + DH]
    gate = proj[..., 2 * FEAT + DH]
    taps = low(convtaps).reshape(TAPS, H, DH)
    conv = taps[0] * raw
    for lag in range(1, TAPS):
        moved = jnp.pad(raw, ((0, 0), (lag, 0), (0, 0), (0, 0)))[:, :SEQ_CAP]
        conv = conv + taps[lag] * moved
    logdec = -rates * jax.nn.softplus(gate)
    values = jnp.concatenate([conv, jnp.ones(conv.shape[:-1] + (1,), conv.dtype)], -1)
    total = mixer(query, keys, values, logdec)
    mixed = low((total[..., :DH] / total[..., DH:]).reshape(-1, H * DH))
    branch = low_back(jnp.dot(mixed, low(outproj), precision=highest))
    middle = flat + branch
    normed_two = low(middle * rms_scale(middle) * gains[1])
    gate_act = low_back(jnp.dot(normed_two, low(gateproj), precision=highest))
    up_act = low_back(jnp.dot(normed_two, low(upproj), precision=highest))
    hidden = low(jax.nn.silu(gate_act) * up_act)
    ffn = low_back(jnp.dot(hidden, low(downproj), precision=highest))
    return (middle + ffn).reshape(NSEQ, SEQ_CAP, D) * keep

def reference(tokens, cotangent, lengths, rate_codes, inproj, inproj_first, inproj_second, outproj, outproj_first, outproj_second, gateproj, gateproj_first, gateproj_second, upproj, upproj_first, upproj_second, downproj, downproj_first, downproj_second, convtaps, convtaps_first, convtaps_second, normgains, normgains_first, normgains_second):
    positions = jnp.arange(SEQ_CAP, dtype=jnp.int32)
    keep = (positions[None, :] < lengths[:, None]).astype(jnp.float32)[..., None]
    rates = jnp.exp2(-rate_codes.astype(jnp.float32) / 4.0)
    params = (inproj, outproj, gateproj, upproj, downproj, convtaps, normgains)
    firsts = (inproj_first, outproj_first, gateproj_first, upproj_first, downproj_first, convtaps_first, normgains_first)
    seconds = (inproj_second, outproj_second, gateproj_second, upproj_second, downproj_second, convtaps_second, normgains_second)

    def wrapped(inputs, w_in, w_out, w_gate, w_up, w_down, w_taps, w_gains):
        return forward(inputs, w_in, w_out, w_gate, w_up, w_down, w_taps, w_gains, rates, keep)
    output, pullback = jax.vjp(wrapped, tokens.astype(jnp.float32), *params)
    grads = pullback(cotangent.astype(jnp.float32))
    fix = 1.0 - beta_value ** STEP
    results = [output.astype(jnp.bfloat16), grads[0].astype(jnp.bfloat16)]
    norm_rows = []
    for index in range(7):
        weight = params[index]
        grad = grads[index + 1]
        moment = beta_value * firsts[index] + (1.0 - beta_value) * grad
        square = beta_value * seconds[index] + (1.0 - beta_value) * grad * grad
        direction = moment / fix / (jnp.sqrt(square / fix) + eps_adam) + decay_rate * weight
        weight_norm = jnp.sqrt(jnp.sum(weight * weight))
        update_norm = jnp.sqrt(jnp.sum(direction * direction))
        results.append(weight - learn_rate * (weight_norm / update_norm) * direction)
        results.append(moment)
        results.append(square)
        norm_rows.append(jnp.stack([weight_norm, update_norm]))
    results.append(jnp.stack(norm_rows))
    return tuple(results)
```

```python
import jax
import jax.numpy as jnp
from jax import lax
from jax.sharding import Mesh
from jax.sharding import PartitionSpec as P

DH = 112
FEAT = 16
TAPS = 3
STEP = 7
LANES = 128
SEQ = ("seq_0", "seq_1", "seq_2")
ALL = ("seq_0", "seq_1", "seq_2", "mp")
MP_SEQ = ("mp", "seq_0", "seq_1", "seq_2")

f32 = jnp.float32
bf16 = jnp.bfloat16
highest = lax.Precision.HIGHEST
root_half = 0.5**0.5
eps_norm = 1e-05
eps_adam = 1e-06
decay_rate = 0.01
learn_rate = 0.3
beta_value = 0.5

UP = [(i, (i + 1) % 4) for i in range(4)]
DOWN = [(i, (i + 3) % 4) for i in range(4)]
SIDE = [(i, i ^ 1) for i in range(4)]
BACK = [(i, 3 - i) for i in range(4)]
SWAP = [(0, 1), (1, 0)]


def shifted(value, axis, steps):
    count = lax.axis_size(axis)
    first, last = (max(0, -steps), min(count, count - steps))
    return lax.ppermute(value, axis, [(source, source + steps) for source in range(first, last)])


def ring_bits():
    place = lax.axis_index("mp")
    high = (place >= 2).astype(jnp.int32)
    return high, jnp.bitwise_xor(high, place % 2), place % 2


def halves(rows, bit):
    count = rows.shape[0] // 2
    kept = lax.dynamic_slice_in_dim(rows, bit * count, count, 0)
    sent = lax.dynamic_slice_in_dim(rows, (1 - bit) * count, count, 0)
    return kept, sent


def joined(mine, theirs, bit):
    return jnp.where(
        bit == 0, jnp.concatenate([mine, theirs], 0), jnp.concatenate([theirs, mine], 0)
    )


def scatter_sum(part):
    high, mixed_bit, low_bit = ring_bits()
    count = part.shape[0] // 2
    keep_a, send_a = halves(part[:count], mixed_bit)
    keep_b, send_b = halves(part[count:], high)
    got_a = lax.ppermute(send_a, "mp", SIDE)
    got_b = lax.ppermute(send_b, "mp", BACK)
    sum_a = (keep_a.astype(f32) + got_a.astype(f32)).astype(bf16)
    sum_b = (keep_b.astype(f32) + got_b.astype(f32)).astype(bf16)
    keep_a, send_a = halves(sum_a, high)
    keep_b, send_b = halves(sum_b, low_bit)
    got_a = lax.ppermute(send_a, "mp", BACK)
    got_b = lax.ppermute(send_b, "mp", SIDE)
    return jnp.concatenate(
        [keep_a.astype(f32) + got_a.astype(f32), keep_b.astype(f32) + got_b.astype(f32)], 0
    )


def gather_rows(own):
    high, mixed_bit, low_bit = ring_bits()
    count = own.shape[0] // 2
    row_a, row_b = own[:count], own[count:]
    got_a = lax.ppermute(row_a, "mp", BACK)
    got_b = lax.ppermute(row_b, "mp", SIDE)
    row_a = joined(row_a, got_a, high)
    row_b = joined(row_b, got_b, low_bit)
    got_a = lax.ppermute(row_a, "mp", SIDE)
    got_b = lax.ppermute(row_b, "mp", BACK)
    return jnp.concatenate([joined(row_a, got_a, mixed_bit), joined(row_b, got_b, high)], 0)


def own_rows(rows):
    high, mixed_bit, low_bit = ring_bits()
    place_a = 2 * mixed_bit + high
    place_b = 2 * high + low_bit
    count = rows.shape[0] // 2
    a = lax.dynamic_slice_in_dim(rows[:count], place_a * (count // 4), count // 4, 0)
    b = lax.dynamic_slice_in_dim(rows[count:], place_b * (count // 4), count // 4, 0)
    return jnp.concatenate([a, b], 0)


def ring_gather(part, axis):
    count = part.shape[0] // 2
    place = lax.axis_index(axis)
    before = lax.ppermute(part, axis, UP)
    after = lax.ppermute(part, axis, DOWN)
    far_a = lax.ppermute(before[:count], axis, UP)
    far_b = lax.ppermute(after[count:], axis, DOWN)
    turned = jnp.stack([part, after, jnp.concatenate([far_a, far_b], 0), before])
    return jnp.roll(turned, place, axis=0)


def seq_gather(part):
    count, width = part.shape
    whole = ring_gather(part, "seq_0").reshape(4 * count, width)
    whole = ring_gather(whole, "seq_1").reshape(4, 4, count, width).transpose(1, 0, 2, 3)
    other = lax.ppermute(whole, "seq_2", SWAP)
    core = lax.axis_index("seq_2")
    both = jnp.where(core == 0, jnp.stack([whole, other], 2), jnp.stack([other, whole], 2))
    return both.reshape(32 * count, width)


def ring_scatter(parts, axis):
    count = parts.shape[1] // 2
    place = lax.axis_index(axis)
    turned = jnp.roll(parts, -place, axis=0)
    far_a = lax.ppermute(turned[2, :count], axis, UP)
    far_b = lax.ppermute(turned[2, count:], axis, DOWN)
    up = jnp.concatenate(
        [(turned[1, :count].astype(f32) + far_a.astype(f32)).astype(bf16), turned[1, count:]], 0
    )
    down = jnp.concatenate(
        [turned[3, :count], (turned[3, count:].astype(f32) + far_b.astype(f32)).astype(bf16)], 0
    )
    got_a = lax.ppermute(up, axis, UP)
    got_b = lax.ppermute(down, axis, DOWN)
    return turned[0].astype(f32) + got_a.astype(f32) + got_b.astype(f32)


def seq_scatter(part):
    rows, width = part.shape
    count = rows // 32
    split = part.reshape(4, 4, 2, count, width)
    core = lax.axis_index("seq_2")
    kept = lax.dynamic_index_in_dim(split, core, 2, False)
    sent = lax.dynamic_index_in_dim(split, 1 - core, 2, False)
    got = lax.ppermute(sent, "seq_2", SWAP)
    both = (kept.astype(f32) + got.astype(f32)).astype(bf16)
    line = ring_scatter(both.reshape(4, 4 * count, width), "seq_0").astype(bf16)
    return ring_scatter(line.reshape(4, count, width), "seq_1")


def split_thrice(value):
    high = value.astype(bf16)
    rest = value - high.astype(f32)
    mid = rest.astype(bf16)
    return jnp.stack([high, mid, (rest - mid.astype(f32)).astype(bf16)], -1)


def to_pieces(state):
    pairs = state.shape[0]
    flat = state.reshape(pairs, -1)
    width = -(-flat.shape[1] // 32)
    flat = jnp.pad(flat, ((0, 0), (0, 32 * width - flat.shape[1])))
    return flat.reshape(pairs, 32, width).transpose(1, 0, 2).astype(bf16)


def from_pieces(pieces, shape):
    flat = pieces.transpose(1, 0, 2).reshape(shape[0], -1)
    return flat[:, : shape[1] * shape[2]].reshape(shape).astype(f32)


def earlier_states(fresh, ending):
    pieces = to_pieces(fresh)
    ends = jnp.broadcast_to(split_thrice(ending)[None], (32,) + ending.shape + (3,))
    sent = jnp.concatenate([pieces, ends], -1)
    got = lax.all_to_all(sent, SEQ, 0, 0, tiled=True)
    width = pieces.shape[-1]
    ends = jnp.sum(got[..., width:].astype(f32), -1)
    total = jnp.cumsum(ends, 0)
    before = (total - ends).T
    order = jnp.arange(32)
    earlier = (order[:, None] > order[None, :])[None]
    log_decay = before[:, :, None] - total.T[:, None, :]
    decay = jnp.where(earlier, jnp.exp(jnp.where(earlier, log_decay, 0.0)), 0.0)
    summed = jnp.einsum(
        "pji,ipn->jpn", decay, got[..., :width].astype(f32), precision=highest
    ).astype(bf16)
    back = lax.all_to_all(summed, SEQ, 0, 0, tiled=True)
    return from_pieces(back, fresh.shape), decay


def later_states(pushed, decay):
    got = lax.all_to_all(to_pieces(pushed), SEQ, 0, 0, tiled=True)
    summed = jnp.einsum("pji,jpn->ipn", decay, got.astype(f32), precision=highest).astype(bf16)
    back = lax.all_to_all(summed, SEQ, 0, 0, tiled=True)
    return from_pieces(back, pushed.shape)


def pair_indices():
    first = [i for i in range(FEAT) for j in range(i, FEAT)]
    second = [j for i in range(FEAT) for j in range(i, FEAT)]
    return first, second


def features(scaled):
    count = scaled.shape[-1]
    outer = (scaled[..., :, None] * scaled[..., None, :]).reshape(
        scaled.shape[:-1] + (count * count,)
    )
    ones = jnp.ones(scaled.shape[:-1] + (1,), scaled.dtype)
    return jnp.concatenate([ones, scaled, outer * root_half], -1)


def features_back(scaled, upstream):
    count = scaled.shape[-1]
    linear = upstream[..., 1 : 1 + count]
    square = upstream[..., 1 + count :].reshape(scaled.shape[:-1] + (count, count)) * root_half
    first_term = jnp.einsum("...ij,...j->...i", square, scaled, precision=highest)
    second_term = jnp.einsum("...ji,...j->...i", square, scaled, precision=highest)
    return linear + first_term + second_term


def norm_backward(upstream, unit, scale, gain):
    weighted = upstream * gain
    return scale * (weighted - unit * jnp.mean(weighted * unit, -1, keepdims=True))


def adapt(weight, moment_old, square_old, grad):
    fix = 1.0 - beta_value**STEP
    moment = beta_value * moment_old + (1.0 - beta_value) * grad
    square = beta_value * square_old + (1.0 - beta_value) * grad * grad
    direction = moment / fix / (jnp.sqrt(square / fix) + eps_adam) + decay_rate * weight
    return (moment, square, direction)


def arranged(shard, heads):
    rows = shard.shape[0]
    split = shard.reshape(rows, heads, 2 * FEAT + DH + 1)
    tiles = jnp.pad(split[..., 2 * FEAT :], ((0, 0), (0, 0), (0, LANES - DH - 1)))
    return jnp.concatenate(
        [
            tiles.reshape(rows, heads * LANES),
            split[..., :FEAT].reshape(rows, heads * FEAT),
            split[..., FEAT : 2 * FEAT].reshape(rows, heads * FEAT),
        ],
        -1,
    )


def rearranged(shard, heads):
    rows = shard.shape[0]
    tiles = shard[:, : heads * LANES].reshape(rows, heads, LANES)
    low = shard[:, heads * LANES :].reshape(rows, 2, heads, FEAT)
    return jnp.concatenate([low[:, 0], low[:, 1], tiles[..., : DH + 1]], -1).reshape(rows, -1)


def padded_heads(shard, heads):
    split = shard.reshape(shard.shape[:-1] + (heads, DH))
    pad = [(0, 0)] * (split.ndim - 1) + [(0, LANES - DH)]
    return jnp.pad(split, pad).reshape(shard.shape[:-1] + (heads * LANES,))


def per_device(
    tokens,
    cotangent,
    lengths,
    rate_codes,
    inproj,
    inproj_first,
    inproj_second,
    outproj,
    outproj_first,
    outproj_second,
    gateproj,
    gateproj_first,
    gateproj_second,
    upproj,
    upproj_first,
    upproj_second,
    downproj,
    downproj_first,
    downproj_second,
    convtaps,
    convtaps_first,
    convtaps_second,
    normgains,
    normgains_first,
    normgains_second,
):
    seqs, group, width = tokens.shape
    heads = rate_codes.shape[0]
    span, feat, lag = DH, FEAT, TAPS - 1
    hidden_units = gateproj.shape[1]
    rank = lax.axis_index(SEQ)

    small = jnp.concatenate(
        [normgains.reshape(-1), convtaps.reshape(-1)]
    ).astype(bf16)
    smalls = lax.all_gather(small, SEQ)
    gains = smalls[:, : normgains.size].reshape(32, 2, -1).transpose(1, 0, 2).reshape(2, width)
    gains = gains.astype(f32)
    taps = smalls[:, normgains.size :].reshape(32, TAPS, -1).transpose(1, 0, 2)
    taps = taps.astype(f32).reshape(TAPS, heads, span)
    w_in = seq_gather(arranged(inproj, heads).astype(bf16))
    rest = jnp.concatenate(
        [padded_heads(outproj.T, heads), gateproj, upproj, downproj.T], 1
    ).astype(bf16)
    rest = lax.all_gather(rest, SEQ, axis=0, tiled=True)
    at = heads * LANES
    w_out = rest[:, :at]
    w_gate = rest[:, at : at + hidden_units]
    w_up = rest[:, at + hidden_units : at + 2 * hidden_units]
    w_down = rest[:, at + 2 * hidden_units :]

    rim_tokens = shifted(tokens[:, group - lag :], SEQ, 1)
    positions = rank * group + jnp.arange(group, dtype=jnp.int32)
    keep = (positions[None, :] < lengths[:, None]).astype(f32).reshape(-1, 1)
    rates = jnp.exp2(-rate_codes.astype(f32) / 4.0)
    rows = tokens.reshape(-1, width)
    both = jnp.concatenate([rows, rim_tokens.reshape(-1, width)], 0).astype(f32)
    scale_both = lax.rsqrt(jnp.mean(both * both, -1, keepdims=True) + eps_norm)
    normed_both = (both * scale_both * gains[0]).astype(bf16)
    normed_one = normed_both[: seqs * group]
    proj_both = jnp.dot(normed_both, w_in, preferred_element_type=f32)
    proj = proj_both[: seqs * group].reshape(seqs, group, -1)
    query = proj[..., at : at + heads * feat].reshape(seqs, group, heads, feat)
    keys = proj[..., at + heads * feat :].reshape(seqs, group, heads, feat)
    tiles = proj[..., :at].reshape(seqs, group, heads, LANES)
    raw = tiles[..., :span]
    gate = tiles[..., span]
    rim = proj_both[seqs * group :, :at].reshape(seqs, lag, heads, LANES)[..., :span]

    extended = jnp.concatenate([rim, raw], 1)
    conv = taps[0] * raw
    for shift_by in range(1, TAPS):
        conv = conv + taps[shift_by] * extended[:, lag - shift_by : lag - shift_by + group]
    logdec = -rates * jax.nn.softplus(gate)
    cumul = jnp.cumsum(logdec, axis=1)
    values = jnp.concatenate([conv, jnp.ones(conv.shape[:-1] + (1,), f32)], -1)
    feat_q = features(query * 0.5)
    feat_k = features(keys * 0.5)
    ending = cumul[:, -1]
    tail = jnp.exp(ending[:, None] - cumul)
    fresh = jnp.einsum("suhf,suhe->shfe", feat_k * tail[..., None], values, precision=highest)
    state_shape = (seqs * heads,) + fresh.shape[2:]
    incoming, decay = earlier_states(fresh.reshape(state_shape), ending.reshape(-1))
    incoming = incoming.reshape(fresh.shape)
    dots = jnp.einsum("sthd,suhd->shtu", query, keys, precision=highest) * 0.25
    kernel = 1.0 + dots + 0.5 * dots * dots
    cumh = jnp.moveaxis(cumul, 1, 2)
    diff = cumh[..., :, None] - cumh[..., None, :]
    causal = jnp.tril(jnp.ones((group, group), bool))
    decayw = jnp.where(causal, jnp.exp(jnp.where(causal, diff, 0.0)), 0.0)
    weights = kernel * decayw
    growth = jnp.exp(cumul)
    inter = jnp.einsum("sthf,shfe->sthe", feat_q * growth[..., None], incoming, precision=highest)
    intra = jnp.einsum("shtu,suhe->sthe", weights, values, precision=highest)
    total = inter + intra
    denom = total[..., span:]
    mixed = total[..., :span] / denom
    mixed_low = padded_heads(mixed.reshape(seqs * group, heads * span), heads).astype(bf16)

    contract = (((1,), (1,)), ((), ()))
    branch = lax.dot_general(mixed_low, w_out, contract, preferred_element_type=f32)
    flat = own_rows(rows).astype(f32)
    middle = flat + scatter_sum(branch.astype(bf16))
    scale_two = lax.rsqrt(jnp.mean(middle * middle, -1, keepdims=True) + eps_norm)
    unit_two = middle * scale_two
    normed_two = gather_rows((unit_two * gains[1]).astype(bf16))

    back = (cotangent.reshape(-1, width).astype(f32) * keep).astype(bf16)
    hidden_back = jnp.dot(back, w_down, preferred_element_type=f32)
    gate_act = jnp.dot(normed_two, w_gate, preferred_element_type=f32)
    up_act = jnp.dot(normed_two, w_up, preferred_element_type=f32)
    sigma = jax.nn.sigmoid(gate_act)
    silu_val = gate_act * sigma
    hidden = (silu_val * up_act).astype(bf16)
    gate_back = (hidden_back * up_act * sigma * (1.0 + gate_act * (1.0 - sigma))).astype(bf16)
    up_back = (hidden_back * silu_val).astype(bf16)
    two_part = lax.dot_general(gate_back, w_gate, contract, preferred_element_type=f32)
    two_part = two_part + lax.dot_general(up_back, w_up, contract, preferred_element_type=f32)
    two_back = scatter_sum(two_part.astype(bf16))
    ffn_part = lax.dot_general(hidden, w_down, contract, preferred_element_type=f32)
    ffn = scatter_sum(ffn_part.astype(bf16))
    block_out = gather_rows(((middle + ffn) * own_rows(keep)).astype(bf16))
    grad_gate = jnp.dot(normed_two.T, gate_back, preferred_element_type=f32).astype(bf16)
    grad_up = jnp.dot(normed_two.T, up_back, preferred_element_type=f32).astype(bf16)
    grad_down = jnp.dot(back.T, hidden, preferred_element_type=f32).astype(bf16)
    ffn_sums = lax.psum_scatter(
        jnp.concatenate([grad_gate, grad_up, grad_down], 1), SEQ, scatter_dimension=0, tiled=True
    ).astype(f32)

    gain_two_grad = jnp.sum(two_back * unit_two, 0)
    middle_back = own_rows(back).astype(f32) + norm_backward(
        two_back, unit_two, scale_two, gains[1]
    )
    out_back = gather_rows(middle_back.astype(bf16))
    grad_out = jnp.dot(out_back.T, mixed_low, preferred_element_type=f32).astype(bf16)

    mixed_back = jnp.dot(out_back, w_out, preferred_element_type=f32)
    mixed_back = mixed_back.reshape(seqs, group, heads, LANES)[..., :span]
    numer_back = mixed_back / denom
    denom_back = -jnp.sum(mixed_back * mixed, -1, keepdims=True) / denom
    total_back = jnp.concatenate([numer_back, denom_back], -1)
    pushed = jnp.einsum(
        "sthf,sthe->shfe", feat_q * growth[..., None], total_back, precision=highest
    )
    outgoing = later_states(pushed.reshape(state_shape), decay).reshape(pushed.shape)
    fq_back = growth[..., None] * jnp.einsum(
        "shfe,sthe->sthf", incoming, total_back, precision=highest
    )
    level_back = jnp.sum(feat_q * fq_back, -1)
    pairing = jnp.einsum("sthe,suhe->shtu", total_back, values, precision=highest)
    moved = weights * pairing
    level_back = (
        level_back + jnp.moveaxis(jnp.sum(moved, -1), 1, 2) - jnp.moveaxis(jnp.sum(moved, -2), 1, 2)
    )
    kernel_back = decayw * pairing * (1.0 + dots) * 0.25
    query_back = jnp.einsum("shtu,suhd->sthd", kernel_back, keys, precision=highest)
    keys_back = jnp.einsum("shtu,sthd->suhd", kernel_back, query, precision=highest)
    values_back = jnp.einsum("shtu,sthe->suhe", weights, total_back, precision=highest)
    fk_back = tail[..., None] * jnp.einsum("shfe,suhe->suhf", outgoing, values, precision=highest)
    values_back = values_back + tail[..., None] * jnp.einsum(
        "suhf,shfe->suhe", feat_k, outgoing, precision=highest
    )
    level_back = level_back - jnp.sum(feat_k * fk_back, -1)
    state_end = jnp.exp(ending)[..., None, None] * incoming + fresh
    end_back = jnp.sum(outgoing * state_end, (-2, -1))
    lastrow = (jnp.arange(group) == group - 1).astype(f32)[None, :, None]
    level_back = level_back + lastrow * end_back[:, None, :]
    step_back = jnp.flip(jnp.cumsum(jnp.flip(level_back, 1), 1), 1)
    gate_grad = step_back * -rates * jax.nn.sigmoid(gate)
    query_back = query_back + 0.5 * features_back(query * 0.5, fq_back)
    keys_back = keys_back + 0.5 * features_back(keys * 0.5, fk_back)
    conv_back = values_back[..., :span]
    ahead = shifted(conv_back[:, :lag], SEQ, -1)
    conv_ext = jnp.concatenate([conv_back, ahead], 1)
    raw_back = taps[0] * conv_back
    tap_rows = [jnp.sum(raw * conv_back, (0, 1))]
    for shift_by in range(1, TAPS):
        raw_back = raw_back + taps[shift_by] * conv_ext[:, shift_by : shift_by + group]
        tap_rows.append(
            jnp.sum(extended[:, lag - shift_by : lag - shift_by + group] * conv_back, (0, 1))
        )
    taps_grad = jnp.stack(tap_rows).reshape(TAPS, heads * span)
    tile_back = jnp.pad(
        jnp.concatenate([raw_back, gate_grad[..., None]], -1),
        ((0, 0), (0, 0), (0, 0), (0, LANES - span - 1)),
    ).reshape(seqs * group, at)
    proj_back = jnp.concatenate(
        [
            tile_back,
            query_back.reshape(seqs * group, heads * feat),
            keys_back.reshape(seqs * group, heads * feat),
        ],
        -1,
    ).astype(bf16)

    one_part = lax.dot_general(proj_back, w_in, contract, preferred_element_type=f32)
    one_back = scatter_sum(one_part.astype(bf16))
    grad_in = jnp.dot(normed_one.T, proj_back, preferred_element_type=f32).astype(bf16)
    mixer_sums = seq_scatter(jnp.concatenate([grad_in, grad_out], 1))
    scale_one = lax.rsqrt(jnp.mean(flat * flat, -1, keepdims=True) + eps_norm)
    unit_one = flat * scale_one
    gain_one_grad = jnp.sum(one_back * unit_one, 0)
    token_back = middle_back + norm_backward(one_back, unit_one, scale_one, gains[0])
    token_grad = gather_rows(token_back.astype(bf16))

    peers = lax.axis_size("mp")
    gains_grad = jnp.stack([gain_one_grad, gain_two_grad]).reshape(2, 32, 1, -1)
    gains_sent = jnp.broadcast_to(
        gains_grad.transpose(1, 2, 0, 3), (32, peers, 2, width // 32)
    ).reshape(32, peers, -1)
    taps_sent = taps_grad.reshape(TAPS, 32, 1, -1).transpose(1, 2, 0, 3).reshape(32, 1, -1)
    to_own = (jnp.arange(peers) == lax.axis_index("mp")).astype(f32)[None, :, None]
    small_sent = jnp.concatenate([gains_sent, taps_sent * to_own], -1)
    small_got = lax.all_to_all(
        small_sent.reshape(32 * peers, -1), ALL, 0, 0, tiled=True
    )
    small_sum = jnp.sum(small_got, 0)
    summed_gains = small_sum[: normgains.size].reshape(normgains.shape)
    summed_taps = small_sum[normgains.size :].reshape(convtaps.shape)

    summed_in = rearranged(mixer_sums[:, : at + 2 * heads * feat], heads)
    out_tiles = mixer_sums[:, at + 2 * heads * feat :].reshape(-1, heads, LANES)[..., :span]
    summed_out = out_tiles.reshape(-1, heads * span).T
    summed_gate = ffn_sums[:, :hidden_units]
    summed_up = ffn_sums[:, hidden_units : 2 * hidden_units]
    summed_down = ffn_sums[:, 2 * hidden_units :].T
    params = (inproj, outproj, gateproj, upproj, downproj, convtaps, normgains)
    firsts = (
        inproj_first,
        outproj_first,
        gateproj_first,
        upproj_first,
        downproj_first,
        convtaps_first,
        normgains_first,
    )
    seconds = (
        inproj_second,
        outproj_second,
        gateproj_second,
        upproj_second,
        downproj_second,
        convtaps_second,
        normgains_second,
    )
    summed = (summed_in, summed_out, summed_gate, summed_up, summed_down, summed_taps, summed_gains)
    states = []
    square_rows = []
    for index in range(7):
        moment, square, direction = adapt(
            params[index], firsts[index], seconds[index], summed[index]
        )
        states.append((moment, square, direction))
        share = 1.0 / peers if index == 6 else 1.0
        square_rows.append(
            jnp.stack([jnp.sum(params[index] * params[index]), jnp.sum(direction * direction)])
            * share
        )
    square_rows = jnp.stack(square_rows).reshape(1, 14)
    totals = lax.all_to_all(
        jnp.broadcast_to(square_rows, (32 * peers, 14)), ALL, 0, 0, tiled=True
    )
    norms = jnp.sqrt(jnp.sum(totals, 0)).reshape(7, 2)
    results = [block_out.reshape(tokens.shape), token_grad.reshape(tokens.shape)]
    for index in range(7):
        moment, square, direction = states[index]
        results.append(params[index] - learn_rate * (norms[index, 0] / norms[index, 1]) * direction)
        results.append(moment)
        results.append(square)
    results.append(norms)
    return tuple(results)


def solution(mesh):
    split = Mesh(mesh.devices.reshape(4, 4, 2, mesh.shape["mp"]), ("seq_0", "seq_1", "seq_2", "mp"))
    in_specs = (
        P(None, SEQ, None),
        P(None, SEQ, None),
        P(),
        P("mp"),
        P(SEQ, "mp"),
        P(SEQ, "mp"),
        P(SEQ, "mp"),
        P("mp", SEQ),
        P("mp", SEQ),
        P("mp", SEQ),
        P(SEQ, "mp"),
        P(SEQ, "mp"),
        P(SEQ, "mp"),
        P(SEQ, "mp"),
        P(SEQ, "mp"),
        P(SEQ, "mp"),
        P("mp", SEQ),
        P("mp", SEQ),
        P("mp", SEQ),
        P(None, MP_SEQ),
        P(None, MP_SEQ),
        P(None, MP_SEQ),
        P(None, SEQ),
        P(None, SEQ),
        P(None, SEQ),
    )
    out_specs = (
        P(None, SEQ, None),
        P(None, SEQ, None),
        P(SEQ, "mp"),
        P(SEQ, "mp"),
        P(SEQ, "mp"),
        P("mp", SEQ),
        P("mp", SEQ),
        P("mp", SEQ),
        P(SEQ, "mp"),
        P(SEQ, "mp"),
        P(SEQ, "mp"),
        P(SEQ, "mp"),
        P(SEQ, "mp"),
        P(SEQ, "mp"),
        P("mp", SEQ),
        P("mp", SEQ),
        P("mp", SEQ),
        P(None, MP_SEQ),
        P(None, MP_SEQ),
        P(None, MP_SEQ),
        P(None, SEQ),
        P(None, SEQ),
        P(None, SEQ),
        P(),
    )
    return jax.shard_map(
        per_device, mesh=split, in_specs=in_specs, out_specs=out_specs, check_vma=False
    )
```

```python
import math

import jax
import jax.numpy as jnp
from jax import lax
from jax.experimental import pallas as pl
from jax.experimental.pallas import tpu as pltpu
from jax.sharding import Mesh
from jax.sharding import PartitionSpec as P

DH = 112
FEAT = 16
TAPS = 3
STEP = 7
LANES = 128
SEQ = ("seq_0", "seq_1", "seq_2")
ALL = ("seq_0", "seq_1", "seq_2", "mp")
MP_SEQ = ("mp", "seq_0", "seq_1", "seq_2")

f32 = jnp.float32
bf16 = jnp.bfloat16
highest = lax.Precision.HIGHEST
root_half = 0.5**0.5
eps_norm = 1e-05
eps_adam = 1e-06
decay_rate = 0.01
learn_rate = 0.3
beta_value = 0.5

UP = [(i, (i + 1) % 4) for i in range(4)]
DOWN = [(i, (i + 3) % 4) for i in range(4)]
SIDE = [(i, i ^ 1) for i in range(4)]
BACK = [(i, 3 - i) for i in range(4)]
SWAP = [(0, 1), (1, 0)]


def shifted(value, axis, steps):
    count = lax.axis_size(axis)
    first, last = (max(0, -steps), min(count, count - steps))
    return lax.ppermute(value, axis, [(source, source + steps) for source in range(first, last)])


def ring_bits():
    place = lax.axis_index("mp")
    high = (place >= 2).astype(jnp.int32)
    return high, jnp.bitwise_xor(high, place % 2), place % 2


def halves(rows, bit):
    count = rows.shape[0] // 2
    kept = lax.dynamic_slice_in_dim(rows, bit * count, count, 0)
    sent = lax.dynamic_slice_in_dim(rows, (1 - bit) * count, count, 0)
    return kept, sent


def joined(mine, theirs, bit):
    return jnp.where(
        bit == 0, jnp.concatenate([mine, theirs], 0), jnp.concatenate([theirs, mine], 0)
    )


def scatter_sum(part):
    high, mixed_bit, low_bit = ring_bits()
    count = part.shape[0] // 2
    keep_a, send_a = halves(part[:count], mixed_bit)
    keep_b, send_b = halves(part[count:], high)
    got_a = lax.ppermute(send_a, "mp", SIDE)
    got_b = lax.ppermute(send_b, "mp", BACK)
    sum_a = (keep_a.astype(f32) + got_a.astype(f32)).astype(bf16)
    sum_b = (keep_b.astype(f32) + got_b.astype(f32)).astype(bf16)
    keep_a, send_a = halves(sum_a, high)
    keep_b, send_b = halves(sum_b, low_bit)
    got_a = lax.ppermute(send_a, "mp", BACK)
    got_b = lax.ppermute(send_b, "mp", SIDE)
    return jnp.concatenate(
        [keep_a.astype(f32) + got_a.astype(f32), keep_b.astype(f32) + got_b.astype(f32)], 0
    )


def gather_rows(own):
    high, mixed_bit, low_bit = ring_bits()
    count = own.shape[0] // 2
    row_a, row_b = own[:count], own[count:]
    got_a = lax.ppermute(row_a, "mp", BACK)
    got_b = lax.ppermute(row_b, "mp", SIDE)
    row_a = joined(row_a, got_a, high)
    row_b = joined(row_b, got_b, low_bit)
    got_a = lax.ppermute(row_a, "mp", SIDE)
    got_b = lax.ppermute(row_b, "mp", BACK)
    return jnp.concatenate([joined(row_a, got_a, mixed_bit), joined(row_b, got_b, high)], 0)


def own_rows(rows):
    high, mixed_bit, low_bit = ring_bits()
    place_a = 2 * mixed_bit + high
    place_b = 2 * high + low_bit
    count = rows.shape[0] // 2
    a = lax.dynamic_slice_in_dim(rows[:count], place_a * (count // 4), count // 4, 0)
    b = lax.dynamic_slice_in_dim(rows[count:], place_b * (count // 4), count // 4, 0)
    return jnp.concatenate([a, b], 0)


def ring_scatter(parts, axis):
    count = parts.shape[1] // 2
    place = lax.axis_index(axis)
    turned = jnp.roll(parts, -place, axis=0)
    far_a = lax.ppermute(turned[2, :count], axis, UP)
    far_b = lax.ppermute(turned[2, count:], axis, DOWN)
    up = jnp.concatenate(
        [(turned[1, :count].astype(f32) + far_a.astype(f32)).astype(bf16), turned[1, count:]], 0
    )
    down = jnp.concatenate(
        [turned[3, :count], (turned[3, count:].astype(f32) + far_b.astype(f32)).astype(bf16)], 0
    )
    got_a = lax.ppermute(up, axis, UP)
    got_b = lax.ppermute(down, axis, DOWN)
    return turned[0].astype(f32) + got_a.astype(f32) + got_b.astype(f32)


def seq_scatter(part):
    rows, width = part.shape
    count = rows // 32
    split = part.reshape(4, 4, 2, count, width)
    core = lax.axis_index("seq_2")
    kept = lax.dynamic_index_in_dim(split, core, 2, False)
    sent = lax.dynamic_index_in_dim(split, 1 - core, 2, False)
    got = lax.ppermute(sent, "seq_2", SWAP)
    both = (kept.astype(f32) + got.astype(f32)).astype(bf16)
    line = ring_scatter(both.reshape(4, 4 * count, width), "seq_0").astype(bf16)
    return ring_scatter(line.reshape(4, count, width), "seq_1")


def norm_backward(upstream, unit, scale, gain):
    weighted = upstream * gain
    return scale * (weighted - unit * jnp.mean(weighted * unit, -1, keepdims=True))


SPAN_LANE = DH
GATE_LANE = DH
GAIN_LANE = DH + 4
GROUP = 256
ROWS = 512
SIDES = 256
PIECE = 40
SLOT = 48
PIECES = 32
MIB = 1 << 20


def selections():
    import numpy as np

    pick = np.zeros((2 * LANES, 2 * SIDES), np.float32)
    ends = np.zeros((8, SIDES), np.float32)
    ends[0, 0] = ends[1, 0] = ends[2, 0] = 1.0
    lane = 1
    for i in range(FEAT):
        pick[i, lane] = 0.5
        ends[1, lane] = ends[2, lane] = 1.0
        lane += 1
    for i in range(FEAT):
        for j in range(i, FEAT):
            pick[i, lane] = 0.5
            pick[j, SIDES + lane] = 0.5
            ends[2, lane] = root_half if i == j else 1.0
            lane += 1
    pick[LANES:] = pick[:LANES]
    return jnp.asarray(pick, bf16), jnp.asarray(ends)


def two_parts(value):
    high = value.astype(bf16)
    return high, (value - high.astype(f32)).astype(bf16)


def product(a, b, contract, passes=3):
    dims = (contract, ((), ()))

    def once(x, y):
        return lax.dot_general(x, y, dims, preferred_element_type=f32)

    if passes == 1:
        return once(a.astype(bf16), b.astype(bf16))
    a_high, a_low = two_parts(a)
    if passes == 2:
        b = b.astype(bf16)
        return once(a_high, b) + once(a_low, b)
    b_high, b_low = two_parts(b)
    return once(a_high, b_high) + (once(a_high, b_low) + once(a_low, b_high))


NN = ((1,), (0,))
NT = ((1,), (1,))
TN = ((0,), (0,))


def lanes_of(shape):
    return lax.broadcasted_iota(jnp.int32, shape, len(shape) - 1)


def rows_of(shape):
    return lax.broadcasted_iota(jnp.int32, shape, 0)


def lower_ones(strict=False):
    row, lane = rows_of((GROUP, GROUP)), lanes_of((GROUP, GROUP))
    return jnp.where(row > lane if strict else row >= lane, 1.0, 0.0).astype(bf16)


def summed_down(ones, value, contract):
    dims = (contract, ((), ()))
    high = value.astype(bf16)
    rest = value - high.astype(f32)
    mid = rest.astype(bf16)
    low = (rest - mid.astype(f32)).astype(bf16)
    parts = [lax.dot_general(ones, part, dims, preferred_element_type=f32) for part in (low, mid, high)]
    return parts[0] + parts[1] + parts[2]


def head_lanes(tile, head, keys):
    first = (4 if keys else 0) * FEAT + head * FEAT
    return pltpu.roll(tile, (LANES - first) % LANES, 1) if first else tile


def factors(moved, pick, ends):
    high, low = two_parts(moved)
    found = lax.dot_general(
        jnp.concatenate([high, low], 1), pick, (NN, ((), ())), preferred_element_type=f32
    )
    return found[:, :SIDES] + ends[0:1], found[:, SIDES:] + ends[1:2]


def factors_back(upstream, one, two, pick, ends):
    scaled = upstream * ends[2:3]
    both = jnp.concatenate([scaled * two, scaled * one], 1)
    return product(both, pick[:LANES], NT, 2)


def scores(tile, head):
    only = lanes_of((GROUP, LANES)) < FEAT
    query = jnp.where(only, head_lanes(tile, head, False), 0.0) * 0.25
    keys = jnp.where(only, head_lanes(tile, head, True), 0.0)
    q_high, k_high = query.astype(bf16), keys.astype(bf16)
    q_wide, k_wide = q_high.astype(f32), k_high.astype(f32)
    q_both = (q_wide + pltpu.roll(query - q_wide, FEAT, 1)).astype(bf16)
    k_both = (pltpu.roll(k_wide, FEAT, 1) + (keys - k_wide)).astype(bf16)
    left = jnp.concatenate([q_high, q_both], 1)
    right = jnp.concatenate([k_high, k_both], 1)
    return lax.dot_general(left, right, (NT, ((), ())), preferred_element_type=f32)


def decays(cum, cum_across, head):
    row, lane = rows_of((GROUP, GROUP)), lanes_of((GROUP, GROUP))
    at = GATE_LANE + head
    diff = cum[:, at : at + 1] - cum_across[at : at + 1, :]
    return jnp.where(row >= lane, jnp.exp(jnp.minimum(diff, 0.0)), 0.0)


def head_column(tile, head):
    at = GATE_LANE + head
    return tile[:, at : at + 1]


def on_head_lane(column, head):
    return jnp.where(lanes_of((column.shape[0], LANES)) == GATE_LANE + head, column, 0.0)


def state_rows(pieces_ref, pair):
    parts = [pieces_ref[4 * pair + q, :PIECE, :].astype(f32) for q in range(4)]
    parts.append(jnp.zeros((SIDES - 4 * PIECE, LANES), f32))
    return jnp.concatenate(parts, 0).astype(bf16)


def store_pieces(ref, pair, state):
    for q in range(4):
        ref[4 * pair + q, :PIECE, :] = state[q * PIECE : (q + 1) * PIECE].astype(bf16)


def whole_call(body, outs, *args, scratch=(), flops=10**9, limit=48, cut=None):
    cut = cut or {}
    shapes = [a.shape[:-1] + (cut.get(i, a.shape[-1]),) for i, a in enumerate(args)]

    def whole(shape):
        return pl.BlockSpec(shape, lambda i: (0,) * len(shape))

    count = sum(math.prod(s) * a.dtype.itemsize for s, a in zip(shapes, args))
    count += sum(math.prod(s) * jnp.dtype(d).itemsize for s, d in outs)
    return pl.pallas_call(
        body,
        grid=(1,),
        out_shape=[jax.ShapeDtypeStruct(s, d) for s, d in outs],
        in_specs=[whole(s) for s in shapes],
        out_specs=[whole(s) for s, d in outs],
        scratch_shapes=list(scratch),
        compiler_params=pltpu.CompilerParams(vmem_limit_bytes=limit * MIB),
        cost_estimate=pl.CostEstimate(flops=flops, bytes_accessed=count, transcendentals=0),
    )(*args)


def project_kernel(
    rows_ref, w_ref, rates_ref, taps_ref, pick_ref, ends_ref,
    normed_ref, proj_ref, gains_ref, values_ref, cum_ref, sent_ref,
):
    wide = w_ref.shape[1]
    chosen = jnp.where(
        lanes_of((16, wide)) == rows_of((16, wide)) + GAIN_LANE, 1.0, 0.0
    )
    chosen = jnp.where(rows_of((16, wide)) < 2, chosen, 0.0).astype(bf16)
    gains = lax.dot_general(chosen, w_ref[...], (NT, ((), ())), preferred_element_type=f32)
    gains_ref[...] = gains[:8]
    gain = gains[0:1]
    for at in range(0, ROWS + 16, 176):
        rows = rows_ref[at : at + 176, :].astype(f32)
        scale = lax.rsqrt(jnp.mean(rows * rows, -1, keepdims=True) + eps_norm)
        normed = (rows * scale * gain).astype(bf16)
        normed_ref[at : at + 176, :] = normed
        proj_ref[at : at + 176, :] = jnp.dot(normed, w_ref[...], preferred_element_type=f32)
    ones = lower_ones()
    pick, ends = pick_ref[...], ends_ref[...]
    lane, row = lanes_of((GROUP, LANES)), rows_of((GROUP, LANES))
    for s in range(2):
        here = slice(s * GROUP, (s + 1) * GROUP)
        steps = rates_ref[...] * jax.nn.softplus(proj_ref[here, :LANES])
        cum = summed_down(ones, steps, NN)
        cum_ref[here, :] = cum
        last = cum[GROUP - 1 : GROUP, :]
        tail = jnp.exp(last - cum)
        qk = proj_ref[here, 4 * LANES :]
        for h in range(4):
            tile = slice(h * LANES, (h + 1) * LANES)
            raw = proj_ref[here, tile]
            rim_two = proj_ref[ROWS + 2 * s : ROWS + 2 * s + 1, tile]
            rim_one = proj_ref[ROWS + 2 * s + 1 : ROWS + 2 * s + 2, tile]
            one = jnp.where(row == 0, rim_one, pltpu.roll(raw, 1, 0))
            two = jnp.where(row == 0, rim_two, jnp.where(row == 1, rim_one, pltpu.roll(raw, 2, 0)))
            conv = (
                taps_ref[0:1, tile] * raw + taps_ref[1:2, tile] * one + taps_ref[2:3, tile] * two
            )
            values = jnp.where(lane < DH, conv, jnp.where(lane == DH, 1.0, 0.0))
            values_ref[here, tile] = values
            left, right = factors(head_lanes(qk, h, True), pick, ends)
            held = left * right * ends[2:3] * head_column(tail, h)
            fresh = product(held, values, TN)
            store_pieces(sent_ref, 4 * s + h, fresh)
            ending = jnp.broadcast_to(head_column(last, h), (8, LANES))
            high, rest = two_parts(ending)
            rest = ending - high.astype(f32)
            mid, low = two_parts(rest)
            few = lanes_of((8, LANES))
            packed = jnp.where(
                few == 0,
                high.astype(f32),
                jnp.where(few == 1, mid.astype(f32), jnp.where(few == 2, low.astype(f32), 0.0)),
            ).astype(bf16)
            for q in range(4):
                sent_ref[16 * s + 4 * h + q, PIECE:, :] = packed


def project(rows, w_in, rates, taps, pick, ends):
    wide = w_in.shape[1]
    return whole_call(
        project_kernel,
        [
            (rows.shape, bf16),
            ((rows.shape[0], wide), f32),
            ((8, rows.shape[1]), f32),
            ((ROWS, 4 * LANES), f32),
            ((ROWS, LANES), f32),
            ((PIECES, SLOT, LANES), bf16),
        ],
        rows, w_in, rates, taps, pick, ends,
        flops=3 * 10**9,
    )


def scan_kernel(got_ref, back_ref, decay_ref):
    state = jnp.zeros((PIECE, LANES), f32)
    for i in range(PIECES):
        back_ref[i, :PIECE, :] = state.astype(bf16)
        back_ref[i, PIECE:, :] = jnp.zeros((SLOT - PIECE, LANES), bf16)
        ending = jnp.sum(got_ref[i, PIECE:, :].astype(f32), -1, keepdims=True)
        decay = jnp.broadcast_to(jnp.exp(ending), (8, LANES))
        decay_ref[i] = decay
        state = state * decay[0:1] + got_ref[i, :PIECE, :].astype(f32)


def earlier_states(sent):
    got = lax.all_to_all(sent, SEQ, 0, 0, tiled=True)
    back, decay = whole_call(
        scan_kernel, [(sent.shape, bf16), ((PIECES, 8, LANES), f32)], got, flops=10**6
    )
    return lax.all_to_all(back, SEQ, 0, 0, tiled=True), decay


def scan_back_kernel(got_ref, decay_ref, back_ref):
    state = jnp.zeros((PIECE, LANES), f32)
    for i in reversed(range(PIECES)):
        back_ref[i, :PIECE, :] = state.astype(bf16)
        back_ref[i, PIECE:, :] = jnp.zeros((SLOT - PIECE, LANES), bf16)
        state = state * decay_ref[i, 0:1, :] + got_ref[i, :PIECE, :].astype(f32)


def later_states(sent, decay):
    got = lax.all_to_all(sent, SEQ, 0, 0, tiled=True)
    (back,) = whole_call(scan_back_kernel, [(sent.shape, bf16)], got, decay, flops=10**6)
    return lax.all_to_all(back, SEQ, 0, 0, tiled=True)


def within_kernel(proj_ref, values_ref, cum_ref, inside_ref):
    for s in range(2):
        here = slice(s * GROUP, (s + 1) * GROUP)
        cum = cum_ref[here, :]
        across = cum.T
        qk = proj_ref[here, 4 * LANES :]
        for h in range(4):
            tile = slice(h * LANES, (h + 1) * LANES)
            dots = scores(qk, h)
            weights = (1.0 + dots + 0.5 * dots * dots) * decays(cum, across, h)
            inside_ref[here, tile] = product(weights, values_ref[here, tile], NN)


def within(proj, values, cum):
    return whole_call(
        within_kernel, [((ROWS, 4 * LANES), f32)], proj, values, cum, flops=3 * 10**9
    )[0]


def mix_kernel(
    proj_ref, cum_ref, inside_ref, earlier_ref, w_ref, pick_ref, ends_ref,
    total_ref, mixed_ref, branch_ref,
):
    pick, ends = pick_ref[...], ends_ref[...]
    lane = lanes_of((GROUP, LANES))
    for s in range(2):
        here = slice(s * GROUP, (s + 1) * GROUP)
        growth = jnp.exp(cum_ref[here, :])
        qk = proj_ref[here, 4 * LANES :]
        for h in range(4):
            tile = slice(h * LANES, (h + 1) * LANES)
            left, right = factors(head_lanes(qk, h, False), pick, ends)
            held = left * right * ends[2:3] * head_column(growth, h)
            total = inside_ref[here, tile] + product(held, state_rows(earlier_ref, 4 * s + h), NN, 2)
            total_ref[here, tile] = total
            mixed = total / total[:, DH : DH + 1]
            mixed_ref[here, tile] = jnp.where(lane < DH, mixed, 0.0).astype(bf16)
    branch_ref[...] = lax.dot_general(
        mixed_ref[...], w_ref[...], (NT, ((), ())), preferred_element_type=f32
    ).astype(bf16)


def mix(proj, cum, inside, earlier, w_out, pick, ends):
    return whole_call(
        mix_kernel,
        [((ROWS, 4 * LANES), f32), ((ROWS, 4 * LANES), bf16), ((ROWS, w_out.shape[0]), bf16)],
        proj, cum, inside, earlier, w_out, pick, ends,
        flops=3 * 10**9,
        cut={4: 4 * LANES},
    )


def unmix_kernel(
    out_back_ref, w_ref, total_ref, proj_ref, cum_ref, pick_ref, ends_ref, total_back_ref, sent_ref
):
    pick, ends = pick_ref[...], ends_ref[...]
    lane = lanes_of((GROUP, LANES))
    total_back_ref[...] = jnp.dot(out_back_ref[...], w_ref[...], preferred_element_type=f32)
    for s in range(2):
        here = slice(s * GROUP, (s + 1) * GROUP)
        growth = jnp.exp(cum_ref[here, :])
        qk = proj_ref[here, 4 * LANES :]
        for h in range(4):
            tile = slice(h * LANES, (h + 1) * LANES)
            total = total_ref[here, tile]
            inverse = 1.0 / total[:, DH : DH + 1]
            numer = total_back_ref[here, tile] * inverse
            numer = jnp.where(lane < DH, numer, 0.0)
            denom = -jnp.sum(numer * total, -1, keepdims=True) * inverse
            total_back = jnp.where(lane == DH, denom, numer)
            total_back_ref[here, tile] = total_back
            left, right = factors(head_lanes(qk, h, False), pick, ends)
            held = left * right * ends[2:3] * head_column(growth, h)
            store_pieces(sent_ref, 4 * s + h, product(held, total_back, TN))
            for q in range(4):
                sent_ref[16 * s + 4 * h + q, PIECE:, :] = jnp.zeros((SLOT - PIECE, LANES), bf16)


def unmix(out_back, w_out, total, proj, cum, pick, ends):
    return whole_call(
        unmix_kernel,
        [((ROWS, 4 * LANES), f32), ((PIECES, SLOT, LANES), bf16)],
        out_back, w_out, total, proj, cum, pick, ends,
        flops=3 * 10**9,
        cut={1: 4 * LANES},
    )


def within_back_kernel(
    proj_ref, values_ref, cum_ref, total_back_ref, earlier_ref, pick_ref, ends_ref,
    qk_back_ref, values_back_ref, level_ref,
):
    pick, ends = pick_ref[...], ends_ref[...]
    only = lanes_of((GROUP, LANES)) < FEAT
    for s in range(2):
        here = slice(s * GROUP, (s + 1) * GROUP)
        cum = cum_ref[here, :]
        across = cum.T
        growth = jnp.exp(cum)
        qk = proj_ref[here, 4 * LANES :]
        qk_back = jnp.zeros((GROUP, LANES), f32)
        level = jnp.zeros((GROUP, LANES), f32)
        level_down = jnp.zeros((LANES, GROUP), f32)
        for h in range(4):
            tile = slice(h * LANES, (h + 1) * LANES)
            total_back = total_back_ref[here, tile]
            decay = decays(cum, across, h)
            dots = scores(qk, h)
            pairing = decay * product(total_back, values_ref[here, tile], NT)
            kernel = 1.0 + dots + 0.5 * dots * dots
            moved = kernel * pairing
            down = jnp.sum(moved, 0, keepdims=True)
            level_down = jnp.where(rows_of((LANES, GROUP)) == GATE_LANE + h, down, level_down)
            kernel_back = pairing * (1.0 + dots) * 0.25
            values_back_ref[here, tile] = product(kernel * decay, total_back, TN)
            query_tile = head_lanes(qk, h, False)
            keys_only = jnp.where(only, head_lanes(qk, h, True), 0.0)
            query_only = jnp.where(only, query_tile, 0.0)
            query_back = product(kernel_back, keys_only, NN)
            keys_back = product(kernel_back, query_only, TN)
            left, right = factors(query_tile, pick, ends)
            features_back = head_column(growth, h) * product(
                total_back, state_rows(earlier_ref, 4 * s + h), NT, 2
            )
            level_here = jnp.sum(moved, 1, keepdims=True) + jnp.sum(
                left * right * ends[2:3] * features_back, 1, keepdims=True
            )
            level = level + on_head_lane(level_here, h)
            query_back = query_back + factors_back(features_back, left, right, pick, ends)
            at = h * FEAT
            qk_back = qk_back + (pltpu.roll(query_back, at, 1) if at else query_back)
            qk_back = qk_back + pltpu.roll(keys_back, at + 4 * FEAT, 1)
        qk_back_ref[here, :] = qk_back
        level_ref[here, :] = level - level_down.T


def within_back(proj, values, cum, total_back, earlier, pick, ends):
    return whole_call(
        within_back_kernel,
        [((ROWS, LANES), f32), ((ROWS, 4 * LANES), f32), ((ROWS, LANES), f32)],
        proj, values, cum, total_back, earlier, pick, ends,
        flops=8 * 10**9,
    )


def later_back_kernel(
    proj_ref, values_ref, cum_ref, rates_ref, earlier_ref, later_ref, pick_ref, ends_ref,
    qk_in_ref, values_in_ref, level_ref,
    qk_back_ref, values_back_ref, gate_back_ref,
):
    pick, ends = pick_ref[...], ends_ref[...]
    ones, before = lower_ones(), lower_ones(True)
    for s in range(2):
        here = slice(s * GROUP, (s + 1) * GROUP)
        cum = cum_ref[here, :]
        last = cum[GROUP - 1 : GROUP, :]
        tail = jnp.exp(last - cum)
        carried = jnp.exp(last)
        qk = proj_ref[here, 4 * LANES :]
        qk_back = qk_in_ref[here, :]
        crossed = jnp.zeros((GROUP, LANES), f32)
        through = jnp.zeros((1, LANES), f32)
        for h in range(4):
            tile = slice(h * LANES, (h + 1) * LANES)
            later = state_rows(later_ref, 4 * s + h)
            left, right = factors(head_lanes(qk, h, True), pick, ends)
            held = left * right * ends[2:3]
            column = head_column(tail, h)
            features_back = column * product(values_ref[here, tile], later, NT, 2)
            values_back_ref[here, tile] = values_in_ref[here, tile] + column * product(
                held, later, NN, 2
            )
            crossed = crossed + on_head_lane(
                jnp.sum(held * features_back, 1, keepdims=True), h
            )
            keys_back = factors_back(features_back, left, right, pick, ends)
            qk_back = qk_back + pltpu.roll(keys_back, (h + 4) * FEAT, 1)
            whole = jnp.sum(
                later.astype(f32) * state_rows(earlier_ref, 4 * s + h).astype(f32), 1, keepdims=True
            )
            whole = jnp.sum(whole, 0, keepdims=True) * head_column(carried, h)
            through = through + on_head_lane(whole, h)
        qk_back_ref[here, :] = qk_back
        step_back = (
            summed_down(ones, level_ref[here, :], TN) + summed_down(before, crossed, NN) + through
        )
        gate_back_ref[here, :] = (
            step_back * rates_ref[...] * jax.nn.sigmoid(proj_ref[here, :LANES])
        )


def later_back(proj, values, cum, rates, earlier, later, pick, ends, qk_back, values_back, level):
    return whole_call(
        later_back_kernel,
        [((ROWS, LANES), f32), ((ROWS, 4 * LANES), f32), ((ROWS, LANES), f32)],
        proj, values, cum, rates, earlier, later, pick, ends, qk_back, values_back, level,
        flops=4 * 10**9,
    )


def unproject_kernel(
    proj_ref, ahead_ref, taps_ref, qk_back_ref, values_back_ref, gate_back_ref, normed_ref, w_ref,
    out_back_ref, mixed_ref,
    part_ref, grads_ref, taps_grad_ref, proj_back_ref,
):
    lane, row = lanes_of((GROUP, LANES)), rows_of((GROUP, LANES))
    taps_grad_ref[...] = jnp.zeros_like(taps_grad_ref)
    for s in range(2):
        here = slice(s * GROUP, (s + 1) * GROUP)
        for h in range(4):
            tile = slice(h * LANES, (h + 1) * LANES)
            raw = proj_ref[here, tile]
            back = values_back_ref[here, tile]
            back = jnp.where(lane < DH, back, 0.0)
            rim_two = proj_ref[ROWS + 2 * s : ROWS + 2 * s + 1, tile]
            rim_one = proj_ref[ROWS + 2 * s + 1 : ROWS + 2 * s + 2, tile]
            one = jnp.where(row == 0, rim_one, pltpu.roll(raw, 1, 0))
            two = jnp.where(row == 0, rim_two, jnp.where(row == 1, rim_one, pltpu.roll(raw, 2, 0)))
            for j, moved in enumerate((raw, one, two)):
                taps_grad_ref[j : j + 1, tile] = taps_grad_ref[j : j + 1, tile] + jnp.sum(
                    moved * back, 0, keepdims=True
                )
            next_one = ahead_ref[2 * s : 2 * s + 1, tile]
            next_two = ahead_ref[2 * s + 1 : 2 * s + 2, tile]
            one = jnp.where(row == GROUP - 1, next_one, pltpu.roll(back, GROUP - 1, 0))
            two = jnp.where(
                row == GROUP - 1,
                next_two,
                jnp.where(row == GROUP - 2, next_one, pltpu.roll(back, GROUP - 2, 0)),
            )
            raw_back = (
                taps_ref[0:1, tile] * back + taps_ref[1:2, tile] * one + taps_ref[2:3, tile] * two
            )
            raw_back = jnp.where(lane < DH, raw_back, 0.0)
            if h == 0:
                gates = (lane >= GATE_LANE) & (lane < GATE_LANE + 4)
                raw_back = jnp.where(gates, gate_back_ref[here, :], raw_back)
            proj_back_ref[here, tile] = raw_back.astype(bf16)
        proj_back_ref[here, 4 * LANES :] = qk_back_ref[here, :].astype(bf16)
    part_ref[...] = lax.dot_general(
        proj_back_ref[...], w_ref[...], (NT, ((), ())), preferred_element_type=f32
    ).astype(bf16)
    wide = w_ref.shape[1]
    grads_ref[:, :wide] = lax.dot_general(
        normed_ref[:ROWS, :], proj_back_ref[...], (TN, ((), ())), preferred_element_type=f32
    ).astype(bf16)
    grads_ref[:, wide:] = lax.dot_general(
        out_back_ref[...], mixed_ref[...], (TN, ((), ())), preferred_element_type=f32
    ).astype(bf16)


def unproject(
    proj, ahead, taps, qk_back, values_back, gate_back, normed, w_in, out_back, mixed
):
    width, wide = w_in.shape
    return whole_call(
        unproject_kernel,
        [
            ((ROWS, width), bf16),
            ((width, wide + 4 * LANES), bf16),
            ((8, 4 * LANES), f32),
        ],
        proj, ahead, taps, qk_back, values_back, gate_back, normed, w_in, out_back, mixed,
        scratch=[pltpu.VMEM((ROWS, wide), bf16)],
        flops=4 * 10**9,
    )


BLOCK = 256
HIDDEN = 1280


def ffn_kernel(
    normed_ref, back_ref, gate_ref, up_ref, down_ref,
    acts_ref, two_ref, ffn_ref, two_sum, ffn_sum,
):
    step = pl.program_id(0)
    normed, back = normed_ref[...], back_ref[...]
    gate = jnp.dot(normed, gate_ref[...], preferred_element_type=f32)
    up = jnp.dot(normed, up_ref[...], preferred_element_type=f32)
    hidden_back = jnp.dot(back, down_ref[...], preferred_element_type=f32)
    sigma = jax.nn.sigmoid(gate)
    silu = gate * sigma
    gate_back = (hidden_back * up * sigma * (1.0 + gate * (1.0 - sigma))).astype(bf16)
    up_back = (hidden_back * silu).astype(bf16)
    hidden = (silu * up).astype(bf16)
    acts_ref[0], acts_ref[1], acts_ref[2] = gate_back, up_back, hidden

    def spread(value, ref):
        return lax.dot_general(value, ref[...], (NT, ((), ())), preferred_element_type=f32)

    two = spread(gate_back, gate_ref) + spread(up_back, up_ref)
    ffn = spread(hidden, down_ref)

    @pl.when(step == 0)
    def _():
        two_sum[...] = two
        ffn_sum[...] = ffn

    @pl.when(step > 0)
    def _():
        two_sum[...] += two
        ffn_sum[...] += ffn

    @pl.when(step == pl.num_programs(0) - 1)
    def _():
        two_ref[...] = two_sum[...].astype(bf16)
        ffn_ref[...] = ffn_sum[...].astype(bf16)


def ffn_both_ways(normed, back, rest):
    width = normed.shape[1]
    steps = HIDDEN // BLOCK
    whole = pl.BlockSpec((ROWS, width), lambda i: (0, 0))

    def columns(which):
        return pl.BlockSpec((width, BLOCK), lambda i: (0, which * steps + i))

    return pl.pallas_call(
        ffn_kernel,
        grid=(steps,),
        out_shape=[
            jax.ShapeDtypeStruct((3, ROWS, HIDDEN), bf16),
            jax.ShapeDtypeStruct((ROWS, width), bf16),
            jax.ShapeDtypeStruct((ROWS, width), bf16),
        ],
        in_specs=[whole, whole, columns(0), columns(1), columns(2)],
        out_specs=[pl.BlockSpec((3, ROWS, BLOCK), lambda i: (0, 0, i)), whole, whole],
        scratch_shapes=[pltpu.VMEM((ROWS, width), f32)] * 2,
        compiler_params=pltpu.CompilerParams(vmem_limit_bytes=48 * MIB),
        cost_estimate=pl.CostEstimate(
            flops=14 * 10**9, bytes_accessed=25 * 10**6, transcendentals=0
        ),
    )(normed, back, rest, rest, rest)


SHARD = 56
SPACED = 64


def ffn_grads_kernel(normed_ref, back_ref, acts_ref, grads_ref, across):
    step = pl.program_id(0)
    width = normed_ref.shape[1]
    blocks = HIDDEN // BLOCK

    @pl.when(step == 0)
    def _():
        across[...] = normed_ref[...].T

    @pl.when(step == 2 * blocks)
    def _():
        across[...] = back_ref[...].T

    grad = jnp.dot(across[...], acts_ref[0], preferred_element_type=f32)
    for r in range(width // SHARD):
        grads_ref[r * SPACED : r * SPACED + SHARD, :] = grad[r * SHARD : (r + 1) * SHARD].astype(
            bf16
        )
        grads_ref[r * SPACED + SHARD : (r + 1) * SPACED, :] = jnp.zeros(
            (SPACED - SHARD, BLOCK), bf16
        )


def ffn_grads(normed, back, acts):
    width = normed.shape[1]
    blocks = HIDDEN // BLOCK
    whole = pl.BlockSpec((ROWS, width), lambda i: (0, 0))
    return pl.pallas_call(
        ffn_grads_kernel,
        grid=(3 * blocks,),
        out_shape=jax.ShapeDtypeStruct((width // SHARD * SPACED, 3 * HIDDEN), bf16),
        in_specs=[
            whole,
            whole,
            pl.BlockSpec((1, ROWS, BLOCK), lambda i: (i // blocks, 0, i % blocks)),
        ],
        out_specs=pl.BlockSpec((width // SHARD * SPACED, BLOCK), lambda i: (0, i)),
        scratch_shapes=[pltpu.VMEM((width, ROWS), bf16)],
        compiler_params=pltpu.CompilerParams(vmem_limit_bytes=48 * MIB),
        cost_estimate=pl.CostEstimate(
            flops=7 * 10**9, bytes_accessed=20 * 10**6, transcendentals=0
        ),
    )(normed, back, acts)


def order_columns(heads):
    import numpy as np

    place = np.zeros((5 * LANES, 5 * LANES), np.float32)
    for h in range(heads):
        at = h * (2 * FEAT + DH + 1)
        for i in range(FEAT):
            place[at + i, heads * LANES + h * FEAT + i] = 1.0
            place[at + FEAT + i, heads * LANES + (heads + h) * FEAT + i] = 1.0
        for i in range(DH):
            place[at + 2 * FEAT + i, h * LANES + i] = 1.0
        place[at + 2 * FEAT + DH, GATE_LANE + h] = 1.0
    return jnp.asarray(place, bf16)


def prepare_kernel(
    rank_ref, in_ref, out_ref, gate_ref, up_ref, down_ref, taps_ref, gains_ref, place_ref,
    shard_ref, out_shard_ref, rest_ref,
):
    wide = 5 * LANES
    columns = in_ref.shape[1]
    whole = jnp.dot(
        in_ref[...].astype(bf16), place_ref[:columns, :], preferred_element_type=f32
    )
    spot = jnp.where(
        lanes_of((2, wide)) == rows_of((2, wide)) + GAIN_LANE, 1.0, 0.0
    ).astype(bf16)
    gains = lax.dot_general(
        gains_ref[...].astype(bf16), spot, (TN, ((), ())), preferred_element_type=f32
    )
    shard_ref[:SHARD, :] = (whole + gains).astype(bf16)
    rank = rank_ref[0]
    own = taps_ref.shape[1]
    each = DH // own
    first = (rank // each) * LANES + (rank % each) * own
    spot = jnp.where(
        lanes_of((own, wide)) == rows_of((own, wide)) + first, 1.0, 0.0
    ).astype(bf16)
    taps = jnp.dot(taps_ref[...].astype(bf16), spot, preferred_element_type=f32)
    shard_ref[SHARD:, :] = jnp.concatenate(
        [taps, jnp.zeros((SPACED - SHARD - TAPS, wide), f32)], 0
    ).astype(bf16)
    out_shard_ref[...] = jnp.zeros_like(out_shard_ref)
    for h in range(4):
        out_shard_ref[:, h * LANES : h * LANES + DH] = (
            out_ref[h * DH : (h + 1) * DH, :].T.astype(bf16)
        )
    rest_ref[...] = jnp.zeros_like(rest_ref)
    units = gate_ref.shape[1]
    rest_ref[:, :units] = gate_ref[...].astype(bf16)
    rest_ref[:, HIDDEN : HIDDEN + units] = up_ref[...].astype(bf16)
    rest_ref[:, 2 * HIDDEN : 2 * HIDDEN + units] = down_ref[...].T.astype(bf16)


def prepare(rank, inproj, outproj, gateproj, upproj, downproj, taps, gains, place):
    args = (inproj, outproj, gateproj, upproj, downproj, taps, gains, place)
    vmem = pl.BlockSpec(memory_space=pltpu.VMEM)
    return pl.pallas_call(
        prepare_kernel,
        out_shape=[
            jax.ShapeDtypeStruct((SPACED, 5 * LANES), bf16),
            jax.ShapeDtypeStruct((SHARD, 4 * LANES), bf16),
            jax.ShapeDtypeStruct((SHARD, 3 * HIDDEN), bf16),
        ],
        in_specs=[pl.BlockSpec(memory_space=pltpu.SMEM)] + [vmem] * len(args),
        out_specs=[vmem] * 3,
        compiler_params=pltpu.CompilerParams(vmem_limit_bytes=24 * MIB),
    )(rank.reshape(1), *args)


def moved_moments(weight, first, second, grad):
    fix = 1.0 - beta_value**STEP
    moment = beta_value * first + (1.0 - beta_value) * grad
    square = beta_value * second + (1.0 - beta_value) * grad * grad
    direction = moment / fix / (jnp.sqrt(square / fix) + eps_adam) + decay_rate * weight
    return moment, square, direction


def moments_kernel(mixer_ref, ffn_ref, small_ref, place_ref, *refs):
    params, outs, sums_ref = refs[:21], refs[21:-1], refs[-1]
    wide = 5 * LANES
    units = params[6].shape[1]
    parts, spare = [], mixer_ref[:, :wide]
    for _ in range(3):
        part = spare.astype(bf16)
        spare = spare - part.astype(f32)
        parts.append(
            lax.dot_general(part, place_ref[...], (NT, ((), ())), preferred_element_type=f32)
        )
    grad_in = (parts[2] + parts[1] + parts[0])[:, : params[0].shape[1]]
    sums = jnp.zeros((8, LANES), f32)
    row, lane = rows_of((8, LANES)), lanes_of((8, LANES))

    def adapt(index, grad, rows=slice(None)):
        weight = params[3 * index][rows, :]
        moment, square, direction = moved_moments(
            weight, params[3 * index + 1][rows, :], params[3 * index + 2][rows, :], grad
        )
        outs[3 * index][rows, :] = moment
        outs[3 * index + 1][rows, :] = square
        outs[3 * index + 2][rows, :] = direction
        both = [jnp.sum(jnp.sum(v * v, 1, keepdims=True), 0, keepdims=True) for v in (weight, direction)]
        return jnp.where(
            (row == 0) & (lane == 2 * index),
            both[0],
            jnp.where((row == 0) & (lane == 2 * index + 1), both[1], 0.0),
        )

    sums = sums + adapt(0, grad_in)
    for h in range(4):
        grad = mixer_ref[:, wide + h * LANES : wide + (h + 1) * LANES].T[:DH]
        sums = sums + adapt(1, grad, slice(h * DH, (h + 1) * DH))
    sums = sums + adapt(2, ffn_ref[:SHARD, :units].astype(f32))
    sums = sums + adapt(3, ffn_ref[:SHARD, HIDDEN : HIDDEN + units].astype(f32))
    sums = sums + adapt(4, ffn_ref[:SHARD, 2 * HIDDEN : 2 * HIDDEN + units].astype(f32).T)
    sums = sums + adapt(5, small_ref[8 : 8 + TAPS, : params[15].shape[1]])
    sums = sums + 0.25 * adapt(6, small_ref[0:2, : params[18].shape[1]])
    sums_ref[...] = jnp.broadcast_to(sums[0:1], sums_ref.shape)


def moments(mixer, ffn, small, place, params):
    outs = []
    for index in range(7):
        outs += [(params[3 * index].shape, f32)] * 3
    outs.append(((LANES, LANES), f32))
    vmem = pl.BlockSpec(memory_space=pltpu.VMEM)
    args = (mixer, ffn, small, place) + tuple(params)
    return pl.pallas_call(
        moments_kernel,
        out_shape=[jax.ShapeDtypeStruct(s, d) for s, d in outs],
        in_specs=[vmem] * len(args),
        out_specs=[vmem] * len(outs),
        compiler_params=pltpu.CompilerParams(vmem_limit_bytes=48 * MIB),
    )(*args)


def update_kernel(totals_ref, *refs):
    weights, directions, outs, norms_ref = refs[:7], refs[7:14], refs[14:21], refs[21]
    norms = jnp.sqrt(jnp.sum(totals_ref[...], 0, keepdims=True))
    norms_ref[...] = jnp.broadcast_to(norms, norms_ref.shape)
    for index in range(7):
        ratio = norms[:, 2 * index : 2 * index + 1] / norms[:, 2 * index + 1 : 2 * index + 2]
        outs[index][...] = weights[index][...] - learn_rate * ratio * directions[index][...]


def update(totals, weights, directions):
    vmem = pl.BlockSpec(memory_space=pltpu.VMEM)
    return pl.pallas_call(
        update_kernel,
        out_shape=[jax.ShapeDtypeStruct(w.shape, f32) for w in weights]
        + [jax.ShapeDtypeStruct((8, LANES), f32)],
        in_specs=[vmem] * 15,
        out_specs=[vmem] * 8,
        compiler_params=pltpu.CompilerParams(vmem_limit_bytes=24 * MIB),
    )(totals, *weights, *directions)


def per_device(
    tokens,
    cotangent,
    lengths,
    rate_codes,
    inproj,
    inproj_first,
    inproj_second,
    outproj,
    outproj_first,
    outproj_second,
    gateproj,
    gateproj_first,
    gateproj_second,
    upproj,
    upproj_first,
    upproj_second,
    downproj,
    downproj_first,
    downproj_second,
    convtaps,
    convtaps_first,
    convtaps_second,
    normgains,
    normgains_first,
    normgains_second,
):
    seqs, group, width = tokens.shape
    heads = rate_codes.shape[0]
    lag = TAPS - 1
    rank = lax.axis_index(SEQ)
    core = lax.axis_index("seq_2")
    pick, ends = selections()
    place = order_columns(heads)

    shard, out_shard, rest_shard = prepare(
        rank, inproj, outproj, gateproj, upproj, downproj, convtaps, normgains, place
    )
    got = lax.all_to_all(
        jnp.broadcast_to(shard[None], (16,) + shard.shape), ("seq_0", "seq_1"), 0, 0, tiled=True
    )
    other = lax.ppermute(got, "seq_2", SWAP)
    both = jnp.where(core == 0, jnp.stack([got, other], 1), jnp.stack([other, got], 1))
    w_in = both[:, :, :SHARD].reshape(width, -1)
    taps = jnp.sum(both[:, :, SHARD:, : heads * LANES].astype(f32), (0, 1))
    w_out = lax.all_gather(out_shard, SEQ, axis=0, tiled=True)
    rest_shard, w_in = lax.optimization_barrier((rest_shard, w_in))
    rest = lax.all_gather(rest_shard, SEQ, axis=0, tiled=True)

    rows = tokens.reshape(-1, width)
    rim_tokens = shifted(tokens[:, group - lag :], SEQ, 1).reshape(-1, width)
    filled = jnp.zeros((16 - seqs * lag, width), bf16)
    positions = rank * group + jnp.arange(group, dtype=jnp.int32)
    keep = (positions[None, :] < lengths[:, None]).astype(f32).reshape(-1, 1)
    rates = -jnp.exp2(-rate_codes.astype(f32) / 4.0)
    rates = jnp.pad(rates[None], ((0, 0), (GATE_LANE, LANES - GATE_LANE - heads)))
    normed_one, proj, gains, values, cum, sent = project(
        jnp.concatenate([rows, rim_tokens, filled], 0), w_in, rates, taps, pick, ends
    )
    earlier, decay = earlier_states(sent)
    inside = within(proj, values, cum)
    total, mixed, branch = mix(proj, cum, inside, earlier, w_out, pick, ends)

    flat = own_rows(rows).astype(f32)
    middle = flat + scatter_sum(branch)
    scale_two = lax.rsqrt(jnp.mean(middle * middle, -1, keepdims=True) + eps_norm)
    unit_two = middle * scale_two
    normed_two = gather_rows((unit_two * gains[1]).astype(bf16))

    back = (cotangent.reshape(-1, width).astype(f32) * keep).astype(bf16)
    acts, two_part, ffn_part = ffn_both_ways(normed_two, back, rest)
    two_back = scatter_sum(two_part)
    ffn_sums = lax.psum_scatter(
        ffn_grads(normed_two, back, acts), SEQ, scatter_dimension=0, tiled=True
    )
    gain_two_grad = jnp.sum(two_back * unit_two, 0)
    middle_back = own_rows(back).astype(f32) + norm_backward(
        two_back, unit_two, scale_two, gains[1]
    )
    out_back = gather_rows(middle_back.astype(bf16))

    total_back, sent = unmix(out_back, w_out, total, proj, cum, pick, ends)
    later = later_states(sent, decay)
    qk_back, values_back, level = within_back(
        proj, values, cum, total_back, earlier, pick, ends
    )
    qk_back, values_back, gate_back = later_back(
        proj, values, cum, rates, earlier, later, pick, ends, qk_back, values_back, level
    )
    edge = values_back.reshape(seqs, group, -1)[:, :lag]
    ahead = shifted(edge, SEQ, -1).reshape(seqs * lag, -1)
    ahead = jnp.concatenate([ahead, jnp.zeros_like(ahead)], 0)
    one_part, grads, taps_grad = unproject(
        proj, ahead, taps, qk_back, values_back, gate_back, normed_one, w_in, out_back, mixed
    )

    one_back = scatter_sum(one_part)
    mixer_sums = seq_scatter(grads)
    scale_one = lax.rsqrt(jnp.mean(flat * flat, -1, keepdims=True) + eps_norm)
    unit_one = flat * scale_one
    gain_one_grad = jnp.sum(one_back * unit_one, 0)
    token_back = middle_back + norm_backward(one_back, unit_one, scale_one, gains[0])
    token_grad = gather_rows(token_back.astype(bf16))
    ffn_part, out_back = lax.optimization_barrier((ffn_part, out_back))
    ffn = scatter_sum(ffn_part)
    block_out = gather_rows(((middle + ffn) * own_rows(keep)).astype(bf16))

    peers = lax.axis_size("mp")
    gains_grad = jnp.stack([gain_one_grad, gain_two_grad]).reshape(2, 32, 1, -1)
    gains_sent = jnp.broadcast_to(
        gains_grad.transpose(1, 2, 0, 3), (32, peers, 2, width // 32)
    ).reshape(32, peers, -1)
    taps_own = taps_grad[:TAPS].reshape(TAPS, heads, LANES)[..., :DH]
    taps_sent = taps_own.reshape(TAPS, 32, 1, -1).transpose(1, 2, 0, 3).reshape(32, 1, -1)
    to_own = (jnp.arange(peers) == lax.axis_index("mp")).astype(f32)[None, :, None]
    small_sent = jnp.concatenate([gains_sent, taps_sent * to_own], -1)
    small_got = lax.all_to_all(small_sent.reshape(32 * peers, -1), ALL, 0, 0, tiled=True)
    small_sum = jnp.sum(small_got, 0)
    gains_sum = small_sum[: normgains.size].reshape(normgains.shape)
    taps_sum = small_sum[normgains.size :].reshape(convtaps.shape)
    small = jnp.concatenate(
        [
            jnp.pad(part, ((0, 8 - part.shape[0]), (0, LANES - part.shape[1])))
            for part in (gains_sum, taps_sum)
        ],
        0,
    )

    params = (
        (inproj, inproj_first, inproj_second)
        + (outproj, outproj_first, outproj_second)
        + (gateproj, gateproj_first, gateproj_second)
        + (upproj, upproj_first, upproj_second)
        + (downproj, downproj_first, downproj_second)
        + (convtaps, convtaps_first, convtaps_second)
        + (normgains, normgains_first, normgains_second)
    )
    *moved, sums = moments(mixer_sums, ffn_sums, small, place, params)
    totals = lax.all_to_all(sums, ALL, 0, 0, tiled=True)
    *updated, norms = update(totals, params[0::3], moved[2::3])
    results = [block_out.reshape(tokens.shape), token_grad.reshape(tokens.shape)]
    for index in range(7):
        results += [updated[index], moved[3 * index], moved[3 * index + 1]]
    results.append(norms[0, :14].reshape(7, 2))
    return tuple(results)


def solution(mesh):
    split = Mesh(mesh.devices.reshape(4, 4, 2, mesh.shape["mp"]), ("seq_0", "seq_1", "seq_2", "mp"))
    in_specs = (
        P(None, SEQ, None),
        P(None, SEQ, None),
        P(),
        P("mp"),
        P(SEQ, "mp"),
        P(SEQ, "mp"),
        P(SEQ, "mp"),
        P("mp", SEQ),
        P("mp", SEQ),
        P("mp", SEQ),
        P(SEQ, "mp"),
        P(SEQ, "mp"),
        P(SEQ, "mp"),
        P(SEQ, "mp"),
        P(SEQ, "mp"),
        P(SEQ, "mp"),
        P("mp", SEQ),
        P("mp", SEQ),
        P("mp", SEQ),
        P(None, MP_SEQ),
        P(None, MP_SEQ),
        P(None, MP_SEQ),
        P(None, SEQ),
        P(None, SEQ),
        P(None, SEQ),
    )
    out_specs = (
        P(None, SEQ, None),
        P(None, SEQ, None),
        P(SEQ, "mp"),
        P(SEQ, "mp"),
        P(SEQ, "mp"),
        P("mp", SEQ),
        P("mp", SEQ),
        P("mp", SEQ),
        P(SEQ, "mp"),
        P(SEQ, "mp"),
        P(SEQ, "mp"),
        P(SEQ, "mp"),
        P(SEQ, "mp"),
        P(SEQ, "mp"),
        P("mp", SEQ),
        P("mp", SEQ),
        P("mp", SEQ),
        P(None, MP_SEQ),
        P(None, MP_SEQ),
        P(None, MP_SEQ),
        P(None, SEQ),
        P(None, SEQ),
        P(None, SEQ),
        P(),
    )
    return jax.shard_map(
        per_device, mesh=split, in_specs=in_specs, out_specs=out_specs, check_vma=False
    )
```

```python
import math

import jax
import jax.numpy as jnp
from jax import lax
from jax.experimental import pallas as pl
from jax.experimental.pallas import tpu as pltpu
from jax.sharding import Mesh
from jax.sharding import PartitionSpec as P

DH = 112
FEAT = 16
TAPS = 3
STEP = 7
LANES = 128
SEQ = ("seq_0", "seq_1", "seq_2")
ALL = ("seq_0", "seq_1", "seq_2", "mp")
MP_SEQ = ("mp", "seq_0", "seq_1", "seq_2")

f32 = jnp.float32
bf16 = jnp.bfloat16
highest = lax.Precision.HIGHEST
root_half = 0.5**0.5
eps_norm = 1e-05
eps_adam = 1e-06
decay_rate = 0.01
learn_rate = 0.3
beta_value = 0.5

SIDE = [(i, i ^ 1) for i in range(4)]
BACK = [(i, 3 - i) for i in range(4)]
SWAP = [(0, 1), (1, 0)]


def shifted(value, axis, steps):
    count = lax.axis_size(axis)
    first, last = (max(0, -steps), min(count, count - steps))
    return lax.ppermute(value, axis, [(source, source + steps) for source in range(first, last)])


SPAN_LANE = DH
GATE_LANE = DH
GAIN_LANE = DH + 4
GROUP = 256
ROWS = 512
SIDES = 256
PIECE = 40
SLOT = 48
PIECES = 32
MIB = 1 << 20


def selections():
    import numpy as np

    pick = np.zeros((2 * LANES, 2 * SIDES), np.float32)
    ends = np.zeros((8, SIDES), np.float32)
    ends[0, 0] = ends[1, 0] = ends[2, 0] = 1.0
    lane = 1
    for i in range(FEAT):
        pick[i, lane] = 0.5
        ends[1, lane] = ends[2, lane] = 1.0
        lane += 1
    for i in range(FEAT):
        for j in range(i, FEAT):
            pick[i, lane] = 0.5
            pick[j, SIDES + lane] = 0.5
            ends[2, lane] = root_half if i == j else 1.0
            lane += 1
    pick[LANES:] = pick[:LANES]
    return jnp.asarray(pick, bf16), jnp.asarray(ends)


def two_parts(value):
    high = value.astype(bf16)
    return high, (value - high.astype(f32)).astype(bf16)


def three_parts(value):
    high = value.astype(bf16)
    rest = value - high.astype(f32)
    mid = rest.astype(bf16)
    return high, mid, (rest - mid.astype(f32)).astype(bf16)


def product(a, b, contract, passes=3):
    dims = (contract, ((), ()))

    def once(x, y):
        return lax.dot_general(x, y, dims, preferred_element_type=f32)

    if passes == 1:
        return once(a.astype(bf16), b.astype(bf16))
    a_high, a_low = two_parts(a)
    if passes == 2:
        b = b.astype(bf16)
        return once(a_high, b) + once(a_low, b)
    b_high, b_low = two_parts(b)
    return once(a_high, b_high) + (once(a_high, b_low) + once(a_low, b_high))


NN = ((1,), (0,))
NT = ((1,), (1,))
TN = ((0,), (0,))


def lanes_of(shape):
    return lax.broadcasted_iota(jnp.int32, shape, len(shape) - 1)


def rows_of(shape):
    return lax.broadcasted_iota(jnp.int32, shape, 0)


def lower_ones(strict=False):
    row, lane = rows_of((GROUP, GROUP)), lanes_of((GROUP, GROUP))
    return jnp.where(row > lane if strict else row >= lane, 1.0, 0.0).astype(bf16)


def summed_down(ones, value, contract):
    high, mid, low = (
        lax.dot_general(ones, part, (contract, ((), ())), preferred_element_type=f32)
        for part in three_parts(value)
    )
    return low + mid + high


def picked(value, place, contract):
    high, mid, low = (
        lax.dot_general(part, place, (contract, ((), ())), preferred_element_type=f32)
        for part in three_parts(value)
    )
    return low + mid + high


def head_lanes(tile, head, keys):
    first = (4 if keys else 0) * FEAT + head * FEAT
    return pltpu.roll(tile, (LANES - first) % LANES, 1) if first else tile


def factors(moved, pick, ends):
    high, low = two_parts(moved)
    found = lax.dot_general(
        jnp.concatenate([high, low], 1), pick, (NN, ((), ())), preferred_element_type=f32
    )
    return found[:, :SIDES] + ends[0:1], found[:, SIDES:] + ends[1:2]


def factors_back(upstream, one, two, pick, ends):
    scaled = upstream * ends[2:3]
    both = jnp.concatenate([scaled * two, scaled * one], 1)
    return product(both, pick[:LANES], NT, 2)


def scores(tile, head):
    only = lanes_of((GROUP, LANES)) < FEAT
    query = jnp.where(only, head_lanes(tile, head, False), 0.0) * 0.25
    keys = jnp.where(only, head_lanes(tile, head, True), 0.0)
    q_high, k_high = query.astype(bf16), keys.astype(bf16)
    q_wide, k_wide = q_high.astype(f32), k_high.astype(f32)
    q_both = (q_wide + pltpu.roll(query - q_wide, FEAT, 1)).astype(bf16)
    k_both = (pltpu.roll(k_wide, FEAT, 1) + (keys - k_wide)).astype(bf16)
    left = jnp.concatenate([q_high, q_both], 1)
    right = jnp.concatenate([k_high, k_both], 1)
    return lax.dot_general(left, right, (NT, ((), ())), preferred_element_type=f32)


def decays(cum, cum_across, head):
    row, lane = rows_of((GROUP, GROUP)), lanes_of((GROUP, GROUP))
    at = GATE_LANE + head
    diff = cum[:, at : at + 1] - cum_across[at : at + 1, :]
    return jnp.where(row >= lane, jnp.exp(jnp.minimum(diff, 0.0)), 0.0)


def head_column(tile, head):
    at = GATE_LANE + head
    return tile[:, at : at + 1]


def on_head_lane(column, head):
    return jnp.where(lanes_of((column.shape[0], LANES)) == GATE_LANE + head, column, 0.0)


def state_rows(pieces_ref, pair):
    parts = [pieces_ref[4 * pair + q, :PIECE, :].astype(f32) for q in range(4)]
    parts.append(jnp.zeros((SIDES - 4 * PIECE, LANES), f32))
    return jnp.concatenate(parts, 0).astype(bf16)


def store_pieces(ref, pair, state):
    for q in range(4):
        ref[4 * pair + q, :PIECE, :] = state[q * PIECE : (q + 1) * PIECE].astype(bf16)


def whole_call(body, outs, *args, scratch=(), flops=10**9, limit=60, cut=None, scalars=0):
    cut = cut or {}
    shapes = [a.shape[:-1] + (cut.get(i, a.shape[-1]),) for i, a in enumerate(args)]

    def whole(shape):
        return pl.BlockSpec(shape, lambda i: (0,) * len(shape))

    count = sum(math.prod(s) * a.dtype.itemsize for s, a in zip(shapes, args))
    count += sum(math.prod(s) * jnp.dtype(d).itemsize for s, d in outs)
    return pl.pallas_call(
        body,
        grid=(1,),
        out_shape=[jax.ShapeDtypeStruct(s, d) for s, d in outs],
        in_specs=[pl.BlockSpec(memory_space=pltpu.SMEM)] * scalars
        + [whole(s) for s in shapes[scalars:]],
        out_specs=[whole(s) for s, d in outs],
        scratch_shapes=list(scratch),
        compiler_params=pltpu.CompilerParams(vmem_limit_bytes=limit * MIB),
        cost_estimate=pl.CostEstimate(flops=flops, bytes_accessed=count, transcendentals=0),
    )(*args)


def project_kernel(
    core_ref, rows_ref, rim_ref, got_ref, other_ref, rates_ref, pick_ref, ends_ref,
    normed_ref, proj_ref, w_ref, gains_ref, taps_ref, states_ref, values_ref, cum_ref, sent_ref,
    wide_ref,
):
    wide = w_ref.shape[1]
    flipped = core_ref[0] == 1
    taps = jnp.zeros((8, 4 * LANES), f32)
    for r in range(2 * got_ref.shape[0]):
        mine, theirs = got_ref[r // 2].astype(f32), other_ref[r // 2].astype(f32)
        part = jnp.where(flipped, theirs, mine) if r % 2 == 0 else jnp.where(flipped, mine, theirs)
        wide_ref[r * SHARD : (r + 1) * SHARD, :] = part[:SHARD]
        rest = part[SHARD:]
        taps = taps + rest[:, : 4 * LANES]
        whole = rest[:, :LANES] + rest[:, LANES : 2 * LANES] + rest[:, 2 * LANES : 3 * LANES]
        for k in range(3):
            states_ref[k, r : r + 1, :] = whole[TAPS + k : TAPS + k + 1]
    taps_ref[...] = taps
    w_ref[...] = wide_ref[...].astype(bf16)
    chosen = jnp.where(
        lanes_of((16, wide)) == rows_of((16, wide)) + GAIN_LANE, 1.0, 0.0
    )
    chosen = jnp.where(rows_of((16, wide)) < 2, chosen, 0.0).astype(bf16)
    gains = lax.dot_general(chosen, w_ref[...], (NT, ((), ())), preferred_element_type=f32)
    gains_ref[...] = gains[:8]
    gain = gains[0:1]

    def projected(rows):
        rows = rows.astype(f32)
        scale = lax.rsqrt(jnp.mean(rows * rows, -1, keepdims=True) + eps_norm)
        normed = (rows * scale * gain).astype(bf16)
        return normed, jnp.dot(normed, w_ref[...], preferred_element_type=f32)

    for at in range(0, ROWS, GROUP):
        normed, proj = projected(rows_ref[at : at + GROUP, :])
        normed_ref[at : at + GROUP, :] = normed
        proj_ref[at : at + GROUP, :] = proj
    proj_ref[ROWS:, :] = projected(rim_ref[...])[1]
    ones = lower_ones()
    pick, ends = pick_ref[...], ends_ref[...]
    lane, row = lanes_of((GROUP, LANES)), rows_of((GROUP, LANES))
    for s in range(2):
        here = slice(s * GROUP, (s + 1) * GROUP)
        steps = rates_ref[...] * jax.nn.softplus(proj_ref[here, :LANES])
        cum = summed_down(ones, steps, NN)
        cum_ref[here, :] = cum
        last = cum[GROUP - 1 : GROUP, :]
        tail = jnp.exp(last - cum)
        qk = proj_ref[here, 4 * LANES :]
        for h in range(4):
            tile = slice(h * LANES, (h + 1) * LANES)
            raw = proj_ref[here, tile]
            rim_two = proj_ref[ROWS + 2 * s : ROWS + 2 * s + 1, tile]
            rim_one = proj_ref[ROWS + 2 * s + 1 : ROWS + 2 * s + 2, tile]
            one = jnp.where(row == 0, rim_one, pltpu.roll(raw, 1, 0))
            two = jnp.where(row == 0, rim_two, jnp.where(row == 1, rim_one, pltpu.roll(raw, 2, 0)))
            conv = (
                taps_ref[0:1, tile] * raw + taps_ref[1:2, tile] * one + taps_ref[2:3, tile] * two
            )
            values = jnp.where(lane < DH, conv, jnp.where(lane == DH, 1.0, 0.0))
            values_ref[here, tile] = values
            left, right = factors(head_lanes(qk, h, True), pick, ends)
            held = left * right * ends[2:3] * head_column(tail, h)
            fresh = product(held, values, TN)
            store_pieces(sent_ref, 4 * s + h, fresh)
            ending = jnp.broadcast_to(head_column(last, h), (8, LANES))
            high, mid, low = three_parts(ending)
            few = lanes_of((8, LANES))
            packed = jnp.where(
                few == 0,
                high.astype(f32),
                jnp.where(few == 1, mid.astype(f32), jnp.where(few == 2, low.astype(f32), 0.0)),
            ).astype(bf16)
            for q in range(4):
                sent_ref[16 * s + 4 * h + q, PIECE:, :] = packed


def project(core, rows, rim, got, other, rates, pick, ends):
    wide, width = got.shape[2], rows.shape[1]
    return whole_call(
        project_kernel,
        [
            (rows.shape, bf16),
            ((ROWS + rim.shape[0], wide), f32),
            ((width, wide), bf16),
            ((8, width), f32),
            ((8, 4 * LANES), f32),
            ((3, 2 * got.shape[0], LANES), f32),
            ((ROWS, 4 * LANES), f32),
            ((ROWS, LANES), f32),
            ((PIECES, SLOT, LANES), bf16),
        ],
        core, rows, rim, got, other, rates, pick, ends,
        scratch=[pltpu.VMEM((width, wide), f32)],
        flops=3 * 10**9,
        scalars=1,
    )


def scan_kernel(got_ref, back_ref, decay_ref):
    state = jnp.zeros((PIECE, LANES), f32)
    for i in range(PIECES):
        back_ref[i, :PIECE, :] = state.astype(bf16)
        back_ref[i, PIECE:, :] = jnp.zeros((SLOT - PIECE, LANES), bf16)
        ending = jnp.sum(got_ref[i, PIECE:, :].astype(f32), -1, keepdims=True)
        decay = jnp.broadcast_to(jnp.exp(ending), (8, LANES))
        decay_ref[i] = decay
        state = state * decay[0:1] + got_ref[i, :PIECE, :].astype(f32)


def earlier_states(sent):
    got = lax.all_to_all(sent, SEQ, 0, 0, tiled=True)
    back, decay = whole_call(
        scan_kernel, [(sent.shape, bf16), ((PIECES, 8, LANES), f32)], got, flops=10**6
    )
    return lax.all_to_all(back, SEQ, 0, 0, tiled=True), decay


def scan_back_kernel(got_ref, decay_ref, back_ref):
    state = jnp.zeros((PIECE, LANES), f32)
    for i in reversed(range(PIECES)):
        back_ref[i, :PIECE, :] = state.astype(bf16)
        back_ref[i, PIECE:, :] = jnp.zeros((SLOT - PIECE, LANES), bf16)
        state = state * decay_ref[i, 0:1, :] + got_ref[i, :PIECE, :].astype(f32)


def later_states(sent, decay):
    got = lax.all_to_all(sent, SEQ, 0, 0, tiled=True)
    (back,) = whole_call(scan_back_kernel, [(sent.shape, bf16)], got, decay, flops=10**6)
    return lax.all_to_all(back, SEQ, 0, 0, tiled=True)


def within_kernel(proj_ref, values_ref, cum_ref, inside_ref):
    for s in range(2):
        here = slice(s * GROUP, (s + 1) * GROUP)
        cum = cum_ref[here, :]
        across = cum.T
        qk = proj_ref[here, 4 * LANES :]
        for h in range(4):
            tile = slice(h * LANES, (h + 1) * LANES)
            dots = scores(qk, h)
            weights = (1.0 + dots + 0.5 * dots * dots) * decays(cum, across, h)
            inside_ref[here, tile] = product(weights, values_ref[here, tile], NN)


def within(proj, values, cum):
    return whole_call(
        within_kernel, [((ROWS, 4 * LANES), f32)], proj, values, cum, flops=3 * 10**9
    )[0]


def mix_kernel(
    proj_ref, cum_ref, inside_ref, earlier_ref, pick_ref, ends_ref, total_ref, mixed_ref
):
    pick, ends = pick_ref[...], ends_ref[...]
    lane = lanes_of((GROUP, LANES))
    for s in range(2):
        here = slice(s * GROUP, (s + 1) * GROUP)
        growth = jnp.exp(cum_ref[here, :])
        qk = proj_ref[here, 4 * LANES :]
        for h in range(4):
            tile = slice(h * LANES, (h + 1) * LANES)
            left, right = factors(head_lanes(qk, h, False), pick, ends)
            held = left * right * ends[2:3] * head_column(growth, h)
            total = inside_ref[here, tile] + product(held, state_rows(earlier_ref, 4 * s + h), NN, 2)
            total_ref[here, tile] = total
            mixed = total / total[:, DH : DH + 1]
            mixed_ref[here, tile] = jnp.where(lane < DH, mixed, 0.0).astype(bf16)


def mix(proj, cum, inside, earlier, pick, ends):
    return whole_call(
        mix_kernel,
        [((ROWS, 4 * LANES), f32), ((ROWS, 4 * LANES), bf16)],
        proj, cum, inside, earlier, pick, ends,
        flops=3 * 10**9,
    )


OWN = ROWS // 4


def own_slice(ref, place):
    return ref[pl.ds(pl.multiple_of(place * OWN, OWN), OWN), :]


def join_kernel(
    place_ref, mixed_ref, w_ref, rows_ref, gains_ref, middle_ref, unit_ref, scale_ref, normed_ref
):
    branch = jnp.zeros(middle_ref.shape, f32)
    for g in range(4):
        branch = branch + lax.dot_general(
            mixed_ref[g],
            w_ref[:, g * 4 * LANES : (g + 1) * 4 * LANES],
            (NT, ((), ())),
            preferred_element_type=f32,
        )
    middle = own_slice(rows_ref, place_ref[0]).astype(f32) + branch
    scale = lax.rsqrt(jnp.mean(middle * middle, -1, keepdims=True) + eps_norm)
    unit = middle * scale
    middle_ref[...] = middle
    unit_ref[...] = unit
    scale_ref[...] = jnp.broadcast_to(scale, scale_ref.shape)
    normed_ref[...] = (unit * gains_ref[1:2]).astype(bf16)


def join(place, mixed, w_out, rows, gains):
    width = rows.shape[1]
    return whole_call(
        join_kernel,
        [
            ((OWN, width), f32),
            ((OWN, width), f32),
            ((OWN, LANES), f32),
            ((OWN, width), bf16),
        ],
        place, mixed, w_out, rows, gains,
        flops=10**9,
        scalars=1,
        cut={2: 16 * LANES},
    )


def turn_kernel(
    place_ref, got_ref, unit_ref, scale_ref, back_ref, gains_ref, w_ref,
    middle_back_ref, gain_ref, out_back_ref, mixed_back_ref,
):
    two_back = got_ref[...].astype(f32)
    unit = unit_ref[...]
    gain_ref[...] = jnp.broadcast_to(
        jnp.sum(two_back * unit, 0, keepdims=True), gain_ref.shape
    )
    weighted = two_back * gains_ref[1:2]
    along = jnp.mean(weighted * unit, -1, keepdims=True)
    middle_back = own_slice(back_ref, place_ref[0]).astype(f32) + scale_ref[:, 0:1] * (
        weighted - unit * along
    )
    middle_back_ref[...] = middle_back
    out_back = middle_back.astype(bf16)
    out_back_ref[...] = out_back
    for g in range(4):
        mixed_back_ref[g] = jnp.dot(
            out_back, w_ref[:, g * 4 * LANES : (g + 1) * 4 * LANES], preferred_element_type=f32
        ).astype(bf16)


def turn(place, got, unit, scale, back, gains, w_out):
    width = back.shape[1]
    return whole_call(
        turn_kernel,
        [
            ((OWN, width), f32),
            ((8, width), f32),
            ((OWN, width), bf16),
            ((4, OWN, 4 * LANES), bf16),
        ],
        place, got, unit, scale, back, gains, w_out,
        flops=10**9,
        scalars=1,
        cut={6: 16 * LANES},
    )


def token_kernel(place_ref, *refs):
    terms, (rows_ref, middle_back_ref, gains_ref, out_ref) = refs[:3], refs[3:]
    one_back = sum(ref[...].astype(f32) for ref in terms)
    rows = own_slice(rows_ref, place_ref[0]).astype(f32)
    scale = lax.rsqrt(jnp.mean(rows * rows, -1, keepdims=True) + eps_norm)
    unit = rows * scale
    weighted = one_back * gains_ref[0:1]
    along = jnp.mean(weighted * unit, -1, keepdims=True)
    token_back = middle_back_ref[...] + scale * (weighted - unit * along)
    out_ref[...] = token_back.astype(bf16)


def token_grads(place, terms, rows, middle_back, gains):
    return whole_call(
        token_kernel, [(terms[0].shape, bf16)], place, *terms, rows, middle_back, gains,
        flops=10**7,
        scalars=1,
    )[0]


def block_kernel(place_ref, *refs):
    terms, (middle_ref, keep_ref, out_ref) = refs[:3], refs[3:]
    ffn = sum(ref[...].astype(f32) for ref in terms)
    keep = own_slice(keep_ref, place_ref[0])[:, 0:1]
    out_ref[...] = ((middle_ref[...] + ffn) * keep).astype(bf16)


def block_outs(place, terms, middle, keep):
    return whole_call(
        block_kernel, [(terms[0].shape, bf16)], place, *terms, middle, keep,
        flops=10**7,
        scalars=1,
    )[0]


def assemble_kernel(place_ref, own_ref, side_ref, back_ref, far_a_ref, far_b_ref, out_ref):
    place = place_ref[0]
    half = OWN // 2

    def at(other):
        return pl.multiple_of(jnp.bitwise_xor(place, other) * OWN, OWN)

    out_ref[pl.ds(at(0), OWN), :] = own_ref[...]
    out_ref[pl.ds(at(1), OWN), :] = side_ref[...]
    out_ref[pl.ds(at(3), OWN), :] = back_ref[...]
    out_ref[pl.ds(at(2), half), :] = far_a_ref[...]
    out_ref[pl.ds(pl.multiple_of(at(2) + half, half), half), :] = far_b_ref[...]


def gather_rows(place, own):
    half = OWN // 2
    back = lax.ppermute(own, "mp", BACK)
    side = lax.ppermute(own, "mp", SIDE)
    far_a = lax.ppermute(back[:half], "mp", SIDE)
    far_b = lax.ppermute(side[half:], "mp", BACK)
    return whole_call(
        assemble_kernel, [((ROWS, own.shape[1]), own.dtype)], place, own, side, back, far_a, far_b,
        flops=10**6,
        scalars=1,
    )[0]


def scatter_terms(part):
    half = OWN // 2
    got_a = lax.ppermute(part[2, :half], "mp", SIDE)
    got_b = lax.ppermute(part[2, half:], "mp", BACK)
    to_back = jnp.concatenate(
        [(part[3, :half].astype(f32) + got_a.astype(f32)).astype(bf16), part[3, half:]], 0
    )
    to_side = jnp.concatenate(
        [part[1, :half], (part[1, half:].astype(f32) + got_b.astype(f32)).astype(bf16)], 0
    )
    return part[0], lax.ppermute(to_back, "mp", BACK), lax.ppermute(to_side, "mp", SIDE)


def store_by_owner(ref, value, place, columns=slice(None)):
    for g in range(4):
        ref[jnp.bitwise_xor(place, g), :, columns] = value[g * OWN : (g + 1) * OWN]


def unmix_kernel(
    mixed_back_ref, total_ref, proj_ref, cum_ref, pick_ref, ends_ref, total_back_ref, sent_ref
):
    pick, ends = pick_ref[...], ends_ref[...]
    lane = lanes_of((GROUP, LANES))
    for s in range(2):
        here = slice(s * GROUP, (s + 1) * GROUP)
        growth = jnp.exp(cum_ref[here, :])
        qk = proj_ref[here, 4 * LANES :]
        for h in range(4):
            tile = slice(h * LANES, (h + 1) * LANES)
            total = total_ref[here, tile]
            inverse = 1.0 / total[:, DH : DH + 1]
            numer = mixed_back_ref[here, tile].astype(f32) * inverse
            numer = jnp.where(lane < DH, numer, 0.0)
            denom = -jnp.sum(numer * total, -1, keepdims=True) * inverse
            total_back = jnp.where(lane == DH, denom, numer)
            total_back_ref[here, tile] = total_back
            left, right = factors(head_lanes(qk, h, False), pick, ends)
            held = left * right * ends[2:3] * head_column(growth, h)
            store_pieces(sent_ref, 4 * s + h, product(held, total_back, TN))
            for q in range(4):
                sent_ref[16 * s + 4 * h + q, PIECE:, :] = jnp.zeros((SLOT - PIECE, LANES), bf16)


def unmix(mixed_back, total, proj, cum, pick, ends):
    return whole_call(
        unmix_kernel,
        [((ROWS, 4 * LANES), f32), ((PIECES, SLOT, LANES), bf16)],
        mixed_back, total, proj, cum, pick, ends,
        flops=3 * 10**9,
    )


def within_back_kernel(
    proj_ref, values_ref, cum_ref, total_back_ref, earlier_ref, pick_ref, ends_ref,
    qk_back_ref, values_back_ref, level_ref,
):
    pick, ends = pick_ref[...], ends_ref[...]
    only = lanes_of((GROUP, LANES)) < FEAT
    for s in range(2):
        here = slice(s * GROUP, (s + 1) * GROUP)
        cum = cum_ref[here, :]
        across = cum.T
        growth = jnp.exp(cum)
        qk = proj_ref[here, 4 * LANES :]
        qk_back = jnp.zeros((GROUP, LANES), f32)
        level = jnp.zeros((GROUP, LANES), f32)
        level_down = jnp.zeros((LANES, GROUP), f32)
        for h in range(4):
            tile = slice(h * LANES, (h + 1) * LANES)
            total_back = total_back_ref[here, tile]
            decay = decays(cum, across, h)
            dots = scores(qk, h)
            pairing = decay * product(total_back, values_ref[here, tile], NT)
            kernel = 1.0 + dots + 0.5 * dots * dots
            moved = kernel * pairing
            down = jnp.sum(moved, 0, keepdims=True)
            level_down = jnp.where(rows_of((LANES, GROUP)) == GATE_LANE + h, down, level_down)
            kernel_back = pairing * (1.0 + dots) * 0.25
            values_back_ref[here, tile] = product(kernel * decay, total_back, TN)
            query_tile = head_lanes(qk, h, False)
            keys_only = jnp.where(only, head_lanes(qk, h, True), 0.0)
            query_only = jnp.where(only, query_tile, 0.0)
            query_back = product(kernel_back, keys_only, NN)
            keys_back = product(kernel_back, query_only, TN)
            left, right = factors(query_tile, pick, ends)
            features_back = head_column(growth, h) * product(
                total_back, state_rows(earlier_ref, 4 * s + h), NT, 2
            )
            level_here = jnp.sum(moved, 1, keepdims=True) + jnp.sum(
                left * right * ends[2:3] * features_back, 1, keepdims=True
            )
            level = level + on_head_lane(level_here, h)
            query_back = query_back + factors_back(features_back, left, right, pick, ends)
            at = h * FEAT
            qk_back = qk_back + (pltpu.roll(query_back, at, 1) if at else query_back)
            qk_back = qk_back + pltpu.roll(keys_back, at + 4 * FEAT, 1)
        qk_back_ref[here, :] = qk_back
        level_ref[here, :] = level - level_down.T


def within_back(proj, values, cum, total_back, earlier, pick, ends):
    return whole_call(
        within_back_kernel,
        [((ROWS, LANES), f32), ((ROWS, 4 * LANES), f32), ((ROWS, LANES), f32)],
        proj, values, cum, total_back, earlier, pick, ends,
        flops=8 * 10**9,
    )


def later_back_kernel(
    proj_ref, values_ref, cum_ref, rates_ref, earlier_ref, later_ref, pick_ref, ends_ref,
    qk_in_ref, values_in_ref, level_ref,
    qk_back_ref, values_back_ref, gate_back_ref,
):
    pick, ends = pick_ref[...], ends_ref[...]
    ones, before = lower_ones(), lower_ones(True)
    for s in range(2):
        here = slice(s * GROUP, (s + 1) * GROUP)
        cum = cum_ref[here, :]
        last = cum[GROUP - 1 : GROUP, :]
        tail = jnp.exp(last - cum)
        carried = jnp.exp(last)
        qk = proj_ref[here, 4 * LANES :]
        qk_back = qk_in_ref[here, :]
        crossed = jnp.zeros((GROUP, LANES), f32)
        through = jnp.zeros((1, LANES), f32)
        for h in range(4):
            tile = slice(h * LANES, (h + 1) * LANES)
            later = state_rows(later_ref, 4 * s + h)
            left, right = factors(head_lanes(qk, h, True), pick, ends)
            held = left * right * ends[2:3]
            column = head_column(tail, h)
            features_back = column * product(values_ref[here, tile], later, NT, 2)
            values_back_ref[here, tile] = values_in_ref[here, tile] + column * product(
                held, later, NN, 2
            )
            crossed = crossed + on_head_lane(
                jnp.sum(held * features_back, 1, keepdims=True), h
            )
            keys_back = factors_back(features_back, left, right, pick, ends)
            qk_back = qk_back + pltpu.roll(keys_back, (h + 4) * FEAT, 1)
            whole = jnp.sum(
                later.astype(f32) * state_rows(earlier_ref, 4 * s + h).astype(f32), 1, keepdims=True
            )
            whole = jnp.sum(whole, 0, keepdims=True) * head_column(carried, h)
            through = through + on_head_lane(whole, h)
        qk_back_ref[here, :] = qk_back
        step_back = (
            summed_down(ones, level_ref[here, :], TN) + summed_down(before, crossed, NN) + through
        )
        gate_back_ref[here, :] = (
            step_back * rates_ref[...] * jax.nn.sigmoid(proj_ref[here, :LANES])
        )


def later_back(proj, values, cum, rates, earlier, later, pick, ends, qk_back, values_back, level):
    return whole_call(
        later_back_kernel,
        [((ROWS, LANES), f32), ((ROWS, 4 * LANES), f32), ((ROWS, LANES), f32)],
        proj, values, cum, rates, earlier, later, pick, ends, qk_back, values_back, level,
        flops=4 * 10**9,
    )


def unproject_kernel(
    place_ref, proj_ref, ahead_ref, taps_ref, qk_back_ref, values_back_ref, gate_back_ref, normed_ref, w_ref,
    out_back_ref, mixed_ref, gain_two_ref,
    part_ref, kept_ref, sent_ref, taps_grad_ref, proj_back_ref,
):
    lane, row = lanes_of((GROUP, LANES)), rows_of((GROUP, LANES))
    taps_grad_ref[...] = jnp.zeros_like(taps_grad_ref)
    for s in range(2):
        here = slice(s * GROUP, (s + 1) * GROUP)
        for h in range(4):
            tile = slice(h * LANES, (h + 1) * LANES)
            raw = proj_ref[here, tile]
            back = values_back_ref[here, tile]
            back = jnp.where(lane < DH, back, 0.0)
            rim_two = proj_ref[ROWS + 2 * s : ROWS + 2 * s + 1, tile]
            rim_one = proj_ref[ROWS + 2 * s + 1 : ROWS + 2 * s + 2, tile]
            one = jnp.where(row == 0, rim_one, pltpu.roll(raw, 1, 0))
            two = jnp.where(row == 0, rim_two, jnp.where(row == 1, rim_one, pltpu.roll(raw, 2, 0)))
            for j, moved in enumerate((raw, one, two)):
                taps_grad_ref[j : j + 1, tile] = taps_grad_ref[j : j + 1, tile] + jnp.sum(
                    moved * back, 0, keepdims=True
                )
            next_one = ahead_ref[2 * s : 2 * s + 1, tile]
            next_two = ahead_ref[2 * s + 1 : 2 * s + 2, tile]
            one = jnp.where(row == GROUP - 1, next_one, pltpu.roll(back, GROUP - 1, 0))
            two = jnp.where(
                row == GROUP - 1,
                next_two,
                jnp.where(row == GROUP - 2, next_one, pltpu.roll(back, GROUP - 2, 0)),
            )
            raw_back = (
                taps_ref[0:1, tile] * back + taps_ref[1:2, tile] * one + taps_ref[2:3, tile] * two
            )
            raw_back = jnp.where(lane < DH, raw_back, 0.0)
            if h == 0:
                gates = (lane >= GATE_LANE) & (lane < GATE_LANE + 4)
                raw_back = jnp.where(gates, gate_back_ref[here, :], raw_back)
            proj_back_ref[here, tile] = raw_back.astype(bf16)
        proj_back_ref[here, 4 * LANES :] = qk_back_ref[here, :].astype(bf16)
    part = lax.dot_general(
        proj_back_ref[...], w_ref[...], (NT, ((), ())), preferred_element_type=f32
    ).astype(bf16)
    store_by_owner(part_ref, part, place_ref[0])
    wide = w_ref.shape[1]
    grad_in = lax.dot_general(
        normed_ref[...], proj_back_ref[...], (TN, ((), ())), preferred_element_type=f32
    )
    weights = w_ref[...].astype(f32)
    gain_one = jnp.sum(grad_in * weights, 1, keepdims=True)
    gain_one = gain_one / weights[:, GAIN_LANE : GAIN_LANE + 1]
    gain_two = gain_two_ref[...].T[:, 0:1]
    first = grad_in[:, :LANES]
    spot = lanes_of(first.shape)
    first = jnp.where(
        spot == GAIN_LANE, gain_one, jnp.where(spot == GAIN_LANE + 1, gain_two, first)
    )
    grad_out = lax.dot_general(
        out_back_ref[...], mixed_ref[...], (TN, ((), ())), preferred_element_type=f32
    )
    core = place_ref[1]

    def store(ref, parity):
        for k in range(ref.shape[0]):
            r = 2 * k + parity
            here = slice(r * SHARD, (r + 1) * SHARD)
            ref[k, :SHARD, :LANES] = first[here].astype(bf16)
            ref[k, :SHARD, LANES:wide] = grad_in[here, LANES:].astype(bf16)
            ref[k, :SHARD, wide:] = grad_out[here].astype(bf16)
            h, at = r // 8, (r % 8) * (DH // 8)
            few = taps_grad_ref[:, h * LANES : (h + 1) * LANES]
            few = pltpu.roll(few, LANES - at, 1) if at else few
            ref[k, SHARD:, :LANES] = few.astype(bf16)
            ref[k, SHARD:, LANES:] = jnp.zeros((SPACED - SHARD, wide + 3 * LANES), bf16)

    for parity in range(2):

        @pl.when(core == parity)
        def _():
            store(kept_ref, parity)
            store(sent_ref, 1 - parity)


def unproject(
    place, proj, ahead, taps, qk_back, values_back, gate_back, normed, w_in, out_back, mixed, gain_two
):
    width, wide = w_in.shape
    return whole_call(
        unproject_kernel,
        [
            ((4, OWN, width), bf16),
            ((width // SHARD // 2, SPACED, wide + 4 * LANES), bf16),
            ((width // SHARD // 2, SPACED, wide + 4 * LANES), bf16),
        ],
        place, proj, ahead, taps, qk_back, values_back, gate_back, normed, w_in, out_back, mixed, gain_two,
        scratch=[pltpu.VMEM((8, 4 * LANES), f32), pltpu.VMEM((ROWS, wide), bf16)],
        flops=4 * 10**9,
        scalars=1,
    )


BLOCK = 256
HIDDEN = 1280
OUT = 16 * LANES
SHARD = 56
SPACED = 64


def ffn_kernel(normed_ref, back_ref, gate_ref, up_ref, down_ref, both_ref, acts_ref, two_ref):
    step = pl.program_id(0)
    blocks = HIDDEN // BLOCK

    @pl.when(step < blocks)
    def _():
        normed = normed_ref[...]
        gate = jnp.dot(normed, gate_ref[...], preferred_element_type=f32)
        up = jnp.dot(normed, up_ref[...], preferred_element_type=f32)
        hidden_back = jnp.dot(back_ref[...], down_ref[...], preferred_element_type=f32)
        sigma = jax.nn.sigmoid(gate)
        silu = gate * sigma
        at = pl.multiple_of(step * BLOCK, BLOCK)
        acts_ref[:, pl.ds(at, BLOCK)] = (
            hidden_back * up * sigma * (1.0 + gate * (1.0 - sigma))
        ).astype(bf16)
        acts_ref[:, pl.ds(HIDDEN + at, BLOCK)] = (hidden_back * silu).astype(bf16)
        acts_ref[:, pl.ds(2 * HIDDEN + at, BLOCK)] = (silu * up).astype(bf16)

    @pl.when(step >= blocks)
    def _():
        two_ref[...] = lax.dot_general(
            acts_ref[:, : 2 * HIDDEN], both_ref[...], (NT, ((), ())), preferred_element_type=f32
        ).astype(bf16)


def ffn_both_ways(normed, back, weights):
    width = normed.shape[1]
    blocks, outs = HIDDEN // BLOCK, width // BLOCK
    whole = pl.BlockSpec((ROWS, width), lambda i: (0, 0))

    def columns(which):
        first = OUT // BLOCK + which * blocks
        return pl.BlockSpec((width, BLOCK), lambda i: (0, first + jnp.minimum(i, blocks - 1)))

    return pl.pallas_call(
        ffn_kernel,
        grid=(blocks + outs,),
        out_shape=[
            jax.ShapeDtypeStruct((ROWS, 3 * HIDDEN), bf16),
            jax.ShapeDtypeStruct((ROWS, width), bf16),
        ],
        in_specs=[
            whole,
            whole,
            columns(0),
            columns(1),
            columns(2),
            pl.BlockSpec(
                (pl.Element(BLOCK), pl.Element(2 * HIDDEN)),
                lambda i: (jnp.maximum(i - blocks, 0) * BLOCK, OUT),
            ),
        ],
        out_specs=[
            pl.BlockSpec((ROWS, 3 * HIDDEN), lambda i: (0, 0)),
            pl.BlockSpec((ROWS, BLOCK), lambda i: (0, jnp.maximum(i - blocks, 0))),
        ],
        compiler_params=pltpu.CompilerParams(vmem_limit_bytes=60 * MIB),
        cost_estimate=pl.CostEstimate(
            flops=12 * 10**9, bytes_accessed=25 * 10**6, transcendentals=0
        ),
    )(normed, back, weights, weights, weights, weights)


def ffn_out_kernel(place_ref, acts_ref, down_ref, out_ref):
    value = lax.dot_general(
        acts_ref[...], down_ref[...], (NT, ((), ())), preferred_element_type=f32
    ).astype(bf16)
    store_by_owner(out_ref, value, place_ref[0])


def ffn_out(place, acts, weights):
    width = weights.shape[0]
    return pl.pallas_call(
        ffn_out_kernel,
        grid=(width // BLOCK,),
        out_shape=jax.ShapeDtypeStruct((4, OWN, width), bf16),
        in_specs=[
            pl.BlockSpec(memory_space=pltpu.SMEM),
            pl.BlockSpec((ROWS, HIDDEN), lambda i: (0, 2)),
            pl.BlockSpec(
                (pl.Element(BLOCK), pl.Element(HIDDEN)), lambda i: (i * BLOCK, OUT + 2 * HIDDEN)
            ),
        ],
        out_specs=pl.BlockSpec((4, OWN, BLOCK), lambda i: (0, 0, i)),
        compiler_params=pltpu.CompilerParams(vmem_limit_bytes=60 * MIB),
        cost_estimate=pl.CostEstimate(
            flops=3 * 10**9, bytes_accessed=8 * 10**6, transcendentals=0
        ),
    )(place, acts, weights)


def ffn_grads_kernel(normed_ref, back_ref, acts_ref, grads_ref):
    def spaced(rows_ref):
        grad = lax.dot_general(
            rows_ref[...], acts_ref[...], (TN, ((), ())), preferred_element_type=f32
        )
        for r in range(grad.shape[0] // SHARD):
            grads_ref[r * SPACED : r * SPACED + SHARD, :] = grad[
                r * SHARD : (r + 1) * SHARD
            ].astype(bf16)
            grads_ref[r * SPACED + SHARD : (r + 1) * SPACED, :] = jnp.zeros(
                (SPACED - SHARD, grad.shape[1]), bf16
            )

    both = pl.program_id(0) < 2 * HIDDEN // WIDER

    @pl.when(both)
    def _():
        spaced(normed_ref)

    @pl.when(jnp.logical_not(both))
    def _():
        spaced(back_ref)


WIDER = 640


def ffn_grads(normed, back, acts):
    width = normed.shape[1]
    whole = pl.BlockSpec((ROWS, width), lambda i: (0, 0))
    return pl.pallas_call(
        ffn_grads_kernel,
        grid=(3 * HIDDEN // WIDER,),
        out_shape=jax.ShapeDtypeStruct((width // SHARD * SPACED, 3 * HIDDEN), bf16),
        in_specs=[whole, whole, pl.BlockSpec((ROWS, WIDER), lambda i: (0, i))],
        out_specs=pl.BlockSpec((width // SHARD * SPACED, WIDER), lambda i: (0, i)),
        compiler_params=pltpu.CompilerParams(vmem_limit_bytes=60 * MIB),
        cost_estimate=pl.CostEstimate(
            flops=7 * 10**9, bytes_accessed=20 * 10**6, transcendentals=0
        ),
    )(normed, back, acts)


def order_columns(heads):
    import numpy as np

    place = np.zeros((5 * LANES, 5 * LANES), np.float32)
    for h in range(heads):
        at = h * (2 * FEAT + DH + 1)
        for i in range(FEAT):
            place[at + i, heads * LANES + h * FEAT + i] = 1.0
            place[at + FEAT + i, heads * LANES + (heads + h) * FEAT + i] = 1.0
        for i in range(DH):
            place[at + 2 * FEAT + i, h * LANES + i] = 1.0
        place[at + 2 * FEAT + DH, GATE_LANE + h] = 1.0
    return jnp.asarray(place, bf16)


def order_heads(heads):
    import numpy as np

    place = np.zeros((heads * DH, heads * LANES), np.float32)
    for h in range(heads):
        for i in range(DH):
            place[h * DH + i, h * LANES + i] = 1.0
    return jnp.asarray(place, bf16)


def prepare_kernel(
    rank_ref, in_ref, out_ref, gate_ref, up_ref, down_ref, taps_ref,
    gains_ref, gains_first_ref, gains_second_ref, place_ref, tiles_ref,
    shard_ref, out_shard_ref, rest_ref, few_ref,
):
    wide = 5 * LANES
    columns = in_ref.shape[1]
    whole = jnp.dot(
        in_ref[...].astype(bf16), place_ref[:columns, :], preferred_element_type=f32
    )
    spot = jnp.where(
        lanes_of((2, wide)) == rows_of((2, wide)) + GAIN_LANE, 1.0, 0.0
    ).astype(bf16)
    gains = lax.dot_general(
        gains_ref[...].astype(bf16), spot, (TN, ((), ())), preferred_element_type=f32
    )
    shard_ref[:SHARD, :] = (whole + gains).astype(bf16)
    rank = rank_ref[0]
    own = taps_ref.shape[1]
    each = DH // own
    first = (rank // each) * LANES + (rank % each) * own
    spot = jnp.where(
        lanes_of((own, wide)) == rows_of((own, wide)) + first, 1.0, 0.0
    ).astype(bf16)
    taps = jnp.dot(taps_ref[...].astype(bf16), spot, preferred_element_type=f32)
    rows = [taps]
    for ref in (gains_ref, gains_first_ref, gains_second_ref):
        few_ref[...] = jnp.zeros_like(few_ref)
        few_ref[0:2, :SHARD] = ref[...]
        both = few_ref[...]
        line = both + pltpu.roll(pltpu.roll(both, SHARD, 1), 7, 0)
        parts = [part.astype(f32)[0:1] for part in three_parts(line)]
        rows.append(jnp.concatenate(parts + [jnp.zeros((1, wide - 3 * LANES), f32)], 1))
    rows.append(jnp.zeros((SPACED - SHARD - TAPS - 3, wide), f32))
    shard_ref[SHARD:, :] = jnp.concatenate(rows, 0).astype(bf16)
    out_shard_ref[...] = jnp.dot(
        out_ref[...].astype(bf16), tiles_ref[...], preferred_element_type=f32
    ).astype(bf16)
    rest_ref[...] = jnp.zeros_like(rest_ref)
    units = gate_ref.shape[1]
    rest_ref[:, :units] = gate_ref[...].astype(bf16)
    rest_ref[:, HIDDEN : HIDDEN + units] = up_ref[...].astype(bf16)
    rest_ref[:, 2 * HIDDEN : 2 * HIDDEN + units] = down_ref[...].astype(bf16)


def prepare(rank, *args):
    return whole_call(
        prepare_kernel,
        [
            ((SPACED, 5 * LANES), bf16),
            ((SHARD, 4 * LANES), bf16),
            ((SHARD, 3 * HIDDEN), bf16),
        ],
        rank, *args,
        scratch=[pltpu.VMEM((8, LANES), f32)],
        scalars=1,
    )


def moved_moments(weight, first, second, grad):
    fix = 1.0 - beta_value**STEP
    moment = beta_value * first + (1.0 - beta_value) * grad
    square = beta_value * second + (1.0 - beta_value) * grad * grad
    direction = moment / fix / (jnp.sqrt(square / fix) + eps_adam) + decay_rate * weight
    return moment, square, direction


def moments_kernel(mixer_ref, ffn_ref, place_ref, tiles_ref, *refs):
    params, outs, sums_ref = refs[:18], refs[18:-1], refs[-1]
    wide = 5 * LANES
    units = params[6].shape[1]
    mixer = mixer_ref[0].astype(f32)
    for k in range(1, mixer_ref.shape[0]):
        mixer = mixer + mixer_ref[k].astype(f32)
    sums = jnp.zeros((1, 2 * LANES), f32)
    lane = lanes_of((1, 2 * LANES))

    def adapt(index, grad):
        weight = params[3 * index][...]
        moment, square, direction = moved_moments(
            weight, params[3 * index + 1][...], params[3 * index + 2][...], grad
        )
        outs[3 * index][...] = moment
        outs[3 * index + 1][...] = square
        outs[3 * index + 2][...] = direction
        both = [
            jnp.sum(jnp.sum(v * v, 1, keepdims=True), 0, keepdims=True)
            for v in (weight, direction)
        ]
        return jnp.where(
            lane == 2 * index, both[0], jnp.where(lane == 2 * index + 1, both[1], 0.0)
        )

    grad_in = picked(mixer[:SHARD, :wide], place_ref[...], NT)
    sums = sums + adapt(0, grad_in[:, : params[0].shape[1]])
    sums = sums + adapt(1, picked(mixer[:SHARD, wide:], tiles_ref[...], NT))
    sums = sums + adapt(2, ffn_ref[:SHARD, :units].astype(f32))
    sums = sums + adapt(3, ffn_ref[:SHARD, HIDDEN : HIDDEN + units].astype(f32))
    sums = sums + adapt(4, ffn_ref[:SHARD, 2 * HIDDEN : 2 * HIDDEN + units].astype(f32))
    sums = sums + adapt(5, mixer[SHARD : SHARD + TAPS, : params[15].shape[1]])
    across = jnp.concatenate([mixer[:, :LANES], jnp.zeros((LANES - SPACED, LANES), f32)], 0).T
    ones = across[GAIN_LANE : GAIN_LANE + 1]
    twos = across[GAIN_LANE + 1 : GAIN_LANE + 2]
    few = lanes_of((1, LANES))
    line = jnp.where(few < SHARD, ones, 0.0) + pltpu.roll(
        jnp.broadcast_to(jnp.where(few < SHARD, twos, 0.0), (8, LANES)), SHARD, 1
    )[0:1]
    sums = sums + jnp.concatenate([jnp.zeros((1, LANES), f32), line], 1)
    sums_ref[...] = jnp.broadcast_to(sums, sums_ref.shape)


def moments(mixer, ffn, place, tiles, params):
    outs = []
    for param in params[0::3]:
        outs += [(param.shape, f32)] * 3
    outs.append(((LANES, 2 * LANES), f32))
    return whole_call(moments_kernel, outs, mixer, ffn, place, tiles, *params)


def update_kernel(rank_ref, totals_ref, states_ref, *refs):
    weights, directions, outs = refs[:6], refs[6:12], refs[12:18]
    gains_refs, norms_ref = refs[18:21], refs[21]
    totals = totals_ref[...]
    sums = jnp.sum(totals[:, :LANES], 0, keepdims=True)
    lane = lanes_of((1, LANES))
    grouped = jnp.where(
        lanes_of((32, LANES)) // 4 == rows_of((32, LANES)), 1.0, 0.0
    ).astype(bf16)
    grad = summed_down(grouped, totals[:, LANES:], NN)
    moment, square, direction = moved_moments(
        states_ref[0], states_ref[1], states_ref[2], grad
    )
    live = lanes_of((32, LANES)) < 2 * SHARD
    for place, value in ((12, states_ref[0]), (13, direction)):
        value = jnp.where(live, value, 0.0)
        value = jnp.sum(jnp.sum(value * value, 1, keepdims=True), 0, keepdims=True)
        sums = jnp.where(lane == place, value, sums)
    norms = jnp.sqrt(sums)
    norms_ref[...] = jnp.broadcast_to(norms, norms_ref.shape)

    def ratio(index):
        return norms[:, 2 * index : 2 * index + 1] / norms[:, 2 * index + 1 : 2 * index + 2]

    for index in range(6):
        outs[index][...] = (
            weights[index][...] - learn_rate * ratio(index) * directions[index][...]
        )
    updated = states_ref[0] - learn_rate * ratio(6) * direction
    for ref, value in zip(gains_refs, (updated, moment, square)):
        own = jnp.where(rows_of((32, LANES)) == rank_ref[0], value, 0.0)
        own = jnp.broadcast_to(jnp.sum(own, 0, keepdims=True), (8, LANES))
        ref[0:1, :] = own[0:1, :SHARD]
        ref[1:2, :] = pltpu.roll(own, LANES - SHARD, 1)[0:1, :SHARD]


def update(rank, totals, states, weights, directions):
    outs = [(w.shape, f32) for w in weights] + [((2, SHARD), f32)] * 3 + [((8, LANES), f32)]
    return whole_call(
        update_kernel, outs, rank, totals, states, *weights, *directions, scalars=1
    )


def per_device(
    tokens,
    cotangent,
    lengths,
    rate_codes,
    inproj,
    inproj_first,
    inproj_second,
    outproj,
    outproj_first,
    outproj_second,
    gateproj,
    gateproj_first,
    gateproj_second,
    upproj,
    upproj_first,
    upproj_second,
    downproj,
    downproj_first,
    downproj_second,
    convtaps,
    convtaps_first,
    convtaps_second,
    normgains,
    normgains_first,
    normgains_second,
):
    seqs, group, width = tokens.shape
    heads = rate_codes.shape[0]
    lag = TAPS - 1
    rank = lax.axis_index(SEQ).reshape(1)
    core = lax.axis_index("seq_2")
    peer = lax.axis_index("mp").reshape(1)
    pick, ends = selections()
    place, tiles = order_columns(heads), order_heads(heads)

    shard, out_shard, rest_shard = prepare(
        rank, inproj, outproj.T, gateproj, upproj, downproj.T, convtaps,
        normgains, normgains_first, normgains_second, place, tiles,
    )
    got = lax.all_to_all(
        jnp.broadcast_to(shard[None], (16,) + shard.shape), ("seq_0", "seq_1"), 0, 0, tiled=True
    )
    other = lax.ppermute(got, "seq_2", SWAP)
    turned = [out_shard] + [
        lax.ppermute(out_shard, "mp", [(i, (i - k) % 4) for i in range(4)]) for k in range(1, 4)
    ]
    out_shards = jnp.roll(jnp.stack(turned), peer[0], axis=0)
    weights_shard = jnp.concatenate([out_shards[g] for g in range(4)] + [rest_shard], 1)
    weights_shard, got = lax.optimization_barrier((weights_shard, got))
    weights = lax.all_gather(weights_shard, SEQ, axis=0, tiled=True)

    rows = tokens.reshape(-1, width)
    rim = shifted(tokens[:, group - lag :], SEQ, 1).reshape(-1, width)
    rim = jnp.pad(rim, ((0, 16 - seqs * lag), (0, 0)))
    positions = rank * group + jnp.arange(group, dtype=jnp.int32)
    keep = (positions[None, :] < lengths[:, None]).astype(f32).reshape(-1, 1)
    back = (cotangent.reshape(-1, width).astype(f32) * keep).astype(bf16)
    rates = -jnp.exp2(-rate_codes.astype(f32) / 4.0)
    rates = jnp.pad(rates[None], ((0, 0), (GATE_LANE, LANES - GATE_LANE - heads)))
    normed_one, proj, w_in, gains, taps, states, values, cum, sent = project(
        core.reshape(1), rows, rim, got, other, rates, pick, ends
    )
    earlier, decay = earlier_states(sent)
    inside = within(proj, values, cum)
    total, mixed = mix(proj, cum, inside, earlier, pick, ends)

    mixed_got = lax.all_to_all(mixed.reshape(4, OWN, -1), "mp", 0, 0, tiled=True)
    middle, unit_two, scale_two, normed_own = join(peer, mixed_got, weights, rows, gains)
    normed_two = lax.all_gather(normed_own, "mp", axis=0, tiled=True)

    acts, two_part = ffn_both_ways(normed_two, back, weights)
    two_back = lax.psum_scatter(two_part, "mp", scatter_dimension=0, tiled=True)
    ffn_part = ffn_out(peer, acts, weights)
    two_back, ffn_part = lax.optimization_barrier((two_back, ffn_part))
    ffn_sums = lax.psum_scatter(
        ffn_grads(normed_two, back, acts), SEQ, scatter_dimension=0, tiled=True
    )
    middle_back, gain_two, out_own, mixed_back = turn(
        peer, two_back, unit_two, scale_two, back, gains, weights
    )
    mixed_back = lax.all_to_all(mixed_back, "mp", 0, 0, tiled=True).reshape(ROWS, -1)

    total_back, sent = unmix(mixed_back, total, proj, cum, pick, ends)
    ffn_part, out_own, sent = lax.optimization_barrier((ffn_part, out_own, sent))
    later = later_states(sent, decay)
    qk_back, values_back, level = within_back(
        proj, values, cum, total_back, earlier, pick, ends
    )
    out_back = gather_rows(peer, out_own)
    ffn_terms = scatter_terms(ffn_part)
    qk_back, values_back, gate_back = later_back(
        proj, values, cum, rates, earlier, later, pick, ends, qk_back, values_back, level
    )
    edge = values_back.reshape(seqs, group, -1)[:, :lag]
    ahead = shifted(edge, SEQ, -1).reshape(seqs * lag, -1)
    ahead = jnp.concatenate([ahead, jnp.zeros_like(ahead)], 0)
    ahead, ffn_terms = lax.optimization_barrier((ahead, ffn_terms))
    one_part, kept, sent = unproject(
        jnp.concatenate([peer, core.reshape(1)]), proj, ahead, taps, qk_back, values_back, gate_back, normed_one, w_in, out_back, mixed,
        gain_two,
    )

    swapped = lax.ppermute(sent, "seq_2", SWAP)
    mixer_part = (kept.astype(f32) + swapped.astype(f32)).astype(bf16)

    one_part, mixer_part = lax.optimization_barrier((one_part, mixer_part))
    mixer_got = lax.all_to_all(mixer_part, ("seq_0", "seq_1"), 0, 0, tiled=True)
    one_terms = scatter_terms(one_part)
    block_out = lax.all_gather(
        block_outs(peer, ffn_terms, middle, jnp.broadcast_to(keep, (ROWS, LANES))),
        "mp",
        axis=0,
        tiled=True,
    )

    params = (
        (inproj, inproj_first, inproj_second)
        + (outproj.T, outproj_first.T, outproj_second.T)
        + (gateproj, gateproj_first, gateproj_second)
        + (upproj, upproj_first, upproj_second)
        + (downproj.T, downproj_first.T, downproj_second.T)
        + (convtaps, convtaps_first, convtaps_second)
    )
    *moved, sums = moments(mixer_got, ffn_sums, place, tiles, params)
    one_terms, _ = lax.optimization_barrier((one_terms, sums))
    token_grad = gather_rows(peer, token_grads(peer, one_terms, rows, middle_back, gains))
    totals = lax.all_to_all(sums, ALL, 0, 0, tiled=True)
    *updated, gains_new, gains_moment, gains_square, norms = update(
        rank, totals, states, params[0::3], moved[2::3]
    )
    results = [block_out.reshape(tokens.shape), token_grad.reshape(tokens.shape)]
    for index in range(6):
        for value in (updated[index], moved[3 * index], moved[3 * index + 1]):
            results.append(value.T if index in (1, 4) else value)
    results += [gains_new, gains_moment, gains_square, norms[0, :14].reshape(7, 2)]
    return tuple(results)


def solution(mesh):
    split = Mesh(mesh.devices.reshape(4, 4, 2, mesh.shape["mp"]), ("seq_0", "seq_1", "seq_2", "mp"))
    in_specs = (
        P(None, SEQ, None),
        P(None, SEQ, None),
        P(),
        P("mp"),
        P(SEQ, "mp"),
        P(SEQ, "mp"),
        P(SEQ, "mp"),
        P("mp", SEQ),
        P("mp", SEQ),
        P("mp", SEQ),
        P(SEQ, "mp"),
        P(SEQ, "mp"),
        P(SEQ, "mp"),
        P(SEQ, "mp"),
        P(SEQ, "mp"),
        P(SEQ, "mp"),
        P("mp", SEQ),
        P("mp", SEQ),
        P("mp", SEQ),
        P(None, MP_SEQ),
        P(None, MP_SEQ),
        P(None, MP_SEQ),
        P(None, SEQ),
        P(None, SEQ),
        P(None, SEQ),
    )
    out_specs = (
        P(None, SEQ, None),
        P(None, SEQ, None),
        P(SEQ, "mp"),
        P(SEQ, "mp"),
        P(SEQ, "mp"),
        P("mp", SEQ),
        P("mp", SEQ),
        P("mp", SEQ),
        P(SEQ, "mp"),
        P(SEQ, "mp"),
        P(SEQ, "mp"),
        P(SEQ, "mp"),
        P(SEQ, "mp"),
        P(SEQ, "mp"),
        P("mp", SEQ),
        P("mp", SEQ),
        P("mp", SEQ),
        P(None, MP_SEQ),
        P(None, MP_SEQ),
        P(None, MP_SEQ),
        P(None, SEQ),
        P(None, SEQ),
        P(None, SEQ),
        P(),
    )
    return jax.shard_map(
        per_device, mesh=split, in_specs=in_specs, out_specs=out_specs, check_vma=False
    )
```

```python
import math

import jax
import jax.numpy as jnp
from jax import lax
from jax.experimental import pallas as pl
from jax.experimental.pallas import tpu as pltpu
from jax.sharding import Mesh
from jax.sharding import PartitionSpec as P

DH = 112
FEAT = 16
TAPS = 3
STEP = 7
LANES = 128
SEQ = ("seq_0", "seq_1", "seq_2")
ALL = ("seq_0", "seq_1", "seq_2", "mp")
MP_SEQ = ("mp", "seq_0", "seq_1", "seq_2")

f32 = jnp.float32
bf16 = jnp.bfloat16
highest = lax.Precision.HIGHEST
root_half = 0.5**0.5
eps_norm = 1e-05
eps_adam = 1e-06
decay_rate = 0.01
learn_rate = 0.3
beta_value = 0.5

SIDE = [(i, i ^ 1) for i in range(4)]
BACK = [(i, 3 - i) for i in range(4)]
SWAP = [(0, 1), (1, 0)]


def shifted(value, axis, steps):
    count = lax.axis_size(axis)
    first, last = (max(0, -steps), min(count, count - steps))
    return lax.ppermute(value, axis, [(source, source + steps) for source in range(first, last)])


SPAN_LANE = DH
GATE_LANE = DH
GAIN_LANE = DH + 4
GROUP = 256
ROWS = 512
SIDES = 256
PIECE = 40
SLOT = 48
PIECES = 32
MIB = 1 << 20


def selections():
    import numpy as np

    pick = np.zeros((2 * LANES, 2 * SIDES), np.float32)
    ends = np.zeros((8, SIDES), np.float32)
    ends[0, 0] = ends[1, 0] = ends[2, 0] = 1.0
    lane = 1
    for i in range(FEAT):
        pick[i, lane] = 0.5
        ends[1, lane] = ends[2, lane] = 1.0
        lane += 1
    for i in range(FEAT):
        for j in range(i, FEAT):
            pick[i, lane] = 0.5
            pick[j, SIDES + lane] = 0.5
            ends[2, lane] = root_half if i == j else 1.0
            lane += 1
    pick[LANES:] = pick[:LANES]
    return jnp.asarray(pick, bf16), jnp.asarray(ends)


def two_parts(value):
    high = value.astype(bf16)
    return high, (value - high.astype(f32)).astype(bf16)


def three_parts(value):
    high = value.astype(bf16)
    rest = value - high.astype(f32)
    mid = rest.astype(bf16)
    return high, mid, (rest - mid.astype(f32)).astype(bf16)


def product(a, b, contract, passes=3):
    dims = (contract, ((), ()))

    def once(x, y):
        return lax.dot_general(x, y, dims, preferred_element_type=f32)

    if passes == 1:
        return once(a.astype(bf16), b.astype(bf16))
    a_high, a_low = two_parts(a)
    if passes == 2:
        b = b.astype(bf16)
        return once(a_high, b) + once(a_low, b)
    b_high, b_low = two_parts(b)
    return once(a_high, b_high) + (once(a_high, b_low) + once(a_low, b_high))


NN = ((1,), (0,))
NT = ((1,), (1,))
TN = ((0,), (0,))


def lanes_of(shape):
    return lax.broadcasted_iota(jnp.int32, shape, len(shape) - 1)


def rows_of(shape):
    return lax.broadcasted_iota(jnp.int32, shape, 0)


def lower_ones(strict=False):
    row, lane = rows_of((GROUP, GROUP)), lanes_of((GROUP, GROUP))
    return jnp.where(row > lane if strict else row >= lane, 1.0, 0.0).astype(bf16)


def summed_down(ones, value, contract):
    high, mid, low = (
        lax.dot_general(ones, part, (contract, ((), ())), preferred_element_type=f32)
        for part in three_parts(value)
    )
    return low + mid + high


def picked(value, place, contract):
    high, mid, low = (
        lax.dot_general(part, place, (contract, ((), ())), preferred_element_type=f32)
        for part in three_parts(value)
    )
    return low + mid + high


def head_lanes(tile, head, keys):
    first = (4 if keys else 0) * FEAT + head * FEAT
    return pltpu.roll(tile, (LANES - first) % LANES, 1) if first else tile


def factors(moved, pick, ends):
    high, low = two_parts(moved)
    found = lax.dot_general(
        jnp.concatenate([high, low], 1), pick, (NN, ((), ())), preferred_element_type=f32
    )
    return found[:, :SIDES] + ends[0:1], found[:, SIDES:] + ends[1:2]


def factors_back(upstream, one, two, pick, ends):
    scaled = upstream * ends[2:3]
    both = jnp.concatenate([scaled * two, scaled * one], 1)
    return product(both, pick[:LANES], NT, 2)


def scores(tile, head):
    only = lanes_of((GROUP, LANES)) < FEAT
    query = jnp.where(only, head_lanes(tile, head, False), 0.0) * 0.25
    keys = jnp.where(only, head_lanes(tile, head, True), 0.0)
    q_high, k_high = query.astype(bf16), keys.astype(bf16)
    q_wide, k_wide = q_high.astype(f32), k_high.astype(f32)
    q_both = (q_wide + pltpu.roll(query - q_wide, FEAT, 1)).astype(bf16)
    k_both = (pltpu.roll(k_wide, FEAT, 1) + (keys - k_wide)).astype(bf16)
    left = jnp.concatenate([q_high, q_both], 1)
    right = jnp.concatenate([k_high, k_both], 1)
    return lax.dot_general(left, right, (NT, ((), ())), preferred_element_type=f32)


def decays(cum, cum_across, head):
    row, lane = rows_of((GROUP, GROUP)), lanes_of((GROUP, GROUP))
    at = GATE_LANE + head
    diff = cum[:, at : at + 1] - cum_across[at : at + 1, :]
    return jnp.where(row >= lane, jnp.exp(jnp.minimum(diff, 0.0)), 0.0)


def head_column(tile, head):
    at = GATE_LANE + head
    return tile[:, at : at + 1]


def on_head_lane(column, head):
    return jnp.where(lanes_of((column.shape[0], LANES)) == GATE_LANE + head, column, 0.0)


def state_rows(pieces_ref, pair):
    parts = [pieces_ref[4 * pair + q, :PIECE, :].astype(f32) for q in range(4)]
    parts.append(jnp.zeros((SIDES - 4 * PIECE, LANES), f32))
    return jnp.concatenate(parts, 0).astype(bf16)


def store_pieces(ref, pair, state):
    for q in range(4):
        ref[4 * pair + q, :PIECE, :] = state[q * PIECE : (q + 1) * PIECE].astype(bf16)


def whole_call(body, outs, *args, scratch=(), flops=10**9, limit=60, views=None, scalars=0):
    views = views or {}
    shapes = [views.get(i, (a.shape,))[0] for i, a in enumerate(args)]

    def whole(shape, place=None):
        return pl.BlockSpec(shape, lambda i: place or (0,) * len(shape))

    count = sum(math.prod(s) * a.dtype.itemsize for s, a in zip(shapes, args))
    count += sum(math.prod(s) * jnp.dtype(d).itemsize for s, d in outs)
    return pl.pallas_call(
        body,
        grid=(1,),
        out_shape=[jax.ShapeDtypeStruct(s, d) for s, d in outs],
        in_specs=[pl.BlockSpec(memory_space=pltpu.SMEM)] * scalars
        + [whole(s, views.get(i, (s, None))[1]) for i, s in enumerate(shapes) if i >= scalars],
        out_specs=[whole(s) for s, d in outs],
        scratch_shapes=list(scratch),
        compiler_params=pltpu.CompilerParams(vmem_limit_bytes=limit * MIB),
        cost_estimate=pl.CostEstimate(flops=flops, bytes_accessed=count, transcendentals=0),
    )(*args)


def project_kernel(
    core_ref, rows_ref, rim_ref, got_ref, other_ref, rates_ref, pick_ref, ends_ref,
    normed_ref, proj_ref, w_ref, gains_ref, taps_ref, states_ref, values_ref, cum_ref, sent_ref,
    wide_ref,
):
    wide = w_ref.shape[1]
    flipped = core_ref[0] == 1
    taps = jnp.zeros((8, 4 * LANES), f32)
    for r in range(2 * got_ref.shape[0]):
        mine, theirs = got_ref[r // 2].astype(f32), other_ref[r // 2].astype(f32)
        part = jnp.where(flipped, theirs, mine) if r % 2 == 0 else jnp.where(flipped, mine, theirs)
        wide_ref[r * SHARD : (r + 1) * SHARD, :] = part[:SHARD]
        rest = part[SHARD:]
        taps = taps + rest[:, : 4 * LANES]
        whole = rest[:, :LANES] + rest[:, LANES : 2 * LANES] + rest[:, 2 * LANES : 3 * LANES]
        for k in range(3):
            states_ref[k, r : r + 1, :] = whole[TAPS + k : TAPS + k + 1]
    taps_ref[...] = taps
    w_ref[...] = wide_ref[...].astype(bf16)
    chosen = jnp.where(
        lanes_of((16, wide)) == rows_of((16, wide)) + GAIN_LANE, 1.0, 0.0
    )
    chosen = jnp.where(rows_of((16, wide)) < 2, chosen, 0.0).astype(bf16)
    gains = lax.dot_general(chosen, w_ref[...], (NT, ((), ())), preferred_element_type=f32)
    gains_ref[...] = gains[:8]
    gain = gains[0:1]

    def projected(rows):
        rows = rows.astype(f32)
        scale = lax.rsqrt(jnp.mean(rows * rows, -1, keepdims=True) + eps_norm)
        normed = (rows * scale * gain).astype(bf16)
        return normed, jnp.dot(normed, w_ref[...], preferred_element_type=f32)

    for at in range(0, ROWS, GROUP):
        normed, proj = projected(rows_ref[at : at + GROUP, :])
        normed_ref[at : at + GROUP, :] = normed
        proj_ref[at : at + GROUP, :] = proj
    proj_ref[ROWS:, :] = projected(rim_ref[...])[1]
    ones = lower_ones()
    pick, ends = pick_ref[...], ends_ref[...]
    lane, row = lanes_of((GROUP, LANES)), rows_of((GROUP, LANES))
    for s in range(2):
        here = slice(s * GROUP, (s + 1) * GROUP)
        steps = rates_ref[...] * jax.nn.softplus(proj_ref[here, :LANES])
        cum = summed_down(ones, steps, NN)
        cum_ref[here, :] = cum
        last = cum[GROUP - 1 : GROUP, :]
        tail = jnp.exp(last - cum)
        qk = proj_ref[here, 4 * LANES :]
        for h in range(4):
            tile = slice(h * LANES, (h + 1) * LANES)
            raw = proj_ref[here, tile]
            rim_two = proj_ref[ROWS + 2 * s : ROWS + 2 * s + 1, tile]
            rim_one = proj_ref[ROWS + 2 * s + 1 : ROWS + 2 * s + 2, tile]
            one = jnp.where(row == 0, rim_one, pltpu.roll(raw, 1, 0))
            two = jnp.where(row == 0, rim_two, jnp.where(row == 1, rim_one, pltpu.roll(raw, 2, 0)))
            conv = (
                taps_ref[0:1, tile] * raw + taps_ref[1:2, tile] * one + taps_ref[2:3, tile] * two
            )
            values = jnp.where(lane < DH, conv, jnp.where(lane == DH, 1.0, 0.0))
            values_ref[here, tile] = values
            left, right = factors(head_lanes(qk, h, True), pick, ends)
            held = left * right * ends[2:3] * head_column(tail, h)
            fresh = product(held, values, TN)
            store_pieces(sent_ref, 4 * s + h, fresh)
            ending = jnp.broadcast_to(head_column(last, h), (8, LANES))
            high, mid, low = three_parts(ending)
            few = lanes_of((8, LANES))
            packed = jnp.where(
                few == 0,
                high.astype(f32),
                jnp.where(few == 1, mid.astype(f32), jnp.where(few == 2, low.astype(f32), 0.0)),
            ).astype(bf16)
            for q in range(4):
                sent_ref[16 * s + 4 * h + q, PIECE:, :] = packed


def project(core, rows, rim, got, other, rates, pick, ends):
    wide, width = got.shape[2], rows.shape[1]
    return whole_call(
        project_kernel,
        [
            (rows.shape, bf16),
            ((ROWS + rim.shape[0], wide), f32),
            ((width, wide), bf16),
            ((8, width), f32),
            ((8, 4 * LANES), f32),
            ((3, 2 * got.shape[0], LANES), f32),
            ((ROWS, 4 * LANES), f32),
            ((ROWS, LANES), f32),
            ((PIECES, SLOT, LANES), bf16),
        ],
        core, rows, rim, got, other, rates, pick, ends,
        scratch=[pltpu.VMEM((width, wide), f32)],
        flops=3 * 10**9,
        scalars=1,
    )


def scan_kernel(got_ref, back_ref, decay_ref):
    state = jnp.zeros((PIECE, LANES), f32)
    for i in range(PIECES):
        back_ref[i, :PIECE, :] = state.astype(bf16)
        back_ref[i, PIECE:, :] = jnp.zeros((SLOT - PIECE, LANES), bf16)
        ending = jnp.sum(got_ref[i, PIECE:, :].astype(f32), -1, keepdims=True)
        decay = jnp.broadcast_to(jnp.exp(ending), (8, LANES))
        decay_ref[i] = decay
        state = state * decay[0:1] + got_ref[i, :PIECE, :].astype(f32)


def earlier_states(sent):
    got = lax.all_to_all(sent, SEQ, 0, 0, tiled=True)
    back, decay = whole_call(
        scan_kernel, [(sent.shape, bf16), ((PIECES, 8, LANES), f32)], got, flops=10**6
    )
    return lax.all_to_all(back, SEQ, 0, 0, tiled=True), decay


def scan_back_kernel(got_ref, decay_ref, back_ref):
    state = jnp.zeros((PIECE, LANES), f32)
    for i in reversed(range(PIECES)):
        back_ref[i, :PIECE, :] = state.astype(bf16)
        back_ref[i, PIECE:, :] = jnp.zeros((SLOT - PIECE, LANES), bf16)
        state = state * decay_ref[i, 0:1, :] + got_ref[i, :PIECE, :].astype(f32)


def later_states(sent, decay):
    got = lax.all_to_all(sent, SEQ, 0, 0, tiled=True)
    (back,) = whole_call(scan_back_kernel, [(sent.shape, bf16)], got, decay, flops=10**6)
    return lax.all_to_all(back, SEQ, 0, 0, tiled=True)


QK = ((ROWS, LANES), (0, 4))
FIRST = ((ROWS, LANES), (0, 0))


def within_kernel(qk_ref, values_ref, cum_ref, inside_ref):
    for s in range(2):
        here = slice(s * GROUP, (s + 1) * GROUP)
        cum = cum_ref[here, :]
        across = cum.T
        qk = qk_ref[here, :]
        for h in range(4):
            tile = slice(h * LANES, (h + 1) * LANES)
            dots = scores(qk, h)
            weights = (1.0 + dots + 0.5 * dots * dots) * decays(cum, across, h)
            inside_ref[here, tile] = product(weights, values_ref[here, tile], NN)


def within(proj, values, cum):
    return whole_call(
        within_kernel,
        [((ROWS, 4 * LANES), f32)],
        proj, values, cum,
        flops=3 * 10**9,
        views={0: QK},
    )[0]


def mix_kernel(
    qk_ref, cum_ref, inside_ref, earlier_ref, pick_ref, ends_ref, total_ref, mixed_ref
):
    pick, ends = pick_ref[...], ends_ref[...]
    lane = lanes_of((GROUP, LANES))
    for s in range(2):
        here = slice(s * GROUP, (s + 1) * GROUP)
        growth = jnp.exp(cum_ref[here, :])
        qk = qk_ref[here, :]
        for h in range(4):
            tile = slice(h * LANES, (h + 1) * LANES)
            left, right = factors(head_lanes(qk, h, False), pick, ends)
            held = left * right * ends[2:3] * head_column(growth, h)
            total = inside_ref[here, tile] + product(held, state_rows(earlier_ref, 4 * s + h), NN, 2)
            total_ref[here, tile] = total
            mixed = total / total[:, DH : DH + 1]
            mixed_ref[here, tile] = jnp.where(lane < DH, mixed, 0.0).astype(bf16)


def mix(proj, cum, inside, earlier, pick, ends):
    return whole_call(
        mix_kernel,
        [((ROWS, 4 * LANES), f32), ((ROWS, 4 * LANES), bf16)],
        proj, cum, inside, earlier, pick, ends,
        flops=3 * 10**9,
        views={0: QK},
    )


OWN = ROWS // 4


def own_slice(ref, place):
    return ref[pl.ds(pl.multiple_of(place * OWN, OWN), OWN), :]


def join_kernel(
    place_ref, own_ref, side_ref, back_ref, far_a_ref, far_b_ref, w_ref, rows_ref, gains_ref,
    middle_ref, unit_ref, scale_ref, normed_ref,
    mixed_ref, sum_ref,
):
    place, step = place_ref[0], pl.program_id(0)

    @pl.when(step == 0)
    def _():
        mixed_ref[place] = own_ref[...]
        mixed_ref[jnp.bitwise_xor(place, 1)] = side_ref[...]
        mixed_ref[jnp.bitwise_xor(place, 3)] = back_ref[...]
        mixed_ref[jnp.bitwise_xor(place, 2), :GROUP, :] = far_a_ref[...]
        mixed_ref[jnp.bitwise_xor(place, 2), GROUP:, :] = far_b_ref[...]
        sum_ref[...] = rows_ref[...].astype(f32)

    for at in range(0, w_ref.shape[0], BLOCK):
        here = slice(at, at + BLOCK)
        sum_ref[:, here] += lax.dot_general(
            mixed_ref[step], w_ref[here, :], (NT, ((), ())), preferred_element_type=f32
        )

    @pl.when(step == pl.num_programs(0) - 1)
    def _():
        for at in range(0, ROWS, OWN):
            here = slice(at, at + OWN)
            middle = sum_ref[here, :]
            scale = lax.rsqrt(jnp.mean(middle * middle, -1, keepdims=True) + eps_norm)
            normed_ref[here, :] = (middle * scale * gains_ref[1:2]).astype(bf16)
        middle = own_slice(sum_ref, place)
        scale = lax.rsqrt(jnp.mean(middle * middle, -1, keepdims=True) + eps_norm)
        middle_ref[...] = middle
        unit_ref[...] = middle * scale
        scale_ref[...] = jnp.broadcast_to(scale, scale_ref.shape)


def join(place, mixed_parts, w_out, rows, gains):
    width = rows.shape[1]
    columns = OUT // 4
    args = (*mixed_parts, w_out, rows, gains)

    def whole(shape):
        return pl.BlockSpec(shape, lambda i: (0,) * len(shape))

    specs = [whole(a.shape) for a in args]
    specs[5] = pl.BlockSpec((width, columns), lambda i: (0, i))
    outs = [((OWN, width), f32), ((OWN, width), f32), ((OWN, LANES), f32), ((ROWS, width), bf16)]
    return pl.pallas_call(
        join_kernel,
        grid=(4,),
        out_shape=[jax.ShapeDtypeStruct(s, d) for s, d in outs],
        in_specs=[pl.BlockSpec(memory_space=pltpu.SMEM)] + specs,
        out_specs=[whole(s) for s, d in outs],
        scratch_shapes=[pltpu.VMEM((4, ROWS, columns), bf16), pltpu.VMEM((ROWS, width), f32)],
        compiler_params=pltpu.CompilerParams(vmem_limit_bytes=60 * MIB),
        cost_estimate=pl.CostEstimate(
            flops=4 * 10**9, bytes_accessed=15 * 10**6, transcendentals=0
        ),
    )(place, *args)


def turn_kernel(
    place_ref, got_ref, unit_ref, scale_ref, back_ref, gains_ref, w_ref,
    middle_back_ref, gain_ref, out_back_ref, mixed_back_ref,
):
    two_back = got_ref[...].astype(f32)
    unit = unit_ref[...]
    gain_ref[...] = jnp.broadcast_to(
        jnp.sum(two_back * unit, 0, keepdims=True), gain_ref.shape
    )
    weighted = two_back * gains_ref[1:2]
    along = jnp.mean(weighted * unit, -1, keepdims=True)
    middle_back = own_slice(back_ref, place_ref[0]).astype(f32) + scale_ref[:, 0:1] * (
        weighted - unit * along
    )
    middle_back_ref[...] = middle_back
    out_back = middle_back.astype(bf16)
    out_back_ref[...] = out_back
    for g in range(4):
        mixed_back_ref[g] = jnp.dot(
            out_back, w_ref[:, g * 4 * LANES : (g + 1) * 4 * LANES], preferred_element_type=f32
        ).astype(bf16)


def turn(place, got, unit, scale, back, gains, w_out):
    width = back.shape[1]
    return whole_call(
        turn_kernel,
        [
            ((OWN, width), f32),
            ((8, width), f32),
            ((OWN, width), bf16),
            ((4, OWN, 4 * LANES), bf16),
        ],
        place, got, unit, scale, back, gains, w_out,
        flops=10**9,
        scalars=1,
        views={6: ((width, OUT), (0, 0))},
    )


def token_kernel(place_ref, *refs):
    terms, (rows_ref, middle_back_ref, gains_ref, out_ref) = refs[:3], refs[3:]
    one_back = sum(ref[...].astype(f32) for ref in terms)
    rows = own_slice(rows_ref, place_ref[0]).astype(f32)
    scale = lax.rsqrt(jnp.mean(rows * rows, -1, keepdims=True) + eps_norm)
    unit = rows * scale
    weighted = one_back * gains_ref[0:1]
    along = jnp.mean(weighted * unit, -1, keepdims=True)
    token_back = middle_back_ref[...] + scale * (weighted - unit * along)
    out_ref[...] = token_back.astype(bf16)


def token_grads(place, terms, rows, middle_back, gains):
    return whole_call(
        token_kernel, [(terms[0].shape, bf16)], place, *terms, rows, middle_back, gains,
        flops=10**7,
        scalars=1,
    )[0]


def block_kernel(place_ref, *refs):
    terms, (middle_ref, keep_ref, out_ref) = refs[:3], refs[3:]
    ffn = sum(ref[...].astype(f32) for ref in terms)
    keep = own_slice(keep_ref, place_ref[0])[:, 0:1]
    out_ref[...] = ((middle_ref[...] + ffn) * keep).astype(bf16)


def block_outs(place, terms, middle, keep):
    return whole_call(
        block_kernel, [(terms[0].shape, bf16)], place, *terms, middle, keep,
        flops=10**7,
        scalars=1,
    )[0]


def assemble_kernel(place_ref, own_ref, side_ref, back_ref, far_a_ref, far_b_ref, out_ref):
    place = place_ref[0]
    half = OWN // 2

    def at(other):
        return pl.multiple_of(jnp.bitwise_xor(place, other) * OWN, OWN)

    out_ref[pl.ds(at(0), OWN), :] = own_ref[...]
    out_ref[pl.ds(at(1), OWN), :] = side_ref[...]
    out_ref[pl.ds(at(3), OWN), :] = back_ref[...]
    out_ref[pl.ds(at(2), half), :] = far_a_ref[...]
    out_ref[pl.ds(pl.multiple_of(at(2) + half, half), half), :] = far_b_ref[...]


def gather_parts(own):
    half = own.shape[0] // 2
    back = lax.ppermute(own, "mp", BACK)
    side = lax.ppermute(own, "mp", SIDE)
    far_a = lax.ppermute(back[:half], "mp", SIDE)
    far_b = lax.ppermute(side[half:], "mp", BACK)
    return own, side, back, far_a, far_b


def gather_rows(place, own):
    return whole_call(
        assemble_kernel, [((ROWS, own.shape[1]), own.dtype)], place, *gather_parts(own),
        flops=10**6,
        scalars=1,
    )[0]


def scatter_terms(part):
    half = OWN // 2
    got_a = lax.ppermute(part[2, :half], "mp", SIDE)
    got_b = lax.ppermute(part[2, half:], "mp", BACK)
    to_back = jnp.concatenate(
        [(part[3, :half].astype(f32) + got_a.astype(f32)).astype(bf16), part[3, half:]], 0
    )
    to_side = jnp.concatenate(
        [part[1, :half], (part[1, half:].astype(f32) + got_b.astype(f32)).astype(bf16)], 0
    )
    return part[0], lax.ppermute(to_back, "mp", BACK), lax.ppermute(to_side, "mp", SIDE)


def store_by_owner(ref, value, place, columns=slice(None)):
    for g in range(4):
        ref[jnp.bitwise_xor(place, g), :, columns] = value[g * OWN : (g + 1) * OWN]


def unmix_kernel(
    mixed_back_ref, total_ref, qk_ref, cum_ref, pick_ref, ends_ref, total_back_ref, sent_ref
):
    pick, ends = pick_ref[...], ends_ref[...]
    lane = lanes_of((GROUP, LANES))
    for s in range(2):
        here = slice(s * GROUP, (s + 1) * GROUP)
        growth = jnp.exp(cum_ref[here, :])
        qk = qk_ref[here, :]
        for h in range(4):
            tile = slice(h * LANES, (h + 1) * LANES)
            total = total_ref[here, tile]
            inverse = 1.0 / total[:, DH : DH + 1]
            numer = mixed_back_ref[here, tile].astype(f32) * inverse
            numer = jnp.where(lane < DH, numer, 0.0)
            denom = -jnp.sum(numer * total, -1, keepdims=True) * inverse
            total_back = jnp.where(lane == DH, denom, numer)
            total_back_ref[here, tile] = total_back
            left, right = factors(head_lanes(qk, h, False), pick, ends)
            held = left * right * ends[2:3] * head_column(growth, h)
            store_pieces(sent_ref, 4 * s + h, product(held, total_back, TN))
            for q in range(4):
                sent_ref[16 * s + 4 * h + q, PIECE:, :] = jnp.zeros((SLOT - PIECE, LANES), bf16)


def unmix(mixed_back, total, proj, cum, pick, ends):
    return whole_call(
        unmix_kernel,
        [((ROWS, 4 * LANES), f32), ((PIECES, SLOT, LANES), bf16)],
        mixed_back, total, proj, cum, pick, ends,
        flops=3 * 10**9,
        views={2: QK},
    )


def within_back_kernel(
    qk_ref, values_ref, cum_ref, total_back_ref, earlier_ref, pick_ref, ends_ref,
    qk_back_ref, values_back_ref, level_ref,
):
    pick, ends = pick_ref[...], ends_ref[...]
    only = lanes_of((GROUP, LANES)) < FEAT
    for s in range(2):
        here = slice(s * GROUP, (s + 1) * GROUP)
        cum = cum_ref[here, :]
        across = cum.T
        growth = jnp.exp(cum)
        qk = qk_ref[here, :]
        qk_back = jnp.zeros((GROUP, LANES), f32)
        level = jnp.zeros((GROUP, LANES), f32)
        level_down = jnp.zeros((LANES, GROUP), f32)
        for h in range(4):
            tile = slice(h * LANES, (h + 1) * LANES)
            total_back = total_back_ref[here, tile]
            decay = decays(cum, across, h)
            dots = scores(qk, h)
            pairing = decay * product(total_back, values_ref[here, tile], NT)
            kernel = 1.0 + dots + 0.5 * dots * dots
            moved = kernel * pairing
            down = jnp.sum(moved, 0, keepdims=True)
            level_down = jnp.where(rows_of((LANES, GROUP)) == GATE_LANE + h, down, level_down)
            kernel_back = pairing * (1.0 + dots) * 0.25
            values_back_ref[here, tile] = product(kernel * decay, total_back, TN)
            query_tile = head_lanes(qk, h, False)
            keys_only = jnp.where(only, head_lanes(qk, h, True), 0.0)
            query_only = jnp.where(only, query_tile, 0.0)
            query_back = product(kernel_back, keys_only, NN)
            keys_back = product(kernel_back, query_only, TN)
            left, right = factors(query_tile, pick, ends)
            features_back = head_column(growth, h) * product(
                total_back, state_rows(earlier_ref, 4 * s + h), NT, 2
            )
            level_here = jnp.sum(moved, 1, keepdims=True) + jnp.sum(
                left * right * ends[2:3] * features_back, 1, keepdims=True
            )
            level = level + on_head_lane(level_here, h)
            query_back = query_back + factors_back(features_back, left, right, pick, ends)
            at = h * FEAT
            qk_back = qk_back + (pltpu.roll(query_back, at, 1) if at else query_back)
            qk_back = qk_back + pltpu.roll(keys_back, at + 4 * FEAT, 1)
        qk_back_ref[here, :] = qk_back
        level_ref[here, :] = level - level_down.T


def within_back(proj, values, cum, total_back, earlier, pick, ends):
    return whole_call(
        within_back_kernel,
        [((ROWS, LANES), f32), ((ROWS, 4 * LANES), f32), ((ROWS, LANES), f32)],
        proj, values, cum, total_back, earlier, pick, ends,
        flops=8 * 10**9,
        views={0: QK},
    )


def later_back_kernel(
    qk_ref, first_ref, values_ref, cum_ref, rates_ref, earlier_ref, later_ref, pick_ref, ends_ref,
    qk_in_ref, values_in_ref, level_ref,
    qk_back_ref, values_back_ref, gate_back_ref,
):
    pick, ends = pick_ref[...], ends_ref[...]
    ones, before = lower_ones(), lower_ones(True)
    for s in range(2):
        here = slice(s * GROUP, (s + 1) * GROUP)
        cum = cum_ref[here, :]
        last = cum[GROUP - 1 : GROUP, :]
        tail = jnp.exp(last - cum)
        carried = jnp.exp(last)
        qk = qk_ref[here, :]
        qk_back = qk_in_ref[here, :]
        crossed = jnp.zeros((GROUP, LANES), f32)
        through = jnp.zeros((1, LANES), f32)
        for h in range(4):
            tile = slice(h * LANES, (h + 1) * LANES)
            later = state_rows(later_ref, 4 * s + h)
            left, right = factors(head_lanes(qk, h, True), pick, ends)
            held = left * right * ends[2:3]
            column = head_column(tail, h)
            features_back = column * product(values_ref[here, tile], later, NT, 2)
            values_back_ref[here, tile] = values_in_ref[here, tile] + column * product(
                held, later, NN, 2
            )
            crossed = crossed + on_head_lane(
                jnp.sum(held * features_back, 1, keepdims=True), h
            )
            keys_back = factors_back(features_back, left, right, pick, ends)
            qk_back = qk_back + pltpu.roll(keys_back, (h + 4) * FEAT, 1)
            whole = jnp.sum(
                later.astype(f32) * state_rows(earlier_ref, 4 * s + h).astype(f32), 1, keepdims=True
            )
            whole = jnp.sum(whole, 0, keepdims=True) * head_column(carried, h)
            through = through + on_head_lane(whole, h)
        qk_back_ref[here, :] = qk_back
        step_back = (
            summed_down(ones, level_ref[here, :], TN) + summed_down(before, crossed, NN) + through
        )
        gate_back_ref[here, :] = (
            step_back * rates_ref[...] * jax.nn.sigmoid(first_ref[here, :])
        )


def later_back(proj, values, cum, rates, earlier, later, pick, ends, qk_back, values_back, level):
    return whole_call(
        later_back_kernel,
        [((ROWS, LANES), f32), ((ROWS, 4 * LANES), f32), ((ROWS, LANES), f32)],
        proj, proj, values, cum, rates, earlier, later, pick, ends, qk_back, values_back, level,
        flops=4 * 10**9,
        views={0: QK, 1: FIRST},
    )


def unproject_kernel(
    place_ref, proj_ref, ahead_ref, taps_ref, qk_back_ref, values_back_ref, gate_back_ref, normed_ref, w_ref,
    own_ref, side_ref, back_ref, far_a_ref, far_b_ref, mixed_ref, gain_two_ref,
    part_ref, kept_ref, sent_ref, taps_grad_ref, proj_back_ref, out_back_ref, turned_ref,
):
    lane, row = lanes_of((GROUP, LANES)), rows_of((GROUP, LANES))
    taps_grad_ref[...] = jnp.zeros_like(taps_grad_ref)
    for s in range(2):
        here = slice(s * GROUP, (s + 1) * GROUP)
        for h in range(4):
            tile = slice(h * LANES, (h + 1) * LANES)
            raw = proj_ref[here, tile]
            back = values_back_ref[here, tile]
            back = jnp.where(lane < DH, back, 0.0)
            rim_two = proj_ref[ROWS + 2 * s : ROWS + 2 * s + 1, tile]
            rim_one = proj_ref[ROWS + 2 * s + 1 : ROWS + 2 * s + 2, tile]
            one = jnp.where(row == 0, rim_one, pltpu.roll(raw, 1, 0))
            two = jnp.where(row == 0, rim_two, jnp.where(row == 1, rim_one, pltpu.roll(raw, 2, 0)))
            for j, moved in enumerate((raw, one, two)):
                taps_grad_ref[j : j + 1, tile] = taps_grad_ref[j : j + 1, tile] + jnp.sum(
                    moved * back, 0, keepdims=True
                )
            next_one = ahead_ref[2 * s : 2 * s + 1, tile]
            next_two = ahead_ref[2 * s + 1 : 2 * s + 2, tile]
            one = jnp.where(row == GROUP - 1, next_one, pltpu.roll(back, GROUP - 1, 0))
            two = jnp.where(
                row == GROUP - 1,
                next_two,
                jnp.where(row == GROUP - 2, next_one, pltpu.roll(back, GROUP - 2, 0)),
            )
            raw_back = (
                taps_ref[0:1, tile] * back + taps_ref[1:2, tile] * one + taps_ref[2:3, tile] * two
            )
            raw_back = jnp.where(lane < DH, raw_back, 0.0)
            if h == 0:
                gates = (lane >= GATE_LANE) & (lane < GATE_LANE + 4)
                raw_back = jnp.where(gates, gate_back_ref[here, :], raw_back)
            proj_back_ref[here, tile] = raw_back.astype(bf16)
        proj_back_ref[here, 4 * LANES :] = qk_back_ref[here, :].astype(bf16)
    part = lax.dot_general(
        proj_back_ref[...], w_ref[...], (NT, ((), ())), preferred_element_type=f32
    ).astype(bf16)
    store_by_owner(part_ref, part, place_ref[0])
    wide = w_ref.shape[1]
    grad_in = lax.dot_general(
        normed_ref[...], proj_back_ref[...], (TN, ((), ())), preferred_element_type=f32
    )
    weights = w_ref[...].astype(f32)
    gain_one = jnp.sum(grad_in * weights, 1, keepdims=True)
    gain_one = gain_one / weights[:, GAIN_LANE : GAIN_LANE + 1]
    gain_two = gain_two_ref[...].T[:, 0:1]
    first = grad_in[:, :LANES]
    spot = lanes_of(first.shape)
    first = jnp.where(
        spot == GAIN_LANE, gain_one, jnp.where(spot == GAIN_LANE + 1, gain_two, first)
    )
    out_back_ref[:OWN] = own_ref[...]
    out_back_ref[OWN : 2 * OWN] = side_ref[...]
    out_back_ref[2 * OWN : 3 * OWN] = back_ref[...]
    out_back_ref[3 * OWN : 3 * OWN + OWN // 2] = far_a_ref[...]
    out_back_ref[3 * OWN + OWN // 2 :] = far_b_ref[...]
    for k, other in enumerate((0, 1, 3, 2)):
        turned_ref[k * OWN : (k + 1) * OWN] = own_slice(
            mixed_ref, jnp.bitwise_xor(place_ref[0], other)
        )
    grad_out = lax.dot_general(
        out_back_ref[...], turned_ref[...], (TN, ((), ())), preferred_element_type=f32
    )
    core = place_ref[1]

    def store(ref, parity):
        for k in range(ref.shape[0]):
            r = 2 * k + parity
            here = slice(r * SHARD, (r + 1) * SHARD)
            ref[k, :SHARD, :LANES] = first[here].astype(bf16)
            ref[k, :SHARD, LANES:wide] = grad_in[here, LANES:].astype(bf16)
            ref[k, :SHARD, wide:] = grad_out[here].astype(bf16)
            h, at = r // 8, (r % 8) * (DH // 8)
            few = taps_grad_ref[:, h * LANES : (h + 1) * LANES]
            few = pltpu.roll(few, LANES - at, 1) if at else few
            ref[k, SHARD:, :LANES] = few.astype(bf16)
            ref[k, SHARD:, LANES:] = jnp.zeros((SPACED - SHARD, wide + 3 * LANES), bf16)

    for parity in range(2):

        @pl.when(core == parity)
        def _():
            store(kept_ref, parity)
            store(sent_ref, 1 - parity)


def unproject(
    place, proj, ahead, taps, qk_back, values_back, gate_back, normed, w_in, out_parts, mixed, gain_two
):
    width, wide = w_in.shape
    return whole_call(
        unproject_kernel,
        [
            ((4, OWN, width), bf16),
            ((width // SHARD // 2, SPACED, wide + 4 * LANES), bf16),
            ((width // SHARD // 2, SPACED, wide + 4 * LANES), bf16),
        ],
        place, proj, ahead, taps, qk_back, values_back, gate_back, normed, w_in, *out_parts, mixed,
        gain_two,
        scratch=[
            pltpu.VMEM((8, 4 * LANES), f32),
            pltpu.VMEM((ROWS, wide), bf16),
            pltpu.VMEM((ROWS, width), bf16),
            pltpu.VMEM((ROWS, 4 * LANES), bf16),
        ],
        flops=4 * 10**9,
        scalars=1,
    )


BLOCK = 256
HIDDEN = 1280
OUT = 16 * LANES
SHARD = 56
SPACED = 64


def ffn_kernel(normed_ref, back_ref, gate_ref, up_ref, down_ref, both_ref, acts_ref, two_ref):
    step = pl.program_id(0)
    blocks = HIDDEN // BLOCK

    @pl.when(step < blocks)
    def _():
        normed = normed_ref[...]
        gate = jnp.dot(normed, gate_ref[...], preferred_element_type=f32)
        up = jnp.dot(normed, up_ref[...], preferred_element_type=f32)
        hidden_back = jnp.dot(back_ref[...], down_ref[...], preferred_element_type=f32)
        sigma = jax.nn.sigmoid(gate)
        silu = gate * sigma
        at = pl.multiple_of(step * BLOCK, BLOCK)
        acts_ref[:, pl.ds(at, BLOCK)] = (
            hidden_back * up * sigma * (1.0 + gate * (1.0 - sigma))
        ).astype(bf16)
        acts_ref[:, pl.ds(HIDDEN + at, BLOCK)] = (hidden_back * silu).astype(bf16)
        acts_ref[:, pl.ds(2 * HIDDEN + at, BLOCK)] = (silu * up).astype(bf16)

    @pl.when(step >= blocks)
    def _():
        two_ref[...] = lax.dot_general(
            acts_ref[:, : 2 * HIDDEN], both_ref[...], (NT, ((), ())), preferred_element_type=f32
        ).astype(bf16)


def ffn_both_ways(normed, back, weights):
    width = normed.shape[1]
    blocks, outs = HIDDEN // BLOCK, width // BLOCK
    whole = pl.BlockSpec((ROWS, width), lambda i: (0, 0))

    def columns(which):
        first = OUT // BLOCK + which * blocks
        return pl.BlockSpec((width, BLOCK), lambda i: (0, first + jnp.minimum(i, blocks - 1)))

    return pl.pallas_call(
        ffn_kernel,
        grid=(blocks + outs,),
        out_shape=[
            jax.ShapeDtypeStruct((ROWS, 3 * HIDDEN), bf16),
            jax.ShapeDtypeStruct((ROWS, width), bf16),
        ],
        in_specs=[
            whole,
            whole,
            columns(0),
            columns(1),
            columns(2),
            pl.BlockSpec(
                (pl.Element(BLOCK), pl.Element(2 * HIDDEN)),
                lambda i: (jnp.maximum(i - blocks, 0) * BLOCK, OUT),
            ),
        ],
        out_specs=[
            pl.BlockSpec((ROWS, 3 * HIDDEN), lambda i: (0, 0)),
            pl.BlockSpec((ROWS, BLOCK), lambda i: (0, jnp.maximum(i - blocks, 0))),
        ],
        compiler_params=pltpu.CompilerParams(vmem_limit_bytes=60 * MIB),
        cost_estimate=pl.CostEstimate(
            flops=12 * 10**9, bytes_accessed=25 * 10**6, transcendentals=0
        ),
    )(normed, back, weights, weights, weights, weights)


def ffn_out_kernel(place_ref, acts_ref, down_ref, out_ref):
    value = lax.dot_general(
        acts_ref[...], down_ref[...], (NT, ((), ())), preferred_element_type=f32
    ).astype(bf16)
    store_by_owner(out_ref, value, place_ref[0])


def ffn_out(place, acts, weights):
    width = weights.shape[0]
    return pl.pallas_call(
        ffn_out_kernel,
        grid=(width // BLOCK,),
        out_shape=jax.ShapeDtypeStruct((4, OWN, width), bf16),
        in_specs=[
            pl.BlockSpec(memory_space=pltpu.SMEM),
            pl.BlockSpec((ROWS, HIDDEN), lambda i: (0, 2)),
            pl.BlockSpec(
                (pl.Element(BLOCK), pl.Element(HIDDEN)), lambda i: (i * BLOCK, OUT + 2 * HIDDEN)
            ),
        ],
        out_specs=pl.BlockSpec((4, OWN, BLOCK), lambda i: (0, 0, i)),
        compiler_params=pltpu.CompilerParams(vmem_limit_bytes=60 * MIB),
        cost_estimate=pl.CostEstimate(
            flops=3 * 10**9, bytes_accessed=8 * 10**6, transcendentals=0
        ),
    )(place, acts, weights)


def ffn_grads_kernel(normed_ref, back_ref, acts_ref, grads_ref):
    def spaced(rows_ref):
        grad = lax.dot_general(
            rows_ref[...], acts_ref[...], (TN, ((), ())), preferred_element_type=f32
        )
        for r in range(grad.shape[0] // SHARD):
            grads_ref[r * SPACED : r * SPACED + SHARD, :] = grad[
                r * SHARD : (r + 1) * SHARD
            ].astype(bf16)
            grads_ref[r * SPACED + SHARD : (r + 1) * SPACED, :] = jnp.zeros(
                (SPACED - SHARD, grad.shape[1]), bf16
            )

    both = pl.program_id(0) < 2 * HIDDEN // WIDER

    @pl.when(both)
    def _():
        spaced(normed_ref)

    @pl.when(jnp.logical_not(both))
    def _():
        spaced(back_ref)


WIDER = 640


def ffn_grads(normed, back, acts):
    width = normed.shape[1]
    whole = pl.BlockSpec((ROWS, width), lambda i: (0, 0))
    return pl.pallas_call(
        ffn_grads_kernel,
        grid=(3 * HIDDEN // WIDER,),
        out_shape=jax.ShapeDtypeStruct((width // SHARD * SPACED, 3 * HIDDEN), bf16),
        in_specs=[whole, whole, pl.BlockSpec((ROWS, WIDER), lambda i: (0, i))],
        out_specs=pl.BlockSpec((width // SHARD * SPACED, WIDER), lambda i: (0, i)),
        compiler_params=pltpu.CompilerParams(vmem_limit_bytes=60 * MIB),
        cost_estimate=pl.CostEstimate(
            flops=7 * 10**9, bytes_accessed=20 * 10**6, transcendentals=0
        ),
    )(normed, back, acts)


def order_columns(heads):
    import numpy as np

    place = np.zeros((5 * LANES, 5 * LANES), np.float32)
    for h in range(heads):
        at = h * (2 * FEAT + DH + 1)
        for i in range(FEAT):
            place[at + i, heads * LANES + h * FEAT + i] = 1.0
            place[at + FEAT + i, heads * LANES + (heads + h) * FEAT + i] = 1.0
        for i in range(DH):
            place[at + 2 * FEAT + i, h * LANES + i] = 1.0
        place[at + 2 * FEAT + DH, GATE_LANE + h] = 1.0
    return jnp.asarray(place, bf16)


def order_heads(heads):
    import numpy as np

    place = np.zeros((heads * DH, heads * LANES), np.float32)
    for h in range(heads):
        for i in range(DH):
            place[h * DH + i, h * LANES + i] = 1.0
    return jnp.asarray(place, bf16)


def prepare_kernel(
    rank_ref, in_ref, out_ref, gate_ref, up_ref, down_ref, taps_ref,
    gains_ref, gains_first_ref, gains_second_ref, place_ref, tiles_ref,
    shard_ref, out_shard_ref, rest_ref, few_ref,
):
    wide = 5 * LANES
    columns = in_ref.shape[1]
    whole = jnp.dot(
        in_ref[...].astype(bf16), place_ref[:columns, :], preferred_element_type=f32
    )
    spot = jnp.where(
        lanes_of((2, wide)) == rows_of((2, wide)) + GAIN_LANE, 1.0, 0.0
    ).astype(bf16)
    gains = lax.dot_general(
        gains_ref[...].astype(bf16), spot, (TN, ((), ())), preferred_element_type=f32
    )
    for k in range(shard_ref.shape[0]):
        shard_ref[k, :SHARD, :] = (whole + gains).astype(bf16)
    rank = rank_ref[0]
    own = taps_ref.shape[1]
    each = DH // own
    first = (rank // each) * LANES + (rank % each) * own
    spot = jnp.where(
        lanes_of((own, wide)) == rows_of((own, wide)) + first, 1.0, 0.0
    ).astype(bf16)
    taps = jnp.dot(taps_ref[...].astype(bf16), spot, preferred_element_type=f32)
    rows = [taps]
    for ref in (gains_ref, gains_first_ref, gains_second_ref):
        few_ref[...] = jnp.zeros_like(few_ref)
        few_ref[0:2, :SHARD] = ref[...]
        both = few_ref[...]
        line = both + pltpu.roll(pltpu.roll(both, SHARD, 1), 7, 0)
        parts = [part.astype(f32)[0:1] for part in three_parts(line)]
        rows.append(jnp.concatenate(parts + [jnp.zeros((1, wide - 3 * LANES), f32)], 1))
    rows.append(jnp.zeros((SPACED - SHARD - TAPS - 3, wide), f32))
    for k in range(shard_ref.shape[0]):
        shard_ref[k, SHARD:, :] = jnp.concatenate(rows, 0).astype(bf16)
    out_shard_ref[...] = jnp.dot(
        out_ref[...].astype(bf16), tiles_ref[...], preferred_element_type=f32
    ).astype(bf16)
    rest_ref[...] = jnp.zeros_like(rest_ref)
    units = gate_ref.shape[1]
    rest_ref[:, :units] = gate_ref[...].astype(bf16)
    rest_ref[:, HIDDEN : HIDDEN + units] = up_ref[...].astype(bf16)
    rest_ref[:, 2 * HIDDEN : 2 * HIDDEN + units] = down_ref[...].astype(bf16)


def prepare(rank, *args):
    return whole_call(
        prepare_kernel,
        [
            ((16, SPACED, 5 * LANES), bf16),
            ((SHARD, 4 * LANES), bf16),
            ((SHARD, 3 * HIDDEN), bf16),
        ],
        rank, *args,
        scratch=[pltpu.VMEM((8, LANES), f32)],
        scalars=1,
    )


def moved_moments(weight, first, second, grad):
    fix = 1.0 - beta_value**STEP
    moment = beta_value * first + (1.0 - beta_value) * grad
    square = beta_value * second + (1.0 - beta_value) * grad * grad
    direction = moment / fix / (jnp.sqrt(square / fix) + eps_adam) + decay_rate * weight
    return moment, square, direction


def moments_kernel(mixer_ref, ffn_ref, place_ref, tiles_ref, *refs):
    params, outs, sums_ref = refs[:18], refs[18:-1], refs[-1]
    wide = 5 * LANES
    units = params[6].shape[1]
    mixer = mixer_ref[0].astype(f32)
    for k in range(1, mixer_ref.shape[0]):
        mixer = mixer + mixer_ref[k].astype(f32)
    sums = jnp.zeros((1, 2 * LANES), f32)
    lane = lanes_of((1, 2 * LANES))

    def adapt(index, grad):
        weight = params[3 * index][...]
        moment, square, direction = moved_moments(
            weight, params[3 * index + 1][...], params[3 * index + 2][...], grad
        )
        outs[3 * index][...] = moment
        outs[3 * index + 1][...] = square
        outs[3 * index + 2][...] = direction
        both = [
            jnp.sum(jnp.sum(v * v, 1, keepdims=True), 0, keepdims=True)
            for v in (weight, direction)
        ]
        return jnp.where(
            lane == 2 * index, both[0], jnp.where(lane == 2 * index + 1, both[1], 0.0)
        )

    grad_in = picked(mixer[:SHARD, :wide], place_ref[...], NT)
    sums = sums + adapt(0, grad_in[:, : params[0].shape[1]])
    sums = sums + adapt(1, picked(mixer[:SHARD, wide:], tiles_ref[...], NT))
    sums = sums + adapt(2, ffn_ref[:SHARD, :units].astype(f32))
    sums = sums + adapt(3, ffn_ref[:SHARD, HIDDEN : HIDDEN + units].astype(f32))
    sums = sums + adapt(4, ffn_ref[:SHARD, 2 * HIDDEN : 2 * HIDDEN + units].astype(f32))
    sums = sums + adapt(5, mixer[SHARD : SHARD + TAPS, : params[15].shape[1]])
    across = jnp.concatenate([mixer[:, :LANES], jnp.zeros((LANES - SPACED, LANES), f32)], 0).T
    ones = across[GAIN_LANE : GAIN_LANE + 1]
    twos = across[GAIN_LANE + 1 : GAIN_LANE + 2]
    few = lanes_of((1, LANES))
    line = jnp.where(few < SHARD, ones, 0.0) + pltpu.roll(
        jnp.broadcast_to(jnp.where(few < SHARD, twos, 0.0), (8, LANES)), SHARD, 1
    )[0:1]
    sums = sums + jnp.concatenate([jnp.zeros((1, LANES), f32), line], 1)
    sums_ref[...] = jnp.broadcast_to(sums[None], sums_ref.shape)


def moments(mixer, ffn, place, tiles, params):
    outs = []
    for param in params[0::3]:
        outs += [(param.shape, f32)] * 3
    outs.append(((LANES, 1, 2 * LANES), f32))
    return whole_call(moments_kernel, outs, mixer, ffn, place, tiles, *params)


def update_kernel(rank_ref, totals_ref, states_ref, *refs):
    weights, directions, outs = refs[:6], refs[6:12], refs[12:18]
    gains_refs, norms_ref = refs[18:21], refs[21]
    totals = totals_ref[:, 0, :]
    sums = jnp.sum(totals[:, :LANES], 0, keepdims=True)
    lane = lanes_of((1, LANES))
    grouped = jnp.where(
        lanes_of((32, LANES)) // 4 == rows_of((32, LANES)), 1.0, 0.0
    ).astype(bf16)
    grad = summed_down(grouped, totals[:, LANES:], NN)
    moment, square, direction = moved_moments(
        states_ref[0], states_ref[1], states_ref[2], grad
    )
    live = lanes_of((32, LANES)) < 2 * SHARD
    for place, value in ((12, states_ref[0]), (13, direction)):
        value = jnp.where(live, value, 0.0)
        value = jnp.sum(jnp.sum(value * value, 1, keepdims=True), 0, keepdims=True)
        sums = jnp.where(lane == place, value, sums)
    norms = jnp.sqrt(sums)
    norms_ref[...] = jnp.broadcast_to(norms, norms_ref.shape)

    def ratio(index):
        return norms[:, 2 * index : 2 * index + 1] / norms[:, 2 * index + 1 : 2 * index + 2]

    for index in range(6):
        outs[index][...] = (
            weights[index][...] - learn_rate * ratio(index) * directions[index][...]
        )
    updated = states_ref[0] - learn_rate * ratio(6) * direction
    for ref, value in zip(gains_refs, (updated, moment, square)):
        own = jnp.where(rows_of((32, LANES)) == rank_ref[0], value, 0.0)
        own = jnp.broadcast_to(jnp.sum(own, 0, keepdims=True), (8, LANES))
        ref[0:1, :] = own[0:1, :SHARD]
        ref[1:2, :] = pltpu.roll(own, LANES - SHARD, 1)[0:1, :SHARD]


def update(rank, totals, states, weights, directions):
    outs = [(w.shape, f32) for w in weights] + [((2, SHARD), f32)] * 3 + [((8, LANES), f32)]
    return whole_call(
        update_kernel, outs, rank, totals, states, *weights, *directions, scalars=1
    )


def per_device(
    tokens,
    cotangent,
    lengths,
    rate_codes,
    inproj,
    inproj_first,
    inproj_second,
    outproj,
    outproj_first,
    outproj_second,
    gateproj,
    gateproj_first,
    gateproj_second,
    upproj,
    upproj_first,
    upproj_second,
    downproj,
    downproj_first,
    downproj_second,
    convtaps,
    convtaps_first,
    convtaps_second,
    normgains,
    normgains_first,
    normgains_second,
):
    seqs, group, width = tokens.shape
    heads = rate_codes.shape[0]
    lag = TAPS - 1
    rank = lax.axis_index(SEQ).reshape(1)
    core = lax.axis_index("seq_2")
    peer = lax.axis_index("mp").reshape(1)
    pick, ends = selections()
    place, tiles = order_columns(heads), order_heads(heads)

    shards, out_shard, rest_shard = prepare(
        rank, inproj, outproj.T, gateproj, upproj, downproj.T, convtaps,
        normgains, normgains_first, normgains_second, place, tiles,
    )
    got = lax.all_to_all(shards, ("seq_0", "seq_1"), 0, 0, tiled=True)
    other = lax.ppermute(got, "seq_2", SWAP)
    turned = [out_shard] + [
        lax.ppermute(out_shard, "mp", [(i, (i - k) % 4) for i in range(4)]) for k in range(1, 4)
    ]
    out_shards = jnp.roll(jnp.stack(turned), peer[0], axis=0)
    weights_shard = jnp.concatenate([out_shards[g] for g in range(4)] + [rest_shard], 1)
    weights_shard, got = lax.optimization_barrier((weights_shard, got))
    weights = lax.all_gather(weights_shard, SEQ, axis=0, tiled=True)

    rows = tokens.reshape(-1, width)
    rim = shifted(tokens[:, group - lag :], SEQ, 1).reshape(-1, width)
    rim = jnp.pad(rim, ((0, 16 - seqs * lag), (0, 0)))
    positions = rank * group + jnp.arange(group, dtype=jnp.int32)
    keep = (positions[None, :] < lengths[:, None]).astype(f32).reshape(-1, 1)
    back = (cotangent.reshape(-1, width).astype(f32) * keep).astype(bf16)
    rates = -jnp.exp2(-rate_codes.astype(f32) / 4.0)
    rates = jnp.pad(rates[None], ((0, 0), (GATE_LANE, LANES - GATE_LANE - heads)))
    normed_one, proj, w_in, gains, taps, states, values, cum, sent = project(
        core.reshape(1), rows, rim, got, other, rates, pick, ends
    )
    earlier, decay = earlier_states(sent)
    inside = within(proj, values, cum)
    total, mixed = mix(proj, cum, inside, earlier, pick, ends)

    middle, unit_two, scale_two, normed_two = join(
        peer, gather_parts(mixed), weights, rows, gains
    )

    acts, two_part = ffn_both_ways(normed_two, back, weights)
    two_back = lax.psum_scatter(two_part, "mp", scatter_dimension=0, tiled=True)
    ffn_part = ffn_out(peer, acts, weights)
    two_back, ffn_part = lax.optimization_barrier((two_back, ffn_part))
    ffn_sums = lax.psum_scatter(
        ffn_grads(normed_two, back, acts), SEQ, scatter_dimension=0, tiled=True
    )
    middle_back, gain_two, out_own, mixed_back = turn(
        peer, two_back, unit_two, scale_two, back, gains, weights
    )
    mixed_back = lax.all_to_all(mixed_back, "mp", 0, 0, tiled=True).reshape(ROWS, -1)

    total_back, sent = unmix(mixed_back, total, proj, cum, pick, ends)
    ffn_part, out_own, sent = lax.optimization_barrier((ffn_part, out_own, sent))
    later = later_states(sent, decay)
    qk_back, values_back, level = within_back(
        proj, values, cum, total_back, earlier, pick, ends
    )
    out_parts = gather_parts(out_own)
    ffn_terms = scatter_terms(ffn_part)
    qk_back, values_back, gate_back = later_back(
        proj, values, cum, rates, earlier, later, pick, ends, qk_back, values_back, level
    )
    edge = values_back.reshape(seqs, group, -1)[:, :lag]
    ahead = shifted(edge, SEQ, -1).reshape(seqs * lag, -1)
    ahead = jnp.concatenate([ahead, jnp.zeros_like(ahead)], 0)
    ahead, ffn_terms = lax.optimization_barrier((ahead, ffn_terms))
    one_part, kept, sent = unproject(
        jnp.concatenate([peer, core.reshape(1)]), proj, ahead, taps, qk_back, values_back, gate_back, normed_one, w_in, out_parts, mixed,
        gain_two,
    )

    swapped = lax.ppermute(sent, "seq_2", SWAP)
    mixer_part = (kept.astype(f32) + swapped.astype(f32)).astype(bf16)

    one_part, mixer_part = lax.optimization_barrier((one_part, mixer_part))
    mixer_got = lax.all_to_all(mixer_part, ("seq_0", "seq_1"), 0, 0, tiled=True)
    one_terms = scatter_terms(one_part)
    block_out = lax.all_gather(
        block_outs(peer, ffn_terms, middle, jnp.broadcast_to(keep, (ROWS, LANES))),
        "mp",
        axis=0,
        tiled=True,
    )

    params = (
        (inproj, inproj_first, inproj_second)
        + (outproj.T, outproj_first.T, outproj_second.T)
        + (gateproj, gateproj_first, gateproj_second)
        + (upproj, upproj_first, upproj_second)
        + (downproj.T, downproj_first.T, downproj_second.T)
        + (convtaps, convtaps_first, convtaps_second)
    )
    *moved, sums = moments(mixer_got, ffn_sums, place, tiles, params)
    token_own, _ = lax.optimization_barrier(
        (token_grads(peer, one_terms, rows, middle_back, gains), sums)
    )
    token_grad = gather_rows(peer, token_own)
    totals = lax.all_to_all(sums, ALL, 0, 0, tiled=True)
    *updated, gains_new, gains_moment, gains_square, norms = update(
        rank, totals, states, params[0::3], moved[2::3]
    )
    results = [block_out.reshape(tokens.shape), token_grad.reshape(tokens.shape)]
    for index in range(6):
        for value in (updated[index], moved[3 * index], moved[3 * index + 1]):
            results.append(value.T if index in (1, 4) else value)
    results += [gains_new, gains_moment, gains_square, norms[0, :14].reshape(7, 2)]
    return tuple(results)


def solution(mesh):
    split = Mesh(mesh.devices.reshape(4, 4, 2, mesh.shape["mp"]), ("seq_0", "seq_1", "seq_2", "mp"))
    in_specs = (
        P(None, SEQ, None),
        P(None, SEQ, None),
        P(),
        P("mp"),
        P(SEQ, "mp"),
        P(SEQ, "mp"),
        P(SEQ, "mp"),
        P("mp", SEQ),
        P("mp", SEQ),
        P("mp", SEQ),
        P(SEQ, "mp"),
        P(SEQ, "mp"),
        P(SEQ, "mp"),
        P(SEQ, "mp"),
        P(SEQ, "mp"),
        P(SEQ, "mp"),
        P("mp", SEQ),
        P("mp", SEQ),
        P("mp", SEQ),
        P(None, MP_SEQ),
        P(None, MP_SEQ),
        P(None, MP_SEQ),
        P(None, SEQ),
        P(None, SEQ),
        P(None, SEQ),
    )
    out_specs = (
        P(None, SEQ, None),
        P(None, SEQ, None),
        P(SEQ, "mp"),
        P(SEQ, "mp"),
        P(SEQ, "mp"),
        P("mp", SEQ),
        P("mp", SEQ),
        P("mp", SEQ),
        P(SEQ, "mp"),
        P(SEQ, "mp"),
        P(SEQ, "mp"),
        P(SEQ, "mp"),
        P(SEQ, "mp"),
        P(SEQ, "mp"),
        P("mp", SEQ),
        P("mp", SEQ),
        P("mp", SEQ),
        P(None, MP_SEQ),
        P(None, MP_SEQ),
        P(None, MP_SEQ),
        P(None, SEQ),
        P(None, SEQ),
        P(None, SEQ),
        P(),
    )
    return jax.shard_map(
        per_device, mesh=split, in_specs=in_specs, out_specs=out_specs, check_vma=False
    )
```

```python
import math

import jax
import jax.numpy as jnp
from jax import lax
from jax.experimental import pallas as pl
from jax.experimental.pallas import tpu as pltpu
from jax.sharding import Mesh
from jax.sharding import PartitionSpec as P

DH = 112
FEAT = 16
TAPS = 3
STEP = 7
LANES = 128
SEQ = ("seq_0", "seq_1", "seq_2")
ALL = ("seq_0", "seq_1", "seq_2", "mp")
MP_SEQ = ("mp", "seq_0", "seq_1", "seq_2")

f32 = jnp.float32
bf16 = jnp.bfloat16
highest = lax.Precision.HIGHEST
root_half = 0.5**0.5
eps_norm = 1e-05
eps_adam = 1e-06
decay_rate = 0.01
learn_rate = 0.3
beta_value = 0.5

SIDE = [(i, i ^ 1) for i in range(4)]
BACK = [(i, 3 - i) for i in range(4)]
SWAP = [(0, 1), (1, 0)]


def shifted(value, axis, steps):
    count = lax.axis_size(axis)
    first, last = (max(0, -steps), min(count, count - steps))
    return lax.ppermute(value, axis, [(source, source + steps) for source in range(first, last)])


SPAN_LANE = DH
GATE_LANE = DH
GAIN_LANE = DH + 4
GROUP = 256
ROWS = 512
SIDES = 256
PIECE = 40
SLOT = 48
PIECES = 32
MIB = 1 << 20


def selections():
    import numpy as np

    pick = np.zeros((2 * LANES, 2 * SIDES), np.float32)
    ends = np.zeros((8, SIDES), np.float32)
    ends[0, 0] = ends[1, 0] = ends[2, 0] = 1.0
    lane = 1
    for i in range(FEAT):
        pick[i, lane] = 0.5
        ends[1, lane] = ends[2, lane] = 1.0
        lane += 1
    for i in range(FEAT):
        for j in range(i, FEAT):
            pick[i, lane] = 0.5
            pick[j, SIDES + lane] = 0.5
            ends[2, lane] = root_half if i == j else 1.0
            lane += 1
    pick[LANES:] = pick[:LANES]
    return jnp.asarray(pick, bf16), jnp.asarray(ends)


def two_parts(value):
    high = value.astype(bf16)
    return high, (value - high.astype(f32)).astype(bf16)


def three_parts(value):
    high = value.astype(bf16)
    rest = value - high.astype(f32)
    mid = rest.astype(bf16)
    return high, mid, (rest - mid.astype(f32)).astype(bf16)


def product(a, b, contract, passes=3):
    dims = (contract, ((), ()))

    def once(x, y):
        return lax.dot_general(x, y, dims, preferred_element_type=f32)

    if passes == 1:
        return once(a.astype(bf16), b.astype(bf16))
    a_high, a_low = two_parts(a)
    if passes == 2:
        b = b.astype(bf16)
        return once(a_high, b) + once(a_low, b)
    b_high, b_low = two_parts(b)
    return once(a_high, b_high) + (once(a_high, b_low) + once(a_low, b_high))


NN = ((1,), (0,))
NT = ((1,), (1,))
TN = ((0,), (0,))


def lanes_of(shape):
    return lax.broadcasted_iota(jnp.int32, shape, len(shape) - 1)


def rows_of(shape):
    return lax.broadcasted_iota(jnp.int32, shape, 0)


def lower_ones(strict=False):
    row, lane = rows_of((GROUP, GROUP)), lanes_of((GROUP, GROUP))
    return jnp.where(row > lane if strict else row >= lane, 1.0, 0.0).astype(bf16)


def summed_down(ones, value, contract):
    high, mid, low = (
        lax.dot_general(ones, part, (contract, ((), ())), preferred_element_type=f32)
        for part in three_parts(value)
    )
    return low + mid + high


def picked(value, place, contract):
    high, mid, low = (
        lax.dot_general(part, place, (contract, ((), ())), preferred_element_type=f32)
        for part in three_parts(value)
    )
    return low + mid + high


def head_lanes(tile, head, keys):
    first = (4 if keys else 0) * FEAT + head * FEAT
    return pltpu.roll(tile, (LANES - first) % LANES, 1) if first else tile


def factors(moved, pick, ends):
    high, low = two_parts(moved)
    found = lax.dot_general(
        jnp.concatenate([high, low], 1), pick, (NN, ((), ())), preferred_element_type=f32
    )
    return found[:, :SIDES] + ends[0:1], found[:, SIDES:] + ends[1:2]


def factors_back(upstream, one, two, pick, ends):
    scaled = upstream * ends[2:3]
    both = jnp.concatenate([scaled * two, scaled * one], 1)
    return product(both, pick[:LANES], NT, 2)


def scores(tile, head):
    only = lanes_of((GROUP, LANES)) < FEAT
    query = jnp.where(only, head_lanes(tile, head, False), 0.0) * 0.25
    keys = jnp.where(only, head_lanes(tile, head, True), 0.0)
    q_high, k_high = query.astype(bf16), keys.astype(bf16)
    q_wide, k_wide = q_high.astype(f32), k_high.astype(f32)
    q_both = (q_wide + pltpu.roll(query - q_wide, FEAT, 1)).astype(bf16)
    k_both = (pltpu.roll(k_wide, FEAT, 1) + (keys - k_wide)).astype(bf16)
    left = jnp.concatenate([q_high, q_both], 1)
    right = jnp.concatenate([k_high, k_both], 1)
    return lax.dot_general(left, right, (NT, ((), ())), preferred_element_type=f32)


def decays(cum, cum_across, head):
    row, lane = rows_of((GROUP, GROUP)), lanes_of((GROUP, GROUP))
    at = GATE_LANE + head
    diff = cum[:, at : at + 1] - cum_across[at : at + 1, :]
    return jnp.where(row >= lane, jnp.exp(jnp.minimum(diff, 0.0)), 0.0)


def head_column(tile, head):
    at = GATE_LANE + head
    return tile[:, at : at + 1]


def on_head_lane(column, head):
    return jnp.where(lanes_of((column.shape[0], LANES)) == GATE_LANE + head, column, 0.0)


def state_rows(pieces_ref, pair):
    parts = [pieces_ref[4 * pair + q, :PIECE, :].astype(f32) for q in range(4)]
    parts.append(jnp.zeros((SIDES - 4 * PIECE, LANES), f32))
    return jnp.concatenate(parts, 0).astype(bf16)


def store_pieces(ref, pair, state):
    for q in range(4):
        ref[4 * pair + q, :PIECE, :] = state[q * PIECE : (q + 1) * PIECE].astype(bf16)


def whole_call(body, outs, *args, scratch=(), flops=10**9, limit=60, views=None, scalars=0):
    views = views or {}
    shapes = [views.get(i, (a.shape,))[0] for i, a in enumerate(args)]

    def whole(shape, place=None):
        return pl.BlockSpec(shape, lambda i: place or (0,) * len(shape))

    count = sum(math.prod(s) * a.dtype.itemsize for s, a in zip(shapes, args))
    count += sum(math.prod(s) * jnp.dtype(d).itemsize for s, d in outs)
    return pl.pallas_call(
        body,
        grid=(1,),
        out_shape=[jax.ShapeDtypeStruct(s, d) for s, d in outs],
        in_specs=[pl.BlockSpec(memory_space=pltpu.SMEM)] * scalars
        + [whole(s, views.get(i, (s, None))[1]) for i, s in enumerate(shapes) if i >= scalars],
        out_specs=[whole(s) for s, d in outs],
        scratch_shapes=list(scratch),
        compiler_params=pltpu.CompilerParams(vmem_limit_bytes=limit * MIB),
        cost_estimate=pl.CostEstimate(flops=flops, bytes_accessed=count, transcendentals=0),
    )(*args)


def project_kernel(
    core_ref, rows_ref, rim_ref, got_ref, other_ref, rates_ref, pick_ref, ends_ref,
    normed_ref, proj_ref, w_ref, gains_ref, taps_ref, states_ref, values_ref, cum_ref, sent_ref,
    wide_ref,
):
    wide = w_ref.shape[1]
    flipped = core_ref[0] == 1
    taps = jnp.zeros((8, 4 * LANES), f32)
    for r in range(2 * got_ref.shape[0]):
        mine, theirs = got_ref[r // 2].astype(f32), other_ref[r // 2].astype(f32)
        part = jnp.where(flipped, theirs, mine) if r % 2 == 0 else jnp.where(flipped, mine, theirs)
        wide_ref[r * SHARD : (r + 1) * SHARD, :] = part[:SHARD]
        rest = part[SHARD:]
        taps = taps + rest[:, : 4 * LANES]
        whole = rest[:, :LANES] + rest[:, LANES : 2 * LANES] + rest[:, 2 * LANES : 3 * LANES]
        for k in range(3):
            states_ref[k, r : r + 1, :] = whole[TAPS + k : TAPS + k + 1]
    taps_ref[...] = taps
    w_ref[...] = wide_ref[...].astype(bf16)
    chosen = jnp.where(
        lanes_of((16, wide)) == rows_of((16, wide)) + GAIN_LANE, 1.0, 0.0
    )
    chosen = jnp.where(rows_of((16, wide)) < 2, chosen, 0.0).astype(bf16)
    gains = lax.dot_general(chosen, w_ref[...], (NT, ((), ())), preferred_element_type=f32)
    gains_ref[...] = gains[:8]
    gain = gains[0:1]

    def projected(rows):
        rows = rows.astype(f32)
        scale = lax.rsqrt(jnp.mean(rows * rows, -1, keepdims=True) + eps_norm)
        normed = (rows * scale * gain).astype(bf16)
        return normed, jnp.dot(normed, w_ref[...], preferred_element_type=f32)

    for at in range(0, ROWS, GROUP):
        normed, proj = projected(rows_ref[at : at + GROUP, :])
        normed_ref[at : at + GROUP, :] = normed
        proj_ref[at : at + GROUP, :] = proj
    proj_ref[ROWS:, :] = projected(rim_ref[...])[1]
    ones = lower_ones()
    pick, ends = pick_ref[...], ends_ref[...]
    lane, row = lanes_of((GROUP, LANES)), rows_of((GROUP, LANES))
    for s in range(2):
        here = slice(s * GROUP, (s + 1) * GROUP)
        steps = rates_ref[...] * jax.nn.softplus(proj_ref[here, :LANES])
        cum = summed_down(ones, steps, NN)
        cum_ref[here, :] = cum
        last = cum[GROUP - 1 : GROUP, :]
        tail = jnp.exp(last - cum)
        qk = proj_ref[here, 4 * LANES :]
        for h in range(4):
            tile = slice(h * LANES, (h + 1) * LANES)
            raw = proj_ref[here, tile]
            rim_two = proj_ref[ROWS + 2 * s : ROWS + 2 * s + 1, tile]
            rim_one = proj_ref[ROWS + 2 * s + 1 : ROWS + 2 * s + 2, tile]
            one = jnp.where(row == 0, rim_one, pltpu.roll(raw, 1, 0))
            two = jnp.where(row == 0, rim_two, jnp.where(row == 1, rim_one, pltpu.roll(raw, 2, 0)))
            conv = (
                taps_ref[0:1, tile] * raw + taps_ref[1:2, tile] * one + taps_ref[2:3, tile] * two
            )
            values = jnp.where(lane < DH, conv, jnp.where(lane == DH, 1.0, 0.0))
            values_ref[here, tile] = values
            left, right = factors(head_lanes(qk, h, True), pick, ends)
            held = left * right * ends[2:3] * head_column(tail, h)
            fresh = product(held, values, TN)
            store_pieces(sent_ref, 4 * s + h, fresh)
            ending = jnp.broadcast_to(head_column(last, h), (8, LANES))
            high, mid, low = three_parts(ending)
            few = lanes_of((8, LANES))
            packed = jnp.where(
                few == 0,
                high.astype(f32),
                jnp.where(few == 1, mid.astype(f32), jnp.where(few == 2, low.astype(f32), 0.0)),
            ).astype(bf16)
            for q in range(4):
                sent_ref[16 * s + 4 * h + q, PIECE:, :] = packed


def project(core, rows, rim, got, other, rates, pick, ends):
    wide, width = got.shape[2], rows.shape[1]
    return whole_call(
        project_kernel,
        [
            (rows.shape, bf16),
            ((ROWS + rim.shape[0], wide), f32),
            ((width, wide), bf16),
            ((8, width), f32),
            ((8, 4 * LANES), f32),
            ((3, 2 * got.shape[0], LANES), f32),
            ((ROWS, 4 * LANES), f32),
            ((ROWS, LANES), f32),
            ((PIECES, SLOT, LANES), bf16),
        ],
        core, rows, rim, got, other, rates, pick, ends,
        scratch=[pltpu.VMEM((width, wide), f32)],
        flops=3 * 10**9,
        scalars=1,
    )


def scan_kernel(got_ref, back_ref, decay_ref):
    state = jnp.zeros((PIECE, LANES), f32)
    for i in range(PIECES):
        back_ref[i, :PIECE, :] = state.astype(bf16)
        back_ref[i, PIECE:, :] = jnp.zeros((SLOT - PIECE, LANES), bf16)
        ending = jnp.sum(got_ref[i, PIECE:, :].astype(f32), -1, keepdims=True)
        decay = jnp.broadcast_to(jnp.exp(ending), (8, LANES))
        decay_ref[i] = decay
        state = state * decay[0:1] + got_ref[i, :PIECE, :].astype(f32)


def earlier_states(sent):
    got = lax.all_to_all(sent, SEQ, 0, 0, tiled=True)
    back, decay = whole_call(
        scan_kernel, [(sent.shape, bf16), ((PIECES, 8, LANES), f32)], got, flops=10**6
    )
    return lax.all_to_all(back, SEQ, 0, 0, tiled=True), decay


def scan_back_kernel(got_ref, decay_ref, back_ref):
    state = jnp.zeros((PIECE, LANES), f32)
    for i in reversed(range(PIECES)):
        back_ref[i, :PIECE, :] = state.astype(bf16)
        back_ref[i, PIECE:, :] = jnp.zeros((SLOT - PIECE, LANES), bf16)
        state = state * decay_ref[i, 0:1, :] + got_ref[i, :PIECE, :].astype(f32)


def later_states(sent, decay):
    got = lax.all_to_all(sent, SEQ, 0, 0, tiled=True)
    (back,) = whole_call(scan_back_kernel, [(sent.shape, bf16)], got, decay, flops=10**6)
    return lax.all_to_all(back, SEQ, 0, 0, tiled=True), back


QK = ((ROWS, LANES), (0, 4))
FIRST = ((ROWS, LANES), (0, 0))


def within_kernel(qk_ref, values_ref, cum_ref, inside_ref):
    for s in range(2):
        here = slice(s * GROUP, (s + 1) * GROUP)
        cum = cum_ref[here, :]
        across = cum.T
        qk = qk_ref[here, :]
        for h in range(4):
            tile = slice(h * LANES, (h + 1) * LANES)
            dots = scores(qk, h)
            weights = (1.0 + dots + 0.5 * dots * dots) * decays(cum, across, h)
            inside_ref[here, tile] = product(weights, values_ref[here, tile], NN)


def within(proj, values, cum):
    return whole_call(
        within_kernel,
        [((ROWS, 4 * LANES), f32)],
        proj, values, cum,
        flops=3 * 10**9,
        views={0: QK},
    )[0]


def mix_kernel(
    qk_ref, cum_ref, inside_ref, earlier_ref, pick_ref, ends_ref, total_ref, mixed_ref
):
    pick, ends = pick_ref[...], ends_ref[...]
    lane = lanes_of((GROUP, LANES))
    for s in range(2):
        here = slice(s * GROUP, (s + 1) * GROUP)
        growth = jnp.exp(cum_ref[here, :])
        qk = qk_ref[here, :]
        for h in range(4):
            tile = slice(h * LANES, (h + 1) * LANES)
            left, right = factors(head_lanes(qk, h, False), pick, ends)
            held = left * right * ends[2:3] * head_column(growth, h)
            total = inside_ref[here, tile] + product(held, state_rows(earlier_ref, 4 * s + h), NN, 2)
            total_ref[here, tile] = total
            mixed = total / total[:, DH : DH + 1]
            mixed_ref[here, tile] = jnp.where(lane < DH, mixed, 0.0).astype(bf16)


def mix(proj, cum, inside, earlier, pick, ends):
    return whole_call(
        mix_kernel,
        [((ROWS, 4 * LANES), f32), ((ROWS, 4 * LANES), bf16)],
        proj, cum, inside, earlier, pick, ends,
        flops=3 * 10**9,
        views={0: QK},
    )


OWN = ROWS // 4


def own_slice(ref, place):
    return ref[pl.ds(pl.multiple_of(place * OWN, OWN), OWN), :]


def turn_kernel(
    place_ref, got_ref, unit_ref, scale_ref, back_ref, gains_ref, w_ref,
    middle_back_ref, gain_ref, out_back_ref, mixed_back_ref,
):
    two_back = got_ref[...].astype(f32)
    unit = unit_ref[...]
    gain_ref[...] = jnp.broadcast_to(
        jnp.sum(two_back * unit, 0, keepdims=True), gain_ref.shape
    )
    weighted = two_back * gains_ref[1:2]
    along = jnp.mean(weighted * unit, -1, keepdims=True)
    middle_back = own_slice(back_ref, place_ref[0]).astype(f32) + scale_ref[:, 0:1] * (
        weighted - unit * along
    )
    middle_back_ref[...] = middle_back
    out_back = middle_back.astype(bf16)
    out_back_ref[...] = out_back
    for g in range(4):
        mixed_back_ref[g] = jnp.dot(
            out_back, w_ref[:, g * 4 * LANES : (g + 1) * 4 * LANES], preferred_element_type=f32
        ).astype(bf16)


def turn(place, got, unit, scale, back, gains, w_out):
    width = back.shape[1]
    return whole_call(
        turn_kernel,
        [
            ((OWN, width), f32),
            ((8, width), f32),
            ((OWN, width), bf16),
            ((4, OWN, 4 * LANES), bf16),
        ],
        place, got, unit, scale, back, gains, w_out,
        flops=10**9,
        scalars=1,
        views={6: ((width, OUT), (0, 0))},
    )


def token_kernel(place_ref, *refs):
    terms, (rows_ref, middle_back_ref, gains_ref, out_ref) = refs[:3], refs[3:]
    one_back = sum(ref[...].astype(f32) for ref in terms)
    rows = own_slice(rows_ref, place_ref[0]).astype(f32)
    scale = lax.rsqrt(jnp.mean(rows * rows, -1, keepdims=True) + eps_norm)
    unit = rows * scale
    weighted = one_back * gains_ref[0:1]
    along = jnp.mean(weighted * unit, -1, keepdims=True)
    token_back = middle_back_ref[...] + scale * (weighted - unit * along)
    out_ref[...] = token_back.astype(bf16)


def token_grads(place, terms, rows, middle_back, gains):
    return whole_call(
        token_kernel, [(terms[0].shape, bf16)], place, *terms, rows, middle_back, gains,
        flops=10**7,
        scalars=1,
    )[0]


def block_kernel(place_ref, *refs):
    terms, (middle_ref, keep_ref, out_ref) = refs[:3], refs[3:]
    ffn = sum(ref[...].astype(f32) for ref in terms)
    keep = own_slice(keep_ref, place_ref[0])[:, 0:1]
    out_ref[...] = ((middle_ref[...] + ffn) * keep).astype(bf16)


def block_outs(place, terms, middle, keep):
    return whole_call(
        block_kernel, [(terms[0].shape, bf16)], place, *terms, middle, keep,
        flops=10**7,
        scalars=1,
    )[0]


def assemble_kernel(place_ref, own_ref, side_ref, back_ref, far_a_ref, far_b_ref, out_ref):
    place = place_ref[0]
    half = OWN // 2

    def at(other):
        return pl.multiple_of(jnp.bitwise_xor(place, other) * OWN, OWN)

    out_ref[pl.ds(at(0), OWN), :] = own_ref[...]
    out_ref[pl.ds(at(1), OWN), :] = side_ref[...]
    out_ref[pl.ds(at(3), OWN), :] = back_ref[...]
    out_ref[pl.ds(at(2), half), :] = far_a_ref[...]
    out_ref[pl.ds(pl.multiple_of(at(2) + half, half), half), :] = far_b_ref[...]


def gather_parts(own, after=None):
    half = own.shape[0] // 2
    back = lax.ppermute(own, "mp", BACK)
    side = lax.ppermute(own, "mp", SIDE)
    if after is not None:
        back, side, _ = lax.optimization_barrier((back, side, after))
    far_a = lax.ppermute(back[:half], "mp", SIDE)
    far_b = lax.ppermute(side[half:], "mp", BACK)
    return own, side, back, far_a, far_b


def gather_rows(place, own, after):
    return whole_call(
        assemble_kernel, [((ROWS, own.shape[1]), own.dtype)], place, *gather_parts(own, after),
        flops=10**6,
        scalars=1,
    )[0]


def scatter_terms(part):
    half = OWN // 2
    got_a = lax.ppermute(part[2, :half], "mp", SIDE)
    got_b = lax.ppermute(part[2, half:], "mp", BACK)
    to_back = jnp.concatenate(
        [(part[3, :half].astype(f32) + got_a.astype(f32)).astype(bf16), part[3, half:]], 0
    )
    to_side = jnp.concatenate(
        [part[1, :half], (part[1, half:].astype(f32) + got_b.astype(f32)).astype(bf16)], 0
    )
    return part[0], lax.ppermute(to_back, "mp", BACK), lax.ppermute(to_side, "mp", SIDE)


def store_by_owner(ref, value, place, columns=slice(None)):
    for g in range(4):
        ref[jnp.bitwise_xor(place, g), :, columns] = value[g * OWN : (g + 1) * OWN]


def unmix_kernel(
    mixed_back_ref, total_ref, qk_ref, cum_ref, pick_ref, ends_ref, total_back_ref, sent_ref
):
    pick, ends = pick_ref[...], ends_ref[...]
    lane = lanes_of((GROUP, LANES))
    for s in range(2):
        here = slice(s * GROUP, (s + 1) * GROUP)
        growth = jnp.exp(cum_ref[here, :])
        qk = qk_ref[here, :]
        for h in range(4):
            tile = slice(h * LANES, (h + 1) * LANES)
            total = total_ref[here, tile]
            inverse = 1.0 / total[:, DH : DH + 1]
            numer = mixed_back_ref[here, tile].astype(f32) * inverse
            numer = jnp.where(lane < DH, numer, 0.0)
            denom = -jnp.sum(numer * total, -1, keepdims=True) * inverse
            total_back = jnp.where(lane == DH, denom, numer)
            total_back_ref[here, tile] = total_back
            left, right = factors(head_lanes(qk, h, False), pick, ends)
            held = left * right * ends[2:3] * head_column(growth, h)
            store_pieces(sent_ref, 4 * s + h, product(held, total_back, TN))
            for q in range(4):
                sent_ref[16 * s + 4 * h + q, PIECE:, :] = jnp.zeros((SLOT - PIECE, LANES), bf16)


def unmix(mixed_back, total, proj, cum, pick, ends):
    return whole_call(
        unmix_kernel,
        [((ROWS, 4 * LANES), f32), ((PIECES, SLOT, LANES), bf16)],
        mixed_back, total, proj, cum, pick, ends,
        flops=3 * 10**9,
        views={2: QK},
    )


def within_back_kernel(
    qk_ref, values_ref, cum_ref, total_back_ref, earlier_ref, pick_ref, ends_ref,
    qk_back_ref, values_back_ref, level_ref,
):
    pick, ends = pick_ref[...], ends_ref[...]
    only = lanes_of((GROUP, LANES)) < FEAT
    cum = cum_ref[:, :]
    across = cum.T
    growth = jnp.exp(cum)
    qk = qk_ref[:, :]
    qk_back = jnp.zeros((GROUP, LANES), f32)
    level = jnp.zeros((GROUP, LANES), f32)
    level_down = jnp.zeros((LANES, GROUP), f32)
    for h in range(4):
        tile = slice(h * LANES, (h + 1) * LANES)
        total_back = total_back_ref[:, tile]
        decay = decays(cum, across, h)
        dots = scores(qk, h)
        pairing = decay * product(total_back, values_ref[:, tile], NT)
        kernel = 1.0 + dots + 0.5 * dots * dots
        moved = kernel * pairing
        down = jnp.sum(moved, 0, keepdims=True)
        level_down = jnp.where(rows_of((LANES, GROUP)) == GATE_LANE + h, down, level_down)
        kernel_back = pairing * (1.0 + dots) * 0.25
        values_back_ref[:, tile] = product(kernel * decay, total_back, TN)
        query_tile = head_lanes(qk, h, False)
        keys_only = jnp.where(only, head_lanes(qk, h, True), 0.0)
        query_only = jnp.where(only, query_tile, 0.0)
        query_back = product(kernel_back, keys_only, NN)
        keys_back = product(kernel_back, query_only, TN)
        left, right = factors(query_tile, pick, ends)
        features_back = head_column(growth, h) * product(
            total_back, state_rows(earlier_ref, h), NT, 2
        )
        level_here = jnp.sum(moved, 1, keepdims=True) + jnp.sum(
            left * right * ends[2:3] * features_back, 1, keepdims=True
        )
        level = level + on_head_lane(level_here, h)
        query_back = query_back + factors_back(features_back, left, right, pick, ends)
        at = h * FEAT
        qk_back = qk_back + (pltpu.roll(query_back, at, 1) if at else query_back)
        qk_back = qk_back + pltpu.roll(keys_back, at + 4 * FEAT, 1)
    qk_back_ref[:, :] = qk_back
    level_ref[:, :] = level - level_down.T


def within_back(s, proj, values, cum, total_back, earlier, pick, ends):
    return whole_call(
        within_back_kernel,
        [((GROUP, LANES), f32), ((GROUP, 4 * LANES), f32), ((GROUP, LANES), f32)],
        proj, values, cum, total_back, earlier, pick, ends,
        flops=4 * 10**9,
        views={
            0: ((GROUP, LANES), (s, 4)),
            1: ((GROUP, 4 * LANES), (s, 0)),
            2: ((GROUP, LANES), (s, 0)),
            3: ((GROUP, 4 * LANES), (s, 0)),
            4: ((PIECES // 2, SLOT, LANES), (s, 0, 0)),
        },
    )


def later_back_kernel(
    qk_ref, first_ref, values_ref, cum_ref, rates_ref, earlier_ref, later_ref, pick_ref, ends_ref,
    qk_in_a_ref, values_in_a_ref, level_a_ref, qk_in_b_ref, values_in_b_ref, level_b_ref,
    qk_back_ref, values_back_ref, gate_back_ref,
):
    pick, ends = pick_ref[...], ends_ref[...]
    ones, before = lower_ones(), lower_ones(True)
    for s in range(2):
        here = slice(s * GROUP, (s + 1) * GROUP)
        cum = cum_ref[here, :]
        last = cum[GROUP - 1 : GROUP, :]
        tail = jnp.exp(last - cum)
        carried = jnp.exp(last)
        qk = qk_ref[here, :]
        qk_in_ref, values_in_ref, level_ref = (
            (qk_in_a_ref, values_in_a_ref, level_a_ref),
            (qk_in_b_ref, values_in_b_ref, level_b_ref),
        )[s]
        qk_back = qk_in_ref[...]
        crossed = jnp.zeros((GROUP, LANES), f32)
        through = jnp.zeros((1, LANES), f32)
        for h in range(4):
            tile = slice(h * LANES, (h + 1) * LANES)
            later = state_rows(later_ref, 4 * s + h)
            left, right = factors(head_lanes(qk, h, True), pick, ends)
            held = left * right * ends[2:3]
            column = head_column(tail, h)
            features_back = column * product(values_ref[here, tile], later, NT, 2)
            values_back_ref[here, tile] = values_in_ref[:, tile] + column * product(
                held, later, NN, 2
            )
            crossed = crossed + on_head_lane(
                jnp.sum(held * features_back, 1, keepdims=True), h
            )
            keys_back = factors_back(features_back, left, right, pick, ends)
            qk_back = qk_back + pltpu.roll(keys_back, (h + 4) * FEAT, 1)
            whole = jnp.sum(
                later.astype(f32) * state_rows(earlier_ref, 4 * s + h).astype(f32), 1, keepdims=True
            )
            whole = jnp.sum(whole, 0, keepdims=True) * head_column(carried, h)
            through = through + on_head_lane(whole, h)
        qk_back_ref[here, :] = qk_back
        step_back = (
            summed_down(ones, level_ref[...], TN) + summed_down(before, crossed, NN) + through
        )
        gate_back_ref[here, :] = (
            step_back * rates_ref[...] * jax.nn.sigmoid(first_ref[here, :])
        )


def later_back(proj, values, cum, rates, earlier, later, pick, ends, within):
    return whole_call(
        later_back_kernel,
        [((ROWS, LANES), f32), ((ROWS, 4 * LANES), f32), ((ROWS, LANES), f32)],
        proj, proj, values, cum, rates, earlier, later, pick, ends, *within,
        flops=4 * 10**9,
        views={0: QK, 1: FIRST},
    )


def unproject_kernel(
    place_ref, proj_ref, ahead_ref, taps_ref, qk_back_ref, values_back_ref, gate_back_ref, normed_ref, w_ref,
    own_ref, side_ref, back_ref, far_a_ref, far_b_ref, mixed_ref, gain_two_ref,
    part_ref, kept_ref, sent_ref, taps_grad_ref, proj_back_ref, out_back_ref, turned_ref,
):
    lane, row = lanes_of((GROUP, LANES)), rows_of((GROUP, LANES))
    taps_grad_ref[...] = jnp.zeros_like(taps_grad_ref)
    for s in range(2):
        here = slice(s * GROUP, (s + 1) * GROUP)
        for h in range(4):
            tile = slice(h * LANES, (h + 1) * LANES)
            raw = proj_ref[here, tile]
            back = values_back_ref[here, tile]
            back = jnp.where(lane < DH, back, 0.0)
            rim_two = proj_ref[ROWS + 2 * s : ROWS + 2 * s + 1, tile]
            rim_one = proj_ref[ROWS + 2 * s + 1 : ROWS + 2 * s + 2, tile]
            one = jnp.where(row == 0, rim_one, pltpu.roll(raw, 1, 0))
            two = jnp.where(row == 0, rim_two, jnp.where(row == 1, rim_one, pltpu.roll(raw, 2, 0)))
            for j, moved in enumerate((raw, one, two)):
                taps_grad_ref[j : j + 1, tile] = taps_grad_ref[j : j + 1, tile] + jnp.sum(
                    moved * back, 0, keepdims=True
                )
            next_one = ahead_ref[2 * s : 2 * s + 1, tile]
            next_two = ahead_ref[2 * s + 1 : 2 * s + 2, tile]
            one = jnp.where(row == GROUP - 1, next_one, pltpu.roll(back, GROUP - 1, 0))
            two = jnp.where(
                row == GROUP - 1,
                next_two,
                jnp.where(row == GROUP - 2, next_one, pltpu.roll(back, GROUP - 2, 0)),
            )
            raw_back = (
                taps_ref[0:1, tile] * back + taps_ref[1:2, tile] * one + taps_ref[2:3, tile] * two
            )
            raw_back = jnp.where(lane < DH, raw_back, 0.0)
            if h == 0:
                gates = (lane >= GATE_LANE) & (lane < GATE_LANE + 4)
                raw_back = jnp.where(gates, gate_back_ref[here, :], raw_back)
            proj_back_ref[here, tile] = raw_back.astype(bf16)
        proj_back_ref[here, 4 * LANES :] = qk_back_ref[here, :].astype(bf16)
    part = lax.dot_general(
        proj_back_ref[...], w_ref[...], (NT, ((), ())), preferred_element_type=f32
    ).astype(bf16)
    store_by_owner(part_ref, part, place_ref[0])
    wide = w_ref.shape[1]
    grad_in = lax.dot_general(
        normed_ref[...], proj_back_ref[...], (TN, ((), ())), preferred_element_type=f32
    )
    weights = w_ref[...].astype(f32)
    gain_one = jnp.sum(grad_in * weights, 1, keepdims=True)
    gain_one = gain_one / weights[:, GAIN_LANE : GAIN_LANE + 1]
    gain_two = gain_two_ref[...].T[:, 0:1]
    first = grad_in[:, :LANES]
    spot = lanes_of(first.shape)
    first = jnp.where(
        spot == GAIN_LANE, gain_one, jnp.where(spot == GAIN_LANE + 1, gain_two, first)
    )
    out_back_ref[:OWN] = own_ref[...]
    out_back_ref[OWN : 2 * OWN] = side_ref[...]
    out_back_ref[2 * OWN : 3 * OWN] = back_ref[...]
    out_back_ref[3 * OWN : 3 * OWN + OWN // 2] = far_a_ref[...]
    out_back_ref[3 * OWN + OWN // 2 :] = far_b_ref[...]
    for k, other in enumerate((0, 1, 3, 2)):
        turned_ref[k * OWN : (k + 1) * OWN] = own_slice(
            mixed_ref, jnp.bitwise_xor(place_ref[0], other)
        )
    grad_out = lax.dot_general(
        out_back_ref[...], turned_ref[...], (TN, ((), ())), preferred_element_type=f32
    )
    core = place_ref[1]

    def store(ref, parity):
        for k in range(ref.shape[0]):
            r = 2 * k + parity
            here = slice(r * SHARD, (r + 1) * SHARD)
            ref[k, :SHARD, :LANES] = first[here].astype(bf16)
            ref[k, :SHARD, LANES:wide] = grad_in[here, LANES:].astype(bf16)
            ref[k, :SHARD, wide:] = grad_out[here].astype(bf16)
            h, at = r // 8, (r % 8) * (DH // 8)
            few = taps_grad_ref[:, h * LANES : (h + 1) * LANES]
            few = pltpu.roll(few, LANES - at, 1) if at else few
            ref[k, SHARD:, :LANES] = few.astype(bf16)
            ref[k, SHARD:, LANES:] = jnp.zeros((SPACED - SHARD, wide + 3 * LANES), bf16)

    for parity in range(2):

        @pl.when(core == parity)
        def _():
            store(kept_ref, parity)
            store(sent_ref, 1 - parity)


def unproject(
    place, proj, ahead, taps, qk_back, values_back, gate_back, normed, w_in, out_parts, mixed, gain_two
):
    width, wide = w_in.shape
    return whole_call(
        unproject_kernel,
        [
            ((4, OWN, width), bf16),
            ((width // SHARD // 2, SPACED, wide + 4 * LANES), bf16),
            ((width // SHARD // 2, SPACED, wide + 4 * LANES), bf16),
        ],
        place, proj, ahead, taps, qk_back, values_back, gate_back, normed, w_in, *out_parts, mixed,
        gain_two,
        scratch=[
            pltpu.VMEM((8, 4 * LANES), f32),
            pltpu.VMEM((ROWS, wide), bf16),
            pltpu.VMEM((ROWS, width), bf16),
            pltpu.VMEM((ROWS, 4 * LANES), bf16),
        ],
        flops=4 * 10**9,
        scalars=1,
    )


BLOCK = 256
HIDDEN = 1280
OUT = 16 * LANES
SHARD = 56
SPACED = 64


GROUPS = 4


def middle_kernel(
    place_ref, own_ref, side_ref, back_ref, far_a_ref, far_b_ref, out_ref, rows_ref, gains_ref,
    cotangent_ref, gate_ref, up_ref, down_ref, both_ref,
    middle_ref, unit_ref, scale_ref, normed_ref, acts_ref, two_ref,
    mixed_ref, sum_ref,
):
    place, step = place_ref[0], pl.program_id(0)
    blocks = HIDDEN // BLOCK

    @pl.when(step == 0)
    def _():
        mixed_ref[place] = own_ref[...]
        mixed_ref[jnp.bitwise_xor(place, 1)] = side_ref[...]
        mixed_ref[jnp.bitwise_xor(place, 3)] = back_ref[...]
        mixed_ref[jnp.bitwise_xor(place, 2), :GROUP, :] = far_a_ref[...]
        mixed_ref[jnp.bitwise_xor(place, 2), GROUP:, :] = far_b_ref[...]
        sum_ref[...] = rows_ref[...].astype(f32)

    @pl.when(step < GROUPS)
    def _():
        for at in range(0, out_ref.shape[0], BLOCK):
            here = slice(at, at + BLOCK)
            sum_ref[:, here] += lax.dot_general(
                mixed_ref[step], out_ref[here, :], (NT, ((), ())), preferred_element_type=f32
            )

    @pl.when(step == GROUPS - 1)
    def _():
        for at in range(0, ROWS, OWN):
            here = slice(at, at + OWN)
            middle = sum_ref[here, :]
            scale = lax.rsqrt(jnp.mean(middle * middle, -1, keepdims=True) + eps_norm)
            normed_ref[here, :] = (middle * scale * gains_ref[1:2]).astype(bf16)
        middle = own_slice(sum_ref, place)
        scale = lax.rsqrt(jnp.mean(middle * middle, -1, keepdims=True) + eps_norm)
        middle_ref[...] = middle
        unit_ref[...] = middle * scale
        scale_ref[...] = jnp.broadcast_to(scale, scale_ref.shape)

    @pl.when((step >= GROUPS) & (step < GROUPS + blocks))
    def _():
        normed = normed_ref[...]
        gate = jnp.dot(normed, gate_ref[...], preferred_element_type=f32)
        up = jnp.dot(normed, up_ref[...], preferred_element_type=f32)
        hidden_back = jnp.dot(cotangent_ref[...], down_ref[...], preferred_element_type=f32)
        sigma = jax.nn.sigmoid(gate)
        silu = gate * sigma
        at = pl.multiple_of((step - GROUPS) * BLOCK, BLOCK)
        acts_ref[:, pl.ds(at, BLOCK)] = (
            hidden_back * up * sigma * (1.0 + gate * (1.0 - sigma))
        ).astype(bf16)
        acts_ref[:, pl.ds(HIDDEN + at, BLOCK)] = (hidden_back * silu).astype(bf16)
        acts_ref[:, pl.ds(2 * HIDDEN + at, BLOCK)] = (silu * up).astype(bf16)

    @pl.when(step >= GROUPS + blocks)
    def _():
        two_ref[...] = lax.dot_general(
            acts_ref[:, : 2 * HIDDEN], both_ref[...], (NT, ((), ())), preferred_element_type=f32
        ).astype(bf16)


def middle_both_ways(place, mixed_parts, weights, rows, gains, back):
    width = rows.shape[1]
    blocks, outs = HIDDEN // BLOCK, width // BLOCK
    columns = OUT // GROUPS

    def whole(shape):
        return pl.BlockSpec(shape, lambda i: (0,) * len(shape))

    def clipped(i, first, count):
        return jnp.clip(i - first, 0, count - 1)

    def block_of(which):
        at = OUT // BLOCK + which * blocks
        return pl.BlockSpec((width, BLOCK), lambda i: (0, at + clipped(i, GROUPS, blocks)))

    last = GROUPS + blocks
    specs = [whole(part.shape) for part in mixed_parts]
    specs.append(pl.BlockSpec((width, columns), lambda i: (0, clipped(i, 0, GROUPS))))
    specs += [whole(rows.shape), whole(gains.shape), whole(back.shape)]
    specs += [block_of(0), block_of(1), block_of(2)]
    specs.append(
        pl.BlockSpec(
            (pl.Element(BLOCK), pl.Element(2 * HIDDEN)),
            lambda i: (clipped(i, last, outs) * BLOCK, OUT),
        )
    )
    results = [
        ((OWN, width), f32),
        ((OWN, width), f32),
        ((OWN, LANES), f32),
        ((ROWS, width), bf16),
        ((ROWS, 3 * HIDDEN), bf16),
        ((ROWS, width), bf16),
    ]
    out_specs = [whole(s) for s, d in results]
    out_specs[-1] = pl.BlockSpec((ROWS, BLOCK), lambda i: (0, clipped(i, last, outs)))
    return pl.pallas_call(
        middle_kernel,
        grid=(last + outs,),
        out_shape=[jax.ShapeDtypeStruct(s, d) for s, d in results],
        in_specs=[pl.BlockSpec(memory_space=pltpu.SMEM)] + specs,
        out_specs=out_specs,
        scratch_shapes=[
            pltpu.VMEM((GROUPS, ROWS, columns), bf16),
            pltpu.VMEM((ROWS, width), f32),
        ],
        compiler_params=pltpu.CompilerParams(vmem_limit_bytes=60 * MIB),
        cost_estimate=pl.CostEstimate(
            flops=16 * 10**9, bytes_accessed=40 * 10**6, transcendentals=0
        ),
    )(place, *mixed_parts, weights, rows, gains, back, weights, weights, weights, weights)


def ffn_out_kernel(place_ref, acts_ref, down_ref, out_ref):
    value = lax.dot_general(
        acts_ref[...], down_ref[...], (NT, ((), ())), preferred_element_type=f32
    ).astype(bf16)
    store_by_owner(out_ref, value, place_ref[0])


def ffn_out(place, acts, weights):
    width = weights.shape[0]
    return pl.pallas_call(
        ffn_out_kernel,
        grid=(width // BLOCK,),
        out_shape=jax.ShapeDtypeStruct((4, OWN, width), bf16),
        in_specs=[
            pl.BlockSpec(memory_space=pltpu.SMEM),
            pl.BlockSpec((ROWS, HIDDEN), lambda i: (0, 2)),
            pl.BlockSpec(
                (pl.Element(BLOCK), pl.Element(HIDDEN)), lambda i: (i * BLOCK, OUT + 2 * HIDDEN)
            ),
        ],
        out_specs=pl.BlockSpec((4, OWN, BLOCK), lambda i: (0, 0, i)),
        compiler_params=pltpu.CompilerParams(vmem_limit_bytes=60 * MIB),
        cost_estimate=pl.CostEstimate(
            flops=3 * 10**9, bytes_accessed=8 * 10**6, transcendentals=0
        ),
    )(place, acts, weights)


def ffn_grads_kernel(normed_ref, back_ref, acts_ref, grads_ref):
    def spaced(rows_ref):
        grad = lax.dot_general(
            rows_ref[...], acts_ref[...], (TN, ((), ())), preferred_element_type=f32
        )
        for r in range(grad.shape[0] // SHARD):
            grads_ref[r * SPACED : r * SPACED + SHARD, :] = grad[
                r * SHARD : (r + 1) * SHARD
            ].astype(bf16)
            grads_ref[r * SPACED + SHARD : (r + 1) * SPACED, :] = jnp.zeros(
                (SPACED - SHARD, grad.shape[1]), bf16
            )

    both = pl.program_id(0) < 2 * HIDDEN // WIDER

    @pl.when(both)
    def _():
        spaced(normed_ref)

    @pl.when(jnp.logical_not(both))
    def _():
        spaced(back_ref)


WIDER = 640


def ffn_grads(normed, back, acts):
    width = normed.shape[1]
    whole = pl.BlockSpec((ROWS, width), lambda i: (0, 0))
    return pl.pallas_call(
        ffn_grads_kernel,
        grid=(3 * HIDDEN // WIDER,),
        out_shape=jax.ShapeDtypeStruct((width // SHARD * SPACED, 3 * HIDDEN), bf16),
        in_specs=[whole, whole, pl.BlockSpec((ROWS, WIDER), lambda i: (0, i))],
        out_specs=pl.BlockSpec((width // SHARD * SPACED, WIDER), lambda i: (0, i)),
        compiler_params=pltpu.CompilerParams(vmem_limit_bytes=60 * MIB),
        cost_estimate=pl.CostEstimate(
            flops=7 * 10**9, bytes_accessed=20 * 10**6, transcendentals=0
        ),
    )(normed, back, acts)


def order_columns(heads):
    import numpy as np

    place = np.zeros((5 * LANES, 5 * LANES), np.float32)
    for h in range(heads):
        at = h * (2 * FEAT + DH + 1)
        for i in range(FEAT):
            place[at + i, heads * LANES + h * FEAT + i] = 1.0
            place[at + FEAT + i, heads * LANES + (heads + h) * FEAT + i] = 1.0
        for i in range(DH):
            place[at + 2 * FEAT + i, h * LANES + i] = 1.0
        place[at + 2 * FEAT + DH, GATE_LANE + h] = 1.0
    return jnp.asarray(place, bf16)


def order_heads(heads):
    import numpy as np

    place = np.zeros((heads * DH, heads * LANES), np.float32)
    for h in range(heads):
        for i in range(DH):
            place[h * DH + i, h * LANES + i] = 1.0
    return jnp.asarray(place, bf16)


def prepare_kernel(
    rank_ref, in_ref, out_ref, gate_ref, up_ref, down_ref, taps_ref,
    gains_ref, gains_first_ref, gains_second_ref, place_ref, tiles_ref,
    shard_ref, out_shard_ref, rest_ref, few_ref,
):
    wide = 5 * LANES
    columns = in_ref.shape[1]
    whole = jnp.dot(
        in_ref[...].astype(bf16), place_ref[:columns, :], preferred_element_type=f32
    )
    spot = jnp.where(
        lanes_of((2, wide)) == rows_of((2, wide)) + GAIN_LANE, 1.0, 0.0
    ).astype(bf16)
    gains = lax.dot_general(
        gains_ref[...].astype(bf16), spot, (TN, ((), ())), preferred_element_type=f32
    )
    for k in range(shard_ref.shape[0]):
        shard_ref[k, :SHARD, :] = (whole + gains).astype(bf16)
    rank = rank_ref[0]
    own = taps_ref.shape[1]
    each = DH // own
    first = (rank // each) * LANES + (rank % each) * own
    spot = jnp.where(
        lanes_of((own, wide)) == rows_of((own, wide)) + first, 1.0, 0.0
    ).astype(bf16)
    taps = jnp.dot(taps_ref[...].astype(bf16), spot, preferred_element_type=f32)
    rows = [taps]
    for ref in (gains_ref, gains_first_ref, gains_second_ref):
        few_ref[...] = jnp.zeros_like(few_ref)
        few_ref[0:2, :SHARD] = ref[...]
        both = few_ref[...]
        line = both + pltpu.roll(pltpu.roll(both, SHARD, 1), 7, 0)
        parts = [part.astype(f32)[0:1] for part in three_parts(line)]
        rows.append(jnp.concatenate(parts + [jnp.zeros((1, wide - 3 * LANES), f32)], 1))
    rows.append(jnp.zeros((SPACED - SHARD - TAPS - 3, wide), f32))
    for k in range(shard_ref.shape[0]):
        shard_ref[k, SHARD:, :] = jnp.concatenate(rows, 0).astype(bf16)
    out_shard_ref[...] = jnp.dot(
        out_ref[...].astype(bf16), tiles_ref[...], preferred_element_type=f32
    ).astype(bf16)
    rest_ref[...] = jnp.zeros_like(rest_ref)
    units = gate_ref.shape[1]
    rest_ref[:, :units] = gate_ref[...].astype(bf16)
    rest_ref[:, HIDDEN : HIDDEN + units] = up_ref[...].astype(bf16)
    rest_ref[:, 2 * HIDDEN : 2 * HIDDEN + units] = down_ref[...].astype(bf16)


def prepare(rank, *args):
    return whole_call(
        prepare_kernel,
        [
            ((16, SPACED, 5 * LANES), bf16),
            ((SHARD, 4 * LANES), bf16),
            ((SHARD, 3 * HIDDEN), bf16),
        ],
        rank, *args,
        scratch=[pltpu.VMEM((8, LANES), f32)],
        scalars=1,
    )


def moved_moments(weight, first, second, grad):
    fix = 1.0 - beta_value**STEP
    moment = beta_value * first + (1.0 - beta_value) * grad
    square = beta_value * second + (1.0 - beta_value) * grad * grad
    direction = moment / fix / (jnp.sqrt(square / fix) + eps_adam) + decay_rate * weight
    return moment, square, direction


def adapted(params, outs, place, grad):
    weight = params[0][...]
    moment, square, direction = moved_moments(weight, params[1][...], params[2][...], grad)
    outs[0][...] = moment
    outs[1][...] = square
    outs[2][...] = direction
    both = [
        jnp.sum(jnp.sum(v * v, 1, keepdims=True), 0, keepdims=True) for v in (weight, direction)
    ]
    lane = lanes_of((1, LANES))
    return jnp.where(lane == place, both[0], jnp.where(lane == place + 1, both[1], 0.0))


def ffn_moments_kernel(ffn_ref, *refs):
    params, outs, sums_ref = refs[:9], refs[9:-1], refs[-1]
    units = params[0].shape[1]
    sums = jnp.zeros((1, LANES), f32)
    for k in range(3):
        grad = ffn_ref[:SHARD, k * HIDDEN : k * HIDDEN + units].astype(f32)
        three = slice(3 * k, 3 * k + 3)
        sums = sums + adapted(params[three], outs[three], 4 + 2 * k, grad)
    sums_ref[...] = jnp.broadcast_to(sums, sums_ref.shape)


def ffn_moments(ffn, params):
    outs = [(param.shape, f32) for param in params]
    return whole_call(ffn_moments_kernel, outs + [((8, LANES), f32)], ffn, *params)


def moments_kernel(mixer_ref, place_ref, tiles_ref, ffn_sums_ref, *refs):
    params, outs, sums_ref = refs[:9], refs[9:-1], refs[-1]

    wide = 5 * LANES
    mixer = mixer_ref[0].astype(f32)
    for k in range(1, mixer_ref.shape[0]):
        mixer = mixer + mixer_ref[k].astype(f32)
    sums = ffn_sums_ref[0:1, :]
    grad_in = picked(mixer[:SHARD, :wide], place_ref[...], NT)
    sums = sums + adapted(params[0:3], outs[0:3], 0, grad_in[:, : params[0].shape[1]])
    sums = sums + adapted(params[3:6], outs[3:6], 2, picked(mixer[:SHARD, wide:], tiles_ref[...], NT))
    taps = mixer[SHARD : SHARD + TAPS, : params[6].shape[1]]
    sums = sums + adapted(params[6:9], outs[6:9], 10, taps)
    across = jnp.concatenate([mixer[:, :LANES], jnp.zeros((LANES - SPACED, LANES), f32)], 0).T
    ones = across[GAIN_LANE : GAIN_LANE + 1]
    twos = across[GAIN_LANE + 1 : GAIN_LANE + 2]
    few = lanes_of((1, LANES))
    line = jnp.where(few < SHARD, ones, 0.0) + pltpu.roll(
        jnp.broadcast_to(jnp.where(few < SHARD, twos, 0.0), (8, LANES)), SHARD, 1
    )[0:1]
    both = jnp.concatenate([sums, line], 1)
    sums_ref[...] = jnp.broadcast_to(both[None], sums_ref.shape)


def moments(mixer, place, tiles, ffn_sums, params):
    outs = [(param.shape, f32) for param in params] + [((LANES, 1, 2 * LANES), f32)]
    return whole_call(
        moments_kernel, outs, mixer, place, tiles, ffn_sums, *params
    )


def update_kernel(rank_ref, totals_ref, states_ref, *refs):
    weights, directions, outs = refs[:6], refs[6:12], refs[12:18]
    gains_refs, norms_ref = refs[18:21], refs[21]
    totals = totals_ref[:, 0, :]
    sums = jnp.sum(totals[:, :LANES], 0, keepdims=True)
    lane = lanes_of((1, LANES))
    grouped = jnp.where(
        lanes_of((32, LANES)) // 4 == rows_of((32, LANES)), 1.0, 0.0
    ).astype(bf16)
    grad = summed_down(grouped, totals[:, LANES:], NN)
    moment, square, direction = moved_moments(
        states_ref[0], states_ref[1], states_ref[2], grad
    )
    live = lanes_of((32, LANES)) < 2 * SHARD
    for place, value in ((12, states_ref[0]), (13, direction)):
        value = jnp.where(live, value, 0.0)
        value = jnp.sum(jnp.sum(value * value, 1, keepdims=True), 0, keepdims=True)
        sums = jnp.where(lane == place, value, sums)
    norms = jnp.sqrt(sums)
    norms_ref[...] = jnp.broadcast_to(norms, norms_ref.shape)

    def ratio(index):
        return norms[:, 2 * index : 2 * index + 1] / norms[:, 2 * index + 1 : 2 * index + 2]

    for index in range(6):
        outs[index][...] = (
            weights[index][...] - learn_rate * ratio(index) * directions[index][...]
        )
    updated = states_ref[0] - learn_rate * ratio(6) * direction
    for ref, value in zip(gains_refs, (updated, moment, square)):
        own = jnp.where(rows_of((32, LANES)) == rank_ref[0], value, 0.0)
        own = jnp.broadcast_to(jnp.sum(own, 0, keepdims=True), (8, LANES))
        ref[0:1, :] = own[0:1, :SHARD]
        ref[1:2, :] = pltpu.roll(own, LANES - SHARD, 1)[0:1, :SHARD]


def update(rank, totals, states, weights, directions):
    outs = [(w.shape, f32) for w in weights] + [((2, SHARD), f32)] * 3 + [((8, LANES), f32)]
    return whole_call(
        update_kernel, outs, rank, totals, states, *weights, *directions, scalars=1
    )


def per_device(
    tokens,
    cotangent,
    lengths,
    rate_codes,
    inproj,
    inproj_first,
    inproj_second,
    outproj,
    outproj_first,
    outproj_second,
    gateproj,
    gateproj_first,
    gateproj_second,
    upproj,
    upproj_first,
    upproj_second,
    downproj,
    downproj_first,
    downproj_second,
    convtaps,
    convtaps_first,
    convtaps_second,
    normgains,
    normgains_first,
    normgains_second,
):
    seqs, group, width = tokens.shape
    heads = rate_codes.shape[0]
    lag = TAPS - 1
    rank = lax.axis_index(SEQ).reshape(1)
    core = lax.axis_index("seq_2")
    peer = lax.axis_index("mp").reshape(1)
    pick, ends = selections()
    place, tiles = order_columns(heads), order_heads(heads)

    shards, out_shard, rest_shard = prepare(
        rank, inproj, outproj.T, gateproj, upproj, downproj.T, convtaps,
        normgains, normgains_first, normgains_second, place, tiles,
    )
    got = lax.all_to_all(shards, ("seq_0", "seq_1"), 0, 0, tiled=True)
    other = lax.ppermute(got, "seq_2", SWAP)
    turned = [out_shard] + [
        lax.ppermute(out_shard, "mp", [(i, (i - k) % 4) for i in range(4)]) for k in range(1, 4)
    ]
    out_shards = jnp.roll(jnp.stack(turned), peer[0], axis=0)
    weights_shard = jnp.concatenate([out_shards[g] for g in range(4)] + [rest_shard], 1)
    weights_shard, got = lax.optimization_barrier((weights_shard, got))
    weights = lax.all_gather(weights_shard, SEQ, axis=0, tiled=True)

    rows = tokens.reshape(-1, width)
    rim = shifted(tokens[:, group - lag :], SEQ, 1).reshape(-1, width)
    rim = jnp.pad(rim, ((0, 16 - seqs * lag), (0, 0)))
    positions = rank * group + jnp.arange(group, dtype=jnp.int32)
    keep = (positions[None, :] < lengths[:, None]).astype(f32).reshape(-1, 1)
    back = (cotangent.reshape(-1, width).astype(f32) * keep).astype(bf16)
    rates = -jnp.exp2(-rate_codes.astype(f32) / 4.0)
    rates = jnp.pad(rates[None], ((0, 0), (GATE_LANE, LANES - GATE_LANE - heads)))
    normed_one, proj, w_in, gains, taps, states, values, cum, sent = project(
        core.reshape(1), rows, rim, got, other, rates, pick, ends
    )
    earlier, decay = earlier_states(sent)
    inside = within(proj, values, cum)
    total, mixed = mix(proj, cum, inside, earlier, pick, ends)

    middle, unit_two, scale_two, normed_two, acts, two_part = middle_both_ways(
        peer, gather_parts(mixed), weights, rows, gains, back
    )
    two_back = lax.psum_scatter(two_part, "mp", scatter_dimension=0, tiled=True)
    ffn_part = ffn_out(peer, acts, weights)
    two_back, ffn_part = lax.optimization_barrier((two_back, ffn_part))
    ffn_sums = lax.psum_scatter(
        ffn_grads(normed_two, back, acts), SEQ, scatter_dimension=0, tiled=True
    )
    middle_back, gain_two, out_own, mixed_back = turn(
        peer, two_back, unit_two, scale_two, back, gains, weights
    )
    mixed_back = lax.all_to_all(mixed_back, "mp", 0, 0, tiled=True).reshape(ROWS, -1)

    total_back, sent = unmix(mixed_back, total, proj, cum, pick, ends)
    ffn_part, out_own, sent = lax.optimization_barrier((ffn_part, out_own, sent))
    later, summed = later_states(sent, decay)
    within_a = within_back(0, proj, values, cum, total_back, earlier, pick, ends)
    total_back, _ = lax.optimization_barrier((total_back, summed))
    within_b = within_back(1, proj, values, cum, total_back, earlier, pick, ends)
    out_parts = gather_parts(out_own)
    ffn_terms = scatter_terms(ffn_part)
    qk_back, values_back, gate_back = later_back(
        proj, values, cum, rates, earlier, later, pick, ends, within_a + within_b
    )
    edge = values_back.reshape(seqs, group, -1)[:, :lag]
    ahead = shifted(edge, SEQ, -1).reshape(seqs * lag, -1)
    ahead = jnp.concatenate([ahead, jnp.zeros_like(ahead)], 0)
    ahead, ffn_terms = lax.optimization_barrier((ahead, ffn_terms))
    one_part, kept, sent = unproject(
        jnp.concatenate([peer, core.reshape(1)]), proj, ahead, taps, qk_back, values_back, gate_back, normed_one, w_in, out_parts, mixed,
        gain_two,
    )

    swapped = lax.ppermute(sent, "seq_2", SWAP)
    mixer_part = (kept.astype(f32) + swapped.astype(f32)).astype(bf16)

    one_part, mixer_part = lax.optimization_barrier((one_part, mixer_part))
    mixer_got = lax.all_to_all(mixer_part, ("seq_0", "seq_1"), 0, 0, tiled=True)
    one_terms = scatter_terms(one_part)
    block_out = lax.all_gather(
        block_outs(peer, ffn_terms, middle, jnp.broadcast_to(keep, (ROWS, LANES))),
        "mp",
        axis=0,
        tiled=True,
    )

    mixer_params = (inproj, inproj_first, inproj_second)
    mixer_params += (outproj.T, outproj_first.T, outproj_second.T)
    mixer_params += (convtaps, convtaps_first, convtaps_second)
    ffn_params = (gateproj, gateproj_first, gateproj_second)
    ffn_params += (upproj, upproj_first, upproj_second)
    ffn_params += (downproj.T, downproj_first.T, downproj_second.T)
    *ffn_moved, ffn_squares = ffn_moments(ffn_sums, ffn_params)
    *moved, sums = moments(mixer_got, place, tiles, ffn_squares, mixer_params)
    moved = moved[:6] + ffn_moved + moved[6:]
    weights_old = mixer_params[0:6:3] + ffn_params[0::3] + mixer_params[6:7]
    token_grad = gather_rows(
        peer, token_grads(peer, one_terms, rows, middle_back, gains), sums
    )
    totals = lax.all_to_all(sums, ALL, 0, 0, tiled=True)
    *updated, gains_new, gains_moment, gains_square, norms = update(
        rank, totals, states, weights_old, moved[2::3]
    )
    results = [block_out.reshape(tokens.shape), token_grad.reshape(tokens.shape)]
    for index in range(6):
        for value in (updated[index], moved[3 * index], moved[3 * index + 1]):
            results.append(value.T if index in (1, 4) else value)
    results += [gains_new, gains_moment, gains_square, norms[0, :14].reshape(7, 2)]
    return tuple(results)


def solution(mesh):
    split = Mesh(mesh.devices.reshape(4, 4, 2, mesh.shape["mp"]), ("seq_0", "seq_1", "seq_2", "mp"))
    in_specs = (
        P(None, SEQ, None),
        P(None, SEQ, None),
        P(),
        P("mp"),
        P(SEQ, "mp"),
        P(SEQ, "mp"),
        P(SEQ, "mp"),
        P("mp", SEQ),
        P("mp", SEQ),
        P("mp", SEQ),
        P(SEQ, "mp"),
        P(SEQ, "mp"),
        P(SEQ, "mp"),
        P(SEQ, "mp"),
        P(SEQ, "mp"),
        P(SEQ, "mp"),
        P("mp", SEQ),
        P("mp", SEQ),
        P("mp", SEQ),
        P(None, MP_SEQ),
        P(None, MP_SEQ),
        P(None, MP_SEQ),
        P(None, SEQ),
        P(None, SEQ),
        P(None, SEQ),
    )
    out_specs = (
        P(None, SEQ, None),
        P(None, SEQ, None),
        P(SEQ, "mp"),
        P(SEQ, "mp"),
        P(SEQ, "mp"),
        P("mp", SEQ),
        P("mp", SEQ),
        P("mp", SEQ),
        P(SEQ, "mp"),
        P(SEQ, "mp"),
        P(SEQ, "mp"),
        P(SEQ, "mp"),
        P(SEQ, "mp"),
        P(SEQ, "mp"),
        P("mp", SEQ),
        P("mp", SEQ),
        P("mp", SEQ),
        P(None, MP_SEQ),
        P(None, MP_SEQ),
        P(None, MP_SEQ),
        P(None, SEQ),
        P(None, SEQ),
        P(None, SEQ),
        P(),
    )
    return jax.shard_map(
        per_device, mesh=split, in_specs=in_specs, out_specs=out_specs, check_vma=False
    )
```

```python
import math

import jax
import jax.numpy as jnp
from jax import lax
from jax.experimental import pallas as pl
from jax.experimental.pallas import tpu as pltpu
from jax.sharding import Mesh
from jax.sharding import PartitionSpec as P

DH = 112
FEAT = 16
TAPS = 3
STEP = 7
LANES = 128
SEQ = ("seq_0", "seq_1", "seq_2")
ALL = ("seq_0", "seq_1", "seq_2", "mp")
MP_SEQ = ("mp", "seq_0", "seq_1", "seq_2")

f32 = jnp.float32
bf16 = jnp.bfloat16
highest = lax.Precision.HIGHEST
root_half = 0.5**0.5
eps_norm = 1e-05
eps_adam = 1e-06
decay_rate = 0.01
learn_rate = 0.3
beta_value = 0.5

SIDE = [(i, i ^ 1) for i in range(4)]
BACK = [(i, 3 - i) for i in range(4)]
SWAP = [(0, 1), (1, 0)]


def shifted(value, axis, steps):
    count = lax.axis_size(axis)
    first, last = (max(0, -steps), min(count, count - steps))
    return lax.ppermute(value, axis, [(source, source + steps) for source in range(first, last)])


SPAN_LANE = DH
GROUPS = 4
GATE_LANE = DH
GAIN_LANE = DH + 4
TAPS_LANE = DH + 6
GROUP = 256
ROWS = 512
SIDES = 256
PIECE = 40
SLOT = 48
PIECES = 32
MIB = 1 << 20


def selections():
    import numpy as np

    pick = np.zeros((2 * LANES, 2 * SIDES), np.float32)
    ends = np.zeros((8, SIDES), np.float32)
    ends[0, 0] = ends[1, 0] = ends[2, 0] = 1.0
    lane = 1
    for i in range(FEAT):
        pick[i, lane] = 0.5
        ends[1, lane] = ends[2, lane] = 1.0
        lane += 1
    for i in range(FEAT):
        for j in range(i, FEAT):
            pick[i, lane] = 0.5
            pick[j, SIDES + lane] = 0.5
            ends[2, lane] = root_half if i == j else 1.0
            lane += 1
    pick[LANES:] = pick[:LANES]
    return jnp.asarray(pick, bf16), jnp.asarray(ends)


def two_parts(value):
    high = value.astype(bf16)
    return high, (value - high.astype(f32)).astype(bf16)


def three_parts(value):
    high = value.astype(bf16)
    rest = value - high.astype(f32)
    mid = rest.astype(bf16)
    return high, mid, (rest - mid.astype(f32)).astype(bf16)


def product(a, b, contract, passes=3):
    dims = (contract, ((), ()))

    def once(x, y):
        return lax.dot_general(x, y, dims, preferred_element_type=f32)

    if passes == 1:
        return once(a.astype(bf16), b.astype(bf16))
    a_high, a_low = two_parts(a)
    if passes == 2:
        b = b.astype(bf16)
        return once(a_high, b) + once(a_low, b)
    b_high, b_low = two_parts(b)
    return once(a_high, b_high) + (once(a_high, b_low) + once(a_low, b_high))


NN = ((1,), (0,))
NT = ((1,), (1,))
TN = ((0,), (0,))


def lanes_of(shape):
    return lax.broadcasted_iota(jnp.int32, shape, len(shape) - 1)


def rows_of(shape):
    return lax.broadcasted_iota(jnp.int32, shape, 0)


def lower_ones(strict=False):
    row, lane = rows_of((GROUP, GROUP)), lanes_of((GROUP, GROUP))
    return jnp.where(row > lane if strict else row >= lane, 1.0, 0.0).astype(bf16)


def summed_down(ones, value, contract):
    high, mid, low = (
        lax.dot_general(ones, part, (contract, ((), ())), preferred_element_type=f32)
        for part in three_parts(value)
    )
    return low + mid + high


def picked(value, place, contract):
    high, mid, low = (
        lax.dot_general(part, place, (contract, ((), ())), preferred_element_type=f32)
        for part in three_parts(value)
    )
    return low + mid + high


def head_lanes(tile, head, keys):
    first = (4 if keys else 0) * FEAT + head * FEAT
    return pltpu.roll(tile, (LANES - first) % LANES, 1) if first else tile


def factors(moved, pick, ends):
    high, low = two_parts(moved)
    found = lax.dot_general(
        jnp.concatenate([high, low], 1), pick, (NN, ((), ())), preferred_element_type=f32
    )
    return found[:, :SIDES] + ends[0:1], found[:, SIDES:] + ends[1:2]


def factors_back(upstream, one, two, pick, ends):
    scaled = upstream * ends[2:3]
    both = jnp.concatenate([scaled * two, scaled * one], 1)
    return product(both, pick[:LANES], NT, 2)


def scores(tile, head):
    only = lanes_of((GROUP, LANES)) < FEAT
    query = jnp.where(only, head_lanes(tile, head, False), 0.0) * 0.25
    keys = jnp.where(only, head_lanes(tile, head, True), 0.0)
    q_high, k_high = query.astype(bf16), keys.astype(bf16)
    q_wide, k_wide = q_high.astype(f32), k_high.astype(f32)
    q_both = (q_wide + pltpu.roll(query - q_wide, FEAT, 1)).astype(bf16)
    k_both = (pltpu.roll(k_wide, FEAT, 1) + (keys - k_wide)).astype(bf16)
    left = jnp.concatenate([q_high, q_both], 1)
    right = jnp.concatenate([k_high, k_both], 1)
    return lax.dot_general(left, right, (NT, ((), ())), preferred_element_type=f32)


def decays(cum, cum_across, head):
    row, lane = rows_of((GROUP, GROUP)), lanes_of((GROUP, GROUP))
    at = GATE_LANE + head
    diff = cum[:, at : at + 1] - cum_across[at : at + 1, :]
    return jnp.where(row >= lane, jnp.exp(jnp.minimum(diff, 0.0)), 0.0)


def head_column(tile, head):
    at = GATE_LANE + head
    return tile[:, at : at + 1]


def on_head_lane(column, head):
    return jnp.where(lanes_of((column.shape[0], LANES)) == GATE_LANE + head, column, 0.0)


def state_rows(pieces_ref, pair):
    parts = [pieces_ref[4 * pair + q, :PIECE, :].astype(f32) for q in range(4)]
    parts.append(jnp.zeros((SIDES - 4 * PIECE, LANES), f32))
    return jnp.concatenate(parts, 0).astype(bf16)


def store_pieces(ref, pair, state):
    for q in range(4):
        ref[4 * pair + q, :PIECE, :] = state[q * PIECE : (q + 1) * PIECE].astype(bf16)


def whole_call(body, outs, *args, scratch=(), flops=10**9, limit=60, views=None, scalars=0):
    views = views or {}
    shapes = [views.get(i, (a.shape,))[0] for i, a in enumerate(args)]

    def whole(shape, place=None):
        return pl.BlockSpec(shape, lambda i: place or (0,) * len(shape))

    count = sum(math.prod(s) * a.dtype.itemsize for s, a in zip(shapes, args))
    count += sum(math.prod(s) * jnp.dtype(d).itemsize for s, d in outs)
    return pl.pallas_call(
        body,
        grid=(1,),
        out_shape=[jax.ShapeDtypeStruct(s, d) for s, d in outs],
        in_specs=[pl.BlockSpec(memory_space=pltpu.SMEM)] * scalars
        + [whole(s, views.get(i, (s, None))[1]) for i, s in enumerate(shapes) if i >= scalars],
        out_specs=[whole(s) for s, d in outs],
        scratch_shapes=list(scratch),
        compiler_params=pltpu.CompilerParams(vmem_limit_bytes=limit * MIB),
        cost_estimate=pl.CostEstimate(flops=flops, bytes_accessed=count, transcendentals=0),
    )(*args)


def sequence_call(body, outs, *args, halves, flops=10**9):
    def half(shape, columns=None, place=0):
        block = (shape[0] // 2,) + tuple(shape[1:-1]) + (columns or shape[-1],)
        rest = (0,) * (len(shape) - 2) + (place,)
        return pl.BlockSpec(block, lambda i: (i,) + rest)

    def whole(shape):
        return pl.BlockSpec(shape, lambda i: (0,) * len(shape))

    specs = [
        half((ROWS,) + a.shape[1:] if a.ndim == 2 else a.shape, *halves[i])
        if i in halves
        else whole(a.shape)
        for i, a in enumerate(args)
    ]
    return pl.pallas_call(
        body,
        grid=(2,),
        out_shape=[jax.ShapeDtypeStruct(s, d) for s, d in outs],
        in_specs=specs,
        out_specs=[half(s) for s, d in outs],
        compiler_params=pltpu.CompilerParams(vmem_limit_bytes=60 * MIB),
        cost_estimate=pl.CostEstimate(flops=flops, bytes_accessed=4 * 10**6, transcendentals=0),
    )(*args)


def project_kernel(
    core_ref, rows_ref, rim_ref, got_ref, other_ref, rates_ref, pick_ref, ends_ref,
    normed_ref, proj_ref, w_ref, gains_ref, taps_ref, states_ref, values_ref, cum_ref, sent_ref,
    wide_ref,
):
    wide = w_ref.shape[1]
    flipped = core_ref[0] == 1
    taps = jnp.zeros((8, 4 * LANES), f32)
    for r in range(2 * got_ref.shape[0]):
        mine, theirs = got_ref[r // 2].astype(f32), other_ref[r // 2].astype(f32)
        part = jnp.where(flipped, theirs, mine) if r % 2 == 0 else jnp.where(flipped, mine, theirs)
        wide_ref[r * SHARD : (r + 1) * SHARD, :] = part[:SHARD]
        rest = part[SHARD:]
        taps = taps + rest[:, : 4 * LANES]
        whole = rest[:, :LANES] + rest[:, LANES : 2 * LANES] + rest[:, 2 * LANES : 3 * LANES]
        for k in range(3):
            states_ref[k, r : r + 1, :] = whole[TAPS + k : TAPS + k + 1]
    taps_ref[...] = taps
    w_ref[...] = wide_ref[...].astype(bf16)
    chosen = jnp.where(
        lanes_of((16, wide)) == rows_of((16, wide)) + GAIN_LANE, 1.0, 0.0
    )
    chosen = jnp.where(rows_of((16, wide)) < 2, chosen, 0.0).astype(bf16)
    gains = lax.dot_general(chosen, w_ref[...], (NT, ((), ())), preferred_element_type=f32)
    gains_ref[...] = gains[:8]
    gain = gains[0:1]

    def projected(rows):
        rows = rows.astype(f32)
        scale = lax.rsqrt(jnp.mean(rows * rows, -1, keepdims=True) + eps_norm)
        normed = (rows * scale * gain).astype(bf16)
        return normed, jnp.dot(normed, w_ref[...], preferred_element_type=f32)

    for at in range(0, ROWS, GROUP):
        normed, proj = projected(rows_ref[at : at + GROUP, :])
        normed_ref[at : at + GROUP, :] = normed
        proj_ref[at : at + GROUP, :] = proj
    proj_ref[ROWS:, :] = projected(rim_ref[...])[1]
    ones = lower_ones()
    pick, ends = pick_ref[...], ends_ref[...]
    lane, row = lanes_of((GROUP, LANES)), rows_of((GROUP, LANES))
    for s in range(2):
        here = slice(s * GROUP, (s + 1) * GROUP)
        steps = rates_ref[...] * jax.nn.softplus(proj_ref[here, :LANES])
        cum = summed_down(ones, steps, NN)
        cum_ref[here, :] = cum
        last = cum[GROUP - 1 : GROUP, :]
        tail = jnp.exp(last - cum)
        qk = proj_ref[here, 4 * LANES :]
        for h in range(4):
            tile = slice(h * LANES, (h + 1) * LANES)
            raw = proj_ref[here, tile]
            rim_two = proj_ref[ROWS + 2 * s : ROWS + 2 * s + 1, tile]
            rim_one = proj_ref[ROWS + 2 * s + 1 : ROWS + 2 * s + 2, tile]
            one = jnp.where(row == 0, rim_one, pltpu.roll(raw, 1, 0))
            two = jnp.where(row == 0, rim_two, jnp.where(row == 1, rim_one, pltpu.roll(raw, 2, 0)))
            conv = (
                taps_ref[0:1, tile] * raw + taps_ref[1:2, tile] * one + taps_ref[2:3, tile] * two
            )
            values = jnp.where(lane < DH, conv, jnp.where(lane == DH, 1.0, 0.0))
            values_ref[here, tile] = values
            left, right = factors(head_lanes(qk, h, True), pick, ends)
            held = left * right * ends[2:3] * head_column(tail, h)
            fresh = product(held, values, TN)
            store_pieces(sent_ref, 4 * s + h, fresh)
            ending = jnp.broadcast_to(head_column(last, h), (8, LANES))
            high, mid, low = three_parts(ending)
            few = lanes_of((8, LANES))
            packed = jnp.where(
                few == 0,
                high.astype(f32),
                jnp.where(few == 1, mid.astype(f32), jnp.where(few == 2, low.astype(f32), 0.0)),
            ).astype(bf16)
            for q in range(4):
                sent_ref[16 * s + 4 * h + q, PIECE:, :] = packed


def project(core, rows, rim, got, other, rates, pick, ends):
    wide, width = got.shape[2], rows.shape[1]
    return whole_call(
        project_kernel,
        [
            (rows.shape, bf16),
            ((ROWS + rim.shape[0], wide), f32),
            ((width, wide), bf16),
            ((8, width), f32),
            ((8, 4 * LANES), f32),
            ((3, 2 * got.shape[0], LANES), f32),
            ((ROWS, 4 * LANES), f32),
            ((ROWS, LANES), f32),
            ((PIECES, SLOT, LANES), bf16),
        ],
        core, rows, rim, got, other, rates, pick, ends,
        scratch=[pltpu.VMEM((width, wide), f32)],
        flops=3 * 10**9,
        scalars=1,
    )


def scan_kernel(got_ref, back_ref, decay_ref):
    state = jnp.zeros((PIECE, LANES), f32)
    for i in range(PIECES):
        back_ref[i, :PIECE, :] = state.astype(bf16)
        back_ref[i, PIECE:, :] = jnp.zeros((SLOT - PIECE, LANES), bf16)
        ending = jnp.sum(got_ref[i, PIECE:, :].astype(f32), -1, keepdims=True)
        decay = jnp.broadcast_to(jnp.exp(ending), (8, LANES))
        decay_ref[i] = decay
        state = state * decay[0:1] + got_ref[i, :PIECE, :].astype(f32)


def earlier_states(sent):
    got = lax.all_to_all(sent, SEQ, 0, 0, tiled=True)
    back, decay = whole_call(
        scan_kernel, [(sent.shape, bf16), ((PIECES, 8, LANES), f32)], got, flops=10**6
    )
    return lax.all_to_all(back, SEQ, 0, 0, tiled=True), decay


def scan_back_kernel(got_ref, decay_ref, back_ref):
    state = jnp.zeros((PIECE, LANES), f32)
    for i in reversed(range(PIECES)):
        back_ref[i, :PIECE, :] = state.astype(bf16)
        back_ref[i, PIECE:, :] = jnp.zeros((SLOT - PIECE, LANES), bf16)
        state = state * decay_ref[i, 0:1, :] + got_ref[i, :PIECE, :].astype(f32)


def later_states(sent, decay):
    got = lax.all_to_all(sent, SEQ, 0, 0, tiled=True)
    (back,) = whole_call(scan_back_kernel, [(sent.shape, bf16)], got, decay, flops=10**6)
    return lax.all_to_all(back, SEQ, 0, 0, tiled=True), back


QK = ((ROWS, LANES), (0, 4))
FIRST = ((ROWS, LANES), (0, 0))


def within_kernel(qk_ref, values_ref, cum_ref, inside_ref):
    for s in range(2):
        here = slice(s * GROUP, (s + 1) * GROUP)
        cum = cum_ref[here, :]
        across = cum.T
        qk = qk_ref[here, :]
        for h in range(4):
            tile = slice(h * LANES, (h + 1) * LANES)
            dots = scores(qk, h)
            weights = (1.0 + dots + 0.5 * dots * dots) * decays(cum, across, h)
            inside_ref[here, tile] = product(weights, values_ref[here, tile], NN)


def within(proj, values, cum):
    return whole_call(
        within_kernel,
        [((ROWS, 4 * LANES), f32)],
        proj, values, cum,
        flops=3 * 10**9,
        views={0: QK},
    )[0]


def mix_kernel(
    qk_ref, cum_ref, inside_ref, earlier_ref, pick_ref, ends_ref, total_ref, mixed_ref
):
    pick, ends = pick_ref[...], ends_ref[...]
    lane = lanes_of((GROUP, LANES))
    growth = jnp.exp(cum_ref[:, :])
    qk = qk_ref[:, :]
    for h in range(4):
        tile = slice(h * LANES, (h + 1) * LANES)
        left, right = factors(head_lanes(qk, h, False), pick, ends)
        held = left * right * ends[2:3] * head_column(growth, h)
        total = inside_ref[:, tile] + product(held, state_rows(earlier_ref, h), NN, 2)
        total_ref[:, tile] = total
        mixed = total / total[:, DH : DH + 1]
        mixed_ref[:, tile] = jnp.where(lane < DH, mixed, 0.0).astype(bf16)


def mix(proj, cum, inside, earlier, pick, ends):
    return sequence_call(
        mix_kernel,
        [((ROWS, 4 * LANES), f32), ((ROWS, 4 * LANES), bf16)],
        proj, cum, inside, earlier, pick, ends,
        halves={0: (LANES, 4), 1: (), 2: (), 3: ()},
        flops=3 * 10**9,
    )


OWN = ROWS // 4


def own_slice(ref, place):
    return ref[pl.ds(pl.multiple_of(place * OWN, OWN), OWN), :]


def turn_kernel(
    place_ref, got_ref, unit_ref, scale_ref, back_ref, gains_ref, w_ref,
    middle_back_ref, gain_ref, out_back_ref, mixed_back_ref,
):
    two_back = got_ref[...].astype(f32)
    unit = unit_ref[...]
    gain_ref[...] = jnp.broadcast_to(
        jnp.sum(two_back * unit, 0, keepdims=True), gain_ref.shape
    )
    weighted = two_back * gains_ref[1:2]
    along = jnp.mean(weighted * unit, -1, keepdims=True)
    middle_back = own_slice(back_ref, place_ref[0]).astype(f32) + scale_ref[:, 0:1] * (
        weighted - unit * along
    )
    middle_back_ref[...] = middle_back
    out_back = middle_back.astype(bf16)
    out_back_ref[...] = out_back
    for g in range(4):
        mixed_back_ref[g] = jnp.dot(
            out_back, w_ref[:, g * 4 * LANES : (g + 1) * 4 * LANES], preferred_element_type=f32
        ).astype(bf16)


def turn(place, got, unit, scale, back, gains, w_out):
    width = back.shape[1]
    return whole_call(
        turn_kernel,
        [
            ((OWN, width), f32),
            ((8, width), f32),
            ((OWN, width), bf16),
            ((4, OWN, 4 * LANES), bf16),
        ],
        place, got, unit, scale, back, gains, w_out,
        flops=10**9,
        scalars=1,
        views={6: ((width, OUT), (0, 0))},
    )


def token_kernel(place_ref, *refs):
    terms, (rows_ref, middle_back_ref, gains_ref, out_ref) = refs[:3], refs[3:]
    one_back = sum(ref[...].astype(f32) for ref in terms)
    rows = own_slice(rows_ref, place_ref[0]).astype(f32)
    scale = lax.rsqrt(jnp.mean(rows * rows, -1, keepdims=True) + eps_norm)
    unit = rows * scale
    weighted = one_back * gains_ref[0:1]
    along = jnp.mean(weighted * unit, -1, keepdims=True)
    token_back = middle_back_ref[...] + scale * (weighted - unit * along)
    out_ref[...] = token_back.astype(bf16)


def token_grads(place, terms, rows, middle_back, gains):
    return whole_call(
        token_kernel, [(terms[0].shape, bf16)], place, *terms, rows, middle_back, gains,
        flops=10**7,
        scalars=1,
    )[0]


def block_kernel(place_ref, *refs):
    terms, (middle_ref, keep_ref, out_ref) = refs[:3], refs[3:]
    ffn = sum(ref[...].astype(f32) for ref in terms)
    keep = own_slice(keep_ref, place_ref[0])[:, 0:1]
    out_ref[...] = ((middle_ref[...] + ffn) * keep).astype(bf16)


def block_outs(place, terms, middle, keep):
    return whole_call(
        block_kernel, [(terms[0].shape, bf16)], place, *terms, middle, keep,
        flops=10**7,
        scalars=1,
    )[0]


def assemble_kernel(place_ref, own_ref, side_ref, back_ref, far_a_ref, far_b_ref, out_ref):
    place = place_ref[0]
    half = OWN // 2

    def at(other):
        return pl.multiple_of(jnp.bitwise_xor(place, other) * OWN, OWN)

    out_ref[pl.ds(at(0), OWN), :] = own_ref[...]
    out_ref[pl.ds(at(1), OWN), :] = side_ref[...]
    out_ref[pl.ds(at(3), OWN), :] = back_ref[...]
    out_ref[pl.ds(at(2), half), :] = far_a_ref[...]
    out_ref[pl.ds(pl.multiple_of(at(2) + half, half), half), :] = far_b_ref[...]


def to_neighbours(own):
    return lax.ppermute(own, "mp", BACK), lax.ppermute(own, "mp", SIDE)


def passed_on(back, side):
    half = back.shape[0] // 2
    return lax.ppermute(back[:half], "mp", SIDE), lax.ppermute(side[half:], "mp", BACK)


def gather_parts(own):
    back, side = to_neighbours(own)
    return own, side, back, *passed_on(back, side)


def assembled(place, parts):
    own = parts[0]
    return whole_call(
        assemble_kernel, [((ROWS, own.shape[1]), own.dtype)], place, *parts,
        flops=10**6,
        scalars=1,
    )[0]


def scatter_terms(part):
    half = OWN // 2
    got_a = lax.ppermute(part[2, :half], "mp", SIDE)
    got_b = lax.ppermute(part[2, half:], "mp", BACK)
    to_back = jnp.concatenate(
        [(part[3, :half].astype(f32) + got_a.astype(f32)).astype(bf16), part[3, half:]], 0
    )
    to_side = jnp.concatenate(
        [part[1, :half], (part[1, half:].astype(f32) + got_b.astype(f32)).astype(bf16)], 0
    )
    return part[0], lax.ppermute(to_back, "mp", BACK), lax.ppermute(to_side, "mp", SIDE)


def store_by_owner(ref, value, place, columns=slice(None)):
    for g in range(4):
        ref[jnp.bitwise_xor(place, g), :, columns] = value[g * OWN : (g + 1) * OWN]


def unmix_kernel(
    mixed_back_ref, total_ref, qk_ref, cum_ref, pick_ref, ends_ref, total_back_ref, sent_ref
):
    pick, ends = pick_ref[...], ends_ref[...]
    lane = lanes_of((GROUP, LANES))
    growth = jnp.exp(cum_ref[:, :])
    qk = qk_ref[:, :]
    for h in range(4):
        tile = slice(h * LANES, (h + 1) * LANES)
        total = total_ref[:, tile]
        inverse = 1.0 / total[:, DH : DH + 1]
        numer = mixed_back_ref[:, tile].astype(f32) * inverse
        numer = jnp.where(lane < DH, numer, 0.0)
        denom = -jnp.sum(numer * total, -1, keepdims=True) * inverse
        total_back = jnp.where(lane == DH, denom, numer)
        total_back_ref[:, tile] = total_back
        left, right = factors(head_lanes(qk, h, False), pick, ends)
        held = left * right * ends[2:3] * head_column(growth, h)
        store_pieces(sent_ref, h, product(held, total_back, TN))
        for q in range(4):
            sent_ref[4 * h + q, PIECE:, :] = jnp.zeros((SLOT - PIECE, LANES), bf16)


def unmix(mixed_back, total, proj, cum, pick, ends):
    return sequence_call(
        unmix_kernel,
        [((ROWS, 4 * LANES), f32), ((PIECES, SLOT, LANES), bf16)],
        mixed_back, total, proj, cum, pick, ends,
        halves={0: (), 1: (), 2: (LANES, 4), 3: ()},
        flops=3 * 10**9,
    )


def within_back_kernel(
    qk_ref, values_ref, cum_ref, total_back_ref, earlier_ref, pick_ref, ends_ref,
    qk_back_ref, values_back_ref, level_ref,
):
    pick, ends = pick_ref[...], ends_ref[...]
    only = lanes_of((GROUP, LANES)) < FEAT
    cum = cum_ref[:, :]
    across = cum.T
    growth = jnp.exp(cum)
    qk = qk_ref[:, :]
    qk_back = jnp.zeros((GROUP, LANES), f32)
    level = jnp.zeros((GROUP, LANES), f32)
    level_down = jnp.zeros((LANES, GROUP), f32)
    for h in range(4):
        tile = slice(h * LANES, (h + 1) * LANES)
        total_back = total_back_ref[:, tile]
        decay = decays(cum, across, h)
        dots = scores(qk, h)
        pairing = decay * product(total_back, values_ref[:, tile], NT)
        kernel = 1.0 + dots + 0.5 * dots * dots
        moved = kernel * pairing
        down = jnp.sum(moved, 0, keepdims=True)
        level_down = jnp.where(rows_of((LANES, GROUP)) == GATE_LANE + h, down, level_down)
        kernel_back = pairing * (1.0 + dots) * 0.25
        values_back_ref[:, tile] = product(kernel * decay, total_back, TN)
        query_tile = head_lanes(qk, h, False)
        keys_only = jnp.where(only, head_lanes(qk, h, True), 0.0)
        query_only = jnp.where(only, query_tile, 0.0)
        query_back = product(kernel_back, keys_only, NN)
        keys_back = product(kernel_back, query_only, TN)
        left, right = factors(query_tile, pick, ends)
        features_back = head_column(growth, h) * product(
            total_back, state_rows(earlier_ref, h), NT, 2
        )
        level_here = jnp.sum(moved, 1, keepdims=True) + jnp.sum(
            left * right * ends[2:3] * features_back, 1, keepdims=True
        )
        level = level + on_head_lane(level_here, h)
        query_back = query_back + factors_back(features_back, left, right, pick, ends)
        at = h * FEAT
        qk_back = qk_back + (pltpu.roll(query_back, at, 1) if at else query_back)
        qk_back = qk_back + pltpu.roll(keys_back, at + 4 * FEAT, 1)
    qk_back_ref[:, :] = qk_back
    level_ref[:, :] = level - level_down.T


def within_back(s, proj, values, cum, total_back, earlier, pick, ends):
    return whole_call(
        within_back_kernel,
        [((GROUP, LANES), f32), ((GROUP, 4 * LANES), f32), ((GROUP, LANES), f32)],
        proj, values, cum, total_back, earlier, pick, ends,
        flops=4 * 10**9,
        views={
            0: ((GROUP, LANES), (s, 4)),
            1: ((GROUP, 4 * LANES), (s, 0)),
            2: ((GROUP, LANES), (s, 0)),
            3: ((GROUP, 4 * LANES), (s, 0)),
            4: ((PIECES // 2, SLOT, LANES), (s, 0, 0)),
        },
    )


def later_back_kernel(
    qk_ref, first_ref, values_ref, cum_ref, rates_ref, earlier_ref, later_ref, pick_ref, ends_ref,
    qk_in_a_ref, values_in_a_ref, level_a_ref, qk_in_b_ref, values_in_b_ref, level_b_ref,
    qk_back_ref, values_back_ref, gate_back_ref,
):
    pick, ends = pick_ref[...], ends_ref[...]
    ones, before = lower_ones(), lower_ones(True)
    cum = cum_ref[:, :]
    last = cum[GROUP - 1 : GROUP, :]
    tail = jnp.exp(last - cum)
    carried = jnp.exp(last)
    qk = qk_ref[:, :]
    second = pl.program_id(0) == 1

    def either(one_ref, two_ref, columns=slice(None)):
        return jnp.where(second, two_ref[:, columns], one_ref[:, columns])

    qk_back = either(qk_in_a_ref, qk_in_b_ref)
    crossed = jnp.zeros((GROUP, LANES), f32)
    through = jnp.zeros((1, LANES), f32)
    for h in range(4):
        tile = slice(h * LANES, (h + 1) * LANES)
        later = state_rows(later_ref, h)
        left, right = factors(head_lanes(qk, h, True), pick, ends)
        held = left * right * ends[2:3]
        column = head_column(tail, h)
        features_back = column * product(values_ref[:, tile], later, NT, 2)
        values_back_ref[:, tile] = either(values_in_a_ref, values_in_b_ref, tile) + column * product(
            held, later, NN, 2
        )
        crossed = crossed + on_head_lane(
            jnp.sum(held * features_back, 1, keepdims=True), h
        )
        keys_back = factors_back(features_back, left, right, pick, ends)
        qk_back = qk_back + pltpu.roll(keys_back, (h + 4) * FEAT, 1)
        whole = jnp.sum(
            later.astype(f32) * state_rows(earlier_ref, h).astype(f32), 1, keepdims=True
        )
        whole = jnp.sum(whole, 0, keepdims=True) * head_column(carried, h)
        through = through + on_head_lane(whole, h)
    qk_back_ref[:, :] = qk_back
    step_back = (
        summed_down(ones, either(level_a_ref, level_b_ref), TN) + summed_down(before, crossed, NN) + through
    )
    gate_back_ref[:, :] = (
        step_back * rates_ref[...] * jax.nn.sigmoid(first_ref[:, :])
    )


def later_back(proj, values, cum, rates, earlier, later, pick, ends, within):
    return sequence_call(
        later_back_kernel,
        [((ROWS, LANES), f32), ((ROWS, 4 * LANES), f32), ((ROWS, LANES), f32)],
        proj, proj, values, cum, rates, earlier, later, pick, ends, *within,
        halves={0: (LANES, 4), 1: (LANES, 0), 2: (), 3: (), 5: (), 6: ()},
        flops=4 * 10**9,
    )


def unproject_kernel(
    place_ref, proj_ref, ahead_ref, taps_ref, qk_back_ref, values_back_ref, gate_back_ref, normed_ref, w_ref,
    own_ref, side_ref, back_ref, far_a_ref, far_b_ref, mixed_ref, gain_two_ref,
    part_ref, kept_ref, sent_ref,
    taps_grad_ref, taps_across_ref, proj_back_ref, out_back_ref, turned_ref,
):
    @pl.when(pl.program_id(0) == 0)
    def _():
        lane, row = lanes_of((GROUP, LANES)), rows_of((GROUP, LANES))
        taps_grad_ref[...] = jnp.zeros_like(taps_grad_ref)
        for s in range(2):
            here = slice(s * GROUP, (s + 1) * GROUP)
            for h in range(4):
                tile = slice(h * LANES, (h + 1) * LANES)
                raw = proj_ref[here, tile]
                back = values_back_ref[here, tile]
                back = jnp.where(lane < DH, back, 0.0)
                rim_two = proj_ref[ROWS + 2 * s : ROWS + 2 * s + 1, tile]
                rim_one = proj_ref[ROWS + 2 * s + 1 : ROWS + 2 * s + 2, tile]
                one = jnp.where(row == 0, rim_one, pltpu.roll(raw, 1, 0))
                two = jnp.where(row == 0, rim_two, jnp.where(row == 1, rim_one, pltpu.roll(raw, 2, 0)))
                for j, moved in enumerate((raw, one, two)):
                    taps_grad_ref[j : j + 1, tile] = taps_grad_ref[j : j + 1, tile] + jnp.sum(
                        moved * back, 0, keepdims=True
                    )
                next_one = ahead_ref[2 * s : 2 * s + 1, tile]
                next_two = ahead_ref[2 * s + 1 : 2 * s + 2, tile]
                one = jnp.where(row == GROUP - 1, next_one, pltpu.roll(back, GROUP - 1, 0))
                two = jnp.where(
                    row == GROUP - 1,
                    next_two,
                    jnp.where(row == GROUP - 2, next_one, pltpu.roll(back, GROUP - 2, 0)),
                )
                raw_back = (
                    taps_ref[0:1, tile] * back + taps_ref[1:2, tile] * one + taps_ref[2:3, tile] * two
                )
                raw_back = jnp.where(lane < DH, raw_back, 0.0)
                if h == 0:
                    gates = (lane >= GATE_LANE) & (lane < GATE_LANE + 4)
                    raw_back = jnp.where(gates, gate_back_ref[here, :], raw_back)
                proj_back_ref[here, tile] = raw_back.astype(bf16)
            proj_back_ref[here, 4 * LANES :] = qk_back_ref[here, :].astype(bf16)
        for h in range(GROUPS):
            tile = slice(h * LANES, (h + 1) * LANES)
            taps_across_ref[tile, :] = pltpu.roll(
                jnp.concatenate(
                    [taps_grad_ref[:, tile], jnp.zeros((LANES - 8, LANES), f32)], 0
                ).T,
                TAPS_LANE,
                1,
            )
        for k, other in enumerate((0, 1, 3, 2)):
            turned_ref[k * OWN : (k + 1) * OWN] = own_slice(
                mixed_ref, jnp.bitwise_xor(place_ref[0], other)
            )

    part = lax.dot_general(
        proj_back_ref[...], w_ref[...], (NT, ((), ())), preferred_element_type=f32
    ).astype(bf16)
    store_by_owner(part_ref, part, place_ref[0])
    wide = w_ref.shape[1]
    grad_in = lax.dot_general(
        normed_ref[...], proj_back_ref[...], (TN, ((), ())), preferred_element_type=f32
    )
    weights = w_ref[...].astype(f32)
    gain_one = jnp.sum(grad_in * weights, 1, keepdims=True)
    gain_one = gain_one / weights[:, GAIN_LANE : GAIN_LANE + 1]
    gain_two = gain_two_ref[...].T[:, 0:1]
    first = grad_in[:, :LANES]
    spot = lanes_of(first.shape)
    first = jnp.where(
        spot == GAIN_LANE, gain_one, jnp.where(spot == GAIN_LANE + 1, gain_two, first)
    )
    out_back_ref[:OWN] = own_ref[...]
    out_back_ref[OWN : 2 * OWN] = side_ref[...]
    out_back_ref[2 * OWN : 3 * OWN] = back_ref[...]
    out_back_ref[3 * OWN : 3 * OWN + OWN // 2] = far_a_ref[...]
    out_back_ref[3 * OWN + OWN // 2 :] = far_b_ref[...]
    grad_out = lax.dot_general(
        out_back_ref[...], turned_ref[...], (TN, ((), ())), preferred_element_type=f32
    )
    core = place_ref[1]

    each = DH // 8
    few = lanes_of((SHARD, LANES))
    spare = (few >= TAPS_LANE) & (few < TAPS_LANE + TAPS) & (rows_of((SHARD, LANES)) < each)

    def store(ref, parity):
        for k in range(ref.shape[0]):
            r = 2 * k + parity
            here = slice(r * SHARD, (r + 1) * SHARD)
            head = pl.program_id(0) * (GROUPS // 2) + r // 8
            taps = taps_across_ref[pl.ds(pl.multiple_of(head * LANES, LANES), LANES), :]
            at = (r % 8) * each
            taps = pltpu.roll(taps, LANES - at, 0) if at else taps
            ref[k, :, :LANES] = jnp.where(spare, taps[:SHARD], first[here]).astype(bf16)
            ref[k, :, LANES:wide] = grad_in[here, LANES:].astype(bf16)
            ref[k, :, wide:] = grad_out[here].astype(bf16)

    for parity in range(2):

        @pl.when(core == parity)
        def _():
            store(kept_ref, parity)
            store(sent_ref, 1 - parity)


def unproject(
    place, proj, ahead, taps, qk_back, values_back, gate_back, normed, w_in, out_parts, mixed, gain_two
):
    width, wide = w_in.shape
    half, shards = width // 2, width // SHARD // 4
    args = (proj, ahead, taps, qk_back, values_back, gate_back, normed, w_in, *out_parts, mixed)
    args += (gain_two,)

    def whole(shape):
        return pl.BlockSpec(shape, lambda i: (0,) * len(shape))

    specs = [whole(a.shape) for a in args]
    specs[0] = pl.BlockSpec((proj.shape[0], 4 * LANES), lambda i: (0, 0))
    specs[7] = pl.BlockSpec((half, wide), lambda i: (i, 0))
    for k in (6, 8, 9, 10, 11, 12, 14):
        specs[k] = pl.BlockSpec((args[k].shape[0], half), lambda i: (0, i))
    sums = pl.BlockSpec((shards, SHARD, wide + 4 * LANES), lambda i: (i, 0, 0))
    return pl.pallas_call(
        unproject_kernel,
        grid=(2,),
        out_shape=[jax.ShapeDtypeStruct((4, OWN, width), bf16)]
        + [jax.ShapeDtypeStruct((2 * shards, SHARD, wide + 4 * LANES), bf16)] * 2,
        in_specs=[pl.BlockSpec(memory_space=pltpu.SMEM)] + specs,
        out_specs=[pl.BlockSpec((4, OWN, half), lambda i: (0, 0, i)), sums, sums],
        scratch_shapes=[
            pltpu.VMEM((8, 4 * LANES), f32),
            pltpu.VMEM((4 * LANES, LANES), f32),
            pltpu.VMEM((ROWS, wide), bf16),
            pltpu.VMEM((ROWS, half), bf16),
            pltpu.VMEM((ROWS, 4 * LANES), bf16),
        ],
        compiler_params=pltpu.CompilerParams(vmem_limit_bytes=60 * MIB),
        cost_estimate=pl.CostEstimate(
            flops=4 * 10**9, bytes_accessed=16 * 10**6, transcendentals=0
        ),
    )(place, *args)


BLOCK = 256
HIDDEN = 1280
OUT = 16 * LANES
SHARD = 56
SPACED = 64


def middle_kernel(
    place_ref, own_ref, side_ref, back_ref, far_a_ref, far_b_ref, out_ref, rows_ref, gains_ref,
    cotangent_ref, gate_ref, up_ref, down_ref, both_ref,
    middle_ref, unit_ref, scale_ref, normed_ref, acts_ref, two_ref,
    mixed_ref, sum_ref,
):
    place, step = place_ref[0], pl.program_id(0)
    blocks = HIDDEN // BLOCK

    @pl.when(step == 0)
    def _():
        mixed_ref[place] = own_ref[...]
        mixed_ref[jnp.bitwise_xor(place, 1)] = side_ref[...]
        mixed_ref[jnp.bitwise_xor(place, 3)] = back_ref[...]
        mixed_ref[jnp.bitwise_xor(place, 2), :GROUP, :] = far_a_ref[...]
        mixed_ref[jnp.bitwise_xor(place, 2), GROUP:, :] = far_b_ref[...]
        sum_ref[...] = rows_ref[...].astype(f32)

    @pl.when(step < GROUPS)
    def _():
        for at in range(0, out_ref.shape[0], BLOCK):
            here = slice(at, at + BLOCK)
            sum_ref[:, here] += lax.dot_general(
                mixed_ref[step], out_ref[here, :], (NT, ((), ())), preferred_element_type=f32
            )

    @pl.when(step == GROUPS - 1)
    def _():
        for at in range(0, ROWS, OWN):
            here = slice(at, at + OWN)
            middle = sum_ref[here, :]
            scale = lax.rsqrt(jnp.mean(middle * middle, -1, keepdims=True) + eps_norm)
            normed_ref[here, :] = (middle * scale * gains_ref[1:2]).astype(bf16)
        middle = own_slice(sum_ref, place)
        scale = lax.rsqrt(jnp.mean(middle * middle, -1, keepdims=True) + eps_norm)
        middle_ref[...] = middle
        unit_ref[...] = middle * scale
        scale_ref[...] = jnp.broadcast_to(scale, scale_ref.shape)

    @pl.when((step >= GROUPS) & (step < GROUPS + blocks))
    def _():
        normed = normed_ref[...]
        gate = jnp.dot(normed, gate_ref[...], preferred_element_type=f32)
        up = jnp.dot(normed, up_ref[...], preferred_element_type=f32)
        hidden_back = jnp.dot(cotangent_ref[...], down_ref[...], preferred_element_type=f32)
        sigma = jax.nn.sigmoid(gate)
        silu = gate * sigma
        at = pl.multiple_of((step - GROUPS) * BLOCK, BLOCK)
        acts_ref[:, pl.ds(at, BLOCK)] = (
            hidden_back * up * sigma * (1.0 + gate * (1.0 - sigma))
        ).astype(bf16)
        acts_ref[:, pl.ds(HIDDEN + at, BLOCK)] = (hidden_back * silu).astype(bf16)
        acts_ref[:, pl.ds(2 * HIDDEN + at, BLOCK)] = (silu * up).astype(bf16)

    @pl.when(step >= GROUPS + blocks)
    def _():
        two_ref[...] = lax.dot_general(
            acts_ref[:, : 2 * HIDDEN], both_ref[...], (NT, ((), ())), preferred_element_type=f32
        ).astype(bf16)


def middle_both_ways(place, mixed_parts, weights, rows, gains, back):
    width = rows.shape[1]
    blocks, outs = HIDDEN // BLOCK, width // BLOCK
    columns = OUT // GROUPS

    def whole(shape):
        return pl.BlockSpec(shape, lambda i: (0,) * len(shape))

    def clipped(i, first, count):
        return jnp.clip(i - first, 0, count - 1)

    def block_of(which):
        at = OUT // BLOCK + which * blocks
        return pl.BlockSpec((width, BLOCK), lambda i: (0, at + clipped(i, GROUPS, blocks)))

    last = GROUPS + blocks
    specs = [whole(part.shape) for part in mixed_parts]
    specs.append(pl.BlockSpec((width, columns), lambda i: (0, clipped(i, 0, GROUPS))))
    specs += [whole(rows.shape), whole(gains.shape), whole(back.shape)]
    specs += [block_of(0), block_of(1), block_of(2)]
    specs.append(
        pl.BlockSpec(
            (pl.Element(BLOCK), pl.Element(2 * HIDDEN)),
            lambda i: (clipped(i, last, outs) * BLOCK, OUT),
        )
    )
    results = [
        ((OWN, width), f32),
        ((OWN, width), f32),
        ((OWN, LANES), f32),
        ((ROWS, width), bf16),
        ((ROWS, 3 * HIDDEN), bf16),
        ((ROWS, width), bf16),
    ]
    out_specs = [whole(s) for s, d in results]
    out_specs[-1] = pl.BlockSpec((ROWS, BLOCK), lambda i: (0, clipped(i, last, outs)))
    return pl.pallas_call(
        middle_kernel,
        grid=(last + outs,),
        out_shape=[jax.ShapeDtypeStruct(s, d) for s, d in results],
        in_specs=[pl.BlockSpec(memory_space=pltpu.SMEM)] + specs,
        out_specs=out_specs,
        scratch_shapes=[
            pltpu.VMEM((GROUPS, ROWS, columns), bf16),
            pltpu.VMEM((ROWS, width), f32),
        ],
        compiler_params=pltpu.CompilerParams(vmem_limit_bytes=60 * MIB),
        cost_estimate=pl.CostEstimate(
            flops=16 * 10**9, bytes_accessed=40 * 10**6, transcendentals=0
        ),
    )(place, *mixed_parts, weights, rows, gains, back, weights, weights, weights, weights)


def ffn_out_kernel(place_ref, acts_ref, down_ref, out_ref):
    value = lax.dot_general(
        acts_ref[...], down_ref[...], (NT, ((), ())), preferred_element_type=f32
    ).astype(bf16)
    store_by_owner(out_ref, value, place_ref[0])


def ffn_out(place, acts, weights):
    width = weights.shape[0]
    return pl.pallas_call(
        ffn_out_kernel,
        grid=(width // BLOCK,),
        out_shape=jax.ShapeDtypeStruct((4, OWN, width), bf16),
        in_specs=[
            pl.BlockSpec(memory_space=pltpu.SMEM),
            pl.BlockSpec((ROWS, HIDDEN), lambda i: (0, 2)),
            pl.BlockSpec(
                (pl.Element(BLOCK), pl.Element(HIDDEN)), lambda i: (i * BLOCK, OUT + 2 * HIDDEN)
            ),
        ],
        out_specs=pl.BlockSpec((4, OWN, BLOCK), lambda i: (0, 0, i)),
        compiler_params=pltpu.CompilerParams(vmem_limit_bytes=60 * MIB),
        cost_estimate=pl.CostEstimate(
            flops=3 * 10**9, bytes_accessed=8 * 10**6, transcendentals=0
        ),
    )(place, acts, weights)


def ffn_grads_kernel(normed_ref, back_ref, acts_ref, grads_ref):
    def spaced(rows_ref):
        grad = lax.dot_general(
            rows_ref[...], acts_ref[...], (TN, ((), ())), preferred_element_type=f32
        )
        for r in range(grad.shape[0] // SHARD):
            grads_ref[r * SPACED : r * SPACED + SHARD, :] = grad[
                r * SHARD : (r + 1) * SHARD
            ].astype(bf16)
            grads_ref[r * SPACED + SHARD : (r + 1) * SPACED, :] = jnp.zeros(
                (SPACED - SHARD, grad.shape[1]), bf16
            )

    both = pl.program_id(0) < 2 * HIDDEN // WIDER

    @pl.when(both)
    def _():
        spaced(normed_ref)

    @pl.when(jnp.logical_not(both))
    def _():
        spaced(back_ref)


WIDER = 640


def ffn_grads(normed, back, acts):
    width = normed.shape[1]
    whole = pl.BlockSpec((ROWS, width), lambda i: (0, 0))
    return pl.pallas_call(
        ffn_grads_kernel,
        grid=(3 * HIDDEN // WIDER,),
        out_shape=jax.ShapeDtypeStruct((width // SHARD * SPACED, 3 * HIDDEN), bf16),
        in_specs=[whole, whole, pl.BlockSpec((ROWS, WIDER), lambda i: (0, i))],
        out_specs=pl.BlockSpec((width // SHARD * SPACED, WIDER), lambda i: (0, i)),
        compiler_params=pltpu.CompilerParams(vmem_limit_bytes=60 * MIB),
        cost_estimate=pl.CostEstimate(
            flops=7 * 10**9, bytes_accessed=20 * 10**6, transcendentals=0
        ),
    )(normed, back, acts)


def order_columns(heads):
    import numpy as np

    place = np.zeros((5 * LANES, 5 * LANES), np.float32)
    for h in range(heads):
        at = h * (2 * FEAT + DH + 1)
        for i in range(FEAT):
            place[at + i, heads * LANES + h * FEAT + i] = 1.0
            place[at + FEAT + i, heads * LANES + (heads + h) * FEAT + i] = 1.0
        for i in range(DH):
            place[at + 2 * FEAT + i, h * LANES + i] = 1.0
        place[at + 2 * FEAT + DH, GATE_LANE + h] = 1.0
    return jnp.asarray(place, bf16)


def order_heads(heads):
    import numpy as np

    place = np.zeros((heads * DH, heads * LANES), np.float32)
    for h in range(heads):
        for i in range(DH):
            place[h * DH + i, h * LANES + i] = 1.0
    return jnp.asarray(place, bf16)


def prepare_kernel(
    rank_ref, in_ref, out_ref, gate_ref, up_ref, down_ref, taps_ref,
    gains_ref, gains_first_ref, gains_second_ref, place_ref, tiles_ref,
    shard_ref, out_shard_ref, rest_ref, few_ref,
):
    wide = 5 * LANES
    columns = in_ref.shape[1]
    whole = jnp.dot(
        in_ref[...].astype(bf16), place_ref[:columns, :], preferred_element_type=f32
    )
    spot = jnp.where(
        lanes_of((2, wide)) == rows_of((2, wide)) + GAIN_LANE, 1.0, 0.0
    ).astype(bf16)
    gains = lax.dot_general(
        gains_ref[...].astype(bf16), spot, (TN, ((), ())), preferred_element_type=f32
    )
    for k in range(shard_ref.shape[0]):
        shard_ref[k, :SHARD, :] = (whole + gains).astype(bf16)
    rank = rank_ref[0]
    own = taps_ref.shape[1]
    each = DH // own
    first = (rank // each) * LANES + (rank % each) * own
    spot = jnp.where(
        lanes_of((own, wide)) == rows_of((own, wide)) + first, 1.0, 0.0
    ).astype(bf16)
    taps = jnp.dot(taps_ref[...].astype(bf16), spot, preferred_element_type=f32)
    rows = [taps]
    for ref in (gains_ref, gains_first_ref, gains_second_ref):
        few_ref[...] = jnp.zeros_like(few_ref)
        few_ref[0:2, :SHARD] = ref[...]
        both = few_ref[...]
        line = both + pltpu.roll(pltpu.roll(both, SHARD, 1), 7, 0)
        parts = [part.astype(f32)[0:1] for part in three_parts(line)]
        rows.append(jnp.concatenate(parts + [jnp.zeros((1, wide - 3 * LANES), f32)], 1))
    rows.append(jnp.zeros((SPACED - SHARD - TAPS - 3, wide), f32))
    for k in range(shard_ref.shape[0]):
        shard_ref[k, SHARD:, :] = jnp.concatenate(rows, 0).astype(bf16)
    out_shard_ref[...] = jnp.dot(
        out_ref[...].astype(bf16), tiles_ref[...], preferred_element_type=f32
    ).astype(bf16)
    rest_ref[...] = jnp.zeros_like(rest_ref)
    units = gate_ref.shape[1]
    rest_ref[:, :units] = gate_ref[...].astype(bf16)
    rest_ref[:, HIDDEN : HIDDEN + units] = up_ref[...].astype(bf16)
    rest_ref[:, 2 * HIDDEN : 2 * HIDDEN + units] = down_ref[...].astype(bf16)


def prepare(rank, *args):
    return whole_call(
        prepare_kernel,
        [
            ((16, SPACED, 5 * LANES), bf16),
            ((SHARD, 4 * LANES), bf16),
            ((SHARD, 3 * HIDDEN), bf16),
        ],
        rank, *args,
        scratch=[pltpu.VMEM((8, LANES), f32)],
        scalars=1,
    )


def moved_moments(weight, first, second, grad):
    fix = 1.0 - beta_value**STEP
    moment = beta_value * first + (1.0 - beta_value) * grad
    square = beta_value * second + (1.0 - beta_value) * grad * grad
    direction = moment / fix / (jnp.sqrt(square / fix) + eps_adam) + decay_rate * weight
    return moment, square, direction


def adapted(params, outs, place, grad):
    weight = params[0][...]
    moment, square, direction = moved_moments(weight, params[1][...], params[2][...], grad)
    outs[0][...] = moment
    outs[1][...] = square
    outs[2][...] = direction
    both = [
        jnp.sum(jnp.sum(v * v, 1, keepdims=True), 0, keepdims=True) for v in (weight, direction)
    ]
    lane = lanes_of((1, LANES))
    return jnp.where(lane == place, both[0], jnp.where(lane == place + 1, both[1], 0.0))


def ffn_moments_kernel(ffn_ref, *refs):
    params, outs, sums_ref = refs[:9], refs[9:-1], refs[-1]
    units = params[0].shape[1]
    sums = jnp.zeros((1, LANES), f32)
    for k in range(3):
        grad = ffn_ref[:SHARD, k * HIDDEN : k * HIDDEN + units].astype(f32)
        three = slice(3 * k, 3 * k + 3)
        sums = sums + adapted(params[three], outs[three], 4 + 2 * k, grad)
    sums_ref[...] = jnp.broadcast_to(sums, sums_ref.shape)


def ffn_moments(ffn, params):
    outs = [(param.shape, f32) for param in params]
    return whole_call(ffn_moments_kernel, outs + [((8, LANES), f32)], ffn, *params)


def moments_kernel(mixer_ref, place_ref, tiles_ref, ffn_sums_ref, *refs):
    params, outs, sums_ref = refs[:9], refs[9:-1], refs[-1]

    wide = 5 * LANES
    mixer = mixer_ref[0].astype(f32)
    for k in range(1, mixer_ref.shape[0]):
        mixer = mixer + mixer_ref[k].astype(f32)
    sums = ffn_sums_ref[0:1, :]
    grad_in = picked(mixer[:, :wide], place_ref[...], NT)
    sums = sums + adapted(params[0:3], outs[0:3], 0, grad_in[:, : params[0].shape[1]])
    sums = sums + adapted(params[3:6], outs[3:6], 2, picked(mixer[:, wide:], tiles_ref[...], NT))
    across = jnp.concatenate([mixer[:, :LANES], jnp.zeros((LANES - SHARD, LANES), f32)], 0).T
    taps = across[TAPS_LANE : TAPS_LANE + TAPS, : params[6].shape[1]]
    sums = sums + adapted(params[6:9], outs[6:9], 10, taps)
    ones = across[GAIN_LANE : GAIN_LANE + 1]
    twos = across[GAIN_LANE + 1 : GAIN_LANE + 2]
    few = lanes_of((1, LANES))
    line = jnp.where(few < SHARD, ones, 0.0) + pltpu.roll(
        jnp.broadcast_to(jnp.where(few < SHARD, twos, 0.0), (8, LANES)), SHARD, 1
    )[0:1]
    both = jnp.concatenate([sums, line], 1)
    sums_ref[...] = jnp.broadcast_to(both[None], sums_ref.shape)


def moments(mixer, place, tiles, ffn_sums, params):
    outs = [(param.shape, f32) for param in params] + [((LANES, 1, 2 * LANES), f32)]
    return whole_call(
        moments_kernel, outs, mixer, place, tiles, ffn_sums, *params
    )


def update_kernel(rank_ref, totals_ref, states_ref, *refs):
    weights, directions, outs = refs[:6], refs[6:12], refs[12:18]
    gains_refs, norms_ref = refs[18:21], refs[21]
    totals = totals_ref[:, 0, :]
    sums = jnp.sum(totals[:, :LANES], 0, keepdims=True)
    lane = lanes_of((1, LANES))
    grouped = jnp.where(
        lanes_of((32, LANES)) // 4 == rows_of((32, LANES)), 1.0, 0.0
    ).astype(bf16)
    grad = summed_down(grouped, totals[:, LANES:], NN)
    moment, square, direction = moved_moments(
        states_ref[0], states_ref[1], states_ref[2], grad
    )
    live = lanes_of((32, LANES)) < 2 * SHARD
    for place, value in ((12, states_ref[0]), (13, direction)):
        value = jnp.where(live, value, 0.0)
        value = jnp.sum(jnp.sum(value * value, 1, keepdims=True), 0, keepdims=True)
        sums = jnp.where(lane == place, value, sums)
    norms = jnp.sqrt(sums)
    each = [
        jnp.sum(
            jnp.where(lanes_of((8, LANES)) == 2 * rows_of((8, LANES)) + k, norms, 0.0),
            1,
            keepdims=True,
        )
        for k in range(2)
    ]
    norms_ref[...] = jnp.where(lanes_of((8, 2)) == 0, each[0], each[1])[:7]

    def ratio(index):
        return norms[:, 2 * index : 2 * index + 1] / norms[:, 2 * index + 1 : 2 * index + 2]

    for index in range(6):
        outs[index][...] = (
            weights[index][...] - learn_rate * ratio(index) * directions[index][...]
        )
    updated = states_ref[0] - learn_rate * ratio(6) * direction
    for ref, value in zip(gains_refs, (updated, moment, square)):
        own = jnp.where(rows_of((32, LANES)) == rank_ref[0], value, 0.0)
        own = jnp.broadcast_to(jnp.sum(own, 0, keepdims=True), (8, LANES))
        ref[0:1, :] = own[0:1, :SHARD]
        ref[1:2, :] = pltpu.roll(own, LANES - SHARD, 1)[0:1, :SHARD]


def update(rank, totals, states, weights, directions):
    outs = [(w.shape, f32) for w in weights] + [((2, SHARD), f32)] * 3 + [((7, 2), f32)]
    return whole_call(
        update_kernel, outs, rank, totals, states, *weights, *directions, scalars=1
    )


def per_device(
    tokens,
    cotangent,
    lengths,
    rate_codes,
    inproj,
    inproj_first,
    inproj_second,
    outproj,
    outproj_first,
    outproj_second,
    gateproj,
    gateproj_first,
    gateproj_second,
    upproj,
    upproj_first,
    upproj_second,
    downproj,
    downproj_first,
    downproj_second,
    convtaps,
    convtaps_first,
    convtaps_second,
    normgains,
    normgains_first,
    normgains_second,
):
    seqs, group, width = tokens.shape
    heads = rate_codes.shape[0]
    lag = TAPS - 1
    rank = lax.axis_index(SEQ).reshape(1)
    core = lax.axis_index("seq_2")
    peer = lax.axis_index("mp").reshape(1)
    pick, ends = selections()
    place, tiles = order_columns(heads), order_heads(heads)

    shards, out_shard, rest_shard = prepare(
        rank, inproj, outproj.T, gateproj, upproj, downproj.T, convtaps,
        normgains, normgains_first, normgains_second, place, tiles,
    )
    got = lax.all_to_all(shards, ("seq_0", "seq_1"), 0, 0, tiled=True)
    other = lax.ppermute(got, "seq_2", SWAP)
    low, high = peer[0] % 2, peer[0] // 2

    def beside(mine, theirs, bit):
        return jnp.where(
            bit == 0, jnp.concatenate([mine, theirs], 1), jnp.concatenate([theirs, mine], 1)
        )

    out_pair = beside(out_shard, lax.ppermute(out_shard, "mp", SIDE), low)
    out_shards = beside(out_pair, lax.ppermute(out_pair, "mp", BACK), high)
    weights_shard = jnp.concatenate([out_shards, rest_shard], 1)
    weights_shard, got = lax.optimization_barrier((weights_shard, got))
    weights = lax.all_gather(weights_shard, SEQ, axis=0, tiled=True)

    rows = tokens.reshape(-1, width)
    rim = shifted(tokens[:, group - lag :], SEQ, 1).reshape(-1, width)
    rim = jnp.pad(rim, ((0, 16 - seqs * lag), (0, 0)))
    positions = rank * group + jnp.arange(group, dtype=jnp.int32)
    keep = (positions[None, :] < lengths[:, None]).astype(f32).reshape(-1, 1)
    back = (cotangent.reshape(-1, width).astype(f32) * keep).astype(bf16)
    rates = -jnp.exp2(-rate_codes.astype(f32) / 4.0)
    rates = jnp.pad(rates[None], ((0, 0), (GATE_LANE, LANES - GATE_LANE - heads)))
    normed_one, proj, w_in, gains, taps, states, values, cum, sent = project(
        core.reshape(1), rows, rim, got, other, rates, pick, ends
    )
    earlier, decay = earlier_states(sent)
    inside = within(proj, values, cum)
    total, mixed = mix(proj, cum, inside, earlier, pick, ends)

    middle, unit_two, scale_two, normed_two, acts, two_part = middle_both_ways(
        peer, gather_parts(mixed), weights, rows, gains, back
    )
    two_back = lax.psum_scatter(two_part, "mp", scatter_dimension=0, tiled=True)
    ffn_part = ffn_out(peer, acts, weights)
    two_back, ffn_part = lax.optimization_barrier((two_back, ffn_part))
    ffn_sums = lax.psum_scatter(
        ffn_grads(normed_two, back, acts), SEQ, scatter_dimension=0, tiled=True
    )
    middle_back, gain_two, out_own, mixed_back = turn(
        peer, two_back, unit_two, scale_two, back, gains, weights
    )
    mixed_back = lax.all_to_all(mixed_back, "mp", 0, 0, tiled=True).reshape(ROWS, -1)

    total_back, sent = unmix(mixed_back, total, proj, cum, pick, ends)
    ffn_part, out_own, sent = lax.optimization_barrier((ffn_part, out_own, sent))
    later, summed = later_states(sent, decay)
    within_a = within_back(0, proj, values, cum, total_back, earlier, pick, ends)
    total_back, _ = lax.optimization_barrier((total_back, summed))
    within_b = within_back(1, proj, values, cum, total_back, earlier, pick, ends)
    out_parts = gather_parts(out_own)
    ffn_terms = scatter_terms(ffn_part)
    qk_back, values_back, gate_back = later_back(
        proj, values, cum, rates, earlier, later, pick, ends, within_a + within_b
    )
    edge = values_back.reshape(seqs, group, -1)[:, :lag]
    ahead = shifted(edge, SEQ, -1).reshape(seqs * lag, -1)
    ahead = jnp.concatenate([ahead, jnp.zeros_like(ahead)], 0)
    ahead, ffn_terms = lax.optimization_barrier((ahead, ffn_terms))
    one_part, kept, sent = unproject(
        jnp.concatenate([peer, core.reshape(1)]), proj, ahead, taps, qk_back, values_back, gate_back, normed_one, w_in, out_parts, mixed,
        gain_two,
    )

    swapped = lax.ppermute(sent, "seq_2", SWAP)
    mixer_part = (kept.astype(f32) + swapped.astype(f32)).astype(bf16)

    one_part, mixer_part = lax.optimization_barrier((one_part, mixer_part))
    mixer_got = lax.all_to_all(mixer_part, ("seq_0", "seq_1"), 0, 0, tiled=True)
    one_terms = scatter_terms(one_part)
    block_out = lax.all_gather(
        block_outs(peer, ffn_terms, middle, jnp.broadcast_to(keep, (ROWS, LANES))),
        "mp",
        axis=0,
        tiled=True,
    )

    mixer_params = (inproj, inproj_first, inproj_second)
    mixer_params += (outproj.T, outproj_first.T, outproj_second.T)
    mixer_params += (convtaps, convtaps_first, convtaps_second)
    ffn_params = (gateproj, gateproj_first, gateproj_second)
    ffn_params += (upproj, upproj_first, upproj_second)
    ffn_params += (downproj.T, downproj_first.T, downproj_second.T)
    *ffn_moved, ffn_squares = ffn_moments(ffn_sums, ffn_params)
    *moved, sums = moments(mixer_got, place, tiles, ffn_squares, mixer_params)
    moved = moved[:6] + ffn_moved + moved[6:]
    weights_old = mixer_params[0:6:3] + ffn_params[0::3] + mixer_params[6:7]
    token_own = token_grads(peer, one_terms, rows, middle_back, gains)
    back, side = to_neighbours(token_own)
    totals = lax.all_to_all(sums, ALL, 0, 0, tiled=True)
    back, side, _ = lax.optimization_barrier((back, side, totals))
    token_grad = assembled(peer, (token_own, side, back, *passed_on(back, side)))
    *updated, gains_new, gains_moment, gains_square, norms = update(
        rank, totals, states, weights_old, moved[2::3]
    )
    results = [block_out.reshape(tokens.shape), token_grad.reshape(tokens.shape)]
    for index in range(6):
        for value in (updated[index], moved[3 * index], moved[3 * index + 1]):
            results.append(value.T if index in (1, 4) else value)
    results += [gains_new, gains_moment, gains_square, norms]
    return tuple(results)


def solution(mesh):
    split = Mesh(mesh.devices.reshape(4, 4, 2, mesh.shape["mp"]), ("seq_0", "seq_1", "seq_2", "mp"))
    in_specs = (
        P(None, SEQ, None),
        P(None, SEQ, None),
        P(),
        P("mp"),
        P(SEQ, "mp"),
        P(SEQ, "mp"),
        P(SEQ, "mp"),
        P("mp", SEQ),
        P("mp", SEQ),
        P("mp", SEQ),
        P(SEQ, "mp"),
        P(SEQ, "mp"),
        P(SEQ, "mp"),
        P(SEQ, "mp"),
        P(SEQ, "mp"),
        P(SEQ, "mp"),
        P("mp", SEQ),
        P("mp", SEQ),
        P("mp", SEQ),
        P(None, MP_SEQ),
        P(None, MP_SEQ),
        P(None, MP_SEQ),
        P(None, SEQ),
        P(None, SEQ),
        P(None, SEQ),
    )
    out_specs = (
        P(None, SEQ, None),
        P(None, SEQ, None),
        P(SEQ, "mp"),
        P(SEQ, "mp"),
        P(SEQ, "mp"),
        P("mp", SEQ),
        P("mp", SEQ),
        P("mp", SEQ),
        P(SEQ, "mp"),
        P(SEQ, "mp"),
        P(SEQ, "mp"),
        P(SEQ, "mp"),
        P(SEQ, "mp"),
        P(SEQ, "mp"),
        P("mp", SEQ),
        P("mp", SEQ),
        P("mp", SEQ),
        P(None, MP_SEQ),
        P(None, MP_SEQ),
        P(None, MP_SEQ),
        P(None, SEQ),
        P(None, SEQ),
        P(None, SEQ),
        P(),
    )
    return jax.shard_map(
        per_device, mesh=split, in_specs=in_specs, out_specs=out_specs, check_vma=False
    )
```

```python
import math

import jax
import jax.numpy as jnp
from jax import lax
from jax.experimental import pallas as pl
from jax.experimental.pallas import tpu as pltpu
from jax.sharding import Mesh
from jax.sharding import PartitionSpec as P

DH = 112
FEAT = 16
TAPS = 3
STEP = 7
LANES = 128
SEQ = ("seq_0", "seq_1", "seq_2")
ALL = ("seq_0", "seq_1", "seq_2", "mp")
MP_SEQ = ("mp", "seq_0", "seq_1", "seq_2")

f32 = jnp.float32
bf16 = jnp.bfloat16
highest = lax.Precision.HIGHEST
root_half = 0.5**0.5
eps_norm = 1e-05
eps_adam = 1e-06
decay_rate = 0.01
learn_rate = 0.3
beta_value = 0.5

SIDE = [(i, i ^ 1) for i in range(4)]
BACK = [(i, 3 - i) for i in range(4)]
SWAP = [(0, 1), (1, 0)]


def shifted(value, axis, steps):
    count = lax.axis_size(axis)
    first, last = (max(0, -steps), min(count, count - steps))
    return lax.ppermute(value, axis, [(source, source + steps) for source in range(first, last)])


SPAN_LANE = DH
GROUPS = 4
GATE_LANE = DH
GAIN_LANE = DH + 4
TAPS_LANE = DH + 6
GROUP = 256
ROWS = 512
SIDES = 256
PIECE = 40
SLOT = 48
PIECES = 32
MIB = 1 << 20


def selections():
    import numpy as np

    pick = np.zeros((2 * LANES, 2 * SIDES), np.float32)
    ends = np.zeros((8, SIDES), np.float32)
    ends[0, 0] = ends[1, 0] = ends[2, 0] = 1.0
    lane = 1
    for i in range(FEAT):
        pick[i, lane] = 0.5
        ends[1, lane] = ends[2, lane] = 1.0
        lane += 1
    for i in range(FEAT):
        for j in range(i, FEAT):
            pick[i, lane] = 0.5
            pick[j, SIDES + lane] = 0.5
            ends[2, lane] = root_half if i == j else 1.0
            lane += 1
    pick[LANES:] = pick[:LANES]
    return jnp.asarray(pick, bf16), jnp.asarray(ends)


def two_parts(value):
    high = value.astype(bf16)
    return high, (value - high.astype(f32)).astype(bf16)


def three_parts(value):
    high = value.astype(bf16)
    rest = value - high.astype(f32)
    mid = rest.astype(bf16)
    return high, mid, (rest - mid.astype(f32)).astype(bf16)


def product(a, b, contract, passes=3):
    dims = (contract, ((), ()))

    def once(x, y):
        return lax.dot_general(x, y, dims, preferred_element_type=f32)

    if passes == 1:
        return once(a.astype(bf16), b.astype(bf16))
    a_high, a_low = two_parts(a)
    if passes == 2:
        b = b.astype(bf16)
        return once(a_high, b) + once(a_low, b)
    b_high, b_low = two_parts(b)
    return once(a_high, b_high) + (once(a_high, b_low) + once(a_low, b_high))


NN = ((1,), (0,))
NT = ((1,), (1,))
TN = ((0,), (0,))


def lanes_of(shape):
    return lax.broadcasted_iota(jnp.int32, shape, len(shape) - 1)


def rows_of(shape):
    return lax.broadcasted_iota(jnp.int32, shape, 0)


def lower_ones(strict=False):
    row, lane = rows_of((GROUP, GROUP)), lanes_of((GROUP, GROUP))
    return jnp.where(row > lane if strict else row >= lane, 1.0, 0.0).astype(bf16)


def summed_down(ones, value, contract):
    high, mid, low = (
        lax.dot_general(ones, part, (contract, ((), ())), preferred_element_type=f32)
        for part in three_parts(value)
    )
    return low + mid + high


def picked(value, place, contract):
    high, mid, low = (
        lax.dot_general(part, place, (contract, ((), ())), preferred_element_type=f32)
        for part in three_parts(value)
    )
    return low + mid + high


def head_lanes(tile, head, keys):
    first = (4 if keys else 0) * FEAT + head * FEAT
    return pltpu.roll(tile, (LANES - first) % LANES, 1) if first else tile


def factors(moved, pick, ends):
    high, low = two_parts(moved)
    found = lax.dot_general(
        jnp.concatenate([high, low], 1), pick, (NN, ((), ())), preferred_element_type=f32
    )
    return found[:, :SIDES] + ends[0:1], found[:, SIDES:] + ends[1:2]


def factors_back(upstream, one, two, pick, ends):
    scaled = upstream * ends[2:3]
    both = jnp.concatenate([scaled * two, scaled * one], 1)
    return product(both, pick[:LANES], NT, 2)


def scores(tile, head):
    only = lanes_of((GROUP, LANES)) < FEAT
    query = jnp.where(only, head_lanes(tile, head, False), 0.0) * 0.25
    keys = jnp.where(only, head_lanes(tile, head, True), 0.0)
    q_high, k_high = query.astype(bf16), keys.astype(bf16)
    q_wide, k_wide = q_high.astype(f32), k_high.astype(f32)
    q_both = (q_wide + pltpu.roll(query - q_wide, FEAT, 1)).astype(bf16)
    k_both = (pltpu.roll(k_wide, FEAT, 1) + (keys - k_wide)).astype(bf16)
    left = jnp.concatenate([q_high, q_both], 1)
    right = jnp.concatenate([k_high, k_both], 1)
    return lax.dot_general(left, right, (NT, ((), ())), preferred_element_type=f32)


def decays(cum, cum_across, head):
    row, lane = rows_of((GROUP, GROUP)), lanes_of((GROUP, GROUP))
    at = GATE_LANE + head
    diff = cum[:, at : at + 1] - cum_across[at : at + 1, :]
    return jnp.where(row >= lane, jnp.exp(jnp.minimum(diff, 0.0)), 0.0)


def head_column(tile, head):
    at = GATE_LANE + head
    return tile[:, at : at + 1]


def on_head_lane(column, head):
    return jnp.where(lanes_of((column.shape[0], LANES)) == GATE_LANE + head, column, 0.0)


def state_rows(pieces_ref, pair):
    parts = [pieces_ref[4 * pair + q, :PIECE, :].astype(f32) for q in range(4)]
    parts.append(jnp.zeros((SIDES - 4 * PIECE, LANES), f32))
    return jnp.concatenate(parts, 0).astype(bf16)


def store_pieces(ref, pair, state):
    for q in range(4):
        ref[4 * pair + q, :PIECE, :] = state[q * PIECE : (q + 1) * PIECE].astype(bf16)


def whole_call(body, outs, *args, scratch=(), flops=10**9, limit=60, views=None, scalars=0):
    views = views or {}
    shapes = [views.get(i, (a.shape,))[0] for i, a in enumerate(args)]

    def whole(shape, place=None):
        return pl.BlockSpec(shape, lambda i: place or (0,) * len(shape))

    count = sum(math.prod(s) * a.dtype.itemsize for s, a in zip(shapes, args))
    count += sum(math.prod(s) * jnp.dtype(d).itemsize for s, d in outs)
    return pl.pallas_call(
        body,
        grid=(1,),
        out_shape=[jax.ShapeDtypeStruct(s, d) for s, d in outs],
        in_specs=[pl.BlockSpec(memory_space=pltpu.SMEM)] * scalars
        + [whole(s, views.get(i, (s, None))[1]) for i, s in enumerate(shapes) if i >= scalars],
        out_specs=[whole(s) for s, d in outs],
        scratch_shapes=list(scratch),
        compiler_params=pltpu.CompilerParams(vmem_limit_bytes=limit * MIB),
        cost_estimate=pl.CostEstimate(flops=flops, bytes_accessed=count, transcendentals=0),
    )(*args)


def sequence_call(body, outs, *args, halves, flops=10**9):
    def half(shape, columns=None, place=0):
        block = (shape[0] // 2,) + tuple(shape[1:-1]) + (columns or shape[-1],)
        rest = (0,) * (len(shape) - 2) + (place,)
        return pl.BlockSpec(block, lambda i: (i,) + rest)

    def whole(shape):
        return pl.BlockSpec(shape, lambda i: (0,) * len(shape))

    specs = [
        half((ROWS,) + a.shape[1:] if a.ndim == 2 else a.shape, *halves[i])
        if i in halves
        else whole(a.shape)
        for i, a in enumerate(args)
    ]
    return pl.pallas_call(
        body,
        grid=(2,),
        out_shape=[jax.ShapeDtypeStruct(s, d) for s, d in outs],
        in_specs=specs,
        out_specs=[half(s) for s, d in outs],
        compiler_params=pltpu.CompilerParams(vmem_limit_bytes=60 * MIB),
        cost_estimate=pl.CostEstimate(flops=flops, bytes_accessed=4 * 10**6, transcendentals=0),
    )(*args)


def project_kernel(
    core_ref, rows_ref, rim_ref, got_ref, other_ref, rates_ref, pick_ref, ends_ref,
    normed_ref, proj_ref, w_ref, gains_ref, taps_ref, states_ref, values_ref, cum_ref, sent_ref,
    wide_ref,
):
    wide = w_ref.shape[1]
    flipped = core_ref[0] == 1
    taps = jnp.zeros((8, 4 * LANES), f32)
    for r in range(2 * got_ref.shape[0]):
        mine, theirs = got_ref[r // 2].astype(f32), other_ref[r // 2].astype(f32)
        part = jnp.where(flipped, theirs, mine) if r % 2 == 0 else jnp.where(flipped, mine, theirs)
        wide_ref[r * SHARD : (r + 1) * SHARD, :] = part[:SHARD]
        rest = part[SHARD:]
        taps = taps + rest[:, : 4 * LANES]
        whole = rest[:, :LANES] + rest[:, LANES : 2 * LANES] + rest[:, 2 * LANES : 3 * LANES]
        for k in range(3):
            states_ref[k, r : r + 1, :] = whole[TAPS + k : TAPS + k + 1]
    taps_ref[...] = taps
    w_ref[...] = wide_ref[...].astype(bf16)
    chosen = jnp.where(
        lanes_of((16, wide)) == rows_of((16, wide)) + GAIN_LANE, 1.0, 0.0
    )
    chosen = jnp.where(rows_of((16, wide)) < 2, chosen, 0.0).astype(bf16)
    gains = lax.dot_general(chosen, w_ref[...], (NT, ((), ())), preferred_element_type=f32)
    gains_ref[...] = gains[:8]
    gain = gains[0:1]

    def projected(rows):
        rows = rows.astype(f32)
        scale = lax.rsqrt(jnp.mean(rows * rows, -1, keepdims=True) + eps_norm)
        normed = (rows * scale * gain).astype(bf16)
        return normed, jnp.dot(normed, w_ref[...], preferred_element_type=f32)

    for at in range(0, ROWS, GROUP):
        normed, proj = projected(rows_ref[at : at + GROUP, :])
        normed_ref[at : at + GROUP, :] = normed
        proj_ref[at : at + GROUP, :] = proj
    proj_ref[ROWS:, :] = projected(rim_ref[...])[1]
    ones = lower_ones()
    pick, ends = pick_ref[...], ends_ref[...]
    lane, row = lanes_of((GROUP, LANES)), rows_of((GROUP, LANES))
    for s in range(2):
        here = slice(s * GROUP, (s + 1) * GROUP)
        steps = rates_ref[...] * jax.nn.softplus(proj_ref[here, :LANES])
        cum = summed_down(ones, steps, NN)
        cum_ref[here, :] = cum
        last = cum[GROUP - 1 : GROUP, :]
        tail = jnp.exp(last - cum)
        qk = proj_ref[here, 4 * LANES :]
        for h in range(4):
            tile = slice(h * LANES, (h + 1) * LANES)
            raw = proj_ref[here, tile]
            rim_two = proj_ref[ROWS + 2 * s : ROWS + 2 * s + 1, tile]
            rim_one = proj_ref[ROWS + 2 * s + 1 : ROWS + 2 * s + 2, tile]
            one = jnp.where(row == 0, rim_one, pltpu.roll(raw, 1, 0))
            two = jnp.where(row == 0, rim_two, jnp.where(row == 1, rim_one, pltpu.roll(raw, 2, 0)))
            conv = (
                taps_ref[0:1, tile] * raw + taps_ref[1:2, tile] * one + taps_ref[2:3, tile] * two
            )
            values = jnp.where(lane < DH, conv, jnp.where(lane == DH, 1.0, 0.0))
            values_ref[here, tile] = values
            left, right = factors(head_lanes(qk, h, True), pick, ends)
            held = left * right * ends[2:3] * head_column(tail, h)
            fresh = product(held, values, TN)
            store_pieces(sent_ref, 4 * s + h, fresh)
            ending = jnp.broadcast_to(head_column(last, h), (8, LANES))
            high, mid, low = three_parts(ending)
            few = lanes_of((8, LANES))
            packed = jnp.where(
                few == 0,
                high.astype(f32),
                jnp.where(few == 1, mid.astype(f32), jnp.where(few == 2, low.astype(f32), 0.0)),
            ).astype(bf16)
            for q in range(4):
                sent_ref[16 * s + 4 * h + q, PIECE:, :] = packed


def project(core, rows, rim, got, other, rates, pick, ends):
    wide, width = got.shape[2], rows.shape[1]
    return whole_call(
        project_kernel,
        [
            (rows.shape, bf16),
            ((ROWS + rim.shape[0], wide), f32),
            ((width, wide), bf16),
            ((8, width), f32),
            ((8, 4 * LANES), f32),
            ((3, 2 * got.shape[0], LANES), f32),
            ((ROWS, 4 * LANES), f32),
            ((ROWS, LANES), f32),
            ((PIECES, SLOT, LANES), bf16),
        ],
        core, rows, rim, got, other, rates, pick, ends,
        scratch=[pltpu.VMEM((width, wide), f32)],
        flops=3 * 10**9,
        scalars=1,
    )


def scan_kernel(got_ref, back_ref, decay_ref):
    state = jnp.zeros((PIECE, LANES), f32)
    for i in range(PIECES):
        back_ref[i, :PIECE, :] = state.astype(bf16)
        back_ref[i, PIECE:, :] = jnp.zeros((SLOT - PIECE, LANES), bf16)
        ending = jnp.sum(got_ref[i, PIECE:, :].astype(f32), -1, keepdims=True)
        decay = jnp.broadcast_to(jnp.exp(ending), (8, LANES))
        decay_ref[i] = decay
        state = state * decay[0:1] + got_ref[i, :PIECE, :].astype(f32)


def earlier_states(sent):
    got = lax.all_to_all(sent, SEQ, 0, 0, tiled=True)
    back, decay = whole_call(
        scan_kernel, [(sent.shape, bf16), ((PIECES, 8, LANES), f32)], got, flops=10**6
    )
    return lax.all_to_all(back, SEQ, 0, 0, tiled=True), decay


def scan_back_kernel(got_ref, decay_ref, back_ref):
    state = jnp.zeros((PIECE, LANES), f32)
    for i in reversed(range(PIECES)):
        back_ref[i, :PIECE, :] = state.astype(bf16)
        back_ref[i, PIECE:, :] = jnp.zeros((SLOT - PIECE, LANES), bf16)
        state = state * decay_ref[i, 0:1, :] + got_ref[i, :PIECE, :].astype(f32)


def later_states(sent, decay):
    got = lax.all_to_all(sent, SEQ, 0, 0, tiled=True)
    (back,) = whole_call(scan_back_kernel, [(sent.shape, bf16)], got, decay, flops=10**6)
    return lax.all_to_all(back, SEQ, 0, 0, tiled=True), back


QK = ((ROWS, LANES), (0, 4))
FIRST = ((ROWS, LANES), (0, 0))


def within_kernel(qk_ref, values_ref, cum_ref, inside_ref):
    for s in range(2):
        here = slice(s * GROUP, (s + 1) * GROUP)
        cum = cum_ref[here, :]
        across = cum.T
        qk = qk_ref[here, :]
        for h in range(4):
            tile = slice(h * LANES, (h + 1) * LANES)
            dots = scores(qk, h)
            weights = (1.0 + dots + 0.5 * dots * dots) * decays(cum, across, h)
            inside_ref[here, tile] = product(weights, values_ref[here, tile], NN)


def within(proj, values, cum):
    return whole_call(
        within_kernel,
        [((ROWS, 4 * LANES), f32)],
        proj, values, cum,
        flops=3 * 10**9,
        views={0: QK},
    )[0]


def mix_kernel(
    qk_ref, cum_ref, inside_ref, earlier_ref, pick_ref, ends_ref, total_ref, mixed_ref
):
    pick, ends = pick_ref[...], ends_ref[...]
    lane = lanes_of((GROUP, LANES))
    growth = jnp.exp(cum_ref[:, :])
    qk = qk_ref[:, :]
    for h in range(4):
        tile = slice(h * LANES, (h + 1) * LANES)
        left, right = factors(head_lanes(qk, h, False), pick, ends)
        held = left * right * ends[2:3] * head_column(growth, h)
        total = inside_ref[:, tile] + product(held, state_rows(earlier_ref, h), NN, 2)
        total_ref[:, tile] = total
        mixed = total / total[:, DH : DH + 1]
        mixed_ref[:, tile] = jnp.where(lane < DH, mixed, 0.0).astype(bf16)


def mix(proj, cum, inside, earlier, pick, ends):
    return sequence_call(
        mix_kernel,
        [((ROWS, 4 * LANES), f32), ((ROWS, 4 * LANES), bf16)],
        proj, cum, inside, earlier, pick, ends,
        halves={0: (LANES, 4), 1: (), 2: (), 3: ()},
        flops=3 * 10**9,
    )


OWN = ROWS // 4


def own_slice(ref, place):
    return ref[pl.ds(pl.multiple_of(place * OWN, OWN), OWN), :]


def turn_kernel(
    place_ref, got_ref, unit_ref, scale_ref, back_ref, gains_ref, w_ref,
    middle_back_ref, gain_ref, out_back_ref, mixed_back_ref,
):
    two_back = got_ref[...].astype(f32)
    unit = unit_ref[...]
    gain_ref[...] = jnp.broadcast_to(
        jnp.sum(two_back * unit, 0, keepdims=True), gain_ref.shape
    )
    weighted = two_back * gains_ref[1:2]
    along = jnp.mean(weighted * unit, -1, keepdims=True)
    middle_back = own_slice(back_ref, place_ref[0]).astype(f32) + scale_ref[:, 0:1] * (
        weighted - unit * along
    )
    middle_back_ref[...] = middle_back
    out_back = middle_back.astype(bf16)
    out_back_ref[...] = out_back
    for g in range(4):
        mixed_back_ref[g] = jnp.dot(
            out_back, w_ref[:, g * 4 * LANES : (g + 1) * 4 * LANES], preferred_element_type=f32
        ).astype(bf16)


def turn(place, got, unit, scale, back, gains, w_out):
    width = back.shape[1]
    return whole_call(
        turn_kernel,
        [
            ((OWN, width), f32),
            ((8, width), f32),
            ((OWN, width), bf16),
            ((4, OWN, 4 * LANES), bf16),
        ],
        place, got, unit, scale, back, gains, w_out,
        flops=10**9,
        scalars=1,
        views={6: ((width, OUT), (0, 0))},
    )


def token_kernel(place_ref, *refs):
    terms, (rows_ref, middle_back_ref, gains_ref, out_ref) = refs[:3], refs[3:]
    one_back = sum(ref[...].astype(f32) for ref in terms)
    rows = own_slice(rows_ref, place_ref[0]).astype(f32)
    scale = lax.rsqrt(jnp.mean(rows * rows, -1, keepdims=True) + eps_norm)
    unit = rows * scale
    weighted = one_back * gains_ref[0:1]
    along = jnp.mean(weighted * unit, -1, keepdims=True)
    token_back = middle_back_ref[...] + scale * (weighted - unit * along)
    out_ref[...] = token_back.astype(bf16)


def token_grads(place, terms, rows, middle_back, gains):
    return whole_call(
        token_kernel, [(terms[0].shape, bf16)], place, *terms, rows, middle_back, gains,
        flops=10**7,
        scalars=1,
    )[0]


def block_kernel(place_ref, *refs):
    terms, (middle_ref, keep_ref, out_ref) = refs[:3], refs[3:]
    ffn = sum(ref[...].astype(f32) for ref in terms)
    keep = own_slice(keep_ref, place_ref[0])[:, 0:1]
    out_ref[...] = ((middle_ref[...] + ffn) * keep).astype(bf16)


def block_outs(place, terms, middle, keep):
    return whole_call(
        block_kernel, [(terms[0].shape, bf16)], place, *terms, middle, keep,
        flops=10**7,
        scalars=1,
    )[0]


def assemble_kernel(place_ref, own_ref, side_ref, back_ref, far_a_ref, far_b_ref, out_ref):
    place = place_ref[0]
    half = OWN // 2

    def at(other):
        return pl.multiple_of(jnp.bitwise_xor(place, other) * OWN, OWN)

    out_ref[pl.ds(at(0), OWN), :] = own_ref[...]
    out_ref[pl.ds(at(1), OWN), :] = side_ref[...]
    out_ref[pl.ds(at(3), OWN), :] = back_ref[...]
    out_ref[pl.ds(at(2), half), :] = far_a_ref[...]
    out_ref[pl.ds(pl.multiple_of(at(2) + half, half), half), :] = far_b_ref[...]


def to_neighbours(own):
    return lax.ppermute(own, "mp", BACK), lax.ppermute(own, "mp", SIDE)


def passed_on(back, side):
    half = back.shape[0] // 2
    return lax.ppermute(back[:half], "mp", SIDE), lax.ppermute(side[half:], "mp", BACK)


def gather_parts(own):
    back, side = to_neighbours(own)
    return own, side, back, *passed_on(back, side)


def assembled(place, parts):
    own = parts[0]
    return whole_call(
        assemble_kernel, [((ROWS, own.shape[1]), own.dtype)], place, *parts,
        flops=10**6,
        scalars=1,
    )[0]


def scatter_terms(part, after=None):
    half = OWN // 2
    got_a = lax.ppermute(part[2, :half], "mp", SIDE)
    got_b = lax.ppermute(part[2, half:], "mp", BACK)
    if after is not None:
        got_a, got_b, _ = lax.optimization_barrier((got_a, got_b, after))
    to_back = jnp.concatenate(
        [(part[3, :half].astype(f32) + got_a.astype(f32)).astype(bf16), part[3, half:]], 0
    )
    to_side = jnp.concatenate(
        [part[1, :half], (part[1, half:].astype(f32) + got_b.astype(f32)).astype(bf16)], 0
    )
    return part[0], lax.ppermute(to_back, "mp", BACK), lax.ppermute(to_side, "mp", SIDE)


def store_by_owner(ref, value, place, columns=slice(None)):
    for g in range(4):
        ref[jnp.bitwise_xor(place, g), :, columns] = value[g * OWN : (g + 1) * OWN]


def unmix_kernel(
    mixed_back_ref, total_ref, qk_ref, cum_ref, pick_ref, ends_ref, total_back_ref, sent_ref
):
    pick, ends = pick_ref[...], ends_ref[...]
    lane = lanes_of((GROUP, LANES))
    growth = jnp.exp(cum_ref[:, :])
    qk = qk_ref[:, :]
    for h in range(4):
        tile = slice(h * LANES, (h + 1) * LANES)
        total = total_ref[:, tile]
        inverse = 1.0 / total[:, DH : DH + 1]
        numer = mixed_back_ref[:, tile].astype(f32) * inverse
        numer = jnp.where(lane < DH, numer, 0.0)
        denom = -jnp.sum(numer * total, -1, keepdims=True) * inverse
        total_back = jnp.where(lane == DH, denom, numer)
        total_back_ref[:, tile] = total_back
        left, right = factors(head_lanes(qk, h, False), pick, ends)
        held = left * right * ends[2:3] * head_column(growth, h)
        store_pieces(sent_ref, h, product(held, total_back, TN))
        for q in range(4):
            sent_ref[4 * h + q, PIECE:, :] = jnp.zeros((SLOT - PIECE, LANES), bf16)


def unmix(mixed_back, total, proj, cum, pick, ends):
    return sequence_call(
        unmix_kernel,
        [((ROWS, 4 * LANES), f32), ((PIECES, SLOT, LANES), bf16)],
        mixed_back, total, proj, cum, pick, ends,
        halves={0: (), 1: (), 2: (LANES, 4), 3: ()},
        flops=3 * 10**9,
    )


def within_back_kernel(
    qk_ref, values_ref, cum_ref, total_back_ref, earlier_ref, pick_ref, ends_ref,
    qk_back_ref, values_back_ref, level_ref,
):
    pick, ends = pick_ref[...], ends_ref[...]
    only = lanes_of((GROUP, LANES)) < FEAT
    cum = cum_ref[:, :]
    across = cum.T
    growth = jnp.exp(cum)
    qk = qk_ref[:, :]
    qk_back = jnp.zeros((GROUP, LANES), f32)
    level = jnp.zeros((GROUP, LANES), f32)
    level_down = jnp.zeros((LANES, GROUP), f32)
    for h in range(4):
        tile = slice(h * LANES, (h + 1) * LANES)
        total_back = total_back_ref[:, tile]
        decay = decays(cum, across, h)
        dots = scores(qk, h)
        pairing = decay * product(total_back, values_ref[:, tile], NT)
        kernel = 1.0 + dots + 0.5 * dots * dots
        moved = kernel * pairing
        down = jnp.sum(moved, 0, keepdims=True)
        level_down = jnp.where(rows_of((LANES, GROUP)) == GATE_LANE + h, down, level_down)
        kernel_back = pairing * (1.0 + dots) * 0.25
        values_back_ref[:, tile] = product(kernel * decay, total_back, TN)
        query_tile = head_lanes(qk, h, False)
        keys_only = jnp.where(only, head_lanes(qk, h, True), 0.0)
        query_only = jnp.where(only, query_tile, 0.0)
        query_back = product(kernel_back, keys_only, NN)
        keys_back = product(kernel_back, query_only, TN)
        left, right = factors(query_tile, pick, ends)
        features_back = head_column(growth, h) * product(
            total_back, state_rows(earlier_ref, h), NT, 2
        )
        level_here = jnp.sum(moved, 1, keepdims=True) + jnp.sum(
            left * right * ends[2:3] * features_back, 1, keepdims=True
        )
        level = level + on_head_lane(level_here, h)
        query_back = query_back + factors_back(features_back, left, right, pick, ends)
        at = h * FEAT
        qk_back = qk_back + (pltpu.roll(query_back, at, 1) if at else query_back)
        qk_back = qk_back + pltpu.roll(keys_back, at + 4 * FEAT, 1)
    qk_back_ref[:, :] = qk_back
    level_ref[:, :] = level - level_down.T


def within_back(s, proj, values, cum, total_back, earlier, pick, ends):
    return whole_call(
        within_back_kernel,
        [((GROUP, LANES), f32), ((GROUP, 4 * LANES), f32), ((GROUP, LANES), f32)],
        proj, values, cum, total_back, earlier, pick, ends,
        flops=4 * 10**9,
        views={
            0: ((GROUP, LANES), (s, 4)),
            1: ((GROUP, 4 * LANES), (s, 0)),
            2: ((GROUP, LANES), (s, 0)),
            3: ((GROUP, 4 * LANES), (s, 0)),
            4: ((PIECES // 2, SLOT, LANES), (s, 0, 0)),
        },
    )


def later_back_kernel(
    qk_ref, first_ref, values_ref, cum_ref, rates_ref, earlier_ref, later_ref, pick_ref, ends_ref,
    qk_in_a_ref, values_in_a_ref, level_a_ref, qk_in_b_ref, values_in_b_ref, level_b_ref,
    qk_back_ref, values_back_ref, gate_back_ref,
):
    pick, ends = pick_ref[...], ends_ref[...]
    ones, before = lower_ones(), lower_ones(True)
    cum = cum_ref[:, :]
    last = cum[GROUP - 1 : GROUP, :]
    tail = jnp.exp(last - cum)
    carried = jnp.exp(last)
    qk = qk_ref[:, :]
    second = pl.program_id(0) == 1

    def either(one_ref, two_ref, columns=slice(None)):
        return jnp.where(second, two_ref[:, columns], one_ref[:, columns])

    qk_back = either(qk_in_a_ref, qk_in_b_ref)
    crossed = jnp.zeros((GROUP, LANES), f32)
    through = jnp.zeros((1, LANES), f32)
    for h in range(4):
        tile = slice(h * LANES, (h + 1) * LANES)
        later = state_rows(later_ref, h)
        left, right = factors(head_lanes(qk, h, True), pick, ends)
        held = left * right * ends[2:3]
        column = head_column(tail, h)
        features_back = column * product(values_ref[:, tile], later, NT, 2)
        values_back_ref[:, tile] = either(values_in_a_ref, values_in_b_ref, tile) + column * product(
            held, later, NN, 2
        )
        crossed = crossed + on_head_lane(
            jnp.sum(held * features_back, 1, keepdims=True), h
        )
        keys_back = factors_back(features_back, left, right, pick, ends)
        qk_back = qk_back + pltpu.roll(keys_back, (h + 4) * FEAT, 1)
        whole = jnp.sum(
            later.astype(f32) * state_rows(earlier_ref, h).astype(f32), 1, keepdims=True
        )
        whole = jnp.sum(whole, 0, keepdims=True) * head_column(carried, h)
        through = through + on_head_lane(whole, h)
    qk_back_ref[:, :] = qk_back
    step_back = (
        summed_down(ones, either(level_a_ref, level_b_ref), TN) + summed_down(before, crossed, NN) + through
    )
    gate_back_ref[:, :] = (
        step_back * rates_ref[...] * jax.nn.sigmoid(first_ref[:, :])
    )


def later_back(proj, values, cum, rates, earlier, later, pick, ends, within):
    return sequence_call(
        later_back_kernel,
        [((ROWS, LANES), f32), ((ROWS, 4 * LANES), f32), ((ROWS, LANES), f32)],
        proj, proj, values, cum, rates, earlier, later, pick, ends, *within,
        halves={0: (LANES, 4), 1: (LANES, 0), 2: (), 3: (), 5: (), 6: ()},
        flops=4 * 10**9,
    )


def unproject_kernel(
    place_ref, proj_ref, ahead_ref, taps_ref, qk_back_ref, values_back_ref, gate_back_ref, normed_ref, w_ref,
    own_ref, side_ref, back_ref, far_a_ref, far_b_ref, mixed_ref, gain_two_ref,
    part_ref, kept_ref, sent_ref,
    taps_grad_ref, taps_across_ref, proj_back_ref, out_back_ref, turned_ref,
):
    @pl.when(pl.program_id(0) == 0)
    def _():
        lane, row = lanes_of((GROUP, LANES)), rows_of((GROUP, LANES))
        taps_grad_ref[...] = jnp.zeros_like(taps_grad_ref)
        for s in range(2):
            here = slice(s * GROUP, (s + 1) * GROUP)
            for h in range(4):
                tile = slice(h * LANES, (h + 1) * LANES)
                raw = proj_ref[here, tile]
                back = values_back_ref[here, tile]
                back = jnp.where(lane < DH, back, 0.0)
                rim_two = proj_ref[ROWS + 2 * s : ROWS + 2 * s + 1, tile]
                rim_one = proj_ref[ROWS + 2 * s + 1 : ROWS + 2 * s + 2, tile]
                one = jnp.where(row == 0, rim_one, pltpu.roll(raw, 1, 0))
                two = jnp.where(row == 0, rim_two, jnp.where(row == 1, rim_one, pltpu.roll(raw, 2, 0)))
                for j, moved in enumerate((raw, one, two)):
                    taps_grad_ref[j : j + 1, tile] = taps_grad_ref[j : j + 1, tile] + jnp.sum(
                        moved * back, 0, keepdims=True
                    )
                next_one = ahead_ref[2 * s : 2 * s + 1, tile]
                next_two = ahead_ref[2 * s + 1 : 2 * s + 2, tile]
                one = jnp.where(row == GROUP - 1, next_one, pltpu.roll(back, GROUP - 1, 0))
                two = jnp.where(
                    row == GROUP - 1,
                    next_two,
                    jnp.where(row == GROUP - 2, next_one, pltpu.roll(back, GROUP - 2, 0)),
                )
                raw_back = (
                    taps_ref[0:1, tile] * back + taps_ref[1:2, tile] * one + taps_ref[2:3, tile] * two
                )
                raw_back = jnp.where(lane < DH, raw_back, 0.0)
                if h == 0:
                    gates = (lane >= GATE_LANE) & (lane < GATE_LANE + 4)
                    raw_back = jnp.where(gates, gate_back_ref[here, :], raw_back)
                proj_back_ref[here, tile] = raw_back.astype(bf16)
            proj_back_ref[here, 4 * LANES :] = qk_back_ref[here, :].astype(bf16)
        for h in range(GROUPS):
            tile = slice(h * LANES, (h + 1) * LANES)
            taps_across_ref[tile, :] = pltpu.roll(
                jnp.concatenate(
                    [taps_grad_ref[:, tile], jnp.zeros((LANES - 8, LANES), f32)], 0
                ).T,
                TAPS_LANE,
                1,
            )
        for k, other in enumerate((0, 1, 3, 2)):
            turned_ref[k * OWN : (k + 1) * OWN] = own_slice(
                mixed_ref, jnp.bitwise_xor(place_ref[0], other)
            )

    part = lax.dot_general(
        proj_back_ref[...], w_ref[...], (NT, ((), ())), preferred_element_type=f32
    ).astype(bf16)
    store_by_owner(part_ref, part, place_ref[0])
    wide = w_ref.shape[1]
    grad_in = lax.dot_general(
        normed_ref[...], proj_back_ref[...], (TN, ((), ())), preferred_element_type=f32
    )
    weights = w_ref[...].astype(f32)
    gain_one = jnp.sum(grad_in * weights, 1, keepdims=True)
    gain_one = gain_one / weights[:, GAIN_LANE : GAIN_LANE + 1]
    gain_two = gain_two_ref[...].T[:, 0:1]
    first = grad_in[:, :LANES]
    spot = lanes_of(first.shape)
    first = jnp.where(
        spot == GAIN_LANE, gain_one, jnp.where(spot == GAIN_LANE + 1, gain_two, first)
    )
    out_back_ref[:OWN] = own_ref[...]
    out_back_ref[OWN : 2 * OWN] = side_ref[...]
    out_back_ref[2 * OWN : 3 * OWN] = back_ref[...]
    out_back_ref[3 * OWN : 3 * OWN + OWN // 2] = far_a_ref[...]
    out_back_ref[3 * OWN + OWN // 2 :] = far_b_ref[...]
    grad_out = lax.dot_general(
        out_back_ref[...], turned_ref[...], (TN, ((), ())), preferred_element_type=f32
    )
    core = place_ref[1]

    each = DH // 8
    few = lanes_of((SHARD, LANES))
    spare = (few >= TAPS_LANE) & (few < TAPS_LANE + TAPS) & (rows_of((SHARD, LANES)) < each)

    def store(ref, parity):
        for k in range(ref.shape[0]):
            r = 2 * k + parity
            here = slice(r * SHARD, (r + 1) * SHARD)
            head = pl.program_id(0) * (GROUPS // 2) + r // 8
            taps = taps_across_ref[pl.ds(pl.multiple_of(head * LANES, LANES), LANES), :]
            at = (r % 8) * each
            taps = pltpu.roll(taps, LANES - at, 0) if at else taps
            ref[k, :, :LANES] = jnp.where(spare, taps[:SHARD], first[here]).astype(bf16)
            ref[k, :, LANES:wide] = grad_in[here, LANES:].astype(bf16)
            ref[k, :, wide:] = grad_out[here].astype(bf16)

    for parity in range(2):

        @pl.when(core == parity)
        def _():
            store(kept_ref, parity)
            store(sent_ref, 1 - parity)


def unproject(
    place, proj, ahead, taps, qk_back, values_back, gate_back, normed, w_in, out_parts, mixed, gain_two
):
    width, wide = w_in.shape
    half, shards = width // 2, width // SHARD // 4
    args = (proj, ahead, taps, qk_back, values_back, gate_back, normed, w_in, *out_parts, mixed)
    args += (gain_two,)

    def whole(shape):
        return pl.BlockSpec(shape, lambda i: (0,) * len(shape))

    specs = [whole(a.shape) for a in args]
    specs[0] = pl.BlockSpec((proj.shape[0], 4 * LANES), lambda i: (0, 0))
    specs[7] = pl.BlockSpec((half, wide), lambda i: (i, 0))
    for k in (6, 8, 9, 10, 11, 12, 14):
        specs[k] = pl.BlockSpec((args[k].shape[0], half), lambda i: (0, i))
    sums = pl.BlockSpec((shards, SHARD, wide + 4 * LANES), lambda i: (i, 0, 0))
    return pl.pallas_call(
        unproject_kernel,
        grid=(2,),
        out_shape=[jax.ShapeDtypeStruct((4, OWN, width), bf16)]
        + [jax.ShapeDtypeStruct((2 * shards, SHARD, wide + 4 * LANES), bf16)] * 2,
        in_specs=[pl.BlockSpec(memory_space=pltpu.SMEM)] + specs,
        out_specs=[pl.BlockSpec((4, OWN, half), lambda i: (0, 0, i)), sums, sums],
        scratch_shapes=[
            pltpu.VMEM((8, 4 * LANES), f32),
            pltpu.VMEM((4 * LANES, LANES), f32),
            pltpu.VMEM((ROWS, wide), bf16),
            pltpu.VMEM((ROWS, half), bf16),
            pltpu.VMEM((ROWS, 4 * LANES), bf16),
        ],
        compiler_params=pltpu.CompilerParams(vmem_limit_bytes=60 * MIB),
        cost_estimate=pl.CostEstimate(
            flops=4 * 10**9, bytes_accessed=16 * 10**6, transcendentals=0
        ),
    )(place, *args)


BLOCK = 256
HIDDEN = 1280
OUT = 16 * LANES
SHARD = 56
SPACED = 64


def middle_kernel(
    place_ref, own_ref, side_ref, back_ref, far_a_ref, far_b_ref, out_ref, rows_ref, gains_ref,
    cotangent_ref, gate_ref, up_ref, down_ref, both_ref,
    middle_ref, unit_ref, scale_ref, normed_ref, acts_ref, two_ref,
    mixed_ref, sum_ref,
):
    place, step = place_ref[0], pl.program_id(0)
    blocks = HIDDEN // BLOCK

    @pl.when(step == 0)
    def _():
        mixed_ref[place] = own_ref[...]
        mixed_ref[jnp.bitwise_xor(place, 1)] = side_ref[...]
        mixed_ref[jnp.bitwise_xor(place, 3)] = back_ref[...]
        mixed_ref[jnp.bitwise_xor(place, 2), :GROUP, :] = far_a_ref[...]
        mixed_ref[jnp.bitwise_xor(place, 2), GROUP:, :] = far_b_ref[...]
        sum_ref[...] = rows_ref[...].astype(f32)

    @pl.when(step < GROUPS)
    def _():
        for at in range(0, out_ref.shape[0], BLOCK):
            here = slice(at, at + BLOCK)
            sum_ref[:, here] += lax.dot_general(
                mixed_ref[step], out_ref[here, :], (NT, ((), ())), preferred_element_type=f32
            )

    @pl.when(step == GROUPS - 1)
    def _():
        for at in range(0, ROWS, OWN):
            here = slice(at, at + OWN)
            middle = sum_ref[here, :]
            scale = lax.rsqrt(jnp.mean(middle * middle, -1, keepdims=True) + eps_norm)
            normed_ref[here, :] = (middle * scale * gains_ref[1:2]).astype(bf16)
        middle = own_slice(sum_ref, place)
        scale = lax.rsqrt(jnp.mean(middle * middle, -1, keepdims=True) + eps_norm)
        middle_ref[...] = middle
        unit_ref[...] = middle * scale
        scale_ref[...] = jnp.broadcast_to(scale, scale_ref.shape)

    @pl.when((step >= GROUPS) & (step < GROUPS + blocks))
    def _():
        normed = normed_ref[...]
        gate = jnp.dot(normed, gate_ref[...], preferred_element_type=f32)
        up = jnp.dot(normed, up_ref[...], preferred_element_type=f32)
        hidden_back = jnp.dot(cotangent_ref[...], down_ref[...], preferred_element_type=f32)
        sigma = jax.nn.sigmoid(gate)
        silu = gate * sigma
        at = pl.multiple_of((step - GROUPS) * BLOCK, BLOCK)
        acts_ref[:, pl.ds(at, BLOCK)] = (
            hidden_back * up * sigma * (1.0 + gate * (1.0 - sigma))
        ).astype(bf16)
        acts_ref[:, pl.ds(HIDDEN + at, BLOCK)] = (hidden_back * silu).astype(bf16)
        acts_ref[:, pl.ds(2 * HIDDEN + at, BLOCK)] = (silu * up).astype(bf16)

    @pl.when(step >= GROUPS + blocks)
    def _():
        two_ref[...] = lax.dot_general(
            acts_ref[:, : 2 * HIDDEN], both_ref[...], (NT, ((), ())), preferred_element_type=f32
        ).astype(bf16)


def middle_both_ways(place, mixed_parts, weights, rows, gains, back):
    width = rows.shape[1]
    blocks, outs = HIDDEN // BLOCK, width // BLOCK
    columns = OUT // GROUPS

    def whole(shape):
        return pl.BlockSpec(shape, lambda i: (0,) * len(shape))

    def clipped(i, first, count):
        return jnp.clip(i - first, 0, count - 1)

    def block_of(which):
        at = OUT // BLOCK + which * blocks
        return pl.BlockSpec((width, BLOCK), lambda i: (0, at + clipped(i, GROUPS, blocks)))

    last = GROUPS + blocks
    specs = [whole(part.shape) for part in mixed_parts]
    specs.append(pl.BlockSpec((width, columns), lambda i: (0, clipped(i, 0, GROUPS))))
    specs += [whole(rows.shape), whole(gains.shape), whole(back.shape)]
    specs += [block_of(0), block_of(1), block_of(2)]
    specs.append(
        pl.BlockSpec(
            (pl.Element(BLOCK), pl.Element(2 * HIDDEN)),
            lambda i: (clipped(i, last, outs) * BLOCK, OUT),
        )
    )
    results = [
        ((OWN, width), f32),
        ((OWN, width), f32),
        ((OWN, LANES), f32),
        ((ROWS, width), bf16),
        ((ROWS, 3 * HIDDEN), bf16),
        ((ROWS, width), bf16),
    ]
    out_specs = [whole(s) for s, d in results]
    out_specs[-1] = pl.BlockSpec((ROWS, BLOCK), lambda i: (0, clipped(i, last, outs)))
    return pl.pallas_call(
        middle_kernel,
        grid=(last + outs,),
        out_shape=[jax.ShapeDtypeStruct(s, d) for s, d in results],
        in_specs=[pl.BlockSpec(memory_space=pltpu.SMEM)] + specs,
        out_specs=out_specs,
        scratch_shapes=[
            pltpu.VMEM((GROUPS, ROWS, columns), bf16),
            pltpu.VMEM((ROWS, width), f32),
        ],
        compiler_params=pltpu.CompilerParams(vmem_limit_bytes=60 * MIB),
        cost_estimate=pl.CostEstimate(
            flops=16 * 10**9, bytes_accessed=40 * 10**6, transcendentals=0
        ),
    )(place, *mixed_parts, weights, rows, gains, back, weights, weights, weights, weights)


def ffn_out_kernel(place_ref, acts_ref, down_ref, out_ref):
    value = lax.dot_general(
        acts_ref[...], down_ref[...], (NT, ((), ())), preferred_element_type=f32
    ).astype(bf16)
    store_by_owner(out_ref, value, place_ref[0])


def ffn_out(place, acts, weights):
    width = weights.shape[0]
    return pl.pallas_call(
        ffn_out_kernel,
        grid=(width // BLOCK,),
        out_shape=jax.ShapeDtypeStruct((4, OWN, width), bf16),
        in_specs=[
            pl.BlockSpec(memory_space=pltpu.SMEM),
            pl.BlockSpec((ROWS, HIDDEN), lambda i: (0, 2)),
            pl.BlockSpec(
                (pl.Element(BLOCK), pl.Element(HIDDEN)), lambda i: (i * BLOCK, OUT + 2 * HIDDEN)
            ),
        ],
        out_specs=pl.BlockSpec((4, OWN, BLOCK), lambda i: (0, 0, i)),
        compiler_params=pltpu.CompilerParams(vmem_limit_bytes=60 * MIB),
        cost_estimate=pl.CostEstimate(
            flops=3 * 10**9, bytes_accessed=8 * 10**6, transcendentals=0
        ),
    )(place, acts, weights)


def ffn_grads_kernel(normed_ref, back_ref, acts_ref, grads_ref):
    def spaced(rows_ref):
        grad = lax.dot_general(
            rows_ref[...], acts_ref[...], (TN, ((), ())), preferred_element_type=f32
        )
        for r in range(grad.shape[0] // SHARD):
            grads_ref[r * SPACED : r * SPACED + SHARD, :] = grad[
                r * SHARD : (r + 1) * SHARD
            ].astype(bf16)
            grads_ref[r * SPACED + SHARD : (r + 1) * SPACED, :] = jnp.zeros(
                (SPACED - SHARD, grad.shape[1]), bf16
            )

    both = pl.program_id(0) < 2 * HIDDEN // WIDER

    @pl.when(both)
    def _():
        spaced(normed_ref)

    @pl.when(jnp.logical_not(both))
    def _():
        spaced(back_ref)


WIDER = 640


def ffn_grads(normed, back, acts):
    width = normed.shape[1]
    whole = pl.BlockSpec((ROWS, width), lambda i: (0, 0))
    return pl.pallas_call(
        ffn_grads_kernel,
        grid=(3 * HIDDEN // WIDER,),
        out_shape=jax.ShapeDtypeStruct((width // SHARD * SPACED, 3 * HIDDEN), bf16),
        in_specs=[whole, whole, pl.BlockSpec((ROWS, WIDER), lambda i: (0, i))],
        out_specs=pl.BlockSpec((width // SHARD * SPACED, WIDER), lambda i: (0, i)),
        compiler_params=pltpu.CompilerParams(vmem_limit_bytes=60 * MIB),
        cost_estimate=pl.CostEstimate(
            flops=7 * 10**9, bytes_accessed=20 * 10**6, transcendentals=0
        ),
    )(normed, back, acts)


def order_columns(heads):
    import numpy as np

    place = np.zeros((5 * LANES, 5 * LANES), np.float32)
    for h in range(heads):
        at = h * (2 * FEAT + DH + 1)
        for i in range(FEAT):
            place[at + i, heads * LANES + h * FEAT + i] = 1.0
            place[at + FEAT + i, heads * LANES + (heads + h) * FEAT + i] = 1.0
        for i in range(DH):
            place[at + 2 * FEAT + i, h * LANES + i] = 1.0
        place[at + 2 * FEAT + DH, GATE_LANE + h] = 1.0
    return jnp.asarray(place, bf16)


def order_heads(heads):
    import numpy as np

    place = np.zeros((heads * DH, heads * LANES), np.float32)
    for h in range(heads):
        for i in range(DH):
            place[h * DH + i, h * LANES + i] = 1.0
    return jnp.asarray(place, bf16)


def prepare_kernel(
    rank_ref, in_ref, out_ref, gate_ref, up_ref, down_ref, taps_ref,
    gains_ref, gains_first_ref, gains_second_ref, place_ref, tiles_ref,
    shard_ref, out_shard_ref, rest_ref, few_ref,
):
    wide = 5 * LANES
    columns = in_ref.shape[1]
    whole = jnp.dot(
        in_ref[...].astype(bf16), place_ref[:columns, :], preferred_element_type=f32
    )
    spot = jnp.where(
        lanes_of((2, wide)) == rows_of((2, wide)) + GAIN_LANE, 1.0, 0.0
    ).astype(bf16)
    gains = lax.dot_general(
        gains_ref[...].astype(bf16), spot, (TN, ((), ())), preferred_element_type=f32
    )
    for k in range(shard_ref.shape[0]):
        shard_ref[k, :SHARD, :] = (whole + gains).astype(bf16)
    rank = rank_ref[0]
    own = taps_ref.shape[1]
    each = DH // own
    first = (rank // each) * LANES + (rank % each) * own
    spot = jnp.where(
        lanes_of((own, wide)) == rows_of((own, wide)) + first, 1.0, 0.0
    ).astype(bf16)
    taps = jnp.dot(taps_ref[...].astype(bf16), spot, preferred_element_type=f32)
    rows = [taps]
    for ref in (gains_ref, gains_first_ref, gains_second_ref):
        few_ref[...] = jnp.zeros_like(few_ref)
        few_ref[0:2, :SHARD] = ref[...]
        both = few_ref[...]
        line = both + pltpu.roll(pltpu.roll(both, SHARD, 1), 7, 0)
        parts = [part.astype(f32)[0:1] for part in three_parts(line)]
        rows.append(jnp.concatenate(parts + [jnp.zeros((1, wide - 3 * LANES), f32)], 1))
    rows.append(jnp.zeros((SPACED - SHARD - TAPS - 3, wide), f32))
    for k in range(shard_ref.shape[0]):
        shard_ref[k, SHARD:, :] = jnp.concatenate(rows, 0).astype(bf16)
    out_shard_ref[...] = jnp.dot(
        out_ref[...].astype(bf16), tiles_ref[...], preferred_element_type=f32
    ).astype(bf16)
    rest_ref[...] = jnp.zeros_like(rest_ref)
    units = gate_ref.shape[1]
    rest_ref[:, :units] = gate_ref[...].astype(bf16)
    rest_ref[:, HIDDEN : HIDDEN + units] = up_ref[...].astype(bf16)
    rest_ref[:, 2 * HIDDEN : 2 * HIDDEN + units] = down_ref[...].astype(bf16)


def prepare(rank, *args):
    return whole_call(
        prepare_kernel,
        [
            ((16, SPACED, 5 * LANES), bf16),
            ((SHARD, 4 * LANES), bf16),
            ((SHARD, 3 * HIDDEN), bf16),
        ],
        rank, *args,
        scratch=[pltpu.VMEM((8, LANES), f32)],
        scalars=1,
    )


def moved_moments(weight, first, second, grad):
    fix = 1.0 - beta_value**STEP
    moment = beta_value * first + (1.0 - beta_value) * grad
    square = beta_value * second + (1.0 - beta_value) * grad * grad
    direction = moment / fix / (jnp.sqrt(square / fix) + eps_adam) + decay_rate * weight
    return moment, square, direction


def adapted(params, outs, place, grad):
    weight = params[0][...]
    moment, square, direction = moved_moments(weight, params[1][...], params[2][...], grad)
    outs[0][...] = moment
    outs[1][...] = square
    outs[2][...] = direction
    both = [
        jnp.sum(jnp.sum(v * v, 1, keepdims=True), 0, keepdims=True) for v in (weight, direction)
    ]
    lane = lanes_of((1, LANES))
    return jnp.where(lane == place, both[0], jnp.where(lane == place + 1, both[1], 0.0))


def ffn_moments_kernel(ffn_ref, *refs):
    params, outs, sums_ref = refs[:9], refs[9:-1], refs[-1]
    units = params[0].shape[1]
    sums = jnp.zeros((1, LANES), f32)
    for k in range(3):
        grad = ffn_ref[:SHARD, k * HIDDEN : k * HIDDEN + units].astype(f32)
        three = slice(3 * k, 3 * k + 3)
        sums = sums + adapted(params[three], outs[three], 4 + 2 * k, grad)
    sums_ref[...] = jnp.broadcast_to(sums, sums_ref.shape)


def ffn_moments(ffn, params):
    outs = [(param.shape, f32) for param in params]
    return whole_call(ffn_moments_kernel, outs + [((8, LANES), f32)], ffn, *params)


def moments_kernel(mixer_ref, place_ref, tiles_ref, ffn_sums_ref, *refs):
    params, outs, sums_ref = refs[:9], refs[9:-1], refs[-1]

    wide = 5 * LANES
    mixer = mixer_ref[0].astype(f32)
    for k in range(1, mixer_ref.shape[0]):
        mixer = mixer + mixer_ref[k].astype(f32)
    sums = ffn_sums_ref[0:1, :]
    grad_in = picked(mixer[:, :wide], place_ref[...], NT)
    sums = sums + adapted(params[0:3], outs[0:3], 0, grad_in[:, : params[0].shape[1]])
    sums = sums + adapted(params[3:6], outs[3:6], 2, picked(mixer[:, wide:], tiles_ref[...], NT))
    across = jnp.concatenate([mixer[:, :LANES], jnp.zeros((LANES - SHARD, LANES), f32)], 0).T
    taps = across[TAPS_LANE : TAPS_LANE + TAPS, : params[6].shape[1]]
    sums = sums + adapted(params[6:9], outs[6:9], 10, taps)
    ones = across[GAIN_LANE : GAIN_LANE + 1]
    twos = across[GAIN_LANE + 1 : GAIN_LANE + 2]
    few = lanes_of((1, LANES))
    line = jnp.where(few < SHARD, ones, 0.0) + pltpu.roll(
        jnp.broadcast_to(jnp.where(few < SHARD, twos, 0.0), (8, LANES)), SHARD, 1
    )[0:1]
    both = jnp.concatenate([sums, line], 1)
    sums_ref[...] = jnp.broadcast_to(both[None], sums_ref.shape)


def moments(mixer, place, tiles, ffn_sums, params):
    outs = [(param.shape, f32) for param in params] + [((LANES, 1, 2 * LANES), f32)]
    return whole_call(
        moments_kernel, outs, mixer, place, tiles, ffn_sums, *params
    )


def update_kernel(rank_ref, totals_ref, states_ref, *refs):
    weights, directions, outs = refs[:6], refs[6:12], refs[12:18]
    gains_refs, norms_ref = refs[18:21], refs[21]
    totals = totals_ref[:, 0, :]
    sums = jnp.sum(totals[:, :LANES], 0, keepdims=True)
    lane = lanes_of((1, LANES))
    grouped = jnp.where(
        lanes_of((32, LANES)) // 4 == rows_of((32, LANES)), 1.0, 0.0
    ).astype(bf16)
    grad = summed_down(grouped, totals[:, LANES:], NN)
    moment, square, direction = moved_moments(
        states_ref[0], states_ref[1], states_ref[2], grad
    )
    live = lanes_of((32, LANES)) < 2 * SHARD
    for place, value in ((12, states_ref[0]), (13, direction)):
        value = jnp.where(live, value, 0.0)
        value = jnp.sum(jnp.sum(value * value, 1, keepdims=True), 0, keepdims=True)
        sums = jnp.where(lane == place, value, sums)
    norms = jnp.sqrt(sums)
    each = [
        jnp.sum(
            jnp.where(lanes_of((8, LANES)) == 2 * rows_of((8, LANES)) + k, norms, 0.0),
            1,
            keepdims=True,
        )
        for k in range(2)
    ]
    norms_ref[...] = jnp.where(lanes_of((8, 2)) == 0, each[0], each[1])[:7]

    def ratio(index):
        return norms[:, 2 * index : 2 * index + 1] / norms[:, 2 * index + 1 : 2 * index + 2]

    for index in range(6):
        outs[index][...] = (
            weights[index][...] - learn_rate * ratio(index) * directions[index][...]
        )
    updated = states_ref[0] - learn_rate * ratio(6) * direction
    for ref, value in zip(gains_refs, (updated, moment, square)):
        own = jnp.where(rows_of((32, LANES)) == rank_ref[0], value, 0.0)
        own = jnp.broadcast_to(jnp.sum(own, 0, keepdims=True), (8, LANES))
        ref[0:1, :] = own[0:1, :SHARD]
        ref[1:2, :] = pltpu.roll(own, LANES - SHARD, 1)[0:1, :SHARD]


def update(rank, totals, states, weights, directions):
    outs = [(w.shape, f32) for w in weights] + [((2, SHARD), f32)] * 3 + [((7, 2), f32)]
    return whole_call(
        update_kernel, outs, rank, totals, states, *weights, *directions, scalars=1
    )


def per_device(
    tokens,
    cotangent,
    lengths,
    rate_codes,
    inproj,
    inproj_first,
    inproj_second,
    outproj,
    outproj_first,
    outproj_second,
    gateproj,
    gateproj_first,
    gateproj_second,
    upproj,
    upproj_first,
    upproj_second,
    downproj,
    downproj_first,
    downproj_second,
    convtaps,
    convtaps_first,
    convtaps_second,
    normgains,
    normgains_first,
    normgains_second,
):
    seqs, group, width = tokens.shape
    heads = rate_codes.shape[0]
    lag = TAPS - 1
    rank = lax.axis_index(SEQ).reshape(1)
    core = lax.axis_index("seq_2")
    peer = lax.axis_index("mp").reshape(1)
    pick, ends = selections()
    place, tiles = order_columns(heads), order_heads(heads)

    shards, out_shard, rest_shard = prepare(
        rank, inproj, outproj.T, gateproj, upproj, downproj.T, convtaps,
        normgains, normgains_first, normgains_second, place, tiles,
    )
    got = lax.all_to_all(shards, ("seq_0", "seq_1"), 0, 0, tiled=True)
    other = lax.ppermute(got, "seq_2", SWAP)
    low, high = peer[0] % 2, peer[0] // 2

    def beside(mine, theirs, bit):
        return jnp.where(
            bit == 0, jnp.concatenate([mine, theirs], 1), jnp.concatenate([theirs, mine], 1)
        )

    out_pair = beside(out_shard, lax.ppermute(out_shard, "mp", SIDE), low)
    out_shards = beside(out_pair, lax.ppermute(out_pair, "mp", BACK), high)
    weights_shard = jnp.concatenate([out_shards, rest_shard], 1)
    weights_shard, got = lax.optimization_barrier((weights_shard, got))
    weights = lax.all_gather(weights_shard, SEQ, axis=0, tiled=True)

    rows = tokens.reshape(-1, width)
    rim = shifted(tokens[:, group - lag :], SEQ, 1).reshape(-1, width)
    rim = jnp.pad(rim, ((0, 16 - seqs * lag), (0, 0)))
    positions = rank * group + jnp.arange(group, dtype=jnp.int32)
    keep = (positions[None, :] < lengths[:, None]).astype(f32).reshape(-1, 1)
    back = (cotangent.reshape(-1, width).astype(f32) * keep).astype(bf16)
    rates = -jnp.exp2(-rate_codes.astype(f32) / 4.0)
    rates = jnp.pad(rates[None], ((0, 0), (GATE_LANE, LANES - GATE_LANE - heads)))
    normed_one, proj, w_in, gains, taps, states, values, cum, sent = project(
        core.reshape(1), rows, rim, got, other, rates, pick, ends
    )
    earlier, decay = earlier_states(sent)
    inside = within(proj, values, cum)
    total, mixed = mix(proj, cum, inside, earlier, pick, ends)

    middle, unit_two, scale_two, normed_two, acts, two_part = middle_both_ways(
        peer, gather_parts(mixed), weights, rows, gains, back
    )
    two_back = lax.psum_scatter(two_part, "mp", scatter_dimension=0, tiled=True)
    ffn_part = ffn_out(peer, acts, weights)
    two_back, ffn_part = lax.optimization_barrier((two_back, ffn_part))
    ffn_sums = lax.psum_scatter(
        ffn_grads(normed_two, back, acts), SEQ, scatter_dimension=0, tiled=True
    )
    middle_back, gain_two, out_own, mixed_back = turn(
        peer, two_back, unit_two, scale_two, back, gains, weights
    )
    mixed_back = lax.all_to_all(mixed_back, "mp", 0, 0, tiled=True).reshape(ROWS, -1)

    total_back, sent = unmix(mixed_back, total, proj, cum, pick, ends)
    ffn_part, out_own, sent = lax.optimization_barrier((ffn_part, out_own, sent))
    later, summed = later_states(sent, decay)
    within_a = within_back(0, proj, values, cum, total_back, earlier, pick, ends)
    total_back, _ = lax.optimization_barrier((total_back, summed))
    within_b = within_back(1, proj, values, cum, total_back, earlier, pick, ends)
    out_parts = gather_parts(out_own)
    ffn_terms = scatter_terms(ffn_part)
    qk_back, values_back, gate_back = later_back(
        proj, values, cum, rates, earlier, later, pick, ends, within_a + within_b
    )
    edge = values_back.reshape(seqs, group, -1)[:, :lag]
    ahead = shifted(edge, SEQ, -1).reshape(seqs * lag, -1)
    ahead = jnp.concatenate([ahead, jnp.zeros_like(ahead)], 0)
    ahead, ffn_terms = lax.optimization_barrier((ahead, ffn_terms))
    one_part, kept, sent = unproject(
        jnp.concatenate([peer, core.reshape(1)]), proj, ahead, taps, qk_back, values_back, gate_back, normed_one, w_in, out_parts, mixed,
        gain_two,
    )

    swapped = lax.ppermute(sent, "seq_2", SWAP)
    mixer_part = (kept.astype(f32) + swapped.astype(f32)).astype(bf16)

    mixer_got = lax.all_to_all(mixer_part, ("seq_0", "seq_1"), 0, 0, tiled=True)
    one_terms = scatter_terms(one_part, mixer_part)
    block_out = lax.all_gather(
        block_outs(peer, ffn_terms, middle, jnp.broadcast_to(keep, (ROWS, LANES))),
        "mp",
        axis=0,
        tiled=True,
    )

    mixer_params = (inproj, inproj_first, inproj_second)
    mixer_params += (outproj.T, outproj_first.T, outproj_second.T)
    mixer_params += (convtaps, convtaps_first, convtaps_second)
    ffn_params = (gateproj, gateproj_first, gateproj_second)
    ffn_params += (upproj, upproj_first, upproj_second)
    ffn_params += (downproj.T, downproj_first.T, downproj_second.T)
    *ffn_moved, ffn_squares = ffn_moments(ffn_sums, ffn_params)
    *moved, sums = moments(mixer_got, place, tiles, ffn_squares, mixer_params)
    moved = moved[:6] + ffn_moved + moved[6:]
    weights_old = mixer_params[0:6:3] + ffn_params[0::3] + mixer_params[6:7]
    token_own = token_grads(peer, one_terms, rows, middle_back, gains)
    back, side = to_neighbours(token_own)
    totals = lax.all_to_all(sums, ALL, 0, 0, tiled=True)
    token_grad = assembled(peer, (token_own, side, back, *passed_on(back, side)))
    *updated, gains_new, gains_moment, gains_square, norms = update(
        rank, totals, states, weights_old, moved[2::3]
    )
    results = [block_out.reshape(tokens.shape), token_grad.reshape(tokens.shape)]
    for index in range(6):
        for value in (updated[index], moved[3 * index], moved[3 * index + 1]):
            results.append(value.T if index in (1, 4) else value)
    results += [gains_new, gains_moment, gains_square, norms]
    return tuple(results)


def solution(mesh):
    split = Mesh(mesh.devices.reshape(4, 4, 2, mesh.shape["mp"]), ("seq_0", "seq_1", "seq_2", "mp"))
    in_specs = (
        P(None, SEQ, None),
        P(None, SEQ, None),
        P(),
        P("mp"),
        P(SEQ, "mp"),
        P(SEQ, "mp"),
        P(SEQ, "mp"),
        P("mp", SEQ),
        P("mp", SEQ),
        P("mp", SEQ),
        P(SEQ, "mp"),
        P(SEQ, "mp"),
        P(SEQ, "mp"),
        P(SEQ, "mp"),
        P(SEQ, "mp"),
        P(SEQ, "mp"),
        P("mp", SEQ),
        P("mp", SEQ),
        P("mp", SEQ),
        P(None, MP_SEQ),
        P(None, MP_SEQ),
        P(None, MP_SEQ),
        P(None, SEQ),
        P(None, SEQ),
        P(None, SEQ),
    )
    out_specs = (
        P(None, SEQ, None),
        P(None, SEQ, None),
        P(SEQ, "mp"),
        P(SEQ, "mp"),
        P(SEQ, "mp"),
        P("mp", SEQ),
        P("mp", SEQ),
        P("mp", SEQ),
        P(SEQ, "mp"),
        P(SEQ, "mp"),
        P(SEQ, "mp"),
        P(SEQ, "mp"),
        P(SEQ, "mp"),
        P(SEQ, "mp"),
        P("mp", SEQ),
        P("mp", SEQ),
        P("mp", SEQ),
        P(None, MP_SEQ),
        P(None, MP_SEQ),
        P(None, MP_SEQ),
        P(None, SEQ),
        P(None, SEQ),
        P(None, SEQ),
        P(),
    )
    return jax.shard_map(
        per_device, mesh=split, in_specs=in_specs, out_specs=out_specs, check_vma=False
    )
```

```python
import math

import jax
import jax.numpy as jnp
from jax import lax
from jax.experimental import pallas as pl
from jax.experimental.pallas import tpu as pltpu
from jax.sharding import Mesh
from jax.sharding import PartitionSpec as P

DH = 112
FEAT = 16
TAPS = 3
STEP = 7
LANES = 128
SEQ = ("seq_0", "seq_1", "seq_2")
ALL = ("seq_0", "seq_1", "seq_2", "mp")
MP_SEQ = ("mp", "seq_0", "seq_1", "seq_2")

f32 = jnp.float32
bf16 = jnp.bfloat16
highest = lax.Precision.HIGHEST
root_half = 0.5**0.5
eps_norm = 1e-05
eps_adam = 1e-06
decay_rate = 0.01
learn_rate = 0.3
beta_value = 0.5

SIDE = [(i, i ^ 1) for i in range(4)]
BACK = [(i, 3 - i) for i in range(4)]
SWAP = [(0, 1), (1, 0)]


def shifted(value, axis, steps):
    count = lax.axis_size(axis)
    first, last = (max(0, -steps), min(count, count - steps))
    return lax.ppermute(value, axis, [(source, source + steps) for source in range(first, last)])


SPAN_LANE = DH
GROUPS = 4
GATE_LANE = DH
GAIN_LANE = DH + 4
TAPS_LANE = DH + 6
GROUP = 256
ROWS = 512
SIDES = 256
PIECE = 40
SLOT = 48
PIECES = 32
MIB = 1 << 20


def selections():
    import numpy as np

    pick = np.zeros((2 * LANES, 2 * SIDES), np.float32)
    ends = np.zeros((8, SIDES), np.float32)
    ends[0, 0] = ends[1, 0] = ends[2, 0] = 1.0
    lane = 1
    for i in range(FEAT):
        pick[i, lane] = 0.5
        ends[1, lane] = ends[2, lane] = 1.0
        lane += 1
    for i in range(FEAT):
        for j in range(i, FEAT):
            pick[i, lane] = 0.5
            pick[j, SIDES + lane] = 0.5
            ends[2, lane] = root_half if i == j else 1.0
            lane += 1
    pick[LANES:] = pick[:LANES]
    return jnp.asarray(pick, bf16), jnp.asarray(ends)


def two_parts(value):
    high = value.astype(bf16)
    return high, (value - high.astype(f32)).astype(bf16)


def three_parts(value):
    high = value.astype(bf16)
    rest = value - high.astype(f32)
    mid = rest.astype(bf16)
    return high, mid, (rest - mid.astype(f32)).astype(bf16)


def product(a, b, contract, passes=3):
    dims = (contract, ((), ()))

    def once(x, y):
        return lax.dot_general(x, y, dims, preferred_element_type=f32)

    if passes == 1:
        return once(a.astype(bf16), b.astype(bf16))
    a_high, a_low = two_parts(a)
    if passes == 2:
        b = b.astype(bf16)
        return once(a_high, b) + once(a_low, b)
    b_high, b_low = two_parts(b)
    return once(a_high, b_high) + (once(a_high, b_low) + once(a_low, b_high))


NN = ((1,), (0,))
NT = ((1,), (1,))
TN = ((0,), (0,))


def lanes_of(shape):
    return lax.broadcasted_iota(jnp.int32, shape, len(shape) - 1)


def rows_of(shape):
    return lax.broadcasted_iota(jnp.int32, shape, 0)


def lower_ones(strict=False):
    row, lane = rows_of((GROUP, GROUP)), lanes_of((GROUP, GROUP))
    return jnp.where(row > lane if strict else row >= lane, 1.0, 0.0).astype(bf16)


def summed_down(ones, value, contract):
    high, mid, low = (
        lax.dot_general(ones, part, (contract, ((), ())), preferred_element_type=f32)
        for part in three_parts(value)
    )
    return low + mid + high


def picked(value, place, contract):
    high, mid, low = (
        lax.dot_general(part, place, (contract, ((), ())), preferred_element_type=f32)
        for part in three_parts(value)
    )
    return low + mid + high


def head_lanes(tile, head, keys):
    first = (4 if keys else 0) * FEAT + head * FEAT
    return pltpu.roll(tile, (LANES - first) % LANES, 1) if first else tile


def factors(moved, pick, ends):
    high, low = two_parts(moved)
    found = lax.dot_general(
        jnp.concatenate([high, low], 1), pick, (NN, ((), ())), preferred_element_type=f32
    )
    return found[:, :SIDES] + ends[0:1], found[:, SIDES:] + ends[1:2]


def factors_back(upstream, one, two, pick, ends):
    scaled = upstream * ends[2:3]
    both = jnp.concatenate([scaled * two, scaled * one], 1)
    return product(both, pick[:LANES], NT, 2)


def scores(tile, head):
    only = lanes_of((GROUP, LANES)) < FEAT
    query = jnp.where(only, head_lanes(tile, head, False), 0.0) * 0.25
    keys = jnp.where(only, head_lanes(tile, head, True), 0.0)
    q_high, k_high = query.astype(bf16), keys.astype(bf16)
    q_wide, k_wide = q_high.astype(f32), k_high.astype(f32)
    q_both = (q_wide + pltpu.roll(query - q_wide, FEAT, 1)).astype(bf16)
    k_both = (pltpu.roll(k_wide, FEAT, 1) + (keys - k_wide)).astype(bf16)
    left = jnp.concatenate([q_high, q_both], 1)
    right = jnp.concatenate([k_high, k_both], 1)
    return lax.dot_general(left, right, (NT, ((), ())), preferred_element_type=f32)


def decays(cum, cum_across, head):
    row, lane = rows_of((GROUP, GROUP)), lanes_of((GROUP, GROUP))
    at = GATE_LANE + head
    diff = cum[:, at : at + 1] - cum_across[at : at + 1, :]
    return jnp.where(row >= lane, jnp.exp(jnp.minimum(diff, 0.0)), 0.0)


def head_column(tile, head):
    at = GATE_LANE + head
    return tile[:, at : at + 1]


def on_head_lane(column, head):
    return jnp.where(lanes_of((column.shape[0], LANES)) == GATE_LANE + head, column, 0.0)


def state_rows(pieces_ref, pair):
    parts = [pieces_ref[4 * pair + q, :PIECE, :].astype(f32) for q in range(4)]
    parts.append(jnp.zeros((SIDES - 4 * PIECE, LANES), f32))
    return jnp.concatenate(parts, 0).astype(bf16)


def store_pieces(ref, pair, state):
    for q in range(4):
        ref[4 * pair + q, :PIECE, :] = state[q * PIECE : (q + 1) * PIECE].astype(bf16)


def whole_call(body, outs, *args, scratch=(), flops=10**9, limit=60, views=None, scalars=0):
    views = views or {}
    shapes = [views.get(i, (a.shape,))[0] for i, a in enumerate(args)]

    def whole(shape, place=None):
        return pl.BlockSpec(shape, lambda i: place or (0,) * len(shape))

    count = sum(math.prod(s) * a.dtype.itemsize for s, a in zip(shapes, args))
    count += sum(math.prod(s) * jnp.dtype(d).itemsize for s, d in outs)
    return pl.pallas_call(
        body,
        grid=(1,),
        out_shape=[jax.ShapeDtypeStruct(s, d) for s, d in outs],
        in_specs=[pl.BlockSpec(memory_space=pltpu.SMEM)] * scalars
        + [whole(s, views.get(i, (s, None))[1]) for i, s in enumerate(shapes) if i >= scalars],
        out_specs=[whole(s) for s, d in outs],
        scratch_shapes=list(scratch),
        compiler_params=pltpu.CompilerParams(vmem_limit_bytes=limit * MIB),
        cost_estimate=pl.CostEstimate(flops=flops, bytes_accessed=count, transcendentals=0),
    )(*args)


def sequence_call(body, outs, *args, halves, flops=10**9):
    def half(shape, columns=None, place=0):
        block = (shape[0] // 2,) + tuple(shape[1:-1]) + (columns or shape[-1],)
        rest = (0,) * (len(shape) - 2) + (place,)
        return pl.BlockSpec(block, lambda i: (i,) + rest)

    def whole(shape):
        return pl.BlockSpec(shape, lambda i: (0,) * len(shape))

    specs = [
        half((ROWS,) + a.shape[1:] if a.ndim == 2 else a.shape, *halves[i])
        if i in halves
        else whole(a.shape)
        for i, a in enumerate(args)
    ]
    return pl.pallas_call(
        body,
        grid=(2,),
        out_shape=[jax.ShapeDtypeStruct(s, d) for s, d in outs],
        in_specs=specs,
        out_specs=[half(s) for s, d in outs],
        compiler_params=pltpu.CompilerParams(vmem_limit_bytes=60 * MIB),
        cost_estimate=pl.CostEstimate(flops=flops, bytes_accessed=4 * 10**6, transcendentals=0),
    )(*args)


def project_kernel(
    core_ref, rows_ref, rim_ref, got_ref, other_ref, rates_ref, pick_ref, ends_ref,
    normed_ref, proj_ref, w_ref, gains_ref, taps_ref, states_ref, values_ref, cum_ref, sent_ref,
    wide_ref,
):
    wide = w_ref.shape[1]
    flipped = core_ref[0] == 1
    taps = jnp.zeros((8, 4 * LANES), f32)
    for r in range(2 * got_ref.shape[0]):
        mine, theirs = got_ref[r // 2].astype(f32), other_ref[r // 2].astype(f32)
        part = jnp.where(flipped, theirs, mine) if r % 2 == 0 else jnp.where(flipped, mine, theirs)
        wide_ref[r * SHARD : (r + 1) * SHARD, :] = part[:SHARD]
        rest = part[SHARD:]
        taps = taps + rest[:, : 4 * LANES]
        whole = rest[:, :LANES] + rest[:, LANES : 2 * LANES] + rest[:, 2 * LANES : 3 * LANES]
        for k in range(3):
            states_ref[k, r : r + 1, :] = whole[TAPS + k : TAPS + k + 1]
    taps_ref[...] = taps
    w_ref[...] = wide_ref[...].astype(bf16)
    chosen = jnp.where(
        lanes_of((16, wide)) == rows_of((16, wide)) + GAIN_LANE, 1.0, 0.0
    )
    chosen = jnp.where(rows_of((16, wide)) < 2, chosen, 0.0).astype(bf16)
    gains = lax.dot_general(chosen, w_ref[...], (NT, ((), ())), preferred_element_type=f32)
    gains_ref[...] = gains[:8]
    gain = gains[0:1]

    def projected(rows):
        rows = rows.astype(f32)
        scale = lax.rsqrt(jnp.mean(rows * rows, -1, keepdims=True) + eps_norm)
        normed = (rows * scale * gain).astype(bf16)
        return normed, jnp.dot(normed, w_ref[...], preferred_element_type=f32)

    for at in range(0, ROWS, GROUP):
        normed, proj = projected(rows_ref[at : at + GROUP, :])
        normed_ref[at : at + GROUP, :] = normed
        proj_ref[at : at + GROUP, :] = proj
    proj_ref[ROWS:, :] = projected(rim_ref[...])[1]
    ones = lower_ones()
    pick, ends = pick_ref[...], ends_ref[...]
    lane, row = lanes_of((GROUP, LANES)), rows_of((GROUP, LANES))
    for s in range(2):
        here = slice(s * GROUP, (s + 1) * GROUP)
        steps = rates_ref[...] * jax.nn.softplus(proj_ref[here, :LANES])
        cum = summed_down(ones, steps, NN)
        cum_ref[here, :] = cum
        last = cum[GROUP - 1 : GROUP, :]
        tail = jnp.exp(last - cum)
        qk = proj_ref[here, 4 * LANES :]
        for h in range(4):
            tile = slice(h * LANES, (h + 1) * LANES)
            raw = proj_ref[here, tile]
            rim_two = proj_ref[ROWS + 2 * s : ROWS + 2 * s + 1, tile]
            rim_one = proj_ref[ROWS + 2 * s + 1 : ROWS + 2 * s + 2, tile]
            one = jnp.where(row == 0, rim_one, pltpu.roll(raw, 1, 0))
            two = jnp.where(row == 0, rim_two, jnp.where(row == 1, rim_one, pltpu.roll(raw, 2, 0)))
            conv = (
                taps_ref[0:1, tile] * raw + taps_ref[1:2, tile] * one + taps_ref[2:3, tile] * two
            )
            values = jnp.where(lane < DH, conv, jnp.where(lane == DH, 1.0, 0.0))
            values_ref[here, tile] = values
            left, right = factors(head_lanes(qk, h, True), pick, ends)
            held = left * right * ends[2:3] * head_column(tail, h)
            fresh = product(held, values, TN)
            store_pieces(sent_ref, 4 * s + h, fresh)
            ending = jnp.broadcast_to(head_column(last, h), (8, LANES))
            high, mid, low = three_parts(ending)
            few = lanes_of((8, LANES))
            packed = jnp.where(
                few == 0,
                high.astype(f32),
                jnp.where(few == 1, mid.astype(f32), jnp.where(few == 2, low.astype(f32), 0.0)),
            ).astype(bf16)
            for q in range(4):
                sent_ref[16 * s + 4 * h + q, PIECE:, :] = packed


def project(core, rows, rim, got, other, rates, pick, ends):
    wide, width = got.shape[2], rows.shape[1]
    return whole_call(
        project_kernel,
        [
            (rows.shape, bf16),
            ((ROWS + rim.shape[0], wide), f32),
            ((width, wide), bf16),
            ((8, width), f32),
            ((8, 4 * LANES), f32),
            ((3, 2 * got.shape[0], LANES), f32),
            ((ROWS, 4 * LANES), f32),
            ((ROWS, LANES), f32),
            ((PIECES, SLOT, LANES), bf16),
        ],
        core, rows, rim, got, other, rates, pick, ends,
        scratch=[pltpu.VMEM((width, wide), f32)],
        flops=3 * 10**9,
        scalars=1,
    )


def scan_kernel(got_ref, back_ref, decay_ref):
    state = jnp.zeros((PIECE, LANES), f32)
    for i in range(PIECES):
        back_ref[i, :PIECE, :] = state.astype(bf16)
        back_ref[i, PIECE:, :] = jnp.zeros((SLOT - PIECE, LANES), bf16)
        ending = jnp.sum(got_ref[i, PIECE:, :].astype(f32), -1, keepdims=True)
        decay = jnp.broadcast_to(jnp.exp(ending), (8, LANES))
        decay_ref[i] = decay
        state = state * decay[0:1] + got_ref[i, :PIECE, :].astype(f32)


def earlier_states(sent):
    got = lax.all_to_all(sent, SEQ, 0, 0, tiled=True)
    back, decay = whole_call(
        scan_kernel, [(sent.shape, bf16), ((PIECES, 8, LANES), f32)], got, flops=10**6
    )
    return lax.all_to_all(back, SEQ, 0, 0, tiled=True), decay


def scan_back_kernel(got_ref, decay_ref, back_ref):
    state = jnp.zeros((PIECE, LANES), f32)
    for i in reversed(range(PIECES)):
        back_ref[i, :PIECE, :] = state.astype(bf16)
        back_ref[i, PIECE:, :] = jnp.zeros((SLOT - PIECE, LANES), bf16)
        state = state * decay_ref[i, 0:1, :] + got_ref[i, :PIECE, :].astype(f32)


def later_states(sent, decay):
    got = lax.all_to_all(sent, SEQ, 0, 0, tiled=True)
    (back,) = whole_call(scan_back_kernel, [(sent.shape, bf16)], got, decay, flops=10**6)
    return lax.all_to_all(back, SEQ, 0, 0, tiled=True), back


QK = ((ROWS, LANES), (0, 4))
FIRST = ((ROWS, LANES), (0, 0))


def within_kernel(qk_ref, values_ref, cum_ref, inside_ref):
    for s in range(2):
        here = slice(s * GROUP, (s + 1) * GROUP)
        cum = cum_ref[here, :]
        across = cum.T
        qk = qk_ref[here, :]
        for h in range(4):
            tile = slice(h * LANES, (h + 1) * LANES)
            dots = scores(qk, h)
            weights = (1.0 + dots + 0.5 * dots * dots) * decays(cum, across, h)
            inside_ref[here, tile] = product(weights, values_ref[here, tile], NN)


def within(proj, values, cum):
    return whole_call(
        within_kernel,
        [((ROWS, 4 * LANES), f32)],
        proj, values, cum,
        flops=3 * 10**9,
        views={0: QK},
    )[0]


def mix_kernel(
    qk_ref, cum_ref, inside_ref, earlier_ref, pick_ref, ends_ref, total_ref, mixed_ref
):
    pick, ends = pick_ref[...], ends_ref[...]
    lane = lanes_of((GROUP, LANES))
    growth = jnp.exp(cum_ref[:, :])
    qk = qk_ref[:, :]
    for h in range(4):
        tile = slice(h * LANES, (h + 1) * LANES)
        left, right = factors(head_lanes(qk, h, False), pick, ends)
        held = left * right * ends[2:3] * head_column(growth, h)
        total = inside_ref[:, tile] + product(held, state_rows(earlier_ref, h), NN, 2)
        total_ref[:, tile] = total
        mixed = total / total[:, DH : DH + 1]
        mixed_ref[:, tile] = jnp.where(lane < DH, mixed, 0.0).astype(bf16)


def mix(proj, cum, inside, earlier, pick, ends):
    return sequence_call(
        mix_kernel,
        [((ROWS, 4 * LANES), f32), ((ROWS, 4 * LANES), bf16)],
        proj, cum, inside, earlier, pick, ends,
        halves={0: (LANES, 4), 1: (), 2: (), 3: ()},
        flops=3 * 10**9,
    )


OWN = ROWS // 4


def own_slice(ref, place):
    return ref[pl.ds(pl.multiple_of(place * OWN, OWN), OWN), :]


def turn_kernel(
    place_ref, got_ref, unit_ref, scale_ref, back_ref, gains_ref, w_ref,
    middle_back_ref, gain_ref, out_back_ref, mixed_back_ref,
):
    two_back = got_ref[...].astype(f32)
    unit = unit_ref[...]
    gain_ref[...] = jnp.broadcast_to(
        jnp.sum(two_back * unit, 0, keepdims=True), gain_ref.shape
    )
    weighted = two_back * gains_ref[1:2]
    along = jnp.mean(weighted * unit, -1, keepdims=True)
    middle_back = own_slice(back_ref, place_ref[0]).astype(f32) + scale_ref[:, 0:1] * (
        weighted - unit * along
    )
    middle_back_ref[...] = middle_back
    out_back = middle_back.astype(bf16)
    out_back_ref[...] = out_back
    for g in range(4):
        mixed_back_ref[g] = jnp.dot(
            out_back, w_ref[:, g * 4 * LANES : (g + 1) * 4 * LANES], preferred_element_type=f32
        ).astype(bf16)


def turn(place, got, unit, scale, back, gains, w_out):
    width = back.shape[1]
    return whole_call(
        turn_kernel,
        [
            ((OWN, width), f32),
            ((8, width), f32),
            ((OWN, width), bf16),
            ((4, OWN, 4 * LANES), bf16),
        ],
        place, got, unit, scale, back, gains, w_out,
        flops=10**9,
        scalars=1,
        views={6: ((width, OUT), (0, 0))},
    )


def token_kernel(place_ref, *refs):
    terms, (rows_ref, middle_back_ref, gains_ref, out_ref) = refs[:3], refs[3:]
    one_back = sum(ref[...].astype(f32) for ref in terms)
    rows = own_slice(rows_ref, place_ref[0]).astype(f32)
    scale = lax.rsqrt(jnp.mean(rows * rows, -1, keepdims=True) + eps_norm)
    unit = rows * scale
    weighted = one_back * gains_ref[0:1]
    along = jnp.mean(weighted * unit, -1, keepdims=True)
    token_back = middle_back_ref[...] + scale * (weighted - unit * along)
    out_ref[...] = token_back.astype(bf16)


def token_grads(place, terms, rows, middle_back, gains):
    return whole_call(
        token_kernel, [(terms[0].shape, bf16)], place, *terms, rows, middle_back, gains,
        flops=10**7,
        scalars=1,
    )[0]


def block_kernel(place_ref, *refs):
    terms, (middle_ref, keep_ref, out_ref) = refs[:3], refs[3:]
    ffn = sum(ref[...].astype(f32) for ref in terms)
    keep = own_slice(keep_ref, place_ref[0])[:, 0:1]
    out_ref[...] = ((middle_ref[...] + ffn) * keep).astype(bf16)


def block_outs(place, terms, middle, keep):
    return whole_call(
        block_kernel, [(terms[0].shape, bf16)], place, *terms, middle, keep,
        flops=10**7,
        scalars=1,
    )[0]


def assemble_kernel(place_ref, own_ref, side_ref, back_ref, far_a_ref, far_b_ref, out_ref):
    place = place_ref[0]
    half = OWN // 2

    def at(other):
        return pl.multiple_of(jnp.bitwise_xor(place, other) * OWN, OWN)

    out_ref[pl.ds(at(0), OWN), :] = own_ref[...]
    out_ref[pl.ds(at(1), OWN), :] = side_ref[...]
    out_ref[pl.ds(at(3), OWN), :] = back_ref[...]
    out_ref[pl.ds(at(2), half), :] = far_a_ref[...]
    out_ref[pl.ds(pl.multiple_of(at(2) + half, half), half), :] = far_b_ref[...]


def to_neighbours(own):
    return lax.ppermute(own, "mp", BACK), lax.ppermute(own, "mp", SIDE)


def passed_on(back, side):
    half = back.shape[0] // 2
    return lax.ppermute(back[:half], "mp", SIDE), lax.ppermute(side[half:], "mp", BACK)


def gather_parts(own):
    back, side = to_neighbours(own)
    return own, side, back, *passed_on(back, side)


def assembled(place, parts):
    own = parts[0]
    return whole_call(
        assemble_kernel, [((ROWS, own.shape[1]), own.dtype)], place, *parts,
        flops=10**6,
        scalars=1,
    )[0]


def scatter_terms(part, after=None):
    half = OWN // 2
    got_a = lax.ppermute(part[2, :half], "mp", SIDE)
    got_b = lax.ppermute(part[2, half:], "mp", BACK)
    if after is not None:
        got_a, got_b, _ = lax.optimization_barrier((got_a, got_b, after))
    to_back = jnp.concatenate(
        [(part[3, :half].astype(f32) + got_a.astype(f32)).astype(bf16), part[3, half:]], 0
    )
    to_side = jnp.concatenate(
        [part[1, :half], (part[1, half:].astype(f32) + got_b.astype(f32)).astype(bf16)], 0
    )
    return part[0], lax.ppermute(to_back, "mp", BACK), lax.ppermute(to_side, "mp", SIDE)


def store_by_owner(ref, value, place, columns=slice(None)):
    for g in range(4):
        ref[jnp.bitwise_xor(place, g), :, columns] = value[g * OWN : (g + 1) * OWN]


def unmix_kernel(
    mixed_back_ref, total_ref, qk_ref, cum_ref, pick_ref, ends_ref, total_back_ref, sent_ref
):
    pick, ends = pick_ref[...], ends_ref[...]
    lane = lanes_of((GROUP, LANES))
    growth = jnp.exp(cum_ref[:, :])
    qk = qk_ref[:, :]
    for h in range(4):
        tile = slice(h * LANES, (h + 1) * LANES)
        total = total_ref[:, tile]
        inverse = 1.0 / total[:, DH : DH + 1]
        numer = mixed_back_ref[:, tile].astype(f32) * inverse
        numer = jnp.where(lane < DH, numer, 0.0)
        denom = -jnp.sum(numer * total, -1, keepdims=True) * inverse
        total_back = jnp.where(lane == DH, denom, numer)
        total_back_ref[:, tile] = total_back
        left, right = factors(head_lanes(qk, h, False), pick, ends)
        held = left * right * ends[2:3] * head_column(growth, h)
        store_pieces(sent_ref, h, product(held, total_back, TN))
        for q in range(4):
            sent_ref[4 * h + q, PIECE:, :] = jnp.zeros((SLOT - PIECE, LANES), bf16)


def unmix(mixed_back, total, proj, cum, pick, ends):
    return sequence_call(
        unmix_kernel,
        [((ROWS, 4 * LANES), f32), ((PIECES, SLOT, LANES), bf16)],
        mixed_back, total, proj, cum, pick, ends,
        halves={0: (), 1: (), 2: (LANES, 4), 3: ()},
        flops=3 * 10**9,
    )


def within_back_kernel(
    qk_ref, values_ref, cum_ref, total_back_ref, earlier_ref, pick_ref, ends_ref,
    qk_back_ref, values_back_ref, level_ref,
):
    pick, ends = pick_ref[...], ends_ref[...]
    only = lanes_of((GROUP, LANES)) < FEAT
    cum = cum_ref[:, :]
    across = cum.T
    growth = jnp.exp(cum)
    qk = qk_ref[:, :]
    qk_back = jnp.zeros((GROUP, LANES), f32)
    level = jnp.zeros((GROUP, LANES), f32)
    level_down = jnp.zeros((LANES, GROUP), f32)
    for h in range(4):
        tile = slice(h * LANES, (h + 1) * LANES)
        total_back = total_back_ref[:, tile]
        decay = decays(cum, across, h)
        dots = scores(qk, h)
        pairing = decay * product(total_back, values_ref[:, tile], NT)
        kernel = 1.0 + dots + 0.5 * dots * dots
        moved = kernel * pairing
        down = jnp.sum(moved, 0, keepdims=True)
        level_down = jnp.where(rows_of((LANES, GROUP)) == GATE_LANE + h, down, level_down)
        kernel_back = pairing * (1.0 + dots) * 0.25
        values_back_ref[:, tile] = product(kernel * decay, total_back, TN)
        query_tile = head_lanes(qk, h, False)
        keys_only = jnp.where(only, head_lanes(qk, h, True), 0.0)
        query_only = jnp.where(only, query_tile, 0.0)
        query_back = product(kernel_back, keys_only, NN)
        keys_back = product(kernel_back, query_only, TN)
        left, right = factors(query_tile, pick, ends)
        features_back = head_column(growth, h) * product(
            total_back, state_rows(earlier_ref, h), NT, 2
        )
        level_here = jnp.sum(moved, 1, keepdims=True) + jnp.sum(
            left * right * ends[2:3] * features_back, 1, keepdims=True
        )
        level = level + on_head_lane(level_here, h)
        query_back = query_back + factors_back(features_back, left, right, pick, ends)
        at = h * FEAT
        qk_back = qk_back + (pltpu.roll(query_back, at, 1) if at else query_back)
        qk_back = qk_back + pltpu.roll(keys_back, at + 4 * FEAT, 1)
    qk_back_ref[:, :] = qk_back
    level_ref[:, :] = level - level_down.T


def within_back(s, proj, values, cum, total_back, earlier, pick, ends):
    return whole_call(
        within_back_kernel,
        [((GROUP, LANES), f32), ((GROUP, 4 * LANES), f32), ((GROUP, LANES), f32)],
        proj, values, cum, total_back, earlier, pick, ends,
        flops=4 * 10**9,
        views={
            0: ((GROUP, LANES), (s, 4)),
            1: ((GROUP, 4 * LANES), (s, 0)),
            2: ((GROUP, LANES), (s, 0)),
            3: ((GROUP, 4 * LANES), (s, 0)),
            4: ((PIECES // 2, SLOT, LANES), (s, 0, 0)),
        },
    )


def later_back_kernel(
    qk_ref, first_ref, values_ref, cum_ref, rates_ref, earlier_ref, later_ref, pick_ref, ends_ref,
    qk_in_a_ref, values_in_a_ref, level_a_ref, qk_in_b_ref, values_in_b_ref, level_b_ref,
    qk_back_ref, values_back_ref, gate_back_ref,
):
    pick, ends = pick_ref[...], ends_ref[...]
    ones, before = lower_ones(), lower_ones(True)
    cum = cum_ref[:, :]
    last = cum[GROUP - 1 : GROUP, :]
    tail = jnp.exp(last - cum)
    carried = jnp.exp(last)
    qk = qk_ref[:, :]
    second = pl.program_id(0) == 1

    def either(one_ref, two_ref, columns=slice(None)):
        return jnp.where(second, two_ref[:, columns], one_ref[:, columns])

    qk_back = either(qk_in_a_ref, qk_in_b_ref)
    crossed = jnp.zeros((GROUP, LANES), f32)
    through = jnp.zeros((1, LANES), f32)
    for h in range(4):
        tile = slice(h * LANES, (h + 1) * LANES)
        later = state_rows(later_ref, h)
        left, right = factors(head_lanes(qk, h, True), pick, ends)
        held = left * right * ends[2:3]
        column = head_column(tail, h)
        features_back = column * product(values_ref[:, tile], later, NT, 2)
        values_back_ref[:, tile] = either(values_in_a_ref, values_in_b_ref, tile) + column * product(
            held, later, NN, 2
        )
        crossed = crossed + on_head_lane(
            jnp.sum(held * features_back, 1, keepdims=True), h
        )
        keys_back = factors_back(features_back, left, right, pick, ends)
        qk_back = qk_back + pltpu.roll(keys_back, (h + 4) * FEAT, 1)
        whole = jnp.sum(
            later.astype(f32) * state_rows(earlier_ref, h).astype(f32), 1, keepdims=True
        )
        whole = jnp.sum(whole, 0, keepdims=True) * head_column(carried, h)
        through = through + on_head_lane(whole, h)
    qk_back_ref[:, :] = qk_back
    step_back = (
        summed_down(ones, either(level_a_ref, level_b_ref), TN) + summed_down(before, crossed, NN) + through
    )
    gate_back_ref[:, :] = (
        step_back * rates_ref[...] * jax.nn.sigmoid(first_ref[:, :])
    )


def later_back(proj, values, cum, rates, earlier, later, pick, ends, within):
    return sequence_call(
        later_back_kernel,
        [((ROWS, LANES), f32), ((ROWS, 4 * LANES), f32), ((ROWS, LANES), f32)],
        proj, proj, values, cum, rates, earlier, later, pick, ends, *within,
        halves={0: (LANES, 4), 1: (LANES, 0), 2: (), 3: (), 5: (), 6: ()},
        flops=4 * 10**9,
    )


def unproject_kernel(
    place_ref, proj_ref, ahead_ref, taps_ref, qk_back_ref, values_back_ref, gate_back_ref, normed_ref, w_ref,
    own_ref, side_ref, back_ref, far_a_ref, far_b_ref, mixed_ref, gain_two_ref,
    part_ref, kept_ref, sent_ref,
    taps_grad_ref, taps_across_ref, proj_back_ref, out_back_ref, turned_ref,
):
    @pl.when(pl.program_id(0) == 0)
    def _():
        lane, row = lanes_of((GROUP, LANES)), rows_of((GROUP, LANES))
        taps_grad_ref[...] = jnp.zeros_like(taps_grad_ref)
        for s in range(2):
            here = slice(s * GROUP, (s + 1) * GROUP)
            for h in range(4):
                tile = slice(h * LANES, (h + 1) * LANES)
                raw = proj_ref[here, tile]
                back = values_back_ref[here, tile]
                back = jnp.where(lane < DH, back, 0.0)
                rim_two = proj_ref[ROWS + 2 * s : ROWS + 2 * s + 1, tile]
                rim_one = proj_ref[ROWS + 2 * s + 1 : ROWS + 2 * s + 2, tile]
                one = jnp.where(row == 0, rim_one, pltpu.roll(raw, 1, 0))
                two = jnp.where(row == 0, rim_two, jnp.where(row == 1, rim_one, pltpu.roll(raw, 2, 0)))
                for j, moved in enumerate((raw, one, two)):
                    taps_grad_ref[j : j + 1, tile] = taps_grad_ref[j : j + 1, tile] + jnp.sum(
                        moved * back, 0, keepdims=True
                    )
                next_one = ahead_ref[2 * s : 2 * s + 1, tile]
                next_two = ahead_ref[2 * s + 1 : 2 * s + 2, tile]
                one = jnp.where(row == GROUP - 1, next_one, pltpu.roll(back, GROUP - 1, 0))
                two = jnp.where(
                    row == GROUP - 1,
                    next_two,
                    jnp.where(row == GROUP - 2, next_one, pltpu.roll(back, GROUP - 2, 0)),
                )
                raw_back = (
                    taps_ref[0:1, tile] * back + taps_ref[1:2, tile] * one + taps_ref[2:3, tile] * two
                )
                raw_back = jnp.where(lane < DH, raw_back, 0.0)
                if h == 0:
                    gates = (lane >= GATE_LANE) & (lane < GATE_LANE + 4)
                    raw_back = jnp.where(gates, gate_back_ref[here, :], raw_back)
                proj_back_ref[here, tile] = raw_back.astype(bf16)
            proj_back_ref[here, 4 * LANES :] = qk_back_ref[here, :].astype(bf16)
        for h in range(GROUPS):
            tile = slice(h * LANES, (h + 1) * LANES)
            taps_across_ref[tile, :] = pltpu.roll(
                jnp.concatenate(
                    [taps_grad_ref[:, tile], jnp.zeros((LANES - 8, LANES), f32)], 0
                ).T,
                TAPS_LANE,
                1,
            )
        for k, other in enumerate((0, 1, 3, 2)):
            turned_ref[k * OWN : (k + 1) * OWN] = own_slice(
                mixed_ref, jnp.bitwise_xor(place_ref[0], other)
            )

    part = lax.dot_general(
        proj_back_ref[...], w_ref[...], (NT, ((), ())), preferred_element_type=f32
    ).astype(bf16)
    store_by_owner(part_ref, part, place_ref[0])
    wide = w_ref.shape[1]
    grad_in = lax.dot_general(
        normed_ref[...], proj_back_ref[...], (TN, ((), ())), preferred_element_type=f32
    )
    weights = w_ref[...].astype(f32)
    gain_one = jnp.sum(grad_in * weights, 1, keepdims=True)
    gain_one = gain_one / weights[:, GAIN_LANE : GAIN_LANE + 1]
    gain_two = gain_two_ref[...].T[:, 0:1]
    first = grad_in[:, :LANES]
    spot = lanes_of(first.shape)
    first = jnp.where(
        spot == GAIN_LANE, gain_one, jnp.where(spot == GAIN_LANE + 1, gain_two, first)
    )
    out_back_ref[:OWN] = own_ref[...]
    out_back_ref[OWN : 2 * OWN] = side_ref[...]
    out_back_ref[2 * OWN : 3 * OWN] = back_ref[...]
    out_back_ref[3 * OWN : 3 * OWN + OWN // 2] = far_a_ref[...]
    out_back_ref[3 * OWN + OWN // 2 :] = far_b_ref[...]
    grad_out = lax.dot_general(
        out_back_ref[...], turned_ref[...], (TN, ((), ())), preferred_element_type=f32
    )
    core = place_ref[1]

    each = DH // 8
    few = lanes_of((SHARD, LANES))
    spare = (few >= TAPS_LANE) & (few < TAPS_LANE + TAPS) & (rows_of((SHARD, LANES)) < each)

    def store(ref, parity):
        for k in range(ref.shape[0]):
            r = 2 * k + parity
            here = slice(r * SHARD, (r + 1) * SHARD)
            head = pl.program_id(0) * (GROUPS // 2) + r // 8
            taps = taps_across_ref[pl.ds(pl.multiple_of(head * LANES, LANES), LANES), :]
            at = (r % 8) * each
            taps = pltpu.roll(taps, LANES - at, 0) if at else taps
            ref[k, :, :LANES] = jnp.where(spare, taps[:SHARD], first[here]).astype(bf16)
            ref[k, :, LANES:wide] = grad_in[here, LANES:].astype(bf16)
            ref[k, :, wide:] = grad_out[here].astype(bf16)

    for parity in range(2):

        @pl.when(core == parity)
        def _():
            store(kept_ref, parity)
            store(sent_ref, 1 - parity)


def unproject(
    place, proj, ahead, taps, qk_back, values_back, gate_back, normed, w_in, out_parts, mixed, gain_two
):
    width, wide = w_in.shape
    half, shards = width // 2, width // SHARD // 4
    args = (proj, ahead, taps, qk_back, values_back, gate_back, normed, w_in, *out_parts, mixed)
    args += (gain_two,)

    def whole(shape):
        return pl.BlockSpec(shape, lambda i: (0,) * len(shape))

    specs = [whole(a.shape) for a in args]
    specs[0] = pl.BlockSpec((proj.shape[0], 4 * LANES), lambda i: (0, 0))
    specs[7] = pl.BlockSpec((half, wide), lambda i: (i, 0))
    for k in (6, 8, 9, 10, 11, 12, 14):
        specs[k] = pl.BlockSpec((args[k].shape[0], half), lambda i: (0, i))
    sums = pl.BlockSpec((shards, SHARD, wide + 4 * LANES), lambda i: (i, 0, 0))
    return pl.pallas_call(
        unproject_kernel,
        grid=(2,),
        out_shape=[jax.ShapeDtypeStruct((4, OWN, width), bf16)]
        + [jax.ShapeDtypeStruct((2 * shards, SHARD, wide + 4 * LANES), bf16)] * 2,
        in_specs=[pl.BlockSpec(memory_space=pltpu.SMEM)] + specs,
        out_specs=[pl.BlockSpec((4, OWN, half), lambda i: (0, 0, i)), sums, sums],
        scratch_shapes=[
            pltpu.VMEM((8, 4 * LANES), f32),
            pltpu.VMEM((4 * LANES, LANES), f32),
            pltpu.VMEM((ROWS, wide), bf16),
            pltpu.VMEM((ROWS, half), bf16),
            pltpu.VMEM((ROWS, 4 * LANES), bf16),
        ],
        compiler_params=pltpu.CompilerParams(vmem_limit_bytes=60 * MIB),
        cost_estimate=pl.CostEstimate(
            flops=4 * 10**9, bytes_accessed=16 * 10**6, transcendentals=0
        ),
    )(place, *args)


BLOCK = 256
HIDDEN = 1280
OUT = 16 * LANES
SHARD = 56
SPACED = 64


def middle_kernel(
    place_ref, own_ref, side_ref, back_ref, far_a_ref, far_b_ref, out_ref, rows_ref, gains_ref,
    cotangent_ref, gate_ref, up_ref, down_ref, both_ref,
    middle_ref, unit_ref, scale_ref, normed_ref, acts_ref, two_ref,
    mixed_ref, sum_ref,
):
    place, step = place_ref[0], pl.program_id(0)
    blocks = HIDDEN // BLOCK

    @pl.when(step == 0)
    def _():
        mixed_ref[place] = own_ref[...]
        mixed_ref[jnp.bitwise_xor(place, 1)] = side_ref[...]
        mixed_ref[jnp.bitwise_xor(place, 3)] = back_ref[...]
        mixed_ref[jnp.bitwise_xor(place, 2), :GROUP, :] = far_a_ref[...]
        mixed_ref[jnp.bitwise_xor(place, 2), GROUP:, :] = far_b_ref[...]
        sum_ref[...] = rows_ref[...].astype(f32)

    @pl.when(step < GROUPS)
    def _():
        for at in range(0, out_ref.shape[0], BLOCK):
            here = slice(at, at + BLOCK)
            sum_ref[:, here] += lax.dot_general(
                mixed_ref[step], out_ref[here, :], (NT, ((), ())), preferred_element_type=f32
            )

    @pl.when(step == GROUPS - 1)
    def _():
        for at in range(0, ROWS, OWN):
            here = slice(at, at + OWN)
            middle = sum_ref[here, :]
            scale = lax.rsqrt(jnp.mean(middle * middle, -1, keepdims=True) + eps_norm)
            normed_ref[here, :] = (middle * scale * gains_ref[1:2]).astype(bf16)
        middle = own_slice(sum_ref, place)
        scale = lax.rsqrt(jnp.mean(middle * middle, -1, keepdims=True) + eps_norm)
        middle_ref[...] = middle
        unit_ref[...] = middle * scale
        scale_ref[...] = jnp.broadcast_to(scale, scale_ref.shape)

    @pl.when((step >= GROUPS) & (step < GROUPS + blocks))
    def _():
        normed = normed_ref[...]
        gate = jnp.dot(normed, gate_ref[...], preferred_element_type=f32)
        up = jnp.dot(normed, up_ref[...], preferred_element_type=f32)
        hidden_back = jnp.dot(cotangent_ref[...], down_ref[...], preferred_element_type=f32)
        sigma = jax.nn.sigmoid(gate)
        silu = gate * sigma
        at = pl.multiple_of((step - GROUPS) * BLOCK, BLOCK)
        acts_ref[:, pl.ds(at, BLOCK)] = (
            hidden_back * up * sigma * (1.0 + gate * (1.0 - sigma))
        ).astype(bf16)
        acts_ref[:, pl.ds(HIDDEN + at, BLOCK)] = (hidden_back * silu).astype(bf16)
        acts_ref[:, pl.ds(2 * HIDDEN + at, BLOCK)] = (silu * up).astype(bf16)

    @pl.when(step >= GROUPS + blocks)
    def _():
        two_ref[...] = lax.dot_general(
            acts_ref[:, : 2 * HIDDEN], both_ref[...], (NT, ((), ())), preferred_element_type=f32
        ).astype(bf16)


def middle_both_ways(place, mixed_parts, weights, rows, gains, back):
    width = rows.shape[1]
    blocks, outs = HIDDEN // BLOCK, width // BLOCK
    columns = OUT // GROUPS

    def whole(shape):
        return pl.BlockSpec(shape, lambda i: (0,) * len(shape))

    def clipped(i, first, count):
        return jnp.clip(i - first, 0, count - 1)

    def block_of(which):
        at = OUT // BLOCK + which * blocks
        return pl.BlockSpec((width, BLOCK), lambda i: (0, at + clipped(i, GROUPS, blocks)))

    last = GROUPS + blocks
    specs = [whole(part.shape) for part in mixed_parts]
    specs.append(pl.BlockSpec((width, columns), lambda i: (0, clipped(i, 0, GROUPS))))
    specs += [whole(rows.shape), whole(gains.shape), whole(back.shape)]
    specs += [block_of(0), block_of(1), block_of(2)]
    specs.append(
        pl.BlockSpec(
            (pl.Element(BLOCK), pl.Element(2 * HIDDEN)),
            lambda i: (clipped(i, last, outs) * BLOCK, OUT),
        )
    )
    results = [
        ((OWN, width), f32),
        ((OWN, width), f32),
        ((OWN, LANES), f32),
        ((ROWS, width), bf16),
        ((ROWS, 3 * HIDDEN), bf16),
        ((ROWS, width), bf16),
    ]
    out_specs = [whole(s) for s, d in results]
    out_specs[-1] = pl.BlockSpec((ROWS, BLOCK), lambda i: (0, clipped(i, last, outs)))
    return pl.pallas_call(
        middle_kernel,
        grid=(last + outs,),
        out_shape=[jax.ShapeDtypeStruct(s, d) for s, d in results],
        in_specs=[pl.BlockSpec(memory_space=pltpu.SMEM)] + specs,
        out_specs=out_specs,
        scratch_shapes=[
            pltpu.VMEM((GROUPS, ROWS, columns), bf16),
            pltpu.VMEM((ROWS, width), f32),
        ],
        compiler_params=pltpu.CompilerParams(vmem_limit_bytes=60 * MIB),
        cost_estimate=pl.CostEstimate(
            flops=16 * 10**9, bytes_accessed=40 * 10**6, transcendentals=0
        ),
    )(place, *mixed_parts, weights, rows, gains, back, weights, weights, weights, weights)


def ffn_out_kernel(place_ref, acts_ref, down_ref, out_ref):
    value = lax.dot_general(
        acts_ref[...], down_ref[...], (NT, ((), ())), preferred_element_type=f32
    ).astype(bf16)
    store_by_owner(out_ref, value, place_ref[0])


def ffn_out(place, acts, weights):
    width = weights.shape[0]
    return pl.pallas_call(
        ffn_out_kernel,
        grid=(width // BLOCK,),
        out_shape=jax.ShapeDtypeStruct((4, OWN, width), bf16),
        in_specs=[
            pl.BlockSpec(memory_space=pltpu.SMEM),
            pl.BlockSpec((ROWS, HIDDEN), lambda i: (0, 2)),
            pl.BlockSpec(
                (pl.Element(BLOCK), pl.Element(HIDDEN)), lambda i: (i * BLOCK, OUT + 2 * HIDDEN)
            ),
        ],
        out_specs=pl.BlockSpec((4, OWN, BLOCK), lambda i: (0, 0, i)),
        compiler_params=pltpu.CompilerParams(vmem_limit_bytes=60 * MIB),
        cost_estimate=pl.CostEstimate(
            flops=3 * 10**9, bytes_accessed=8 * 10**6, transcendentals=0
        ),
    )(place, acts, weights)


def ffn_grads_kernel(normed_ref, back_ref, acts_ref, grads_ref):
    def spaced(rows_ref):
        grad = lax.dot_general(
            rows_ref[...], acts_ref[...], (TN, ((), ())), preferred_element_type=f32
        )
        for r in range(grad.shape[0] // SHARD):
            grads_ref[r * SPACED : r * SPACED + SHARD, :] = grad[
                r * SHARD : (r + 1) * SHARD
            ].astype(bf16)
            grads_ref[r * SPACED + SHARD : (r + 1) * SPACED, :] = jnp.zeros(
                (SPACED - SHARD, grad.shape[1]), bf16
            )

    both = pl.program_id(0) < 2 * HIDDEN // WIDER

    @pl.when(both)
    def _():
        spaced(normed_ref)

    @pl.when(jnp.logical_not(both))
    def _():
        spaced(back_ref)


WIDER = 640


def ffn_grads(normed, back, acts):
    width = normed.shape[1]
    whole = pl.BlockSpec((ROWS, width), lambda i: (0, 0))
    return pl.pallas_call(
        ffn_grads_kernel,
        grid=(3 * HIDDEN // WIDER,),
        out_shape=jax.ShapeDtypeStruct((width // SHARD * SPACED, 3 * HIDDEN), bf16),
        in_specs=[whole, whole, pl.BlockSpec((ROWS, WIDER), lambda i: (0, i))],
        out_specs=pl.BlockSpec((width // SHARD * SPACED, WIDER), lambda i: (0, i)),
        compiler_params=pltpu.CompilerParams(vmem_limit_bytes=60 * MIB),
        cost_estimate=pl.CostEstimate(
            flops=7 * 10**9, bytes_accessed=20 * 10**6, transcendentals=0
        ),
    )(normed, back, acts)


def order_columns(heads):
    import numpy as np

    place = np.zeros((5 * LANES, 5 * LANES), np.float32)
    for h in range(heads):
        at = h * (2 * FEAT + DH + 1)
        for i in range(FEAT):
            place[at + i, heads * LANES + h * FEAT + i] = 1.0
            place[at + FEAT + i, heads * LANES + (heads + h) * FEAT + i] = 1.0
        for i in range(DH):
            place[at + 2 * FEAT + i, h * LANES + i] = 1.0
        place[at + 2 * FEAT + DH, GATE_LANE + h] = 1.0
    return jnp.asarray(place, bf16)


def order_heads(heads):
    import numpy as np

    place = np.zeros((heads * DH, heads * LANES), np.float32)
    for h in range(heads):
        for i in range(DH):
            place[h * DH + i, h * LANES + i] = 1.0
    return jnp.asarray(place, bf16)


def prepare_kernel(
    rank_ref, in_ref, out_ref, gate_ref, up_ref, down_ref, taps_ref,
    gains_ref, gains_first_ref, gains_second_ref, place_ref, tiles_ref,
    shard_ref, out_shard_ref, rest_ref, few_ref,
):
    wide = 5 * LANES
    columns = in_ref.shape[1]
    whole = jnp.dot(
        in_ref[...].astype(bf16), place_ref[:columns, :], preferred_element_type=f32
    )
    spot = jnp.where(
        lanes_of((2, wide)) == rows_of((2, wide)) + GAIN_LANE, 1.0, 0.0
    ).astype(bf16)
    gains = lax.dot_general(
        gains_ref[...].astype(bf16), spot, (TN, ((), ())), preferred_element_type=f32
    )
    for k in range(shard_ref.shape[0]):
        shard_ref[k, :SHARD, :] = (whole + gains).astype(bf16)
    rank = rank_ref[0]
    own = taps_ref.shape[1]
    each = DH // own
    first = (rank // each) * LANES + (rank % each) * own
    spot = jnp.where(
        lanes_of((own, wide)) == rows_of((own, wide)) + first, 1.0, 0.0
    ).astype(bf16)
    taps = jnp.dot(taps_ref[...].astype(bf16), spot, preferred_element_type=f32)
    rows = [taps]
    for ref in (gains_ref, gains_first_ref, gains_second_ref):
        few_ref[...] = jnp.zeros_like(few_ref)
        few_ref[0:2, :SHARD] = ref[...]
        both = few_ref[...]
        line = both + pltpu.roll(pltpu.roll(both, SHARD, 1), 7, 0)
        parts = [part.astype(f32)[0:1] for part in three_parts(line)]
        rows.append(jnp.concatenate(parts + [jnp.zeros((1, wide - 3 * LANES), f32)], 1))
    rows.append(jnp.zeros((SPACED - SHARD - TAPS - 3, wide), f32))
    for k in range(shard_ref.shape[0]):
        shard_ref[k, SHARD:, :] = jnp.concatenate(rows, 0).astype(bf16)
    out_shard_ref[...] = jnp.dot(
        out_ref[...].astype(bf16), tiles_ref[...], preferred_element_type=f32
    ).astype(bf16)
    rest_ref[...] = jnp.zeros_like(rest_ref)
    units = gate_ref.shape[1]
    rest_ref[:, :units] = gate_ref[...].astype(bf16)
    rest_ref[:, HIDDEN : HIDDEN + units] = up_ref[...].astype(bf16)
    rest_ref[:, 2 * HIDDEN : 2 * HIDDEN + units] = down_ref[...].astype(bf16)


def prepare(rank, *args):
    return whole_call(
        prepare_kernel,
        [
            ((16, SPACED, 5 * LANES), bf16),
            ((SHARD, 4 * LANES), bf16),
            ((SHARD, 3 * HIDDEN), bf16),
        ],
        rank, *args,
        scratch=[pltpu.VMEM((8, LANES), f32)],
        scalars=1,
    )


def moved_moments(weight, first, second, grad):
    fix = 1.0 - beta_value**STEP
    moment = beta_value * first + (1.0 - beta_value) * grad
    square = beta_value * second + (1.0 - beta_value) * grad * grad
    direction = moment / fix / (jnp.sqrt(square / fix) + eps_adam) + decay_rate * weight
    return moment, square, direction


def adapted(params, outs, place, grad):
    weight = params[0][...]
    moment, square, direction = moved_moments(weight, params[1][...], params[2][...], grad)
    outs[0][...] = moment
    outs[1][...] = square
    outs[2][...] = direction
    both = [
        jnp.sum(jnp.sum(v * v, 1, keepdims=True), 0, keepdims=True) for v in (weight, direction)
    ]
    lane = lanes_of((1, LANES))
    return jnp.where(lane == place, both[0], jnp.where(lane == place + 1, both[1], 0.0))


def ffn_moments_kernel(ffn_ref, *refs):
    params, outs, sums_ref = refs[:9], refs[9:-1], refs[-1]
    units = params[0].shape[1]
    sums = jnp.zeros((1, LANES), f32)
    for k in range(3):
        grad = ffn_ref[:SHARD, k * HIDDEN : k * HIDDEN + units].astype(f32)
        three = slice(3 * k, 3 * k + 3)
        sums = sums + adapted(params[three], outs[three], 4 + 2 * k, grad)
    sums_ref[...] = jnp.broadcast_to(sums, sums_ref.shape)


def ffn_moments(ffn, params):
    outs = [(param.shape, f32) for param in params]
    return whole_call(ffn_moments_kernel, outs + [((8, LANES), f32)], ffn, *params)


def moments_kernel(mixer_ref, place_ref, tiles_ref, ffn_sums_ref, *refs):
    params, outs, sums_ref = refs[:9], refs[9:-1], refs[-1]

    wide = 5 * LANES
    mixer = mixer_ref[0].astype(f32)
    for k in range(1, mixer_ref.shape[0]):
        mixer = mixer + mixer_ref[k].astype(f32)
    sums = ffn_sums_ref[0:1, :]
    grad_in = picked(mixer[:, :wide], place_ref[...], NT)
    sums = sums + adapted(params[0:3], outs[0:3], 0, grad_in[:, : params[0].shape[1]])
    sums = sums + adapted(params[3:6], outs[3:6], 2, picked(mixer[:, wide:], tiles_ref[...], NT))
    across = jnp.concatenate([mixer[:, :LANES], jnp.zeros((LANES - SHARD, LANES), f32)], 0).T
    taps = across[TAPS_LANE : TAPS_LANE + TAPS, : params[6].shape[1]]
    sums = sums + adapted(params[6:9], outs[6:9], 10, taps)
    ones = across[GAIN_LANE : GAIN_LANE + 1]
    twos = across[GAIN_LANE + 1 : GAIN_LANE + 2]
    few = lanes_of((1, LANES))
    line = jnp.where(few < SHARD, ones, 0.0) + pltpu.roll(
        jnp.broadcast_to(jnp.where(few < SHARD, twos, 0.0), (8, LANES)), SHARD, 1
    )[0:1]
    both = jnp.concatenate([sums, line], 1)
    sums_ref[...] = jnp.broadcast_to(both[None], sums_ref.shape)


def moments(mixer, place, tiles, ffn_sums, params):
    outs = [(param.shape, f32) for param in params] + [((LANES, 1, 2 * LANES), f32)]
    return whole_call(
        moments_kernel, outs, mixer, place, tiles, ffn_sums, *params
    )


def update_kernel(rank_ref, totals_ref, states_ref, *refs):
    weights, directions, outs = refs[:6], refs[6:12], refs[12:18]
    gains_refs, norms_ref = refs[18:21], refs[21]
    totals = totals_ref[:, 0, :]
    sums = jnp.sum(totals[:, :LANES], 0, keepdims=True)
    lane = lanes_of((1, LANES))
    grouped = jnp.where(
        lanes_of((32, LANES)) // 4 == rows_of((32, LANES)), 1.0, 0.0
    ).astype(bf16)
    grad = summed_down(grouped, totals[:, LANES:], NN)
    moment, square, direction = moved_moments(
        states_ref[0], states_ref[1], states_ref[2], grad
    )
    live = lanes_of((32, LANES)) < 2 * SHARD
    for place, value in ((12, states_ref[0]), (13, direction)):
        value = jnp.where(live, value, 0.0)
        value = jnp.sum(jnp.sum(value * value, 1, keepdims=True), 0, keepdims=True)
        sums = jnp.where(lane == place, value, sums)
    norms = jnp.sqrt(sums)
    each = [
        jnp.sum(
            jnp.where(lanes_of((8, LANES)) == 2 * rows_of((8, LANES)) + k, norms, 0.0),
            1,
            keepdims=True,
        )
        for k in range(2)
    ]
    norms_ref[...] = jnp.where(lanes_of((8, 2)) == 0, each[0], each[1])[:7]

    def ratio(index):
        return norms[:, 2 * index : 2 * index + 1] / norms[:, 2 * index + 1 : 2 * index + 2]

    for index in range(6):
        outs[index][...] = (
            weights[index][...] - learn_rate * ratio(index) * directions[index][...]
        )
    updated = states_ref[0] - learn_rate * ratio(6) * direction
    for ref, value in zip(gains_refs, (updated, moment, square)):
        own = jnp.where(rows_of((32, LANES)) == rank_ref[0], value, 0.0)
        own = jnp.broadcast_to(jnp.sum(own, 0, keepdims=True), (8, LANES))
        ref[0:1, :] = own[0:1, :SHARD]
        ref[1:2, :] = pltpu.roll(own, LANES - SHARD, 1)[0:1, :SHARD]


def update(rank, totals, states, weights, directions):
    outs = [(w.shape, f32) for w in weights] + [((2, SHARD), f32)] * 3 + [((7, 2), f32)]
    return whole_call(
        update_kernel, outs, rank, totals, states, *weights, *directions, scalars=1
    )


def per_device(
    tokens,
    cotangent,
    lengths,
    rate_codes,
    inproj,
    inproj_first,
    inproj_second,
    outproj,
    outproj_first,
    outproj_second,
    gateproj,
    gateproj_first,
    gateproj_second,
    upproj,
    upproj_first,
    upproj_second,
    downproj,
    downproj_first,
    downproj_second,
    convtaps,
    convtaps_first,
    convtaps_second,
    normgains,
    normgains_first,
    normgains_second,
):
    seqs, group, width = tokens.shape
    heads = rate_codes.shape[0]
    lag = TAPS - 1
    rank = lax.axis_index(SEQ).reshape(1)
    core = lax.axis_index("seq_2")
    peer = lax.axis_index("mp").reshape(1)
    pick, ends = selections()
    place, tiles = order_columns(heads), order_heads(heads)

    shards, out_shard, rest_shard = prepare(
        rank, inproj, outproj.T, gateproj, upproj, downproj.T, convtaps,
        normgains, normgains_first, normgains_second, place, tiles,
    )
    got = lax.all_to_all(shards, ("seq_0", "seq_1"), 0, 0, tiled=True)
    other = lax.ppermute(got, "seq_2", SWAP)
    low, high = peer[0] % 2, peer[0] // 2

    def beside(mine, theirs, bit):
        return jnp.where(
            bit == 0, jnp.concatenate([mine, theirs], 1), jnp.concatenate([theirs, mine], 1)
        )

    out_pair = beside(out_shard, lax.ppermute(out_shard, "mp", SIDE), low)
    out_shards = beside(out_pair, lax.ppermute(out_pair, "mp", BACK), high)
    weights_shard = jnp.concatenate([out_shards, rest_shard], 1)
    weights_shard, got = lax.optimization_barrier((weights_shard, got))
    weights = lax.all_gather(weights_shard, SEQ, axis=0, tiled=True)

    rows = tokens.reshape(-1, width)
    rim = shifted(tokens[:, group - lag :], SEQ, 1).reshape(-1, width)
    rim = jnp.pad(rim, ((0, 16 - seqs * lag), (0, 0)))
    positions = rank * group + jnp.arange(group, dtype=jnp.int32)
    keep = (positions[None, :] < lengths[:, None]).astype(f32).reshape(-1, 1)
    back = (cotangent.reshape(-1, width).astype(f32) * keep).astype(bf16)
    rates = -jnp.exp2(-rate_codes.astype(f32) / 4.0)
    rates = jnp.pad(rates[None], ((0, 0), (GATE_LANE, LANES - GATE_LANE - heads)))
    normed_one, proj, w_in, gains, taps, states, values, cum, sent = project(
        core.reshape(1), rows, rim, got, other, rates, pick, ends
    )
    earlier, decay = earlier_states(sent)
    inside = within(proj, values, cum)
    total, mixed = mix(proj, cum, inside, earlier, pick, ends)

    middle, unit_two, scale_two, normed_two, acts, two_part = middle_both_ways(
        peer, gather_parts(mixed), weights, rows, gains, back
    )
    two_back = lax.psum_scatter(two_part, "mp", scatter_dimension=0, tiled=True)
    ffn_part = ffn_out(peer, acts, weights)
    two_back, ffn_part = lax.optimization_barrier((two_back, ffn_part))
    ffn_sums = lax.psum_scatter(
        ffn_grads(normed_two, back, acts), SEQ, scatter_dimension=0, tiled=True
    )
    middle_back, gain_two, out_own, mixed_back = turn(
        peer, two_back, unit_two, scale_two, back, gains, weights
    )
    mixed_back = lax.all_to_all(mixed_back, "mp", 0, 0, tiled=True).reshape(ROWS, -1)

    total_back, sent = unmix(mixed_back, total, proj, cum, pick, ends)
    ffn_part, out_own, sent = lax.optimization_barrier((ffn_part, out_own, sent))
    later, summed = later_states(sent, decay)
    within_a = within_back(0, proj, values, cum, total_back, earlier, pick, ends)
    total_back, _ = lax.optimization_barrier((total_back, summed))
    within_b = within_back(1, proj, values, cum, total_back, earlier, pick, ends)
    out_parts = gather_parts(out_own)
    ffn_terms = scatter_terms(ffn_part)
    qk_back, values_back, gate_back = later_back(
        proj, values, cum, rates, earlier, later, pick, ends, within_a + within_b
    )
    edge = values_back.reshape(seqs, group, -1)[:, :lag]
    ahead = shifted(edge, SEQ, -1).reshape(seqs * lag, -1)
    ahead = jnp.concatenate([ahead, jnp.zeros_like(ahead)], 0)
    ahead, ffn_terms = lax.optimization_barrier((ahead, ffn_terms))
    one_part, kept, sent = unproject(
        jnp.concatenate([peer, core.reshape(1)]), proj, ahead, taps, qk_back, values_back, gate_back, normed_one, w_in, out_parts, mixed,
        gain_two,
    )

    swapped = lax.ppermute(sent, "seq_2", SWAP)
    mixer_part = (kept.astype(f32) + swapped.astype(f32)).astype(bf16)

    mixer_got = lax.all_to_all(mixer_part, ("seq_0", "seq_1"), 0, 0, tiled=True)
    one_terms = scatter_terms(one_part, mixer_part)
    block_out = lax.all_gather(
        block_outs(peer, ffn_terms, middle, jnp.broadcast_to(keep, (ROWS, LANES))),
        "mp",
        axis=0,
        tiled=True,
    )

    mixer_params = (inproj, inproj_first, inproj_second)
    mixer_params += (outproj.T, outproj_first.T, outproj_second.T)
    mixer_params += (convtaps, convtaps_first, convtaps_second)
    ffn_params = (gateproj, gateproj_first, gateproj_second)
    ffn_params += (upproj, upproj_first, upproj_second)
    ffn_params += (downproj.T, downproj_first.T, downproj_second.T)
    *ffn_moved, ffn_squares = ffn_moments(ffn_sums, ffn_params)
    *moved, sums = moments(mixer_got, place, tiles, ffn_squares, mixer_params)
    moved = moved[:6] + ffn_moved + moved[6:]
    weights_old = mixer_params[0:6:3] + ffn_params[0::3] + mixer_params[6:7]
    token_own = token_grads(peer, one_terms, rows, middle_back, gains)
    back, side = to_neighbours(token_own)
    totals = lax.all_to_all(sums, ALL, 0, 0, tiled=True)
    back, side, _ = lax.optimization_barrier((back, side, sums))
    token_grad = assembled(peer, (token_own, side, back, *passed_on(back, side)))
    *updated, gains_new, gains_moment, gains_square, norms = update(
        rank, totals, states, weights_old, moved[2::3]
    )
    results = [block_out.reshape(tokens.shape), token_grad.reshape(tokens.shape)]
    for index in range(6):
        for value in (updated[index], moved[3 * index], moved[3 * index + 1]):
            results.append(value.T if index in (1, 4) else value)
    results += [gains_new, gains_moment, gains_square, norms]
    return tuple(results)


def solution(mesh):
    split = Mesh(mesh.devices.reshape(4, 4, 2, mesh.shape["mp"]), ("seq_0", "seq_1", "seq_2", "mp"))
    in_specs = (
        P(None, SEQ, None),
        P(None, SEQ, None),
        P(),
        P("mp"),
        P(SEQ, "mp"),
        P(SEQ, "mp"),
        P(SEQ, "mp"),
        P("mp", SEQ),
        P("mp", SEQ),
        P("mp", SEQ),
        P(SEQ, "mp"),
        P(SEQ, "mp"),
        P(SEQ, "mp"),
        P(SEQ, "mp"),
        P(SEQ, "mp"),
        P(SEQ, "mp"),
        P("mp", SEQ),
        P("mp", SEQ),
        P("mp", SEQ),
        P(None, MP_SEQ),
        P(None, MP_SEQ),
        P(None, MP_SEQ),
        P(None, SEQ),
        P(None, SEQ),
        P(None, SEQ),
    )
    out_specs = (
        P(None, SEQ, None),
        P(None, SEQ, None),
        P(SEQ, "mp"),
        P(SEQ, "mp"),
        P(SEQ, "mp"),
        P("mp", SEQ),
        P("mp", SEQ),
        P("mp", SEQ),
        P(SEQ, "mp"),
        P(SEQ, "mp"),
        P(SEQ, "mp"),
        P(SEQ, "mp"),
        P(SEQ, "mp"),
        P(SEQ, "mp"),
        P("mp", SEQ),
        P("mp", SEQ),
        P("mp", SEQ),
        P(None, MP_SEQ),
        P(None, MP_SEQ),
        P(None, MP_SEQ),
        P(None, SEQ),
        P(None, SEQ),
        P(None, SEQ),
        P(),
    )
    return jax.shard_map(
        per_device, mesh=split, in_specs=in_specs, out_specs=out_specs, check_vma=False
    )
```

```python
import math

import jax
import jax.numpy as jnp
from jax import lax
from jax.experimental import pallas as pl
from jax.experimental.pallas import tpu as pltpu
from jax.sharding import Mesh
from jax.sharding import PartitionSpec as P

DH = 112
FEAT = 16
TAPS = 3
STEP = 7
LANES = 128
SEQ = ("seq_0", "seq_1", "seq_2")
ALL = ("seq_0", "seq_1", "seq_2", "mp")
MP_SEQ = ("mp", "seq_0", "seq_1", "seq_2")

f32 = jnp.float32
bf16 = jnp.bfloat16
highest = lax.Precision.HIGHEST
root_half = 0.5**0.5
eps_norm = 1e-05
eps_adam = 1e-06
decay_rate = 0.01
learn_rate = 0.3
beta_value = 0.5

SIDE = [(i, i ^ 1) for i in range(4)]
BACK = [(i, 3 - i) for i in range(4)]
SWAP = [(0, 1), (1, 0)]


def shifted(value, axis, steps):
    count = lax.axis_size(axis)
    first, last = (max(0, -steps), min(count, count - steps))
    return lax.ppermute(value, axis, [(source, source + steps) for source in range(first, last)])


SPAN_LANE = DH
GROUPS = 4
GATE_LANE = DH
GAIN_LANE = DH + 4
TAPS_LANE = DH + 6
GROUP = 256
ROWS = 512
SIDES = 256
PIECE = 40
SLOT = 48
PIECES = 32
MIB = 1 << 20


def selections():
    import numpy as np

    pick = np.zeros((2 * LANES, 2 * SIDES), np.float32)
    ends = np.zeros((8, SIDES), np.float32)
    ends[0, 0] = ends[1, 0] = ends[2, 0] = 1.0
    lane = 1
    for i in range(FEAT):
        pick[i, lane] = 0.5
        ends[1, lane] = ends[2, lane] = 1.0
        lane += 1
    for i in range(FEAT):
        for j in range(i, FEAT):
            pick[i, lane] = 0.5
            pick[j, SIDES + lane] = 0.5
            ends[2, lane] = root_half if i == j else 1.0
            lane += 1
    pick[LANES:] = pick[:LANES]
    return jnp.asarray(pick, bf16), jnp.asarray(ends)


def two_parts(value):
    high = value.astype(bf16)
    return high, (value - high.astype(f32)).astype(bf16)


def three_parts(value):
    high = value.astype(bf16)
    rest = value - high.astype(f32)
    mid = rest.astype(bf16)
    return high, mid, (rest - mid.astype(f32)).astype(bf16)


def product(a, b, contract, passes=3):
    dims = (contract, ((), ()))

    def once(x, y):
        return lax.dot_general(x, y, dims, preferred_element_type=f32)

    if passes == 1:
        return once(a.astype(bf16), b.astype(bf16))
    a_high, a_low = two_parts(a)
    if passes == 2:
        b = b.astype(bf16)
        return once(a_high, b) + once(a_low, b)
    b_high, b_low = two_parts(b)
    return once(a_high, b_high) + (once(a_high, b_low) + once(a_low, b_high))


NN = ((1,), (0,))
NT = ((1,), (1,))
TN = ((0,), (0,))


def lanes_of(shape):
    return lax.broadcasted_iota(jnp.int32, shape, len(shape) - 1)


def rows_of(shape):
    return lax.broadcasted_iota(jnp.int32, shape, 0)


def lower_ones(strict=False):
    row, lane = rows_of((GROUP, GROUP)), lanes_of((GROUP, GROUP))
    return jnp.where(row > lane if strict else row >= lane, 1.0, 0.0).astype(bf16)


def summed_down(ones, value, contract):
    high, mid, low = (
        lax.dot_general(ones, part, (contract, ((), ())), preferred_element_type=f32)
        for part in three_parts(value)
    )
    return low + mid + high


def picked(value, place, contract):
    high, mid, low = (
        lax.dot_general(part, place, (contract, ((), ())), preferred_element_type=f32)
        for part in three_parts(value)
    )
    return low + mid + high


def head_lanes(tile, head, keys):
    first = (4 if keys else 0) * FEAT + head * FEAT
    return pltpu.roll(tile, (LANES - first) % LANES, 1) if first else tile


def factors(moved, pick, ends):
    high, low = two_parts(moved)
    found = lax.dot_general(
        jnp.concatenate([high, low], 1), pick, (NN, ((), ())), preferred_element_type=f32
    )
    return found[:, :SIDES] + ends[0:1], found[:, SIDES:] + ends[1:2]


def factors_back(upstream, one, two, pick, ends):
    scaled = upstream * ends[2:3]
    both = jnp.concatenate([scaled * two, scaled * one], 1)
    return product(both, pick[:LANES], NT, 2)


def scores(tile, head):
    only = lanes_of((GROUP, LANES)) < FEAT
    query = jnp.where(only, head_lanes(tile, head, False), 0.0) * 0.25
    keys = jnp.where(only, head_lanes(tile, head, True), 0.0)
    q_high, k_high = query.astype(bf16), keys.astype(bf16)
    q_wide, k_wide = q_high.astype(f32), k_high.astype(f32)
    q_both = (q_wide + pltpu.roll(query - q_wide, FEAT, 1)).astype(bf16)
    k_both = (pltpu.roll(k_wide, FEAT, 1) + (keys - k_wide)).astype(bf16)
    left = jnp.concatenate([q_high, q_both], 1)
    right = jnp.concatenate([k_high, k_both], 1)
    return lax.dot_general(left, right, (NT, ((), ())), preferred_element_type=f32)


def decays(cum, cum_across, head):
    row, lane = rows_of((GROUP, GROUP)), lanes_of((GROUP, GROUP))
    at = GATE_LANE + head
    diff = cum[:, at : at + 1] - cum_across[at : at + 1, :]
    return jnp.where(row >= lane, jnp.exp(jnp.minimum(diff, 0.0)), 0.0)


def head_column(tile, head):
    at = GATE_LANE + head
    return tile[:, at : at + 1]


def on_head_lane(column, head):
    return jnp.where(lanes_of((column.shape[0], LANES)) == GATE_LANE + head, column, 0.0)


def state_rows(pieces_ref, pair):
    parts = [pieces_ref[4 * pair + q, :PIECE, :].astype(f32) for q in range(4)]
    parts.append(jnp.zeros((SIDES - 4 * PIECE, LANES), f32))
    return jnp.concatenate(parts, 0).astype(bf16)


def store_pieces(ref, pair, state):
    for q in range(4):
        ref[4 * pair + q, :PIECE, :] = state[q * PIECE : (q + 1) * PIECE].astype(bf16)


def whole_call(body, outs, *args, scratch=(), flops=10**9, limit=62, views=None, scalars=0):
    views = views or {}
    shapes = [views.get(i, (a.shape,))[0] for i, a in enumerate(args)]

    def whole(shape, place=None):
        return pl.BlockSpec(shape, lambda i: place or (0,) * len(shape))

    count = sum(math.prod(s) * a.dtype.itemsize for s, a in zip(shapes, args))
    count += sum(math.prod(s) * jnp.dtype(d).itemsize for s, d in outs)
    return pl.pallas_call(
        body,
        grid=(1,),
        out_shape=[jax.ShapeDtypeStruct(s, d) for s, d in outs],
        in_specs=[pl.BlockSpec(memory_space=pltpu.SMEM)] * scalars
        + [whole(s, views.get(i, (s, None))[1]) for i, s in enumerate(shapes) if i >= scalars],
        out_specs=[whole(s) for s, d in outs],
        scratch_shapes=list(scratch),
        compiler_params=pltpu.CompilerParams(vmem_limit_bytes=limit * MIB),
        cost_estimate=pl.CostEstimate(flops=flops, bytes_accessed=count, transcendentals=0),
    )(*args)


def sequence_call(body, outs, *args, halves, flops=10**9):
    def half(shape, columns=None, place=0):
        block = (shape[0] // 2,) + tuple(shape[1:-1]) + (columns or shape[-1],)
        rest = (0,) * (len(shape) - 2) + (place,)
        return pl.BlockSpec(block, lambda i: (i,) + rest)

    def whole(shape):
        return pl.BlockSpec(shape, lambda i: (0,) * len(shape))

    specs = [
        half((ROWS,) + a.shape[1:] if a.ndim == 2 else a.shape, *halves[i])
        if i in halves
        else whole(a.shape)
        for i, a in enumerate(args)
    ]
    return pl.pallas_call(
        body,
        grid=(2,),
        out_shape=[jax.ShapeDtypeStruct(s, d) for s, d in outs],
        in_specs=specs,
        out_specs=[half(s) for s, d in outs],
        compiler_params=pltpu.CompilerParams(vmem_limit_bytes=62 * MIB),
        cost_estimate=pl.CostEstimate(flops=flops, bytes_accessed=4 * 10**6, transcendentals=0),
    )(*args)


def project_kernel(
    core_ref, rows_ref, rim_ref, got_ref, other_ref, rates_ref, pick_ref, ends_ref,
    normed_ref, proj_ref, w_ref, gains_ref, taps_ref, states_ref, values_ref, cum_ref, sent_ref,
    wide_ref,
):
    wide = w_ref.shape[1]
    flipped = core_ref[0] == 1
    taps = jnp.zeros((8, 4 * LANES), f32)
    for r in range(2 * got_ref.shape[0]):
        mine, theirs = got_ref[r // 2].astype(f32), other_ref[r // 2].astype(f32)
        part = jnp.where(flipped, theirs, mine) if r % 2 == 0 else jnp.where(flipped, mine, theirs)
        wide_ref[r * SHARD : (r + 1) * SHARD, :] = part[:SHARD]
        rest = part[SHARD:]
        taps = taps + rest[:, : 4 * LANES]
        whole = rest[:, :LANES] + rest[:, LANES : 2 * LANES] + rest[:, 2 * LANES : 3 * LANES]
        for k in range(3):
            states_ref[k, r : r + 1, :] = whole[TAPS + k : TAPS + k + 1]
    taps_ref[...] = taps
    w_ref[...] = wide_ref[...].astype(bf16)
    chosen = jnp.where(
        lanes_of((16, wide)) == rows_of((16, wide)) + GAIN_LANE, 1.0, 0.0
    )
    chosen = jnp.where(rows_of((16, wide)) < 2, chosen, 0.0).astype(bf16)
    gains = lax.dot_general(chosen, w_ref[...], (NT, ((), ())), preferred_element_type=f32)
    gains_ref[...] = gains[:8]
    gain = gains[0:1]

    def projected(rows):
        rows = rows.astype(f32)
        scale = lax.rsqrt(jnp.mean(rows * rows, -1, keepdims=True) + eps_norm)
        normed = (rows * scale * gain).astype(bf16)
        return normed, jnp.dot(normed, w_ref[...], preferred_element_type=f32)

    for at in range(0, ROWS, GROUP):
        normed, proj = projected(rows_ref[at : at + GROUP, :])
        normed_ref[at : at + GROUP, :] = normed
        proj_ref[at : at + GROUP, :] = proj
    proj_ref[ROWS:, :] = projected(rim_ref[...])[1]
    ones = lower_ones()
    pick, ends = pick_ref[...], ends_ref[...]
    lane, row = lanes_of((GROUP, LANES)), rows_of((GROUP, LANES))
    for s in range(2):
        here = slice(s * GROUP, (s + 1) * GROUP)
        steps = rates_ref[...] * jax.nn.softplus(proj_ref[here, :LANES])
        cum = summed_down(ones, steps, NN)
        cum_ref[here, :] = cum
        last = cum[GROUP - 1 : GROUP, :]
        tail = jnp.exp(last - cum)
        qk = proj_ref[here, 4 * LANES :]
        for h in range(4):
            tile = slice(h * LANES, (h + 1) * LANES)
            raw = proj_ref[here, tile]
            rim_two = proj_ref[ROWS + 2 * s : ROWS + 2 * s + 1, tile]
            rim_one = proj_ref[ROWS + 2 * s + 1 : ROWS + 2 * s + 2, tile]
            one = jnp.where(row == 0, rim_one, pltpu.roll(raw, 1, 0))
            two = jnp.where(row == 0, rim_two, jnp.where(row == 1, rim_one, pltpu.roll(raw, 2, 0)))
            conv = (
                taps_ref[0:1, tile] * raw + taps_ref[1:2, tile] * one + taps_ref[2:3, tile] * two
            )
            values = jnp.where(lane < DH, conv, jnp.where(lane == DH, 1.0, 0.0))
            values_ref[here, tile] = values
            left, right = factors(head_lanes(qk, h, True), pick, ends)
            held = left * right * ends[2:3] * head_column(tail, h)
            fresh = product(held, values, TN)
            store_pieces(sent_ref, 4 * s + h, fresh)
            ending = jnp.broadcast_to(head_column(last, h), (8, LANES))
            high, mid, low = three_parts(ending)
            few = lanes_of((8, LANES))
            packed = jnp.where(
                few == 0,
                high.astype(f32),
                jnp.where(few == 1, mid.astype(f32), jnp.where(few == 2, low.astype(f32), 0.0)),
            ).astype(bf16)
            for q in range(4):
                sent_ref[16 * s + 4 * h + q, PIECE:, :] = packed


def project(core, rows, rim, got, other, rates, pick, ends):
    wide, width = got.shape[2], rows.shape[1]
    return whole_call(
        project_kernel,
        [
            (rows.shape, bf16),
            ((ROWS + rim.shape[0], wide), f32),
            ((width, wide), bf16),
            ((8, width), f32),
            ((8, 4 * LANES), f32),
            ((3, 2 * got.shape[0], LANES), f32),
            ((ROWS, 4 * LANES), f32),
            ((ROWS, LANES), f32),
            ((PIECES, SLOT, LANES), bf16),
        ],
        core, rows, rim, got, other, rates, pick, ends,
        scratch=[pltpu.VMEM((width, wide), f32)],
        flops=3 * 10**9,
        scalars=1,
    )


def scan_kernel(got_ref, back_ref, decay_ref):
    state = jnp.zeros((PIECE, LANES), f32)
    for i in range(PIECES):
        back_ref[i, :PIECE, :] = state.astype(bf16)
        back_ref[i, PIECE:, :] = jnp.zeros((SLOT - PIECE, LANES), bf16)
        ending = jnp.sum(got_ref[i, PIECE:, :].astype(f32), -1, keepdims=True)
        decay = jnp.broadcast_to(jnp.exp(ending), (8, LANES))
        decay_ref[i] = decay
        state = state * decay[0:1] + got_ref[i, :PIECE, :].astype(f32)


def earlier_states(sent):
    got = lax.all_to_all(sent, SEQ, 0, 0, tiled=True)
    back, decay = whole_call(
        scan_kernel, [(sent.shape, bf16), ((PIECES, 8, LANES), f32)], got, flops=10**6
    )
    return lax.all_to_all(back, SEQ, 0, 0, tiled=True), decay


def scan_back_kernel(got_ref, decay_ref, back_ref):
    state = jnp.zeros((PIECE, LANES), f32)
    for i in reversed(range(PIECES)):
        back_ref[i, :PIECE, :] = state.astype(bf16)
        back_ref[i, PIECE:, :] = jnp.zeros((SLOT - PIECE, LANES), bf16)
        state = state * decay_ref[i, 0:1, :] + got_ref[i, :PIECE, :].astype(f32)


def later_states(sent, decay):
    got = lax.all_to_all(sent, SEQ, 0, 0, tiled=True)
    (back,) = whole_call(scan_back_kernel, [(sent.shape, bf16)], got, decay, flops=10**6)
    return lax.all_to_all(back, SEQ, 0, 0, tiled=True), back


QK = ((ROWS, LANES), (0, 4))
FIRST = ((ROWS, LANES), (0, 0))


def within_kernel(qk_ref, values_ref, cum_ref, inside_ref):
    for s in range(2):
        here = slice(s * GROUP, (s + 1) * GROUP)
        cum = cum_ref[here, :]
        across = cum.T
        qk = qk_ref[here, :]
        for h in range(4):
            tile = slice(h * LANES, (h + 1) * LANES)
            dots = scores(qk, h)
            weights = (1.0 + dots + 0.5 * dots * dots) * decays(cum, across, h)
            inside_ref[here, tile] = product(weights, values_ref[here, tile], NN)


def within(proj, values, cum):
    return whole_call(
        within_kernel,
        [((ROWS, 4 * LANES), f32)],
        proj, values, cum,
        flops=3 * 10**9,
        views={0: QK},
    )[0]


def mix_kernel(
    qk_ref, cum_ref, inside_ref, earlier_ref, pick_ref, ends_ref, total_ref, mixed_ref
):
    pick, ends = pick_ref[...], ends_ref[...]
    lane = lanes_of((GROUP, LANES))
    growth = jnp.exp(cum_ref[:, :])
    qk = qk_ref[:, :]
    for h in range(4):
        tile = slice(h * LANES, (h + 1) * LANES)
        left, right = factors(head_lanes(qk, h, False), pick, ends)
        held = left * right * ends[2:3] * head_column(growth, h)
        total = inside_ref[:, tile] + product(held, state_rows(earlier_ref, h), NN, 2)
        total_ref[:, tile] = total
        mixed = total / total[:, DH : DH + 1]
        mixed_ref[:, tile] = jnp.where(lane < DH, mixed, 0.0).astype(bf16)


def mix(proj, cum, inside, earlier, pick, ends):
    return sequence_call(
        mix_kernel,
        [((ROWS, 4 * LANES), f32), ((ROWS, 4 * LANES), bf16)],
        proj, cum, inside, earlier, pick, ends,
        halves={0: (LANES, 4), 1: (), 2: (), 3: ()},
        flops=3 * 10**9,
    )


OWN = ROWS // 4


def own_slice(ref, place):
    return ref[pl.ds(pl.multiple_of(place * OWN, OWN), OWN), :]


def turn_kernel(
    place_ref, got_ref, unit_ref, scale_ref, back_ref, gains_ref, w_ref,
    middle_back_ref, gain_ref, out_back_ref, mixed_back_ref,
):
    two_back = got_ref[...].astype(f32)
    unit = unit_ref[...]
    gain_ref[...] = jnp.broadcast_to(
        jnp.sum(two_back * unit, 0, keepdims=True), gain_ref.shape
    )
    weighted = two_back * gains_ref[1:2]
    along = jnp.mean(weighted * unit, -1, keepdims=True)
    middle_back = own_slice(back_ref, place_ref[0]).astype(f32) + scale_ref[:, 0:1] * (
        weighted - unit * along
    )
    middle_back_ref[...] = middle_back
    out_back = middle_back.astype(bf16)
    out_back_ref[...] = out_back
    for g in range(4):
        mixed_back_ref[g] = jnp.dot(
            out_back, w_ref[:, g * 4 * LANES : (g + 1) * 4 * LANES], preferred_element_type=f32
        ).astype(bf16)


def turn(place, got, unit, scale, back, gains, w_out):
    width = back.shape[1]
    return whole_call(
        turn_kernel,
        [
            ((OWN, width), f32),
            ((8, width), f32),
            ((OWN, width), bf16),
            ((4, OWN, 4 * LANES), bf16),
        ],
        place, got, unit, scale, back, gains, w_out,
        flops=10**9,
        scalars=1,
        views={6: ((width, OUT), (0, 0))},
    )


def token_kernel(place_ref, *refs):
    terms, (rows_ref, middle_back_ref, gains_ref, out_ref) = refs[:3], refs[3:]
    one_back = sum(ref[...].astype(f32) for ref in terms)
    rows = own_slice(rows_ref, place_ref[0]).astype(f32)
    scale = lax.rsqrt(jnp.mean(rows * rows, -1, keepdims=True) + eps_norm)
    unit = rows * scale
    weighted = one_back * gains_ref[0:1]
    along = jnp.mean(weighted * unit, -1, keepdims=True)
    token_back = middle_back_ref[...] + scale * (weighted - unit * along)
    out_ref[...] = token_back.astype(bf16)


def token_grads(place, terms, rows, middle_back, gains):
    return whole_call(
        token_kernel, [(terms[0].shape, bf16)], place, *terms, rows, middle_back, gains,
        flops=10**7,
        scalars=1,
    )[0]


def block_kernel(place_ref, *refs):
    terms, (middle_ref, keep_ref, out_ref) = refs[:3], refs[3:]
    ffn = sum(ref[...].astype(f32) for ref in terms)
    keep = own_slice(keep_ref, place_ref[0])[:, 0:1]
    out_ref[...] = ((middle_ref[...] + ffn) * keep).astype(bf16)


def block_outs(place, terms, middle, keep):
    return whole_call(
        block_kernel, [(terms[0].shape, bf16)], place, *terms, middle, keep,
        flops=10**7,
        scalars=1,
    )[0]


def assemble_kernel(place_ref, own_ref, side_ref, back_ref, far_a_ref, far_b_ref, out_ref):
    place = place_ref[0]
    half = OWN // 2

    def at(other):
        return pl.multiple_of(jnp.bitwise_xor(place, other) * OWN, OWN)

    out_ref[pl.ds(at(0), OWN), :] = own_ref[...]
    out_ref[pl.ds(at(1), OWN), :] = side_ref[...]
    out_ref[pl.ds(at(3), OWN), :] = back_ref[...]
    out_ref[pl.ds(at(2), half), :] = far_a_ref[...]
    out_ref[pl.ds(pl.multiple_of(at(2) + half, half), half), :] = far_b_ref[...]


def to_neighbours(own):
    return lax.ppermute(own, "mp", BACK), lax.ppermute(own, "mp", SIDE)


def passed_on(back, side):
    half = back.shape[0] // 2
    return lax.ppermute(back[:half], "mp", SIDE), lax.ppermute(side[half:], "mp", BACK)


def gather_parts(own):
    back, side = to_neighbours(own)
    return own, side, back, *passed_on(back, side)


def assembled(place, parts):
    own = parts[0]
    return whole_call(
        assemble_kernel, [((ROWS, own.shape[1]), own.dtype)], place, *parts,
        flops=10**6,
        scalars=1,
    )[0]


def scatter_terms(part):
    half = OWN // 2
    got_a = lax.ppermute(part[2, :half], "mp", SIDE)
    got_b = lax.ppermute(part[2, half:], "mp", BACK)
    to_back = jnp.concatenate(
        [(part[3, :half].astype(f32) + got_a.astype(f32)).astype(bf16), part[3, half:]], 0
    )
    to_side = jnp.concatenate(
        [part[1, :half], (part[1, half:].astype(f32) + got_b.astype(f32)).astype(bf16)], 0
    )
    return part[0], lax.ppermute(to_back, "mp", BACK), lax.ppermute(to_side, "mp", SIDE)


def store_by_owner(ref, value, place, columns=slice(None)):
    for g in range(4):
        ref[jnp.bitwise_xor(place, g), :, columns] = value[g * OWN : (g + 1) * OWN]


def unmix_kernel(
    mixed_back_ref, total_ref, qk_ref, cum_ref, pick_ref, ends_ref, total_back_ref, sent_ref
):
    pick, ends = pick_ref[...], ends_ref[...]
    lane = lanes_of((GROUP, LANES))
    growth = jnp.exp(cum_ref[:, :])
    qk = qk_ref[:, :]
    for h in range(4):
        tile = slice(h * LANES, (h + 1) * LANES)
        total = total_ref[:, tile]
        inverse = 1.0 / total[:, DH : DH + 1]
        numer = mixed_back_ref[:, tile].astype(f32) * inverse
        numer = jnp.where(lane < DH, numer, 0.0)
        denom = -jnp.sum(numer * total, -1, keepdims=True) * inverse
        total_back = jnp.where(lane == DH, denom, numer)
        total_back_ref[:, tile] = total_back
        left, right = factors(head_lanes(qk, h, False), pick, ends)
        held = left * right * ends[2:3] * head_column(growth, h)
        store_pieces(sent_ref, h, product(held, total_back, TN))
        for q in range(4):
            sent_ref[4 * h + q, PIECE:, :] = jnp.zeros((SLOT - PIECE, LANES), bf16)


def unmix(mixed_back, total, proj, cum, pick, ends):
    return sequence_call(
        unmix_kernel,
        [((ROWS, 4 * LANES), f32), ((PIECES, SLOT, LANES), bf16)],
        mixed_back, total, proj, cum, pick, ends,
        halves={0: (), 1: (), 2: (LANES, 4), 3: ()},
        flops=3 * 10**9,
    )


def within_back_kernel(
    qk_ref, values_ref, cum_ref, total_back_ref, earlier_ref, pick_ref, ends_ref,
    qk_back_ref, values_back_ref, level_ref,
):
    pick, ends = pick_ref[...], ends_ref[...]
    only = lanes_of((GROUP, LANES)) < FEAT
    cum = cum_ref[:, :]
    across = cum.T
    growth = jnp.exp(cum)
    qk = qk_ref[:, :]
    qk_back = jnp.zeros((GROUP, LANES), f32)
    level = jnp.zeros((GROUP, LANES), f32)
    level_down = jnp.zeros((LANES, GROUP), f32)
    for h in range(4):
        tile = slice(h * LANES, (h + 1) * LANES)
        total_back = total_back_ref[:, tile]
        decay = decays(cum, across, h)
        dots = scores(qk, h)
        pairing = decay * product(total_back, values_ref[:, tile], NT)
        kernel = 1.0 + dots + 0.5 * dots * dots
        moved = kernel * pairing
        down = jnp.sum(moved, 0, keepdims=True)
        level_down = jnp.where(rows_of((LANES, GROUP)) == GATE_LANE + h, down, level_down)
        kernel_back = pairing * (1.0 + dots) * 0.25
        values_back_ref[:, tile] = product(kernel * decay, total_back, TN)
        query_tile = head_lanes(qk, h, False)
        keys_only = jnp.where(only, head_lanes(qk, h, True), 0.0)
        query_only = jnp.where(only, query_tile, 0.0)
        query_back = product(kernel_back, keys_only, NN)
        keys_back = product(kernel_back, query_only, TN)
        left, right = factors(query_tile, pick, ends)
        features_back = head_column(growth, h) * product(
            total_back, state_rows(earlier_ref, h), NT, 2
        )
        level_here = jnp.sum(moved, 1, keepdims=True) + jnp.sum(
            left * right * ends[2:3] * features_back, 1, keepdims=True
        )
        level = level + on_head_lane(level_here, h)
        query_back = query_back + factors_back(features_back, left, right, pick, ends)
        at = h * FEAT
        qk_back = qk_back + (pltpu.roll(query_back, at, 1) if at else query_back)
        qk_back = qk_back + pltpu.roll(keys_back, at + 4 * FEAT, 1)
    qk_back_ref[:, :] = qk_back
    level_ref[:, :] = level - level_down.T


def within_back(s, proj, values, cum, total_back, earlier, pick, ends):
    return whole_call(
        within_back_kernel,
        [((GROUP, LANES), f32), ((GROUP, 4 * LANES), f32), ((GROUP, LANES), f32)],
        proj, values, cum, total_back, earlier, pick, ends,
        flops=4 * 10**9,
        views={
            0: ((GROUP, LANES), (s, 4)),
            1: ((GROUP, 4 * LANES), (s, 0)),
            2: ((GROUP, LANES), (s, 0)),
            3: ((GROUP, 4 * LANES), (s, 0)),
            4: ((PIECES // 2, SLOT, LANES), (s, 0, 0)),
        },
    )


def later_back_kernel(
    qk_ref, first_ref, values_ref, cum_ref, rates_ref, earlier_ref, later_ref, pick_ref, ends_ref,
    qk_in_a_ref, values_in_a_ref, level_a_ref, qk_in_b_ref, values_in_b_ref, level_b_ref,
    qk_back_ref, values_back_ref, gate_back_ref,
):
    pick, ends = pick_ref[...], ends_ref[...]
    ones, before = lower_ones(), lower_ones(True)
    cum = cum_ref[:, :]
    last = cum[GROUP - 1 : GROUP, :]
    tail = jnp.exp(last - cum)
    carried = jnp.exp(last)
    qk = qk_ref[:, :]
    second = pl.program_id(0) == 1

    def either(one_ref, two_ref, columns=slice(None)):
        return jnp.where(second, two_ref[:, columns], one_ref[:, columns])

    qk_back = either(qk_in_a_ref, qk_in_b_ref)
    crossed = jnp.zeros((GROUP, LANES), f32)
    through = jnp.zeros((1, LANES), f32)
    for h in range(4):
        tile = slice(h * LANES, (h + 1) * LANES)
        later = state_rows(later_ref, h)
        left, right = factors(head_lanes(qk, h, True), pick, ends)
        held = left * right * ends[2:3]
        column = head_column(tail, h)
        features_back = column * product(values_ref[:, tile], later, NT, 2)
        values_back_ref[:, tile] = either(values_in_a_ref, values_in_b_ref, tile) + column * product(
            held, later, NN, 2
        )
        crossed = crossed + on_head_lane(
            jnp.sum(held * features_back, 1, keepdims=True), h
        )
        keys_back = factors_back(features_back, left, right, pick, ends)
        qk_back = qk_back + pltpu.roll(keys_back, (h + 4) * FEAT, 1)
        whole = jnp.sum(
            later.astype(f32) * state_rows(earlier_ref, h).astype(f32), 1, keepdims=True
        )
        whole = jnp.sum(whole, 0, keepdims=True) * head_column(carried, h)
        through = through + on_head_lane(whole, h)
    qk_back_ref[:, :] = qk_back
    step_back = (
        summed_down(ones, either(level_a_ref, level_b_ref), TN) + summed_down(before, crossed, NN) + through
    )
    gate_back_ref[:, :] = (
        step_back * rates_ref[...] * jax.nn.sigmoid(first_ref[:, :])
    )


def later_back(proj, values, cum, rates, earlier, later, pick, ends, within):
    return sequence_call(
        later_back_kernel,
        [((ROWS, LANES), f32), ((ROWS, 4 * LANES), f32), ((ROWS, LANES), f32)],
        proj, proj, values, cum, rates, earlier, later, pick, ends, *within,
        halves={0: (LANES, 4), 1: (LANES, 0), 2: (), 3: (), 5: (), 6: ()},
        flops=4 * 10**9,
    )


def unproject_kernel(
    place_ref, proj_ref, ahead_ref, taps_ref, qk_back_ref, values_back_ref, gate_back_ref, normed_ref, w_ref,
    own_ref, side_ref, back_ref, far_a_ref, far_b_ref, mixed_ref, gain_two_ref,
    part_ref, kept_ref, sent_ref,
    taps_grad_ref, taps_across_ref, proj_back_ref, out_back_ref, turned_ref,
):
    @pl.when(pl.program_id(0) == 0)
    def _():
        lane, row = lanes_of((GROUP, LANES)), rows_of((GROUP, LANES))
        taps_grad_ref[...] = jnp.zeros_like(taps_grad_ref)
        for s in range(2):
            here = slice(s * GROUP, (s + 1) * GROUP)
            for h in range(4):
                tile = slice(h * LANES, (h + 1) * LANES)
                raw = proj_ref[here, tile]
                back = values_back_ref[here, tile]
                back = jnp.where(lane < DH, back, 0.0)
                rim_two = proj_ref[ROWS + 2 * s : ROWS + 2 * s + 1, tile]
                rim_one = proj_ref[ROWS + 2 * s + 1 : ROWS + 2 * s + 2, tile]
                one = jnp.where(row == 0, rim_one, pltpu.roll(raw, 1, 0))
                two = jnp.where(row == 0, rim_two, jnp.where(row == 1, rim_one, pltpu.roll(raw, 2, 0)))
                for j, moved in enumerate((raw, one, two)):
                    taps_grad_ref[j : j + 1, tile] = taps_grad_ref[j : j + 1, tile] + jnp.sum(
                        moved * back, 0, keepdims=True
                    )
                next_one = ahead_ref[2 * s : 2 * s + 1, tile]
                next_two = ahead_ref[2 * s + 1 : 2 * s + 2, tile]
                one = jnp.where(row == GROUP - 1, next_one, pltpu.roll(back, GROUP - 1, 0))
                two = jnp.where(
                    row == GROUP - 1,
                    next_two,
                    jnp.where(row == GROUP - 2, next_one, pltpu.roll(back, GROUP - 2, 0)),
                )
                raw_back = (
                    taps_ref[0:1, tile] * back + taps_ref[1:2, tile] * one + taps_ref[2:3, tile] * two
                )
                raw_back = jnp.where(lane < DH, raw_back, 0.0)
                if h == 0:
                    gates = (lane >= GATE_LANE) & (lane < GATE_LANE + 4)
                    raw_back = jnp.where(gates, gate_back_ref[here, :], raw_back)
                proj_back_ref[here, tile] = raw_back.astype(bf16)
            proj_back_ref[here, 4 * LANES :] = qk_back_ref[here, :].astype(bf16)
        for h in range(GROUPS):
            tile = slice(h * LANES, (h + 1) * LANES)
            taps_across_ref[tile, :] = pltpu.roll(
                jnp.concatenate(
                    [taps_grad_ref[:, tile], jnp.zeros((LANES - 8, LANES), f32)], 0
                ).T,
                TAPS_LANE,
                1,
            )
        for k, other in enumerate((0, 1, 3, 2)):
            turned_ref[k * OWN : (k + 1) * OWN] = own_slice(
                mixed_ref, jnp.bitwise_xor(place_ref[0], other)
            )

    part = lax.dot_general(
        proj_back_ref[...], w_ref[...], (NT, ((), ())), preferred_element_type=f32
    ).astype(bf16)
    store_by_owner(part_ref, part, place_ref[0])
    wide = w_ref.shape[1]
    grad_in = lax.dot_general(
        normed_ref[...], proj_back_ref[...], (TN, ((), ())), preferred_element_type=f32
    )
    weights = w_ref[...].astype(f32)
    gain_one = jnp.sum(grad_in * weights, 1, keepdims=True)
    gain_one = gain_one / weights[:, GAIN_LANE : GAIN_LANE + 1]
    gain_two = gain_two_ref[...].T[:, 0:1]
    first = grad_in[:, :LANES]
    spot = lanes_of(first.shape)
    first = jnp.where(
        spot == GAIN_LANE, gain_one, jnp.where(spot == GAIN_LANE + 1, gain_two, first)
    )
    out_back_ref[:OWN] = own_ref[...]
    out_back_ref[OWN : 2 * OWN] = side_ref[...]
    out_back_ref[2 * OWN : 3 * OWN] = back_ref[...]
    out_back_ref[3 * OWN : 3 * OWN + OWN // 2] = far_a_ref[...]
    out_back_ref[3 * OWN + OWN // 2 :] = far_b_ref[...]
    grad_out = lax.dot_general(
        out_back_ref[...], turned_ref[...], (TN, ((), ())), preferred_element_type=f32
    )
    core = place_ref[1]

    each = DH // 8
    few = lanes_of((SHARD, LANES))
    spare = (few >= TAPS_LANE) & (few < TAPS_LANE + TAPS) & (rows_of((SHARD, LANES)) < each)

    def store(ref, parity):
        for k in range(ref.shape[0]):
            r = 2 * k + parity
            here = slice(r * SHARD, (r + 1) * SHARD)
            head = pl.program_id(0) * (GROUPS // 2) + r // 8
            taps = taps_across_ref[pl.ds(pl.multiple_of(head * LANES, LANES), LANES), :]
            at = (r % 8) * each
            taps = pltpu.roll(taps, LANES - at, 0) if at else taps
            ref[k, :, :LANES] = jnp.where(spare, taps[:SHARD], first[here]).astype(bf16)
            ref[k, :, LANES:wide] = grad_in[here, LANES:].astype(bf16)
            ref[k, :, wide:] = grad_out[here].astype(bf16)

    for parity in range(2):

        @pl.when(core == parity)
        def _():
            store(kept_ref, parity)
            store(sent_ref, 1 - parity)


def unproject(
    place, proj, ahead, taps, qk_back, values_back, gate_back, normed, w_in, out_parts, mixed, gain_two
):
    width, wide = w_in.shape
    half, shards = width // 2, width // SHARD // 4
    args = (proj, ahead, taps, qk_back, values_back, gate_back, normed, w_in, *out_parts, mixed)
    args += (gain_two,)

    def whole(shape):
        return pl.BlockSpec(shape, lambda i: (0,) * len(shape))

    specs = [whole(a.shape) for a in args]
    specs[0] = pl.BlockSpec((proj.shape[0], 4 * LANES), lambda i: (0, 0))
    specs[7] = pl.BlockSpec((half, wide), lambda i: (i, 0))
    for k in (6, 8, 9, 10, 11, 12, 14):
        specs[k] = pl.BlockSpec((args[k].shape[0], half), lambda i: (0, i))
    sums = pl.BlockSpec((shards, SHARD, wide + 4 * LANES), lambda i: (i, 0, 0))
    return pl.pallas_call(
        unproject_kernel,
        grid=(2,),
        out_shape=[jax.ShapeDtypeStruct((4, OWN, width), bf16)]
        + [jax.ShapeDtypeStruct((2 * shards, SHARD, wide + 4 * LANES), bf16)] * 2,
        in_specs=[pl.BlockSpec(memory_space=pltpu.SMEM)] + specs,
        out_specs=[pl.BlockSpec((4, OWN, half), lambda i: (0, 0, i)), sums, sums],
        scratch_shapes=[
            pltpu.VMEM((8, 4 * LANES), f32),
            pltpu.VMEM((4 * LANES, LANES), f32),
            pltpu.VMEM((ROWS, wide), bf16),
            pltpu.VMEM((ROWS, half), bf16),
            pltpu.VMEM((ROWS, 4 * LANES), bf16),
        ],
        compiler_params=pltpu.CompilerParams(vmem_limit_bytes=62 * MIB),
        cost_estimate=pl.CostEstimate(
            flops=4 * 10**9, bytes_accessed=16 * 10**6, transcendentals=0
        ),
    )(place, *args)


BLOCK = 256
HIDDEN = 1280
OUT = 16 * LANES
SHARD = 56
SPACED = 64


def middle_kernel(
    place_ref, own_ref, side_ref, back_ref, far_a_ref, far_b_ref, out_ref, rows_ref, gains_ref,
    cotangent_ref, gate_ref, up_ref, down_ref, both_ref,
    middle_ref, unit_ref, scale_ref, normed_ref, acts_ref, two_ref,
    mixed_ref, sum_ref,
):
    place, step = place_ref[0], pl.program_id(0)
    blocks = HIDDEN // BLOCK

    @pl.when(step == 0)
    def _():
        mixed_ref[place] = own_ref[...]
        mixed_ref[jnp.bitwise_xor(place, 1)] = side_ref[...]
        mixed_ref[jnp.bitwise_xor(place, 3)] = back_ref[...]
        mixed_ref[jnp.bitwise_xor(place, 2), :GROUP, :] = far_a_ref[...]
        mixed_ref[jnp.bitwise_xor(place, 2), GROUP:, :] = far_b_ref[...]
        sum_ref[...] = rows_ref[...].astype(f32)

    @pl.when(step < GROUPS)
    def _():
        for at in range(0, out_ref.shape[0], BLOCK):
            here = slice(at, at + BLOCK)
            sum_ref[:, here] += lax.dot_general(
                mixed_ref[step], out_ref[here, :], (NT, ((), ())), preferred_element_type=f32
            )

    @pl.when(step == GROUPS - 1)
    def _():
        for at in range(0, ROWS, OWN):
            here = slice(at, at + OWN)
            middle = sum_ref[here, :]
            scale = lax.rsqrt(jnp.mean(middle * middle, -1, keepdims=True) + eps_norm)
            normed_ref[here, :] = (middle * scale * gains_ref[1:2]).astype(bf16)
        middle = own_slice(sum_ref, place)
        scale = lax.rsqrt(jnp.mean(middle * middle, -1, keepdims=True) + eps_norm)
        middle_ref[...] = middle
        unit_ref[...] = middle * scale
        scale_ref[...] = jnp.broadcast_to(scale, scale_ref.shape)

    @pl.when((step >= GROUPS) & (step < GROUPS + blocks))
    def _():
        normed = normed_ref[...]
        gate = jnp.dot(normed, gate_ref[...], preferred_element_type=f32)
        up = jnp.dot(normed, up_ref[...], preferred_element_type=f32)
        hidden_back = jnp.dot(cotangent_ref[...], down_ref[...], preferred_element_type=f32)
        sigma = jax.nn.sigmoid(gate)
        silu = gate * sigma
        at = pl.multiple_of((step - GROUPS) * BLOCK, BLOCK)
        acts_ref[:, pl.ds(at, BLOCK)] = (
            hidden_back * up * sigma * (1.0 + gate * (1.0 - sigma))
        ).astype(bf16)
        acts_ref[:, pl.ds(HIDDEN + at, BLOCK)] = (hidden_back * silu).astype(bf16)
        acts_ref[:, pl.ds(2 * HIDDEN + at, BLOCK)] = (silu * up).astype(bf16)

    @pl.when(step >= GROUPS + blocks)
    def _():
        two_ref[...] = lax.dot_general(
            acts_ref[:, : 2 * HIDDEN], both_ref[...], (NT, ((), ())), preferred_element_type=f32
        ).astype(bf16)


def middle_both_ways(place, mixed_parts, weights, rows, gains, back):
    width = rows.shape[1]
    blocks, outs = HIDDEN // BLOCK, width // BLOCK
    columns = OUT // GROUPS

    def whole(shape):
        return pl.BlockSpec(shape, lambda i: (0,) * len(shape))

    def clipped(i, first, count):
        return jnp.clip(i - first, 0, count - 1)

    def block_of(which):
        at = OUT // BLOCK + which * blocks
        return pl.BlockSpec((width, BLOCK), lambda i: (0, at + clipped(i, GROUPS, blocks)))

    last = GROUPS + blocks
    specs = [whole(part.shape) for part in mixed_parts]
    specs.append(pl.BlockSpec((width, columns), lambda i: (0, clipped(i, 0, GROUPS))))
    specs += [whole(rows.shape), whole(gains.shape), whole(back.shape)]
    specs += [block_of(0), block_of(1), block_of(2)]
    specs.append(
        pl.BlockSpec(
            (pl.Element(BLOCK), pl.Element(2 * HIDDEN)),
            lambda i: (clipped(i, last, outs) * BLOCK, OUT),
        )
    )
    results = [
        ((OWN, width), f32),
        ((OWN, width), f32),
        ((OWN, LANES), f32),
        ((ROWS, width), bf16),
        ((ROWS, 3 * HIDDEN), bf16),
        ((ROWS, width), bf16),
    ]
    out_specs = [whole(s) for s, d in results]
    out_specs[-1] = pl.BlockSpec((ROWS, BLOCK), lambda i: (0, clipped(i, last, outs)))
    return pl.pallas_call(
        middle_kernel,
        grid=(last + outs,),
        out_shape=[jax.ShapeDtypeStruct(s, d) for s, d in results],
        in_specs=[pl.BlockSpec(memory_space=pltpu.SMEM)] + specs,
        out_specs=out_specs,
        scratch_shapes=[
            pltpu.VMEM((GROUPS, ROWS, columns), bf16),
            pltpu.VMEM((ROWS, width), f32),
        ],
        compiler_params=pltpu.CompilerParams(vmem_limit_bytes=62 * MIB),
        cost_estimate=pl.CostEstimate(
            flops=16 * 10**9, bytes_accessed=40 * 10**6, transcendentals=0
        ),
    )(place, *mixed_parts, weights, rows, gains, back, weights, weights, weights, weights)


def ffn_out_kernel(place_ref, acts_ref, down_ref, out_ref):
    value = lax.dot_general(
        acts_ref[...], down_ref[...], (NT, ((), ())), preferred_element_type=f32
    ).astype(bf16)
    store_by_owner(out_ref, value, place_ref[0])


def ffn_out(place, acts, weights):
    width = weights.shape[0]
    return pl.pallas_call(
        ffn_out_kernel,
        grid=(width // BLOCK,),
        out_shape=jax.ShapeDtypeStruct((4, OWN, width), bf16),
        in_specs=[
            pl.BlockSpec(memory_space=pltpu.SMEM),
            pl.BlockSpec((ROWS, HIDDEN), lambda i: (0, 2)),
            pl.BlockSpec(
                (pl.Element(BLOCK), pl.Element(HIDDEN)), lambda i: (i * BLOCK, OUT + 2 * HIDDEN)
            ),
        ],
        out_specs=pl.BlockSpec((4, OWN, BLOCK), lambda i: (0, 0, i)),
        compiler_params=pltpu.CompilerParams(vmem_limit_bytes=62 * MIB),
        cost_estimate=pl.CostEstimate(
            flops=3 * 10**9, bytes_accessed=8 * 10**6, transcendentals=0
        ),
    )(place, acts, weights)


def ffn_grads_kernel(normed_ref, back_ref, acts_ref, grads_ref):
    def spaced(rows_ref):
        grad = lax.dot_general(
            rows_ref[...], acts_ref[...], (TN, ((), ())), preferred_element_type=f32
        )
        for r in range(grad.shape[0] // SHARD):
            grads_ref[r * SPACED : r * SPACED + SHARD, :] = grad[
                r * SHARD : (r + 1) * SHARD
            ].astype(bf16)
            grads_ref[r * SPACED + SHARD : (r + 1) * SPACED, :] = jnp.zeros(
                (SPACED - SHARD, grad.shape[1]), bf16
            )

    both = pl.program_id(0) < 2 * HIDDEN // WIDER

    @pl.when(both)
    def _():
        spaced(normed_ref)

    @pl.when(jnp.logical_not(both))
    def _():
        spaced(back_ref)


WIDER = 640


def ffn_grads(normed, back, acts):
    width = normed.shape[1]
    whole = pl.BlockSpec((ROWS, width), lambda i: (0, 0))
    return pl.pallas_call(
        ffn_grads_kernel,
        grid=(3 * HIDDEN // WIDER,),
        out_shape=jax.ShapeDtypeStruct((width // SHARD * SPACED, 3 * HIDDEN), bf16),
        in_specs=[whole, whole, pl.BlockSpec((ROWS, WIDER), lambda i: (0, i))],
        out_specs=pl.BlockSpec((width // SHARD * SPACED, WIDER), lambda i: (0, i)),
        compiler_params=pltpu.CompilerParams(vmem_limit_bytes=62 * MIB),
        cost_estimate=pl.CostEstimate(
            flops=7 * 10**9, bytes_accessed=20 * 10**6, transcendentals=0
        ),
    )(normed, back, acts)


def order_columns(heads):
    import numpy as np

    place = np.zeros((5 * LANES, 5 * LANES), np.float32)
    for h in range(heads):
        at = h * (2 * FEAT + DH + 1)
        for i in range(FEAT):
            place[at + i, heads * LANES + h * FEAT + i] = 1.0
            place[at + FEAT + i, heads * LANES + (heads + h) * FEAT + i] = 1.0
        for i in range(DH):
            place[at + 2 * FEAT + i, h * LANES + i] = 1.0
        place[at + 2 * FEAT + DH, GATE_LANE + h] = 1.0
    return jnp.asarray(place, bf16)


def order_heads(heads):
    import numpy as np

    place = np.zeros((heads * DH, heads * LANES), np.float32)
    for h in range(heads):
        for i in range(DH):
            place[h * DH + i, h * LANES + i] = 1.0
    return jnp.asarray(place, bf16)


def prepare_kernel(
    rank_ref, in_ref, out_ref, gate_ref, up_ref, down_ref, taps_ref,
    gains_ref, gains_first_ref, gains_second_ref, place_ref, tiles_ref,
    shard_ref, out_shard_ref, rest_ref, few_ref,
):
    wide = 5 * LANES
    columns = in_ref.shape[1]
    whole = jnp.dot(
        in_ref[...].astype(bf16), place_ref[:columns, :], preferred_element_type=f32
    )
    spot = jnp.where(
        lanes_of((2, wide)) == rows_of((2, wide)) + GAIN_LANE, 1.0, 0.0
    ).astype(bf16)
    gains = lax.dot_general(
        gains_ref[...].astype(bf16), spot, (TN, ((), ())), preferred_element_type=f32
    )
    for k in range(shard_ref.shape[0]):
        shard_ref[k, :SHARD, :] = (whole + gains).astype(bf16)
    rank = rank_ref[0]
    own = taps_ref.shape[1]
    each = DH // own
    first = (rank // each) * LANES + (rank % each) * own
    spot = jnp.where(
        lanes_of((own, wide)) == rows_of((own, wide)) + first, 1.0, 0.0
    ).astype(bf16)
    taps = jnp.dot(taps_ref[...].astype(bf16), spot, preferred_element_type=f32)
    rows = [taps]
    for ref in (gains_ref, gains_first_ref, gains_second_ref):
        few_ref[...] = jnp.zeros_like(few_ref)
        few_ref[0:2, :SHARD] = ref[...]
        both = few_ref[...]
        line = both + pltpu.roll(pltpu.roll(both, SHARD, 1), 7, 0)
        parts = [part.astype(f32)[0:1] for part in three_parts(line)]
        rows.append(jnp.concatenate(parts + [jnp.zeros((1, wide - 3 * LANES), f32)], 1))
    rows.append(jnp.zeros((SPACED - SHARD - TAPS - 3, wide), f32))
    for k in range(shard_ref.shape[0]):
        shard_ref[k, SHARD:, :] = jnp.concatenate(rows, 0).astype(bf16)
    out_shard_ref[...] = jnp.dot(
        out_ref[...].astype(bf16), tiles_ref[...], preferred_element_type=f32
    ).astype(bf16)
    rest_ref[...] = jnp.zeros_like(rest_ref)
    units = gate_ref.shape[1]
    rest_ref[:, :units] = gate_ref[...].astype(bf16)
    rest_ref[:, HIDDEN : HIDDEN + units] = up_ref[...].astype(bf16)
    rest_ref[:, 2 * HIDDEN : 2 * HIDDEN + units] = down_ref[...].astype(bf16)


def prepare(rank, *args):
    return whole_call(
        prepare_kernel,
        [
            ((16, SPACED, 5 * LANES), bf16),
            ((SHARD, 4 * LANES), bf16),
            ((SHARD, 3 * HIDDEN), bf16),
        ],
        rank, *args,
        scratch=[pltpu.VMEM((8, LANES), f32)],
        scalars=1,
    )


def moved_moments(weight, first, second, grad):
    fix = 1.0 - beta_value**STEP
    moment = beta_value * first + (1.0 - beta_value) * grad
    square = beta_value * second + (1.0 - beta_value) * grad * grad
    direction = moment / fix / (jnp.sqrt(square / fix) + eps_adam) + decay_rate * weight
    return moment, square, direction


def adapted(params, outs, place, grad):
    weight = params[0][...]
    moment, square, direction = moved_moments(weight, params[1][...], params[2][...], grad)
    outs[0][...] = moment
    outs[1][...] = square
    outs[2][...] = direction
    both = [
        jnp.sum(jnp.sum(v * v, 1, keepdims=True), 0, keepdims=True) for v in (weight, direction)
    ]
    lane = lanes_of((1, LANES))
    return jnp.where(lane == place, both[0], jnp.where(lane == place + 1, both[1], 0.0))


def ffn_moments_kernel(ffn_ref, *refs):
    params, outs, sums_ref = refs[:9], refs[9:-1], refs[-1]
    units = params[0].shape[1]
    sums = jnp.zeros((1, LANES), f32)
    for k in range(3):
        grad = ffn_ref[:SHARD, k * HIDDEN : k * HIDDEN + units].astype(f32)
        three = slice(3 * k, 3 * k + 3)
        sums = sums + adapted(params[three], outs[three], 4 + 2 * k, grad)
    sums_ref[...] = jnp.broadcast_to(sums, sums_ref.shape)


def ffn_moments(ffn, params):
    outs = [(param.shape, f32) for param in params]
    return whole_call(ffn_moments_kernel, outs + [((8, LANES), f32)], ffn, *params)


def moments_kernel(mixer_ref, place_ref, tiles_ref, ffn_sums_ref, *refs):
    params, outs, sums_ref = refs[:9], refs[9:-1], refs[-1]

    wide = 5 * LANES
    mixer = mixer_ref[0].astype(f32)
    for k in range(1, mixer_ref.shape[0]):
        mixer = mixer + mixer_ref[k].astype(f32)
    sums = ffn_sums_ref[0:1, :]
    grad_in = picked(mixer[:, :wide], place_ref[...], NT)
    sums = sums + adapted(params[0:3], outs[0:3], 0, grad_in[:, : params[0].shape[1]])
    sums = sums + adapted(params[3:6], outs[3:6], 2, picked(mixer[:, wide:], tiles_ref[...], NT))
    across = jnp.concatenate([mixer[:, :LANES], jnp.zeros((LANES - SHARD, LANES), f32)], 0).T
    taps = across[TAPS_LANE : TAPS_LANE + TAPS, : params[6].shape[1]]
    sums = sums + adapted(params[6:9], outs[6:9], 10, taps)
    ones = across[GAIN_LANE : GAIN_LANE + 1]
    twos = across[GAIN_LANE + 1 : GAIN_LANE + 2]
    few = lanes_of((1, LANES))
    line = jnp.where(few < SHARD, ones, 0.0) + pltpu.roll(
        jnp.broadcast_to(jnp.where(few < SHARD, twos, 0.0), (8, LANES)), SHARD, 1
    )[0:1]
    both = jnp.concatenate([sums, line], 1)
    sums_ref[...] = jnp.broadcast_to(both[None], sums_ref.shape)


def moments(mixer, place, tiles, ffn_sums, params):
    outs = [(param.shape, f32) for param in params] + [((LANES, 1, 2 * LANES), f32)]
    return whole_call(
        moments_kernel, outs, mixer, place, tiles, ffn_sums, *params
    )


def update_kernel(rank_ref, totals_ref, states_ref, *refs):
    weights, directions, outs = refs[:6], refs[6:12], refs[12:18]
    gains_refs, norms_ref = refs[18:21], refs[21]
    totals = totals_ref[:, 0, :]
    sums = jnp.sum(totals[:, :LANES], 0, keepdims=True)
    lane = lanes_of((1, LANES))
    grouped = jnp.where(
        lanes_of((32, LANES)) // 4 == rows_of((32, LANES)), 1.0, 0.0
    ).astype(bf16)
    grad = summed_down(grouped, totals[:, LANES:], NN)
    moment, square, direction = moved_moments(
        states_ref[0], states_ref[1], states_ref[2], grad
    )
    live = lanes_of((32, LANES)) < 2 * SHARD
    for place, value in ((12, states_ref[0]), (13, direction)):
        value = jnp.where(live, value, 0.0)
        value = jnp.sum(jnp.sum(value * value, 1, keepdims=True), 0, keepdims=True)
        sums = jnp.where(lane == place, value, sums)
    norms = jnp.sqrt(sums)
    each = [
        jnp.sum(
            jnp.where(lanes_of((8, LANES)) == 2 * rows_of((8, LANES)) + k, norms, 0.0),
            1,
            keepdims=True,
        )
        for k in range(2)
    ]
    norms_ref[...] = jnp.where(lanes_of((8, 2)) == 0, each[0], each[1])[:7]

    def ratio(index):
        return norms[:, 2 * index : 2 * index + 1] / norms[:, 2 * index + 1 : 2 * index + 2]

    for index in range(6):
        outs[index][...] = (
            weights[index][...] - learn_rate * ratio(index) * directions[index][...]
        )
    updated = states_ref[0] - learn_rate * ratio(6) * direction
    for ref, value in zip(gains_refs, (updated, moment, square)):
        own = jnp.where(rows_of((32, LANES)) == rank_ref[0], value, 0.0)
        own = jnp.broadcast_to(jnp.sum(own, 0, keepdims=True), (8, LANES))
        ref[0:1, :] = own[0:1, :SHARD]
        ref[1:2, :] = pltpu.roll(own, LANES - SHARD, 1)[0:1, :SHARD]


def update(rank, totals, states, weights, directions):
    outs = [(w.shape, f32) for w in weights] + [((2, SHARD), f32)] * 3 + [((7, 2), f32)]
    return whole_call(
        update_kernel, outs, rank, totals, states, *weights, *directions, scalars=1
    )


def per_device(
    tokens,
    cotangent,
    lengths,
    rate_codes,
    inproj,
    inproj_first,
    inproj_second,
    outproj,
    outproj_first,
    outproj_second,
    gateproj,
    gateproj_first,
    gateproj_second,
    upproj,
    upproj_first,
    upproj_second,
    downproj,
    downproj_first,
    downproj_second,
    convtaps,
    convtaps_first,
    convtaps_second,
    normgains,
    normgains_first,
    normgains_second,
):
    seqs, group, width = tokens.shape
    heads = rate_codes.shape[0]
    lag = TAPS - 1
    rank = lax.axis_index(SEQ).reshape(1)
    core = lax.axis_index("seq_2")
    peer = lax.axis_index("mp").reshape(1)
    pick, ends = selections()
    place, tiles = order_columns(heads), order_heads(heads)

    shards, out_shard, rest_shard = prepare(
        rank, inproj, outproj.T, gateproj, upproj, downproj.T, convtaps,
        normgains, normgains_first, normgains_second, place, tiles,
    )
    got = lax.all_to_all(shards, ("seq_0", "seq_1"), 0, 0, tiled=True)
    other = lax.ppermute(got, "seq_2", SWAP)
    low, high = peer[0] % 2, peer[0] // 2

    def beside(mine, theirs, bit):
        return jnp.where(
            bit == 0, jnp.concatenate([mine, theirs], 1), jnp.concatenate([theirs, mine], 1)
        )

    out_pair = beside(out_shard, lax.ppermute(out_shard, "mp", SIDE), low)
    out_shards = beside(out_pair, lax.ppermute(out_pair, "mp", BACK), high)
    weights_shard = jnp.concatenate([out_shards, rest_shard], 1)
    weights_shard, got = lax.optimization_barrier((weights_shard, got))
    weights = lax.all_gather(weights_shard, SEQ, axis=0, tiled=True)

    rows = tokens.reshape(-1, width)
    rim = shifted(tokens[:, group - lag :], SEQ, 1).reshape(-1, width)
    rim = jnp.pad(rim, ((0, 16 - seqs * lag), (0, 0)))
    positions = rank * group + jnp.arange(group, dtype=jnp.int32)
    keep = (positions[None, :] < lengths[:, None]).astype(f32).reshape(-1, 1)
    back = (cotangent.reshape(-1, width).astype(f32) * keep).astype(bf16)
    rates = -jnp.exp2(-rate_codes.astype(f32) / 4.0)
    rates = jnp.pad(rates[None], ((0, 0), (GATE_LANE, LANES - GATE_LANE - heads)))
    normed_one, proj, w_in, gains, taps, states, values, cum, sent = project(
        core.reshape(1), rows, rim, got, other, rates, pick, ends
    )
    earlier, decay = earlier_states(sent)
    inside = within(proj, values, cum)
    total, mixed = mix(proj, cum, inside, earlier, pick, ends)

    middle, unit_two, scale_two, normed_two, acts, two_part = middle_both_ways(
        peer, gather_parts(mixed), weights, rows, gains, back
    )
    two_back = lax.psum_scatter(two_part, "mp", scatter_dimension=0, tiled=True)
    ffn_part = ffn_out(peer, acts, weights)
    two_back, ffn_part = lax.optimization_barrier((two_back, ffn_part))
    ffn_sums = lax.psum_scatter(
        ffn_grads(normed_two, back, acts), SEQ, scatter_dimension=0, tiled=True
    )
    middle_back, gain_two, out_own, mixed_back = turn(
        peer, two_back, unit_two, scale_two, back, gains, weights
    )
    mixed_back = lax.all_to_all(mixed_back, "mp", 0, 0, tiled=True).reshape(ROWS, -1)

    total_back, sent = unmix(mixed_back, total, proj, cum, pick, ends)
    ffn_part, out_own, sent = lax.optimization_barrier((ffn_part, out_own, sent))
    later, summed = later_states(sent, decay)
    within_a = within_back(0, proj, values, cum, total_back, earlier, pick, ends)
    total_back, _ = lax.optimization_barrier((total_back, summed))
    within_b = within_back(1, proj, values, cum, total_back, earlier, pick, ends)
    out_parts = gather_parts(out_own)
    ffn_terms = scatter_terms(ffn_part)
    qk_back, values_back, gate_back = later_back(
        proj, values, cum, rates, earlier, later, pick, ends, within_a + within_b
    )
    edge = values_back.reshape(seqs, group, -1)[:, :lag]
    ahead = shifted(edge, SEQ, -1).reshape(seqs * lag, -1)
    ahead = jnp.concatenate([ahead, jnp.zeros_like(ahead)], 0)
    ahead, ffn_terms = lax.optimization_barrier((ahead, ffn_terms))
    one_part, kept, sent = unproject(
        jnp.concatenate([peer, core.reshape(1)]), proj, ahead, taps, qk_back, values_back, gate_back, normed_one, w_in, out_parts, mixed,
        gain_two,
    )

    swapped = lax.ppermute(sent, "seq_2", SWAP)
    mixer_part = (kept.astype(f32) + swapped.astype(f32)).astype(bf16)

    one_part, mixer_part = lax.optimization_barrier((one_part, mixer_part))
    mixer_got = lax.all_to_all(mixer_part, ("seq_0", "seq_1"), 0, 0, tiled=True)
    one_terms = scatter_terms(one_part)
    block_out = lax.all_gather(
        block_outs(peer, ffn_terms, middle, jnp.broadcast_to(keep, (ROWS, LANES))),
        "mp",
        axis=0,
        tiled=True,
    )

    mixer_params = (inproj, inproj_first, inproj_second)
    mixer_params += (outproj.T, outproj_first.T, outproj_second.T)
    mixer_params += (convtaps, convtaps_first, convtaps_second)
    ffn_params = (gateproj, gateproj_first, gateproj_second)
    ffn_params += (upproj, upproj_first, upproj_second)
    ffn_params += (downproj.T, downproj_first.T, downproj_second.T)
    *ffn_moved, ffn_squares = ffn_moments(ffn_sums, ffn_params)
    *moved, sums = moments(mixer_got, place, tiles, ffn_squares, mixer_params)
    moved = moved[:6] + ffn_moved + moved[6:]
    weights_old = mixer_params[0:6:3] + ffn_params[0::3] + mixer_params[6:7]
    token_own = token_grads(peer, one_terms, rows, middle_back, gains)
    back, side = to_neighbours(token_own)
    totals = lax.all_to_all(sums, ALL, 0, 0, tiled=True)
    back, side, _ = lax.optimization_barrier((back, side, totals))
    token_grad = assembled(peer, (token_own, side, back, *passed_on(back, side)))
    *updated, gains_new, gains_moment, gains_square, norms = update(
        rank, totals, states, weights_old, moved[2::3]
    )
    results = [block_out.reshape(tokens.shape), token_grad.reshape(tokens.shape)]
    for index in range(6):
        for value in (updated[index], moved[3 * index], moved[3 * index + 1]):
            results.append(value.T if index in (1, 4) else value)
    results += [gains_new, gains_moment, gains_square, norms]
    return tuple(results)


def solution(mesh):
    split = Mesh(mesh.devices.reshape(4, 4, 2, mesh.shape["mp"]), ("seq_0", "seq_1", "seq_2", "mp"))
    in_specs = (
        P(None, SEQ, None),
        P(None, SEQ, None),
        P(),
        P("mp"),
        P(SEQ, "mp"),
        P(SEQ, "mp"),
        P(SEQ, "mp"),
        P("mp", SEQ),
        P("mp", SEQ),
        P("mp", SEQ),
        P(SEQ, "mp"),
        P(SEQ, "mp"),
        P(SEQ, "mp"),
        P(SEQ, "mp"),
        P(SEQ, "mp"),
        P(SEQ, "mp"),
        P("mp", SEQ),
        P("mp", SEQ),
        P("mp", SEQ),
        P(None, MP_SEQ),
        P(None, MP_SEQ),
        P(None, MP_SEQ),
        P(None, SEQ),
        P(None, SEQ),
        P(None, SEQ),
    )
    out_specs = (
        P(None, SEQ, None),
        P(None, SEQ, None),
        P(SEQ, "mp"),
        P(SEQ, "mp"),
        P(SEQ, "mp"),
        P("mp", SEQ),
        P("mp", SEQ),
        P("mp", SEQ),
        P(SEQ, "mp"),
        P(SEQ, "mp"),
        P(SEQ, "mp"),
        P(SEQ, "mp"),
        P(SEQ, "mp"),
        P(SEQ, "mp"),
        P("mp", SEQ),
        P("mp", SEQ),
        P("mp", SEQ),
        P(None, MP_SEQ),
        P(None, MP_SEQ),
        P(None, MP_SEQ),
        P(None, SEQ),
        P(None, SEQ),
        P(None, SEQ),
        P(),
    )
    return jax.shard_map(
        per_device, mesh=split, in_specs=in_specs, out_specs=out_specs, check_vma=False
    )
```
